32 devices in a mesh: dp: 8 (over z, y), mp: 4 (over x, core).
Axes of the slice: x: 2, y: 2, z: 4, core: 2. Of those that a mesh axis runs over, the one named last changes fastest.
Arguments:
- layer_input: float32 [16, 1024, 512], P('dp', 'mp'), may hold values from -6 to 6
- qkv_weight: bfloat16 [512, 1536], replicated, may hold values from -0.25 to 0.25
- gate_weight: bfloat16 [512, 8], replicated, may hold values from -0.25 to 0.25
- gate_bias: float32 [8], replicated, may hold values from 2.9 to 7.5
- out_weight: bfloat16 [512, 512], replicated, may hold values from -0.75 to 0.75
- inner_weight: bfloat16 [512, 2048], P(None, 'mp'), may hold values from -0.25 to 0.25
- outer_weight: bfloat16 [2048, 512], P('mp'), may hold values from -0.125 to 0.125
- leading_norm_gain: float32 [512], replicated, may hold values from 0.1 to 1.9
- leading_norm_bias: float32 [512], replicated, may hold values from -3 to 3
- trailing_norm_gain: float32 [512], replicated, may hold values from 0.1 to 1.9
- trailing_norm_bias: float32 [512], replicated, may hold values from -3 to 3
- random_features: float32 [8, 64, 128], replicated, may hold values from -0.5 to 0.5
- output_grad: float32 [16, 1024, 512], P('dp', 'mp'), may hold values from -6 to 6
Outputs:
- layer_out: float32 [16, 1024, 512], P('dp', 'mp')
- layer_input_gradient: float32 [16, 1024, 512], P('dp', 'mp')
- qkv_weight_grad: float32 [512, 1536], replicated
- gate_weight_grad: float32 [512, 8], replicated
- gate_bias_grad: float32 [8], replicated
- out_weight_grad: float32 [512, 512], replicated
- inner_weight_grad: float32 [512, 2048], P(None, 'mp')
- outer_weight_grad: float32 [2048, 512], P('mp')
- leading_norm_gain_gradient: float32 [512], replicated
- first_shift_grad: float32 [512], replicated
- trailing_norm_gain_gradient: float32 [512], replicated
- second_shift_grad: float32 [512], replicated
The draws below stay inside these ranges and needn't reach their ends.
All inputs are finite; a program needn't handle non-finite values.
Results may differ from the reference program's by a relative error of at most 0.0066.
Values may be sent and summed in bfloat16 or wider, within the bound.
No kernel may reach another device: no remote copies, remote signals or barrier semaphores. Data moves between devices by JAX's collectives and lax.ppermute only.
A program may use at most 128 MiB of HBM per device.

```python
import math
import jax
import jax.numpy as jnp
from jax import lax

D = 512
HEADS = 8
HEAD = 64
FEAT = 128
FF = 2048
LENGTH = 1024
BATCH = 16
N_MP = 4


def draw_gate_bias(key, part):
    key = jax.random.fold_in(key, 11)
    pick_key, offset_key = jax.random.split(key)
    share = 0.5
    slowly = jax.random.uniform(pick_key, (HEADS,)) < share
    offset = jax.random.uniform(offset_key, (HEADS,), minval=-0.5, maxval=0.5)
    slow_value = math.log(LENGTH) + offset
    fast_value = 3.6 + 0.6 * offset
    return jnp.where(slowly, slow_value, fast_value).astype(jnp.float32)


def block_levels(stream_key, shape, cuts, smallest, top_value):
    level, own = 1.0, jax.random.fold_in(stream_key, 6)
    for axis_at, parts in cuts:
        steps = jnp.exp(jax.random.uniform(jax.random.fold_in(own, axis_at), (parts,), jnp.float32, smallest / len(cuts), top_value / len(cuts)))
        level = level * jnp.repeat(steps, shape[axis_at] // parts).reshape([-1 if axis == axis_at else 1 for axis in range(len(shape))])
    return level


def scatter_about(own_key, shape, scale, limit, cuts=(), held_as=jnp.bfloat16):
    gain = block_levels(own_key, shape, cuts, -0.22, 0.18) if cuts else 1.0
    entries = jax.random.normal(own_key, shape, jnp.float32) * scale * gain
    return jnp.minimum(jnp.maximum(entries, -limit), limit).astype(held_as)


def setup_inputs(seed: int = 0) -> dict:
    seeds = jax.random.split(jax.random.key(seed), 14)
    return {
        "layer_input": scatter_about(seeds[0], (BATCH, LENGTH, D), 1.0, 6.0, ((0, 8), (1, 4)), jnp.float32),
        "qkv_weight": scatter_about(seeds[1], (D, 3 * D), D ** -0.5, 0.25),
        "gate_weight": scatter_about(seeds[2], (D, HEADS), D ** -0.5, 0.25),
        "gate_bias": draw_gate_bias(jax.random.fold_in(seeds[13], 71), 0),
        "out_weight": scatter_about(seeds[4], (D, D), (D // 8) ** -0.5, 0.75),
        "inner_weight": scatter_about(seeds[5], (D, FF), D ** -0.5, 0.25, ((1, 4),)),
        "outer_weight": scatter_about(seeds[6], (FF, D), FF ** -0.5, 0.125, ((0, 4),)),
        "leading_norm_gain": jnp.clip(1.0 + 0.18 * jax.random.normal(seeds[7], (D,), jnp.float32), 0.1, 1.9),
        "leading_norm_bias": scatter_about(seeds[8], (D,), 0.5, 3.0, (), jnp.float32),
        "trailing_norm_gain": jnp.clip(1.0 + 0.18 * jax.random.normal(seeds[9], (D,), jnp.float32), 0.1, 1.9),
        "trailing_norm_bias": scatter_about(seeds[10], (D,), 0.5, 3.0, (), jnp.float32),
        "random_features": scatter_about(seeds[11], (HEADS, HEAD, FEAT), (2 * HEAD) ** -0.5, 0.5, (), jnp.float32),
        "output_grad": scatter_about(seeds[12], (BATCH, LENGTH, D), 1.0, 6.0, ((0, 8), (1, 4)), jnp.float32),
    }


@jax.custom_vjp
def low(v):
    return lax.optimization_barrier(v.astype(jnp.bfloat16)).astype(jnp.float32)

@jax.custom_vjp
def low_back(v):
    return v

def low_keep(v):
    return (low(v), None)

def low_pass(kept, upstream_gradient):
    return (upstream_gradient,)

def back_keep(v):
    return (v, None)

def back_low(kept, upstream_gradient):
    return (low(upstream_gradient),)
low.defvjp(low_keep, low_pass)
low_back.defvjp(back_keep, back_low)
exact = lax.Precision.HIGHEST
epsilon = 1e-05
guard = 0.01

def normalize(token_row_values, norm_gain, shift):
    centred = token_row_values - lax.optimization_barrier(jnp.mean(token_row_values, axis=-1, keepdims=True))
    spread = lax.optimization_barrier(jnp.mean(centred * centred, axis=-1, keepdims=True))
    return centred * lax.rsqrt(spread + epsilon) * norm_gain + shift

def features(values, frequencies):
    angles = jnp.einsum('...hd,hdf->...hf', values, frequencies, precision=exact)
    return jnp.concatenate([jnp.sin(angles), jnp.cos(angles)], axis=-1) / math.sqrt(frequencies.shape[-1])

def block_parts(phi_query, phi_keys, values, log_keep, admit):
    length = log_keep.shape[1]
    cumul = jnp.cumsum(jnp.swapaxes(log_keep, 1, 2), axis=-1)
    admit_t = jnp.swapaxes(admit, 1, 2)
    rowid = lax.broadcasted_iota(jnp.int32, (length, length), 0)
    colid = lax.broadcasted_iota(jnp.int32, (length, length), 1)
    causal = rowid >= colid
    gap = cumul[..., :, None] - cumul[..., None, :]
    decay = jnp.where(causal, jnp.exp(jnp.where(causal, gap, 0.0)), 0.0)
    weights = decay * admit_t[..., None, :]
    kernel = jnp.einsum('sthf,suhf->shtu', phi_query, phi_keys, precision=exact)
    scores = kernel * weights
    inner_num = jnp.einsum('shtu,suhd->sthd', scores, values, precision=exact)
    inner_den = jnp.swapaxes(lax.optimization_barrier(jnp.sum(scores, axis=-1)), 1, 2)
    total = cumul[..., -1]
    carried = jnp.exp(total)
    tail = jnp.exp(total[..., None] - cumul) * admit_t
    scaled = phi_keys * jnp.swapaxes(tail, 1, 2)[..., None]
    state_part = jnp.einsum('suhf,suhd->shfd', scaled, values, precision=exact)
    norm_part = lax.optimization_barrier(jnp.sum(scaled, axis=1))
    return (cumul, inner_num, inner_den, carried, state_part, norm_part)

def block_finish(phi_query, cumul, inner_num, inner_den, state, norm):
    growth = jnp.exp(jnp.swapaxes(cumul, 1, 2))
    numer = growth[..., None] * jnp.einsum('sthf,shfd->sthd', phi_query, state, precision=exact) + inner_num
    sden = growth * jnp.einsum('sthf,shf->sth', phi_query, norm, precision=exact) + inner_den
    denom = jnp.sqrt(sden * sden + guard)
    return (numer / denom[..., None], numer, denom, sden, growth)

def attend(phi_query, phi_keys, values, log_keep, admit):
    pieces = N_MP

    def split(block):
        return block.reshape((pieces, 1, block.shape[0] // pieces) + block.shape[1:])

    def advance(carry, block):
        state, norm = carry
        part_q, part_k, part_v, part_l, part_a = block
        cumul, inner_num, inner_den, carried, state_part, norm_part = block_parts(part_q, part_k, part_v, part_l, part_a)
        mixed = block_finish(part_q, cumul, inner_num, inner_den, state, norm)[0]
        state = carried[..., None, None] * state + state_part
        norm = carried[..., None] * norm + norm_part
        return ((state, norm), mixed)
    heads = phi_query.shape[1]
    start = (jnp.zeros((1, heads, phi_query.shape[2], values.shape[2]), jnp.float32), jnp.zeros((1, heads, phi_query.shape[2]), jnp.float32))
    blocks = (split(phi_query), split(phi_keys), split(values), split(log_keep), split(admit))
    _, mixed = lax.scan(jax.checkpoint(advance), start, blocks)
    return mixed.reshape(values.shape)

def layer_sequence(sequence, trained, frequencies):
    qkv_w, gate_w, gate_b, out_w, inner_w, outer_w, gain_one, shift_one, gain_two, shift_two = trained
    width = sequence.shape[-1]
    heads = gate_w.shape[1]
    head = width // heads
    leading_normalized = low(normalize(sequence, gain_one, shift_one))
    proj = low_back(jnp.dot(leading_normalized, qkv_w, precision=exact))
    logit = low_back(jnp.dot(leading_normalized, gate_w, precision=exact) + gate_b)
    query = proj[:, :width].reshape(-1, heads, head)
    keys = proj[:, width:2 * width].reshape(-1, heads, head)
    values = proj[:, 2 * width:].reshape(-1, heads, head)
    mixed = attend(features(query, frequencies), features(keys, frequencies), values, jax.nn.log_sigmoid(logit), jax.nn.sigmoid(-logit))
    mixed_low = low(mixed.reshape(-1, width))
    residual_stream = sequence + low_back(jnp.dot(mixed_low, out_w, precision=exact))
    trailing_normalized = low(normalize(residual_stream, gain_two, shift_two))
    pre = low_back(jnp.dot(trailing_normalized, inner_w, precision=exact))
    active = low(jax.nn.gelu(pre))
    return residual_stream + low_back(jnp.dot(active, outer_w, precision=exact))

def reference(layer_input, qkv_weight, gate_weight, gate_bias, out_weight, inner_weight, outer_weight, leading_norm_gain, leading_norm_bias, trailing_norm_gain, trailing_norm_bias, random_features, output_grad):
    frequencies = random_features.astype(jnp.float32)
    trained = tuple((item.astype(jnp.float32) for item in (qkv_weight, gate_weight, gate_bias, out_weight, inner_weight, outer_weight, leading_norm_gain, leading_norm_bias, trailing_norm_gain, trailing_norm_bias)))
    per_sequence = jax.checkpoint(layer_sequence)

    def forward(inputs, *weights):
        return lax.map(lambda sequence: per_sequence(sequence, weights, frequencies), inputs)
    layer_out, pullback = jax.vjp(forward, layer_input.astype(jnp.float32), *trained)
    grads = pullback(output_grad.astype(jnp.float32))
    return (layer_out, grads[0], grads[1], grads[2], grads[3], grads[4], grads[5], grads[6], grads[7], grads[8], grads[9], grads[10])
```

```python
import math

import jax
import jax.numpy as jnp
from jax import lax
from jax.experimental import pallas as pl
from jax.experimental.pallas import tpu as pltpu
from jax.sharding import PartitionSpec as P

BF = jnp.bfloat16
F32 = jnp.float32
epsilon = 1e-05
guard = 0.01
LANES = 128
EXTRA = 16
VMEM_BYTES = 56 * 1024 * 1024


def nn(a, b):
    return lax.dot_general(a, b, (((1,), (0,)), ((), ())), preferred_element_type=F32)


def nt(a, b):
    return lax.dot_general(a, b, (((1,), (1,)), ((), ())), preferred_element_type=F32)


def tn(a, b):
    return lax.dot_general(a, b, (((0,), (0,)), ((), ())), preferred_element_type=F32)


def two_terms(v):
    high = v.astype(BF)
    return high, (v - high.astype(F32)).astype(BF)


def iota(shape, dim):
    return lax.broadcasted_iota(jnp.int32, shape, dim)


def triangle(length, upper):
    rows, cols = iota((length, length), 0), iota((length, length), 1)
    return jnp.where((cols >= rows) if upper else (rows >= cols), 1.0, 0.0).astype(BF)


def running_sum(v, upper):
    ones = triangle(v.shape[0], upper)
    high, rest = two_terms(v)
    low = (v - high.astype(F32) - rest.astype(F32)).astype(BF)
    return nn(ones, high) + nn(ones, rest) + nn(ones, low)


def norm_rows(v):
    centred = v - jnp.mean(v, axis=-1, keepdims=True)
    scale = lax.rsqrt(jnp.mean(centred * centred, axis=-1, keepdims=True) + epsilon)
    return centred * scale, scale


def norm_rows_backward(grad, xhat, scale, gain):
    g = grad * gain
    return scale * (
        g
        - jnp.mean(g, axis=-1, keepdims=True)
        - xhat * jnp.mean(g * xhat, axis=-1, keepdims=True)
    )


def pair_frequencies(freq_ref, pair):
    even, odd = freq_ref[2 * pair], freq_ref[2 * pair + 1]
    none = jnp.zeros_like(even)
    return jnp.concatenate(
        [jnp.concatenate([even, none], axis=1), jnp.concatenate([none, odd], axis=1)], axis=0
    )


def scaled_sine_cosine(angles, scale):
    turns = jnp.floor(angles * (1.0 / math.pi) + 0.5)
    r = angles - turns * 3.140625
    r = r - turns * 0.0009675025939941406
    r = r - turns * 1.509958e-07
    odd = turns - 2.0 * jnp.floor(turns * 0.5)
    sign = scale - (2.0 * scale) * odd
    r2 = r * r
    sine = -0.00018362251175623582 * r2 + 0.008306273552368303
    sine = sine * r2 - 0.1666482311215342
    sine = sine * r2 + 0.9999966031254778
    cosine = -0.0012711240835350962 * r2 + 0.041487518673719546
    cosine = cosine * r2 - 0.4999123281046797
    cosine = cosine * r2 + 0.9999933132015835
    return sine * (r * sign), cosine * sign


def pair_features(values, freq, scale):
    high, low = two_terms(values)
    freq_high, freq_low = two_terms(freq)
    angles = nn(high, freq_high) + nn(low, freq_high) + nn(high, freq_low)
    sine, cosine = scaled_sine_cosine(angles, scale)
    sine, cosine = sine.astype(BF), cosine.astype(BF)
    feat = freq.shape[1] // 2
    return [
        jnp.concatenate([sine[:, h * feat : (h + 1) * feat], cosine[:, h * feat : (h + 1) * feat]], axis=1)
        for h in (0, 1)
    ]


def own_lanes(shape, half):
    lane = iota(shape, len(shape) - 1)
    return (lane >= LANES // 2) if half else (lane < LANES // 2)


def one_lane(shape, half):
    return iota(shape, len(shape) - 1) == (0 if half else LANES // 2)


def second_lane(shape, half):
    return iota(shape, len(shape) - 1) == (1 if half else LANES // 2 + 1)


def with_ones(values, half, both=False):
    v = values.astype(F32)
    ones = one_lane(v.shape, half) | (both & second_lane(v.shape, half))
    return jnp.where(own_lanes(v.shape, half), v, jnp.where(ones, 1.0, 0.0))


def pack_states(even, odd, decay_even, decay_odd):
    half = LANES // 2
    row = iota(even.shape, 0)
    states = jnp.where(row < half, even, odd).astype(BF)
    extra = iota((EXTRA, even.shape[1]), 0)
    parts = []
    for value in (even[half : half + 1], odd[0:1], decay_even, decay_odd):
        high = value.astype(BF).astype(F32)
        parts += [high, value - high]
    rows = jnp.zeros((EXTRA, even.shape[1]), F32)
    for at, part in enumerate(parts):
        rows = jnp.where(extra == at, part, rows)
    return states, rows.astype(BF)


def extra_row(packed, at):
    at = LANES + 2 * at
    return packed[at : at + 1] + packed[at + 1 : at + 2]


def decays(packed):
    return extra_row(packed, 2), extra_row(packed, 3)


def unpack_states(packed):
    half = LANES // 2
    states = packed[:LANES]
    row = iota(states.shape, 0)
    even = jnp.where(row < half, states, jnp.where(row == half, extra_row(packed, 0), 0.0))
    odd = jnp.where(row >= half, states, jnp.where(row == 0, extra_row(packed, 1), 0.0))
    return even, odd


def join_states(first, second):
    return [
        a + decay * b
        for a, b, decay in zip(unpack_states(first), unpack_states(second), decays(first))
    ]


def as_operand(state, half):
    at = 0 if half else LANES // 2
    norm = state[at : at + 1]
    rest = norm - norm.astype(BF).astype(F32)
    return jnp.where(iota(state.shape, 0) == at + 1, rest, state).astype(BF)


def decay_weights(c_col, c_row, a_row):
    length = c_col.shape[0]
    gap = jnp.minimum(c_col - c_row, 0.0)
    causal = iota((length, length), 0) >= iota((length, length), 1)
    return jnp.where(causal, jnp.exp(gap) * a_row, 0.0)


def lane_sum(v):
    return jnp.sum(v, axis=1, keepdims=True)


def front_kernel(
    x_ref, wqkv_ref, gw_ref, gb_ref, gain_ref, shift_ref, freq_ref,
    n1_ref, v_ref, c_ref, a_ref, crow_ref, arow_ref, pq_ref, pk_ref, st_ref,
):
    heads = freq_ref.shape[0]
    feat = freq_ref.shape[2]
    width = x_ref.shape[2]
    scale = 1.0 / math.sqrt(feat)
    xhat, _ = norm_rows(x_ref[0])
    n1 = (xhat * gain_ref[...] + shift_ref[...]).astype(BF)
    n1_ref[0] = n1
    z = nn(n1, gw_ref[...]) + gb_ref[...]
    e = jnp.exp(-jnp.abs(z))
    log_keep = jnp.minimum(z, 0.0) - jnp.log1p(e)
    inverse = 1.0 / (1.0 + e)
    admit = jnp.where(z > 0.0, e * inverse, inverse)
    c = running_sum(log_keep, False)
    c_ref[0] = c
    a_ref[0] = admit
    crow_ref[0] = jnp.transpose(c)[:heads]
    arow_ref[0] = jnp.transpose(admit)[:heads]
    last = c[c.shape[0] - 1 :]
    tail = jnp.exp(last - c) * admit
    decay = jnp.exp(last)
    for pair in range(heads // 2):
        at = pair * LANES
        freq = pair_frequencies(freq_ref, pair)
        q = nn(n1, wqkv_ref[:, at : at + LANES])
        k = nn(n1, wqkv_ref[:, width + at : width + at + LANES])
        v = nn(n1, wqkv_ref[:, 2 * width + at : 2 * width + at + LANES])
        v_ref[0, :, at : at + LANES] = v
        phi_q = pair_features(q, freq, scale)
        phi_k = pair_features(k, freq, scale)
        states = []
        for half in (0, 1):
            h = 2 * pair + half
            pq_ref[0, h] = phi_q[half]
            pk_ref[0, h] = phi_k[half]
            weighted = jnp.concatenate(two_terms(with_ones(v, half) * tail[:, h : h + 1]), axis=1)
            both = tn(weighted, phi_k[half])
            states.append(both[:LANES] + both[LANES:])
        main, rest = pack_states(
            *states, decay[:, 2 * pair : 2 * pair + 1], decay[:, 2 * pair + 1 : 2 * pair + 2]
        )
        st_ref[0, pair, :LANES] = main
        st_ref[0, pair, LANES:] = rest


def scores_kernel(pq_ref, pk_ref, v_ref, c_ref, crow_ref, arow_ref, p_ref, num_ref):
    heads = pq_ref.shape[1]
    for h in range(heads):
        pair, half = divmod(h, 2)
        v = with_ones(v_ref[0, :, pair * LANES : (pair + 1) * LANES], half)
        weights = decay_weights(c_ref[0, :, h : h + 1], crow_ref[0, h : h + 1], arow_ref[0, h : h + 1])
        p = (nt(pq_ref[0, h], pk_ref[0, h]) * weights).astype(BF)
        p_ref[0, h] = p
        both = nn(p, jnp.concatenate(two_terms(v), axis=1))
        num_ref[0, h] = both[:, :LANES] + both[:, LANES:]


def mix_kernel(
    place_ref, x_ref, got_ref, swapped_ref, partner_ref, pq_ref, c_ref, num_ref, wo_ref, gain_ref, shift_ref,
    full_ref, start_ref, mixed_ref, resid_ref, n2_ref,
):
    heads = pq_ref.shape[1]
    core = place_ref[0]
    mine = pl.program_id(0) == core
    growth = jnp.exp(c_ref[0])
    for pair in range(heads // 2):
        before = jnp.where(mine, got_ref[pair], swapped_ref[pair]).astype(F32)
        partner = partner_ref[0, pair].astype(F32)
        states = [
            jnp.where(core == 0, a, b)
            for a, b in zip(unpack_states(before), join_states(partner, before))
        ]
        none = jnp.zeros((1, 1), F32)
        main, rest = pack_states(*states, none, none)
        start_ref[0, pair, :LANES] = main
        start_ref[0, pair, LANES:] = rest
        mixed = []
        for half in (0, 1):
            h = 2 * pair + half
            full = num_ref[0, h] + growth[:, h : h + 1] * nt(
                pq_ref[0, h], as_operand(states[half], half)
            )
            full_ref[0, h] = full
            at = 0 if half else LANES // 2
            sden = full[:, at : at + 1] + full[:, at + 1 : at + 2]
            mixed.append(full * lax.rsqrt(sden * sden + guard))
        pair_mixed = jnp.where(own_lanes(mixed[0].shape, 0), mixed[0], mixed[1])
        mixed_ref[0, :, pair * LANES : (pair + 1) * LANES] = pair_mixed.astype(BF)
    resid = x_ref[0] + nn(mixed_ref[0], wo_ref[...])
    resid_ref[0] = resid
    xhat, _ = norm_rows(resid)
    n2_ref[0] = (xhat * gain_ref[...] + shift_ref[...]).astype(BF)


def gelu_and_slope(v):
    root = math.sqrt(2.0 / math.pi)
    v2 = v * v
    t = jnp.tanh(v * (root + (root * 0.044715) * v2))
    half = 0.5 * (1.0 + t)
    slope = half + (0.5 * v) * (1.0 - t * t) * (root + (root * 3.0 * 0.044715) * v2)
    return v * half, slope


def feed_kernel(
    n2_ref, og_ref, resid_ref, wi0, wi1, wi2, wi3, wo0, wo1, wo2, wo3,
    out_ref, dn2_ref, keep_ref, send_ref,
):
    n2 = n2_ref[...]
    out_low = og_ref[...].astype(BF)
    total = resid_ref[...]
    dn2 = None
    for block, (wi, wo) in enumerate(((wi0, wo0), (wi1, wo1), (wi2, wo2), (wi3, wo3))):
        pre = nn(n2, wi[...])
        active, slope = gelu_and_slope(pre)
        active = active.astype(BF)
        total = total + nn(active, wo[...])
        pre_grad = (nt(out_low, wo[...]) * slope).astype(BF)
        part = nt(pre_grad, wi[...])
        dn2 = part if dn2 is None else dn2 + part
        inner = tn(n2, pre_grad)
        outer = tn(active, out_low)
        if block < 2:
            keep_ref[2 * block] = inner
            keep_ref[2 * block + 1] = outer
        else:
            send_ref[2 * block - 4] = inner.astype(BF)
            send_ref[2 * block - 3] = outer.astype(BF)
    out_ref[...] = total
    dn2_ref[...] = dn2


def turn_kernel(
    place_ref, og_ref, dn2_ref, resid_ref, gain_ref, wo_ref, mixed_ref, full_ref, pq_ref, c_ref,
    dres_ref, dwo_ref, sums_ref, ng_ref, r_ref, sd_ref,
):
    heads = pq_ref.shape[1]
    step = pl.program_id(0)
    own = place_ref[2]
    xhat, scale = norm_rows(resid_ref[0])
    dn2 = dn2_ref[0]
    dres = og_ref[0] + norm_rows_backward(dn2, xhat, scale, gain_ref[...])
    dres_ref[0] = dres
    low = dres.astype(BF)

    @pl.when(step == 0)
    def _():
        sums_ref[...] = jnp.zeros_like(sums_ref)
        dwo_ref[...] = jnp.zeros_like(dwo_ref)

    sums_ref[2:3] += jnp.sum(dn2 * xhat, axis=0, keepdims=True)
    sums_ref[3:4] += jnp.sum(dn2, axis=0, keepdims=True)
    rows = dwo_ref.shape[1]
    for block in range(4):
        at = pl.multiple_of((own ^ block) * rows, rows)
        dwo_ref[block] += tn(mixed_ref[0, :, pl.ds(at, rows)], low)
    dmixed = nt(low, wo_ref[...])
    c = c_ref[0]
    growth = jnp.exp(c)
    decay = jnp.exp(c[c.shape[0] - 1 :])
    lane = iota(c.shape, 1)
    r_all = jnp.zeros_like(c)
    for pair in range(heads // 2):
        g = dmixed[:, pair * LANES : (pair + 1) * LANES]
        states = []
        for half in (0, 1):
            h = 2 * pair + half
            full = full_ref[0, h]
            at = 0 if half else LANES // 2
            sden = full[:, at : at + 1] + full[:, at + 1 : at + 2]
            inverse = lax.rsqrt(sden * sden + guard)
            inverse2 = inverse * inverse
            mine = own_lanes(g.shape, half)
            dot = lane_sum(jnp.where(mine, g * full, 0.0)) * inverse
            sden_grad = -dot * sden * inverse2
            r_all = jnp.where(lane == h, dot * inverse2 * guard, r_all)
            grads = jnp.where(
                mine, g * inverse, jnp.where(one_lane(g.shape, half), sden_grad, 0.0)
            )
            ng_ref[0, h] = jnp.concatenate(two_terms(grads), axis=1)
            lifted = jnp.concatenate(two_terms(grads * growth[:, h : h + 1]), axis=1)
            both = tn(lifted, pq_ref[0, h])
            states.append(both[:LANES] + both[LANES:])
        main, rest = pack_states(
            *states, decay[:, 2 * pair : 2 * pair + 1], decay[:, 2 * pair + 1 : 2 * pair + 2]
        )
        sd_ref[0, pair, :LANES] = main
        sd_ref[0, pair, LANES:] = rest
    r_ref[0] = r_all


def angle_grads(phi, dphi):
    feat = phi.shape[1] // 2
    phi = phi.astype(F32)
    return phi[:, feat:] * dphi[:, :feat] - phi[:, :feat] * dphi[:, feat:]


def back_kernel(
    place_ref, pq_ref, pk_ref, v_ref, ng_ref, p_ref, c_ref, crow_ref, arow_ref, start_ref, freq_ref, n1_ref, dwo_ref,
    qg_ref, kg_ref, vg_ref, kcol_ref, keep_ref, send_ref, acc_ref,
):
    heads = pq_ref.shape[1]
    step = pl.program_id(0)
    own = place_ref[2]
    c = c_ref[0]
    growth = jnp.exp(c)
    lane = iota(c.shape, 1)
    kcol = jnp.zeros_like(c)
    for pair in range(heads // 2):
        at = pair * LANES
        freq = pair_frequencies(freq_ref, pair).astype(BF)
        states = unpack_states(start_ref[0, pair].astype(F32))
        q_angles, k_angles, v_grads = [], [], []
        for half in (0, 1):
            h = 2 * pair + half
            phi_q, phi_k = pq_ref[0, h], pk_ref[0, h]
            grads = ng_ref[0, h, :, :LANES]
            v = with_ones(v_ref[0, :, at : at + LANES], half)
            weights = decay_weights(c[:, h : h + 1], crow_ref[0, h : h + 1], arow_ref[0, h : h + 1])
            dk = (nt(grads, v.astype(BF)) * weights).astype(BF)
            lifted = (grads.astype(F32) * growth[:, h : h + 1]).astype(BF)
            dphi_q = nn(dk, phi_k) + nn(lifted, states[half].astype(BF))
            q_angles.append(angle_grads(phi_q, dphi_q))
            k_angles.append(angle_grads(phi_k, tn(dk, phi_q)))
            both = tn(p_ref[0, h], ng_ref[0, h])
            dv = both[:, :LANES] + both[:, LANES:]
            v_grads.append(dv)
            kcol = jnp.where(lane == h, lane_sum(v * dv), kcol)
        qg_ref[0, :, at : at + LANES] = nt(jnp.concatenate(q_angles, axis=1).astype(BF), freq).astype(BF)
        kg_ref[0, :, at : at + LANES] = nt(jnp.concatenate(k_angles, axis=1).astype(BF), freq)
        vg_ref[0, :, at : at + LANES] = jnp.where(own_lanes(v_grads[0].shape, 0), v_grads[0], v_grads[1])
    kcol_ref[0] = kcol

    @pl.when(step == 0)
    def _():
        acc_ref[...] = jnp.zeros_like(acc_ref)

    rows = acc_ref.shape[1]
    width = acc_ref.shape[2]
    for block in range(4):
        at = pl.multiple_of((own ^ block) * rows, rows)
        acc_ref[block] += tn(n1_ref[0, :, pl.ds(at, rows)], qg_ref[0])

    @pl.when(step == pl.num_programs(0) - 1)
    def _():
        for block in range(2):
            keep_ref[block, :, :width] = dwo_ref[block]
            keep_ref[block, :, width:] = acc_ref[block]
            send_ref[block, :, :width] = dwo_ref[2 + block].astype(BF)
            send_ref[block, :, width:] = acc_ref[2 + block].astype(BF)


def last_kernel(
    place_ref, got_ref, swapped_ref, partner_ref, st_ref, start_ref, pk_ref, v_ref, c_ref, a_ref, r_ref, kcol_ref,
    qg_ref, kg_ref, vg_ref, freq_ref, n1_ref, x_ref, dres_ref, wqkv_ref, gw_ref, gain_ref, sums2_ref,
    dx_ref, keep_ref, send_ref, sums_ref, acc_ref, kv_ref,
):
    heads = pk_ref.shape[1]
    step = pl.program_id(0)
    core, own = place_ref[0], place_ref[2]
    mine = step == core
    width = x_ref.shape[2]
    c, a = c_ref[0], a_ref[0]
    tail = jnp.exp(c[c.shape[0] - 1 :] - c) * a
    lane = iota(c.shape, 1)
    lane_row = iota((1, c.shape[1]), 1)
    kcol = kcol_ref[0]
    ends = jnp.zeros((1, c.shape[1]), F32)
    for pair in range(heads // 2):
        at = pair * LANES
        freq = pair_frequencies(freq_ref, pair).astype(BF)
        after = jnp.where(mine, got_ref[pair], swapped_ref[pair]).astype(F32)
        partner = partner_ref[0, pair].astype(F32)
        grads = [
            jnp.where(core == 1, a, b)
            for a, b in zip(unpack_states(after), join_states(partner, after))
        ]
        reached = join_states(st_ref[0, pair].astype(F32), start_ref[0, pair].astype(F32))
        k_angles, v_grads = [], []
        for half in (0, 1):
            h = 2 * pair + half
            phi_k = pk_ref[0, h]
            v = with_ones(v_ref[0, :, at : at + LANES], half, True)
            grad_low = as_operand(grads[half], half)
            weight = tail[:, h : h + 1]
            k_angles.append(angle_grads(phi_k, nn(v.astype(BF), grad_low)) * weight)
            dv = nt(phi_k, grad_low) * weight
            v_grads.append(dv)
            kcol = kcol + jnp.where(lane == h, lane_sum(v * dv), 0.0)
            end = jnp.sum(lane_sum(grads[half] * reached[half]), axis=0, keepdims=True)
            ends = jnp.where(lane_row == h, end, ends)
        kg = kg_ref[0, :, at : at + LANES] + nt(jnp.concatenate(k_angles, axis=1).astype(BF), freq)
        vg = vg_ref[0, :, at : at + LANES] + jnp.where(own_lanes(v_grads[0].shape, 0), v_grads[0], v_grads[1])
        kv_ref[:, at : at + LANES] = kg.astype(BF)
        kv_ref[:, width + at : width + at + LANES] = vg.astype(BF)
    keep_grad = running_sum(r_ref[0] - kcol, True) + ends
    logit_grad = a * keep_grad - (1.0 - a) * kcol
    logit_low = logit_grad.astype(BF)
    n1 = n1_ref[0]
    dn1 = (
        nt(qg_ref[0], wqkv_ref[:, :width])
        + nt(kv_ref[...], wqkv_ref[:, width:])
        + nt(logit_low, gw_ref[...])
    )
    xhat, scale = norm_rows(x_ref[0])
    dx_ref[0] = dres_ref[0] + norm_rows_backward(dn1, xhat, scale, gain_ref[...])

    @pl.when(step == 0)
    def _():
        acc_ref[...] = jnp.zeros_like(acc_ref)
        sums_ref[...] = jnp.zeros_like(sums_ref)
        sums_ref[0:8] = sums2_ref[...]

    sums_ref[0:1] += jnp.sum(dn1 * xhat, axis=0, keepdims=True)
    sums_ref[1:2] += jnp.sum(dn1, axis=0, keepdims=True)
    sums_ref[4:5, :LANES] += jnp.sum(logit_grad, axis=0, keepdims=True)
    sums_ref[8 : 8 + heads] += tn(logit_low, n1)[:heads]
    rows = acc_ref.shape[1]
    for block in range(4):
        at = pl.multiple_of((own ^ block) * rows, rows)
        acc_ref[block] += tn(n1_ref[0, :, pl.ds(at, rows)], kv_ref[...])

    @pl.when(step == pl.num_programs(0) - 1)
    def _():
        for block in range(2):
            keep_ref[block] = acc_ref[block]
            send_ref[block] = acc_ref[2 + block].astype(BF)


def chain_kernel(place_ref, me_ref, partner_ref, out_ref, *, reverse):
    core = place_ref[0]
    lead = (core == 0) if reverse else (core == 1)
    for pair in range(out_ref.shape[0]):
        mine, other = me_ref[core, pair].astype(F32), partner_ref[core, pair].astype(F32)
        first = jnp.where(lead, mine, other)
        second = jnp.where(lead, other, mine)
        none = jnp.zeros((1, 1), F32)
        main, rest = pack_states(*join_states(first, second), none, none)
        out_ref[pair, :LANES] = main
        out_ref[pair, LANES:] = rest


def assemble_kernel(place_ref, g1_ref, g2_ref, qkv_ref, wo_ref):
    width = wo_ref.shape[1]
    wo_ref[...] = g1_ref[0, :, :width].astype(F32)
    qkv_ref[:, :width] = g1_ref[0, :, width:].astype(F32)
    qkv_ref[:, width:] = g2_ref[0].astype(F32)


def params():
    return pltpu.CompilerParams(vmem_limit_bytes=VMEM_BYTES)


def whole(array):
    zeros = (0,) * array.ndim
    return pl.BlockSpec(array.shape, lambda *_: zeros)


def per_step(array):
    rest = (0,) * (array.ndim - 1)
    return pl.BlockSpec((1, *array.shape[1:]), lambda s, *_: (s, *rest))


def scalars():
    return pl.BlockSpec(memory_space=pltpu.SMEM)


def shaped(shape, dtype):
    return jax.ShapeDtypeStruct(shape, dtype)


def core_swap(v):
    return jax.tree.map(lambda a: lax.ppermute(a, "mp", [(i, i ^ 1) for i in range(4)]), v)


def chip_swap(v):
    return jax.tree.map(lambda a: lax.ppermute(a, "mp", [(i, i ^ 2) for i in range(4)]), v)


def sum_and_share(v):
    count = lax.axis_size("dp")
    rows = v.shape[0]
    parts = lax.all_to_all(v.astype(BF), "dp", 0, 0, tiled=True)
    total = jnp.sum(parts.reshape(count, rows // count, -1).astype(F32), axis=0).astype(BF)
    copies = jnp.broadcast_to(total[None], (count, *total.shape)).reshape(rows, -1)
    return lax.all_to_all(copies, "dp", 0, 0, tiled=True)


def sum_over_all(keep, send):
    both = keep + core_swap(send).astype(F32)
    mine = both[0] + chip_swap(both[1].astype(BF)).astype(F32)
    mine = sum_and_share(mine)
    pair = jnp.stack([mine, chip_swap(mine)])
    return jnp.concatenate([pair, core_swap(pair)])


def exchange(packed, partner, place, reverse):
    pairs = packed.shape[1]
    total = pl.pallas_call(
        lambda *refs: chain_kernel(*refs, reverse=reverse),
        out_shape=shaped(packed.shape[1:], BF),
        in_specs=[scalars(), whole(packed), whole(partner)],
        out_specs=pl.BlockSpec(packed.shape[1:], lambda *_: (0, 0, 0)),
        compiler_params=params(),
        name="chain",
    )(place, packed, partner)
    way = [(2, 0), (3, 1)] if reverse else [(0, 2), (1, 3)]
    got = lax.ppermute(total, "mp", way)
    return got, core_swap(got)


def per_device(
    layer_input,
    qkv_weight,
    gate_weight,
    gate_bias,
    out_weight,
    inner_weight,
    outer_weight,
    leading_norm_gain,
    leading_norm_bias,
    trailing_norm_gain,
    trailing_norm_bias,
    random_features,
    output_grad,
):
    seqs, length, width = layer_input.shape
    heads, head, feat = random_features.shape
    pairs = heads // 2
    count = seqs * length
    spot = lax.axis_index("mp")
    core, chip = spot % 2, spot // 2
    place = jnp.stack([core, chip, 2 * core + chip]).astype(jnp.int32)
    gate_wide = jnp.pad(gate_weight, ((0, 0), (0, LANES - heads)))
    bias_wide = jnp.pad(gate_bias, (0, LANES - heads)).reshape(1, LANES)
    gain1, shift1 = leading_norm_gain.reshape(1, width), leading_norm_bias.reshape(1, width)
    gain2, shift2 = trailing_norm_gain.reshape(1, width), trailing_norm_bias.reshape(1, width)

    inner_chip, outer_chip = chip_swap(inner_weight), chip_swap(outer_weight)
    inner_core, outer_core = core_swap(inner_weight), core_swap(outer_weight)
    inner_both, outer_both = core_swap(inner_chip), core_swap(outer_chip)

    front_in = (layer_input, qkv_weight, gate_wide, bias_wide, gain1, shift1, random_features)
    front_out = (
        shaped((seqs, length, width), BF),
        shaped((seqs, length, width), F32),
        shaped((seqs, length, LANES), F32),
        shaped((seqs, length, LANES), F32),
        shaped((seqs, heads, length), F32),
        shaped((seqs, heads, length), F32),
        shaped((seqs, heads, length, 2 * feat), BF),
        shaped((seqs, heads, length, 2 * feat), BF),
        shaped((seqs, pairs, LANES + EXTRA, 2 * feat), BF),
    )
    normed1, values, c, admit, c_row, a_row, phi_q, phi_k, packed = pl.pallas_call(
        front_kernel,
        grid=(seqs,),
        out_shape=front_out,
        in_specs=[per_step(layer_input)] + [whole(a) for a in front_in[1:]],
        out_specs=[per_step(a) for a in front_out],
        compiler_params=params(),
        name="front",
    )(*front_in)

    partner = core_swap(packed)
    got, swapped = exchange(packed, partner, place, False)

    scores_in = (phi_q, phi_k, values, c, c_row, a_row)
    scores_out = (
        shaped((seqs, heads, length, length), BF),
        shaped((seqs, heads, length, LANES), F32),
    )
    scores, num = pl.pallas_call(
        scores_kernel,
        grid=(seqs,),
        out_shape=scores_out,
        in_specs=[per_step(a) for a in scores_in],
        out_specs=[per_step(a) for a in scores_out],
        compiler_params=params(),
        name="scores",
    )(*scores_in)

    mix_in = (place, layer_input, got, swapped, partner, phi_q, c, num, out_weight, gain2, shift2)
    mix_out = (
        shaped((seqs, heads, length, LANES), F32),
        shaped(packed.shape, BF),
        shaped((seqs, length, width), BF),
        shaped((seqs, length, width), F32),
        shaped((seqs, length, width), BF),
    )
    full, start, mixed_low, resid, normed2 = pl.pallas_call(
        mix_kernel,
        grid=(seqs,),
        out_shape=mix_out,
        in_specs=[
            scalars(), per_step(layer_input), whole(got), whole(swapped), per_step(partner), per_step(phi_q),
            per_step(c), per_step(num), whole(out_weight), whole(gain2), whole(shift2),
        ],
        out_specs=[per_step(a) for a in mix_out],
        compiler_params=params(),
        name="mix",
    )(*mix_in)

    hidden = inner_weight.shape[1]
    feed_in = (
        normed2.reshape(count, width), output_grad.reshape(count, width), resid.reshape(count, width),
        inner_weight, inner_chip, inner_core, inner_both, outer_weight, outer_chip, outer_core, outer_both,
    )
    feed_out = (
        shaped((count, width), F32),
        shaped((count, width), F32),
        shaped((4, width, hidden), F32),
        shaped((4, width, hidden), BF),
    )
    layer_out, dn2, ff_keep, ff_send = pl.pallas_call(
        feed_kernel,
        out_shape=feed_out,
        in_specs=[whole(a) for a in feed_in],
        out_specs=[whole(a) for a in feed_out],
        compiler_params=params(),
        name="feed",
    )(*feed_in)

    ff_both = ff_keep + core_swap(ff_send).astype(F32)
    ff_mine = ff_both[:2] + chip_swap(ff_both[2:].astype(BF)).astype(F32)
    ff_total = sum_and_share(ff_mine.reshape(2 * width, hidden)).reshape(2, width, hidden)

    dn2 = dn2.reshape(seqs, length, width)
    turn_in = (place, output_grad, dn2, resid, gain2, out_weight, mixed_low, full, phi_q, c)
    turn_out = (
        shaped((seqs, length, width), F32),
        shaped((4, width // 4, width), F32),
        shaped((8, width), F32),
        shaped((seqs, heads, length, 2 * LANES), BF),
        shaped((seqs, length, LANES), F32),
        shaped(packed.shape, BF),
    )
    dres, dwo, sums2, num_grads, r, packed_grads = pl.pallas_call(
        turn_kernel,
        grid=(seqs,),
        out_shape=turn_out,
        in_specs=[
            scalars(), per_step(output_grad), per_step(dn2), per_step(resid), whole(gain2), whole(out_weight),
            per_step(mixed_low), per_step(full), per_step(phi_q), per_step(c),
        ],
        out_specs=[
            per_step(turn_out[0]), whole(turn_out[1]), whole(turn_out[2]), per_step(turn_out[3]), per_step(turn_out[4]),
            per_step(turn_out[5]),
        ],
        compiler_params=params(),
        name="turn",
    )(*turn_in)

    partner_grads = core_swap(packed_grads)
    got_grads, swapped_grads = exchange(packed_grads, partner_grads, place, True)

    back_in = (
        place, phi_q, phi_k, values, num_grads, scores, c, c_row, a_row, start, random_features, normed1, dwo,
    )
    back_out = (
        shaped((seqs, length, width), BF),
        shaped((seqs, length, width), F32),
        shaped((seqs, length, width), F32),
        shaped((seqs, length, LANES), F32),
        shaped((2, width // 4, 2 * width), F32),
        shaped((2, width // 4, 2 * width), BF),
    )
    q_grad, k_part, v_part, k_col, keep1, send1 = pl.pallas_call(
        back_kernel,
        grid=(seqs,),
        out_shape=back_out,
        in_specs=[scalars()] + [per_step(a) for a in back_in[1:10]] + [
            whole(random_features), per_step(normed1), whole(dwo),
        ],
        out_specs=[per_step(a) for a in back_out[:4]] + [whole(a) for a in back_out[4:]],
        scratch_shapes=[pltpu.VMEM((4, width // 4, width), F32)],
        compiler_params=params(),
        name="back",
    )(*back_in)
    blocks1 = sum_over_all(keep1, send1)

    last_in = (
        place, got_grads, swapped_grads, partner_grads, packed, start, phi_k, values, c, admit, r, k_col,
        q_grad, k_part, v_part, random_features, normed1, layer_input, dres, qkv_weight, gate_wide, gain1, sums2,
    )
    last_out = (
        shaped((seqs, length, width), F32),
        shaped((2, width // 4, 2 * width), F32),
        shaped((2, width // 4, 2 * width), BF),
        shaped((16, width), F32),
    )
    dx, keep2, send2, sums = pl.pallas_call(
        last_kernel,
        grid=(seqs,),
        out_shape=last_out,
        in_specs=[scalars(), whole(got_grads), whole(swapped_grads)]
        + [per_step(a) for a in last_in[3:15]]
        + [whole(random_features)]
        + [per_step(a) for a in last_in[16:19]]
        + [whole(a) for a in last_in[19:]],
        out_specs=[per_step(last_out[0])] + [whole(a) for a in last_out[1:]],
        scratch_shapes=[
            pltpu.VMEM((4, width // 4, 2 * width), F32),
            pltpu.VMEM((length, 2 * width), BF),
        ],
        compiler_params=params(),
        name="last",
    )(*last_in)
    blocks2 = sum_over_all(keep2, send2)
    sums = sums + core_swap(sums)
    sums = sums + chip_swap(sums)
    n_dp = lax.axis_size("dp")
    bit = 1
    while bit < n_dp:
        sums = sums + lax.ppermute(sums, "dp", [(i, i ^ bit) for i in range(n_dp)])
        bit *= 2

    rows = width // 4
    qkv_grad, wo_grad = pl.pallas_call(
        assemble_kernel,
        grid_spec=pltpu.PrefetchScalarGridSpec(
            num_scalar_prefetch=1,
            grid=(4,),
            in_specs=[
                pl.BlockSpec((1, rows, 2 * width), lambda i, p: (i ^ p[2], 0, 0)),
                pl.BlockSpec((1, rows, 2 * width), lambda i, p: (i ^ p[2], 0, 0)),
            ],
            out_specs=[
                pl.BlockSpec((rows, 3 * width), lambda i, p: (i, 0)),
                pl.BlockSpec((rows, width), lambda i, p: (i, 0)),
            ],
        ),
        out_shape=(shaped((width, 3 * width), F32), shaped((width, width), F32)),
        compiler_params=params(),
        name="assemble",
    )(place, blocks1, blocks2)
    return (
        layer_out.reshape(seqs, length, width),
        dx,
        qkv_grad,
        jnp.transpose(sums[8 : 8 + heads]),
        sums[4, :heads],
        wo_grad,
        ff_total[0].astype(F32),
        ff_total[1].astype(F32),
        sums[0],
        sums[1],
        sums[2],
        sums[3],
    )


def solution(mesh):
    in_specs = (
        P("dp", "mp", None),
        P(),
        P(),
        P(),
        P(),
        P(None, "mp"),
        P("mp", None),
        P(),
        P(),
        P(),
        P(),
        P(),
        P("dp", "mp", None),
    )
    out_specs = (
        P("dp", "mp", None),
        P("dp", "mp", None),
        P(),
        P(),
        P(),
        P(),
        P(None, "mp"),
        P("mp", None),
        P(),
        P(),
        P(),
        P(),
    )
    return jax.shard_map(
        per_device, mesh=mesh, in_specs=in_specs, out_specs=out_specs, check_vma=False
    )
```

```python
import functools
import math

import jax
import jax.numpy as jnp
from jax import lax
from jax.experimental import pallas as pl
from jax.experimental.pallas import tpu as pltpu
from jax.sharding import PartitionSpec as P

BF = jnp.bfloat16
F32 = jnp.float32
epsilon = 1e-05
guard = 0.01
LANES = 128
EXTRA = 16
VMEM_BYTES = 16 * 1024 * 1024


def nn(a, b):
    return lax.dot_general(a, b, (((1,), (0,)), ((), ())), preferred_element_type=F32)


def nt(a, b):
    return lax.dot_general(a, b, (((1,), (1,)), ((), ())), preferred_element_type=F32)


def tn(a, b):
    return lax.dot_general(a, b, (((0,), (0,)), ((), ())), preferred_element_type=F32)


def two_terms(v):
    high = v.astype(BF)
    return high, (v - high.astype(F32)).astype(BF)


def iota(shape, dim):
    return lax.broadcasted_iota(jnp.int32, shape, dim)


def triangle(length, upper):
    rows, cols = iota((length, length), 0), iota((length, length), 1)
    return jnp.where((cols >= rows) if upper else (rows >= cols), 1.0, 0.0).astype(BF)


def running_sum(v, upper):
    ones = triangle(v.shape[0], upper)
    high, rest = two_terms(v)
    low = (v - high.astype(F32) - rest.astype(F32)).astype(BF)
    return nn(ones, high) + nn(ones, rest) + nn(ones, low)


def norm_rows(v):
    centred = v - jnp.mean(v, axis=-1, keepdims=True)
    scale = lax.rsqrt(jnp.mean(centred * centred, axis=-1, keepdims=True) + epsilon)
    return centred * scale, scale


def norm_rows_backward(grad, xhat, scale, gain):
    g = grad * gain
    return scale * (
        g
        - jnp.mean(g, axis=-1, keepdims=True)
        - xhat * jnp.mean(g * xhat, axis=-1, keepdims=True)
    )


def pair_frequencies(freq_ref, pair):
    even, odd = freq_ref[2 * pair], freq_ref[2 * pair + 1]
    none = jnp.zeros_like(even)
    return jnp.concatenate(
        [jnp.concatenate([even, none], axis=1), jnp.concatenate([none, odd], axis=1)], axis=0
    )


def scaled_sine_cosine(angles, scale):
    turns = jnp.floor(angles * (1.0 / math.pi) + 0.5)
    r = angles - turns * 3.140625
    r = r - turns * 0.0009675025939941406
    r = r - turns * 1.509958e-07
    odd = turns - 2.0 * jnp.floor(turns * 0.5)
    sign = scale - (2.0 * scale) * odd
    r2 = r * r
    sine = -0.00018362251175623582 * r2 + 0.008306273552368303
    sine = sine * r2 - 0.1666482311215342
    sine = sine * r2 + 0.9999966031254778
    cosine = -0.0012711240835350962 * r2 + 0.041487518673719546
    cosine = cosine * r2 - 0.4999123281046797
    cosine = cosine * r2 + 0.9999933132015835
    return sine * (r * sign), cosine * sign


def pair_features(values, freq, scale):
    high, low = two_terms(values)
    freq_high, freq_low = two_terms(freq)
    angles = nn(high, freq_high) + nn(low, freq_high) + nn(high, freq_low)
    sine, cosine = scaled_sine_cosine(angles, scale)
    sine, cosine = sine.astype(BF), cosine.astype(BF)
    feat = freq.shape[1] // 2
    return [
        jnp.concatenate([sine[:, h * feat : (h + 1) * feat], cosine[:, h * feat : (h + 1) * feat]], axis=1)
        for h in (0, 1)
    ]


def own_lanes(shape, half):
    lane = iota(shape, len(shape) - 1)
    return (lane >= LANES // 2) if half else (lane < LANES // 2)


def one_lane(shape, half):
    return iota(shape, len(shape) - 1) == (0 if half else LANES // 2)


def second_lane(shape, half):
    return iota(shape, len(shape) - 1) == (1 if half else LANES // 2 + 1)


def with_ones(values, half, both=False):
    v = values.astype(F32)
    ones = one_lane(v.shape, half) | (both & second_lane(v.shape, half))
    return jnp.where(own_lanes(v.shape, half), v, jnp.where(ones, 1.0, 0.0))


def pack_states(even, odd, decay_even, decay_odd):
    half = LANES // 2
    row = iota(even.shape, 0)
    states = jnp.where(row < half, even, odd).astype(BF)
    extra = iota((EXTRA, even.shape[1]), 0)
    parts = []
    for value in (even[half : half + 1], odd[0:1], decay_even, decay_odd):
        high = value.astype(BF).astype(F32)
        parts += [high, value - high]
    rows = jnp.zeros((EXTRA, even.shape[1]), F32)
    for at, part in enumerate(parts):
        rows = jnp.where(extra == at, part, rows)
    return states, rows.astype(BF)


def extra_row(packed, at):
    at = LANES + 2 * at
    return packed[at : at + 1] + packed[at + 1 : at + 2]


def decays(packed):
    return extra_row(packed, 2), extra_row(packed, 3)


def unpack_states(packed):
    half = LANES // 2
    states = packed[:LANES]
    row = iota(states.shape, 0)
    even = jnp.where(row < half, states, jnp.where(row == half, extra_row(packed, 0), 0.0))
    odd = jnp.where(row >= half, states, jnp.where(row == 0, extra_row(packed, 1), 0.0))
    return even, odd


def join_states(first, second):
    return [
        a + decay * b
        for a, b, decay in zip(unpack_states(first), unpack_states(second), decays(first))
    ]


def as_operand(state, half):
    at = 0 if half else LANES // 2
    norm = state[at : at + 1]
    rest = norm - norm.astype(BF).astype(F32)
    return jnp.where(iota(state.shape, 0) == at + 1, rest, state).astype(BF)


def decay_weights(c_col, c_row, a_row):
    length = c_col.shape[0]
    gap = jnp.minimum(c_col - c_row, 0.0)
    causal = iota((length, length), 0) >= iota((length, length), 1)
    return jnp.where(causal, jnp.exp(gap) * a_row, 0.0)


def lane_sum(v):
    return jnp.sum(v, axis=1, keepdims=True)


def each(count, step):
    lax.fori_loop(0, count, lambda i, none: (step(i), none)[1], 0)


def wide(v, axis):
    none = list(v.shape)
    none[axis] = LANES - v.shape[axis]
    return jnp.concatenate([v, jnp.zeros(none, v.dtype)], axis=axis)


def aligned(at, size):
    return pl.ds(pl.multiple_of(at * size, size), size)


def my_core():
    return lax.axis_index("mp") % 2


def my_chip():
    return lax.axis_index("mp") // 2


def pack_kernel(inner_ref, outer_ref, out_ref, sems):
    rows = out_ref.shape[1]
    mine = aligned(lax.axis_index("dp") % 2, rows)
    copies = [
        pltpu.make_async_copy(source.at[mine], out_ref.at[i], sems.at[i])
        for i, source in enumerate((inner_ref, outer_ref))
    ]
    for copy in copies:
        copy.start()
    for copy in copies:
        copy.wait()


def put_states(s, pair, main, rest, away_ref, home_ref):
    home = s == my_core()

    @pl.when(home)
    def _():
        home_ref[pair, :LANES] = main
        home_ref[pair, LANES:] = rest

    @pl.when(jnp.logical_not(home))
    def _():
        away_ref[pair, :LANES] = main
        away_ref[pair, LANES:] = rest


def keys_kernel(*refs):
    sources, refs = refs[:7], refs[7:]
    n1_ref, v_ref, c_ref, a_ref, crow_ref, arow_ref, pk_ref, away_ref, home_ref = refs[:9]
    buffers, sems = refs[9:16], refs[16]
    copies = [
        pltpu.make_async_copy(source, buffer, sems.at[i])
        for i, (source, buffer) in enumerate(zip(sources, buffers))
    ]
    for copy in copies:
        copy.start()
    for copy in copies:
        copy.wait()
    x_ref, wqkv_ref, gw_ref, gb_ref, gain_ref, shift_ref, freq_ref = buffers
    heads, _, feat = freq_ref.shape
    seqs, length, width = x_ref.shape
    scale = 1.0 / math.sqrt(feat)
    gate_weight, gate_bias = wide(gw_ref[...], 0), wide(gb_ref[...], 1)

    def one(s):
        xhat, _ = norm_rows(x_ref[s])
        n1 = (xhat * gain_ref[...] + shift_ref[...]).astype(BF)
        n1_ref[s] = n1
        z = nt(n1, gate_weight) + gate_bias
        e = jnp.exp(-jnp.abs(z))
        log_keep = jnp.minimum(z, 0.0) - jnp.log1p(e)
        inverse = 1.0 / (1.0 + e)
        admit = jnp.where(z > 0.0, e * inverse, inverse)
        c = running_sum(log_keep, False)
        c_ref[s] = c
        a_ref[s] = admit
        crow_ref[s] = jnp.transpose(c)[:heads]
        arow_ref[s] = jnp.transpose(admit)[:heads]
        last = c[length - 1 :]
        tail = jnp.exp(last - c) * admit
        decay = jnp.exp(last)
        for pair in range(heads // 2):
            at = pair * LANES
            freq = pair_frequencies(freq_ref, pair)
            k = nn(n1, wqkv_ref[:, width + at : width + at + LANES])
            v = nn(n1, wqkv_ref[:, 2 * width + at : 2 * width + at + LANES])
            v_ref[s, :, at : at + LANES] = v
            phi_k = pair_features(k, freq, scale)
            states = []
            for half in (0, 1):
                h = 2 * pair + half
                pk_ref[s, h] = phi_k[half]
                weighted = jnp.concatenate(
                    two_terms(with_ones(v, half) * tail[:, h : h + 1]), axis=1
                )
                both = tn(weighted, phi_k[half])
                states.append(both[:LANES] + both[LANES:])
            main, rest = pack_states(
                *states, decay[:, 2 * pair : 2 * pair + 1], decay[:, 2 * pair + 1 : 2 * pair + 2]
            )
            put_states(s, pair, main, rest, away_ref, home_ref)

    each(seqs, one)


def scores_kernel(wqkv_ref, freq_ref, n1_ref, pk_ref, v_ref, c_ref, crow_ref, arow_ref, pq_ref, p_ref, num_ref):
    seqs, heads = pk_ref.shape[:2]
    scale = 1.0 / math.sqrt(freq_ref.shape[2])

    def one(s):
        for pair in range(heads // 2):
            at = pair * LANES
            q = nn(n1_ref[s], wqkv_ref[:, at : at + LANES])
            phi_q = pair_features(q, pair_frequencies(freq_ref, pair), scale)
            for half in (0, 1):
                h = 2 * pair + half
                pq_ref[s, h] = phi_q[half]
                v = with_ones(v_ref[s, :, at : at + LANES], half)
                weights = decay_weights(
                    c_ref[s, :, h : h + 1], crow_ref[s, h : h + 1], arow_ref[s, h : h + 1]
                )
                p = (nt(phi_q[half], pk_ref[s, h]) * weights).astype(BF)
                p_ref[s, h] = p
                both = nn(p, jnp.concatenate(two_terms(v), axis=1))
                num_ref[s, h] = both[:, :LANES] + both[:, LANES:]

    each(seqs, one)


def mix_kernel(
    x_ref, got_ref, swapped_ref, partner_home_ref, partner_away_ref, wo_ref, gain_ref, shift_ref, pq_ref, c_ref, num_ref,
    full_ref, start_ref, mixed_ref, resid_ref, n2_ref,
):
    seqs, heads = pq_ref.shape[:2]
    core = my_core()

    def one(s):
        growth = jnp.exp(c_ref[s])
        for pair in range(heads // 2):
            before = jnp.where(s == core, got_ref[pair], swapped_ref[pair]).astype(F32)
            partner = jnp.where(s == core, partner_home_ref[pair], partner_away_ref[pair]).astype(F32)
            states = [
                jnp.where(core == 0, a, b)
                for a, b in zip(unpack_states(before), join_states(partner, before))
            ]
            none = jnp.zeros((1, 1), F32)
            main, rest = pack_states(*states, none, none)
            start_ref[s, pair, :LANES] = main
            start_ref[s, pair, LANES:] = rest
            mixed = []
            for half in (0, 1):
                h = 2 * pair + half
                full = num_ref[s, h] + growth[:, h : h + 1] * nt(
                    pq_ref[s, h], as_operand(states[half], half)
                )
                full_ref[s, h] = full
                at = 0 if half else LANES // 2
                sden = full[:, at : at + 1] + full[:, at + 1 : at + 2]
                mixed.append(full * lax.rsqrt(sden * sden + guard))
            pair_mixed = jnp.where(own_lanes(mixed[0].shape, 0), mixed[0], mixed[1])
            mixed_ref[s, :, pair * LANES : (pair + 1) * LANES] = pair_mixed.astype(BF)
        resid = x_ref[s] + nn(mixed_ref[s], wo_ref[...])
        resid_ref[s] = resid
        xhat, _ = norm_rows(resid)
        n2_ref[s] = (xhat * gain_ref[...] + shift_ref[...]).astype(BF)

    each(seqs, one)


def gelu_and_slope(v):
    root = math.sqrt(2.0 / math.pi)
    v2 = v * v
    t = jnp.tanh(v * (root + (root * 0.044715) * v2))
    half = 0.5 * (1.0 + t)
    slope = half + (0.5 * v) * (1.0 - t * t) * (root + (root * 3.0 * 0.044715) * v2)
    return v * half, slope


def feed_kernel(
    og_ref, wi0, wo0, wi2, wo2, half_chip_ref, half_twin_ref, half_both_ref, half_both_twin_ref, n2_ref, resid_ref,
    out_ref, dn2_ref, back_ref, keep_ref, send_ref, far_ref,
):
    twin = lax.axis_index("dp") % 2
    for at, one, two in ((0, half_chip_ref, half_twin_ref), (1, half_both_ref, half_both_twin_ref)):
        for which in range(2):
            rows = one.shape[1]
            far_ref[at, which, aligned(twin, rows)] = one[which]
            far_ref[at, which, aligned(1 - twin, rows)] = two[which]
    (wi1, wo1), (wi3, wo3) = ((far_ref.at[at, 0], far_ref.at[at, 1]) for at in (0, 1))
    n2 = n2_ref[...]
    out_low = og_ref[...].astype(BF)
    total = resid_ref[...]
    dn2 = None
    for block, (wi, wo) in enumerate(((wi0, wo0), (wi1, wo1), (wi2, wo2), (wi3, wo3))):
        active, slope = gelu_and_slope(nn(n2, wi[...]))
        active = active.astype(BF)
        total = total + nn(active, wo[...])
        pre_grad = (nt(out_low, wo[...]) * slope).astype(BF)
        back_ref[block] = pre_grad
        part = nt(pre_grad, wi[...])
        dn2 = part if dn2 is None else dn2 + part
        outer = tn(active, out_low)
        if block < 2:
            keep_ref[block] = outer
        else:
            send_ref[block - 2] = outer.astype(BF)
    out_ref[...] = total
    dn2_ref[...] = dn2


def inner_kernel(n2_ref, back_ref, mixed_ref, low_ref, keep_ref, send_ref):
    own = 2 * my_core() + my_chip()
    width = n2_ref.shape[1]
    rows = width // 4
    for block in range(4):
        inner = tn(n2_ref[...], back_ref[block])
        mixed = tn(mixed_ref[:, aligned(own ^ block, rows)], low_ref[...])
        if block < 2:
            keep_ref[block, :width] = inner
            keep_ref[block, width:] = mixed
        else:
            send_ref[block - 2, :width] = inner.astype(BF)
            send_ref[block - 2, width:] = mixed.astype(BF)


def place_bit(bits):
    place = lax.axis_index("dp")
    return jnp.where(my_core() == 0, (place // (1 << bits[0])) % 2, (place // (1 << bits[1])) % 2)


def split_rows(total, bits, mine_ref, send_ref):
    rows = mine_ref.shape[1]
    high = place_bit(bits) == 1
    first, second = total[:, :rows], total[:, rows:]
    mine_ref[...] = jnp.where(high, second, first)
    send_ref[...] = jnp.where(high, first, second).astype(BF)


def first_kernel(keep1_ref, got1_ref, keep2_ref, got2_ref, mine_ref, send_ref, *, bits):
    total1 = keep1_ref[...] + got1_ref[...].astype(F32)
    total2 = keep2_ref[...] + got2_ref[...].astype(F32)
    split_rows(jnp.concatenate([total1, total2], axis=1), bits, mine_ref, send_ref)


def halve_kernel(keep_ref, got_ref, mine_ref, send_ref, *, bits):
    split_rows(keep_ref[...] + got_ref[...].astype(F32), bits, mine_ref, send_ref)


def third_kernel(keep_ref, got_ref, mine_ref, send_ref, *, bit):
    rows = mine_ref.shape[1]
    total = keep_ref[...] + got_ref[...].astype(F32)
    low, high = total[:, :rows], total[:, rows:]
    by_bit = place_bit((bit, bit)) == 1
    one, two = jnp.where(by_bit, high, low), jnp.where(by_bit, low, high)
    even = my_core() == 0
    for part in range(2):
        of_block = (low, high)[part]
        mine_ref[part] = jnp.where(even, one[part], of_block[0])
        send_ref[part] = jnp.where(even, two[part], of_block[1]).astype(BF)


def fourth_kernel(keep_ref, got_ref, mine_ref, send_ref, *, bit):
    total = keep_ref[...] + got_ref[...].astype(F32)
    second = (my_core() == 1) & (place_bit((bit, bit)) == 1)
    mine_ref[...] = jnp.where(second, total[1], total[0])
    send_ref[...] = jnp.where(second, total[0], total[1]).astype(BF)


def add_kernel(keep_ref, got_ref, out_ref):
    out_ref[...] = (keep_ref[...] + got_ref[...].astype(F32)).astype(out_ref.dtype)


def joined(mine_ref, got_ref, bits):
    high = place_bit(bits) == 1
    mine, got = mine_ref[...].astype(F32), got_ref[...].astype(F32)
    return jnp.concatenate([jnp.where(high, got, mine), jnp.where(high, mine, got)], axis=0)


def join_kernel(mine_ref, got_ref, out_ref, *, bits):
    out_ref[...] = joined(mine_ref, got_ref, bits).astype(BF)


def final_kernel(mine_ref, got_ref, outer_ref, inner_ref, quarter_ref, *, bits):
    both = joined(mine_ref, got_ref, bits)
    rows = outer_ref.shape[0]
    outer_ref[...] = both[:rows]
    inner_ref[...] = both[rows : 2 * rows]
    quarter_ref[...] = both[2 * rows :].astype(BF)


def turn_kernel(
    og_ref, gain_ref, wo_ref, dn2_ref, resid_ref, full_ref, pq_ref, c_ref,
    dres_ref, low_ref, sums_ref, ng_ref, r_ref, away_ref, home_ref,
):
    seqs, heads, length, _ = pq_ref.shape
    sums_ref[...] = jnp.zeros_like(sums_ref)

    def one(s):
        xhat, scale = norm_rows(resid_ref[s])
        dn2 = dn2_ref[s]
        dres = og_ref[s] + norm_rows_backward(dn2, xhat, scale, gain_ref[...])
        dres_ref[s] = dres
        low = dres.astype(BF)
        low_ref[aligned(s, length)] = low
        sums_ref[2:3] += jnp.sum(dn2 * xhat, axis=0, keepdims=True)
        sums_ref[3:4] += jnp.sum(dn2, axis=0, keepdims=True)
        dmixed = nt(low, wo_ref[...])
        c = c_ref[s]
        growth = jnp.exp(c)
        decay = jnp.exp(c[length - 1 :])
        lane = iota(c.shape, 1)
        r_all = jnp.zeros_like(c)
        for pair in range(heads // 2):
            g = dmixed[:, pair * LANES : (pair + 1) * LANES]
            states = []
            for half in (0, 1):
                h = 2 * pair + half
                full = full_ref[s, h]
                at = 0 if half else LANES // 2
                sden = full[:, at : at + 1] + full[:, at + 1 : at + 2]
                inverse = lax.rsqrt(sden * sden + guard)
                inverse2 = inverse * inverse
                mine = own_lanes(g.shape, half)
                dot = lane_sum(jnp.where(mine, g * full, 0.0)) * inverse
                sden_grad = -dot * sden * inverse2
                r_all = jnp.where(lane == h, dot * inverse2 * guard, r_all)
                grads = jnp.where(
                    mine, g * inverse, jnp.where(one_lane(g.shape, half), sden_grad, 0.0)
                )
                ng_ref[s, h] = jnp.concatenate(two_terms(grads), axis=1)
                lifted = jnp.concatenate(two_terms(grads * growth[:, h : h + 1]), axis=1)
                both = tn(lifted, pq_ref[s, h])
                states.append(both[:LANES] + both[LANES:])
            main, rest = pack_states(
                *states, decay[:, 2 * pair : 2 * pair + 1], decay[:, 2 * pair + 1 : 2 * pair + 2]
            )
            put_states(s, pair, main, rest, away_ref, home_ref)
        r_ref[s] = r_all

    each(seqs, one)


def angle_grads(phi, dphi):
    feat = phi.shape[1] // 2
    phi = phi.astype(F32)
    return phi[:, feat:] * dphi[:, :feat] - phi[:, :feat] * dphi[:, feat:]


def weight_grads(left_ref, right_ref, keep_ref, send_ref):
    rows = keep_ref.shape[0]
    core = my_core()
    keep_ref[...] = tn(left_ref[:, aligned(core, rows)], right_ref[...])
    send_ref[...] = tn(left_ref[:, aligned(1 - core, rows)], right_ref[...]).astype(BF)


def back_kernel(
    freq_ref, pq_ref, pk_ref, v_ref, ng_ref, p_ref, c_ref, crow_ref, arow_ref, start_ref,
    qg_ref, kg_ref, vg_ref, kcol_ref,
):
    seqs, heads, length, _ = pq_ref.shape

    def one(s):
        tokens = aligned(s, length)
        c = c_ref[s]
        growth = jnp.exp(c)
        lane = iota(c.shape, 1)
        kcol = jnp.zeros_like(c)
        for pair in range(heads // 2):
            at = pair * LANES
            freq = pair_frequencies(freq_ref, pair).astype(BF)
            states = unpack_states(start_ref[s, pair].astype(F32))
            q_angles, k_angles, v_grads = [], [], []
            for half in (0, 1):
                h = 2 * pair + half
                phi_q, phi_k = pq_ref[s, h], pk_ref[s, h]
                grads = ng_ref[s, h, :, :LANES]
                v = with_ones(v_ref[s, :, at : at + LANES], half)
                weights = decay_weights(c[:, h : h + 1], crow_ref[s, h : h + 1], arow_ref[s, h : h + 1])
                dk = (nt(grads, v.astype(BF)) * weights).astype(BF)
                lifted = (grads.astype(F32) * growth[:, h : h + 1]).astype(BF)
                dphi_q = nn(dk, phi_k) + nn(lifted, states[half].astype(BF))
                q_angles.append(angle_grads(phi_q, dphi_q))
                k_angles.append(angle_grads(phi_k, tn(dk, phi_q)))
                both = tn(p_ref[s, h], ng_ref[s, h])
                dv = both[:, :LANES] + both[:, LANES:]
                v_grads.append(dv)
                kcol = jnp.where(lane == h, lane_sum(v * dv), kcol)
            qg_ref[tokens, at : at + LANES] = nt(
                jnp.concatenate(q_angles, axis=1).astype(BF), freq
            ).astype(BF)
            kg_ref[s, :, at : at + LANES] = nt(jnp.concatenate(k_angles, axis=1).astype(BF), freq)
            vg_ref[s, :, at : at + LANES] = jnp.where(
                own_lanes(v_grads[0].shape, 0), v_grads[0], v_grads[1]
            )
        kcol_ref[s] = kcol

    each(seqs, one)


def queries_kernel(n1_ref, qg_ref, keep_ref, send_ref):
    weight_grads(n1_ref, qg_ref, keep_ref, send_ref)


def cross_kernel(
    got_ref, swapped_ref, partner_home_ref, partner_away_ref, freq_ref, away_ref, home_ref, start_ref, pk_ref, v_ref,
    c_ref, a_ref, r_ref, kcol_ref,
    kg_ref, vg_ref, n1_ref,
    kv_ref, logit_ref, bias_ref, keep_ref, send_ref,
):
    seqs, heads, length, _ = pk_ref.shape
    core = my_core()
    width = kg_ref.shape[2]
    bias_ref[...] = jnp.zeros_like(bias_ref)

    def one(s):
        tokens = aligned(s, length)
        c, a = c_ref[s], a_ref[s]
        tail = jnp.exp(c[length - 1 :] - c) * a
        lane = iota(c.shape, 1)
        lane_row = iota((1, c.shape[1]), 1)
        kcol = kcol_ref[s]
        ends = jnp.zeros((1, c.shape[1]), F32)
        for pair in range(heads // 2):
            at = pair * LANES
            freq = pair_frequencies(freq_ref, pair).astype(BF)
            after = jnp.where(s == core, got_ref[pair], swapped_ref[pair]).astype(F32)
            partner = jnp.where(s == core, partner_home_ref[pair], partner_away_ref[pair]).astype(F32)
            grads = [
                jnp.where(core == 1, a, b)
                for a, b in zip(unpack_states(after), join_states(partner, after))
            ]
            local = jnp.where(s == core, home_ref[pair], away_ref[pair]).astype(F32)
            reached = join_states(local, start_ref[s, pair].astype(F32))
            k_angles, v_grads = [], []
            for half in (0, 1):
                h = 2 * pair + half
                phi_k = pk_ref[s, h]
                v = with_ones(v_ref[s, :, at : at + LANES], half, True)
                grad_low = as_operand(grads[half], half)
                weight = tail[:, h : h + 1]
                k_angles.append(angle_grads(phi_k, nn(v.astype(BF), grad_low)) * weight)
                dv = nt(phi_k, grad_low) * weight
                v_grads.append(dv)
                kcol = kcol + jnp.where(lane == h, lane_sum(v * dv), 0.0)
                end = jnp.sum(lane_sum(grads[half] * reached[half]), axis=0, keepdims=True)
                ends = jnp.where(lane_row == h, end, ends)
            kg = kg_ref[s, :, at : at + LANES] + nt(
                jnp.concatenate(k_angles, axis=1).astype(BF), freq
            )
            vg = vg_ref[s, :, at : at + LANES] + jnp.where(
                own_lanes(v_grads[0].shape, 0), v_grads[0], v_grads[1]
            )
            kv_ref[tokens, at : at + LANES] = kg.astype(BF)
            kv_ref[tokens, width + at : width + at + LANES] = vg.astype(BF)
        keep_grad = running_sum(r_ref[s] - kcol, True) + ends
        logit_grad = a * keep_grad - (1.0 - a) * kcol
        logit_ref[tokens] = logit_grad.astype(BF)
        bias_ref[0:1] += jnp.sum(logit_grad, axis=0, keepdims=True)

    each(seqs, one)
    weight_grads(n1_ref, kv_ref, keep_ref, send_ref)


def close_kernel(
    x_ref, wqkv_ref, gw_ref, gain_ref, qg_ref, kv_ref, logit_ref, bias_ref, n1_ref, dres_ref, sums2_ref,
    dx_ref, small_ref,
):
    width = x_ref.shape[1]
    logit_low = logit_ref[...]
    dn1 = (
        nt(qg_ref[...], wqkv_ref[:, :width])
        + nt(kv_ref[...], wqkv_ref[:, width:])
        + nn(logit_low, wide(gw_ref[...], 0))
    )
    xhat, scale = norm_rows(x_ref[...])
    dx_ref[...] = dres_ref[...] + norm_rows_backward(dn1, xhat, scale, gain_ref[...])
    row = iota((8, width), 0)
    sums = jnp.where(row == 0, jnp.sum(dn1 * xhat, axis=0, keepdims=True), sums2_ref[...])
    sums = jnp.where(row == 1, jnp.sum(dn1, axis=0, keepdims=True), sums)
    bias = jnp.concatenate([bias_ref[0:1], jnp.zeros((1, width - LANES), F32)], axis=1)
    sums = jnp.where(row == 4, bias, sums)
    gates = tn(logit_low, n1_ref[...])[:8]
    stacked = jnp.concatenate([sums, gates, jnp.zeros((LANES - 16, width), F32)], axis=0)
    columns = jnp.transpose(stacked)
    rows = small_ref.shape[0]
    both = columns[:rows] + pltpu.roll(columns[rows:], 16, 1)
    high, low = two_terms(both)
    small_ref[...] = (high.astype(F32) + pltpu.roll(low.astype(F32), LANES // 2, 1)).astype(BF)


def chain_kernel(me_ref, partner_ref, out_ref, *, reverse):
    core = my_core()
    lead = (core == 0) if reverse else (core == 1)
    for pair in range(out_ref.shape[0]):
        mine, other = me_ref[pair].astype(F32), partner_ref[pair].astype(F32)
        first = jnp.where(lead, mine, other)
        second = jnp.where(lead, other, mine)
        none = jnp.zeros((1, 1), F32)
        main, rest = pack_states(*join_states(first, second), none, none)
        out_ref[pair, :LANES] = main
        out_ref[pair, LANES:] = rest


def assemble_kernel(mine_ref, other_ref, quarters_ref, far_ref, qkv_ref, wo_ref, gate_ref, bias_ref, *norm_refs):
    rows, wide = mine_ref.shape[0], qkv_ref.shape[1]
    core, own = my_core(), 2 * my_core() + my_chip()
    qkv_ref[aligned(core, rows)] = mine_ref[:, :wide].astype(F32)
    qkv_ref[aligned(1 - core, rows)] = other_ref[:, :wide].astype(F32)
    for block in range(4):
        quarter = (quarters_ref, far_ref)[block // 2][block % 2]
        wo_ref[aligned(own ^ block, quarter.shape[0])] = quarter.astype(F32)
    columns = mine_ref[:, wide:].astype(F32) + other_ref[:, wide:].astype(F32)
    columns = columns + pltpu.roll(columns, LANES // 2, 1)
    stacked = jnp.transpose(columns)
    heads = gate_ref.shape[0]
    gate_ref[:, :rows] = stacked[8 : 8 + heads]
    gate_ref[:, rows:] = stacked[24 : 24 + heads]
    bias_ref[...] = stacked[4:5, : bias_ref.shape[1]]
    for row, norm_ref in enumerate(norm_refs):
        norm_ref[:, :rows] = stacked[row : row + 1]
        norm_ref[:, rows:] = stacked[16 + row : 17 + row]


class Order:
    def __init__(self):
        self.last = ()

    def call(self, kernel, name, given, kept, outs, scratch=(), wait=(), hbm=False):
        wait = (*self.last, *wait)
        space = pltpu.HBM if hbm else pltpu.VMEM
        given = [pltpu.with_memory_space_constraint(a, space) if hbm else a for a in given]
        kept = [pltpu.with_memory_space_constraint(a, pltpu.VMEM) for a in kept]
        got = pl.pallas_call(
            lambda *refs: kernel(*refs[len(wait) :]),
            out_shape=outs,
            in_specs=[pl.BlockSpec(memory_space=pl.ANY)] * len(wait)
            + [pl.BlockSpec(memory_space=space)] * len(given)
            + [pl.BlockSpec(memory_space=pltpu.VMEM)] * len(kept),
            out_specs=jax.tree.map(lambda _: pl.BlockSpec(memory_space=pltpu.VMEM), outs),
            scratch_shapes=scratch,
            compiler_params=pltpu.CompilerParams(vmem_limit_bytes=VMEM_BYTES),
            cost_estimate=pl.CostEstimate(flops=0, bytes_accessed=0, transcendentals=0),
            name=name,
        )(*wait, *given, *kept)
        self.last = (min(jax.tree.leaves(got), key=lambda a: a.size),)
        return got


def kept(shape, dtype):
    return pltpu.VMEM(shape, dtype)


def shaped(shape, dtype):
    return jax.ShapeDtypeStruct(shape, dtype)


def core_swap(v):
    return jax.tree.map(lambda a: lax.ppermute(a, "mp", [(i, i ^ 1) for i in range(4)]), v)


def chip_swap(v):
    return jax.tree.map(lambda a: lax.ppermute(a, "mp", [(i, i ^ 2) for i in range(4)]), v)


def core_groups():
    count = lax.axis_size("dp")
    return [[4 * d + 2 * x + c for d in range(count) for x in range(2)] for c in range(2)]


def ready_kernel(keep_q_ref, got_q_ref, keep_kv_ref, got_kv_ref, small_ref, out_ref):
    at = 0
    for keep_ref, got_ref in ((keep_q_ref, got_q_ref), (keep_kv_ref, got_kv_ref)):
        width = keep_ref.shape[1]
        out_ref[:, at : at + width] = (keep_ref[...] + got_ref[...].astype(F32)).astype(BF)
        at += width
    out_ref[:, at:] = small_ref[...]


def total_kernel(parts_ref, out_ref, *, width):
    total = jnp.sum(parts_ref[...].astype(F32), axis=0)
    small = total[:, width:]
    small = small + pltpu.roll(small, LANES // 2, 1)
    high, low = two_terms(small)
    lane = iota(small.shape, 1)
    small = jnp.where(lane < LANES // 2, high.astype(F32), low.astype(F32))
    total = jnp.concatenate([total[:, :width], small], axis=1).astype(BF)
    for place in range(out_ref.shape[0]):
        out_ref[place] = total


def to_group(v):
    groups = core_groups()
    return lax.all_to_all(v, ("dp", "mp"), 0, 0, tiled=True, axis_index_groups=groups)


def totals(order, parts, width):
    rows, columns = parts.shape
    count = len(core_groups()[0])
    shape = (count, rows // count, columns)
    kernel = functools.partial(total_kernel, width=width)
    return order.call(kernel, "total", (parts.reshape(shape),), (), shaped(shape, BF)).reshape(rows, columns)


class Stream:
    def __init__(self, order, *first):
        self.order, self.first = order, first
        bits = list(range(lax.axis_size("dp").bit_length() - 1))
        self.bits = [(0, 1), (1, 0)] + [(bit, bit) for bit in bits[2:]]
        self.steps = [self.start]
        self.steps += [functools.partial(self.halve, bits) for bits in self.bits[1:-1]]
        self.steps += [self.third, self.fourth]
        self.steps += [functools.partial(self.double, at) for at in range(len(bits), 0, -1)]

    def step(self):
        self.steps.pop(0)()

    def to_places(self, v, bits):
        way = []
        for place in range(lax.axis_size("dp")):
            for spot in range(4):
                bit = bits[spot % 2]
                to = 4 * place + (spot ^ 2) if bit is None else 4 * (place ^ (1 << bit)) + spot
                way.append((4 * place + spot, to))
        return lax.ppermute(v, ("dp", "mp"), way)

    def split(self, kernel, name, operands, shape, bits):
        self.keep, sent = self.order.call(kernel, name, operands, (), (shaped(shape, F32), shaped(shape, BF)))
        self.got = self.to_places(sent, bits)

    def start(self):
        bits = self.bits[0]
        rows, columns = self.first[0].shape[1] + self.first[2].shape[1], self.first[0].shape[2]
        kernel = functools.partial(first_kernel, bits=bits)
        self.split(kernel, "first", self.first, (2, rows // 2, columns), bits)

    def halve(self, bits):
        _, rows, columns = self.keep.shape
        kernel = functools.partial(halve_kernel, bits=bits)
        self.split(kernel, "halve", (self.keep, self.got), (2, rows // 2, columns), bits)

    def third(self):
        _, rows, columns = self.keep.shape
        bit = self.bits[-1][0]
        kernel = functools.partial(third_kernel, bit=bit)
        self.split(kernel, "third", (self.keep, self.got), (2, rows // 2, columns), (bit, None))

    def fourth(self):
        bit = self.bits[-1][0]
        kernel = functools.partial(fourth_kernel, bit=bit)
        self.split(kernel, "fourth", (self.keep, self.got), self.keep.shape[1:], (None, bit))

    def double(self, at):
        if at == len(self.bits):
            kernel, name, shape = add_kernel, "add", self.keep.shape
        else:
            kernel, name = functools.partial(join_kernel, bits=self.bits[at]), "join"
            shape = (2 * self.keep.shape[0], self.keep.shape[1])
        self.keep = self.order.call(kernel, name, (self.keep, self.got), (), shaped(shape, BF))
        self.got = self.to_places(self.keep, self.bits[at - 1])

    def finish(self, outs):
        while self.steps:
            self.step()
        kernel = functools.partial(final_kernel, bits=self.bits[0])
        return self.order.call(kernel, "final", (self.keep, self.got), (), outs)


def after(v, *others):
    return lax.optimization_barrier((v, others))[0]


def exchange(order, home, partner, reverse, wait=()):
    kernel = functools.partial(chain_kernel, reverse=reverse)
    total = order.call(kernel, "chain", (home, partner), (), shaped(home.shape, BF), wait=wait)
    return lax.ppermute(total, "mp", [(2, 0), (3, 1)] if reverse else [(0, 2), (1, 3)])


def per_device(
    layer_input,
    qkv_weight,
    gate_weight,
    gate_bias,
    out_weight,
    inner_weight,
    outer_weight,
    leading_norm_gain,
    leading_norm_bias,
    trailing_norm_gain,
    trailing_norm_bias,
    random_features,
    output_grad,
):
    seqs, length, width = layer_input.shape
    heads, head, feat = random_features.shape
    pairs = heads // 2
    count = seqs * length
    hidden = inner_weight.shape[1]
    bias = gate_bias.reshape(1, heads)
    gain1, shift1 = leading_norm_gain.reshape(1, width), leading_norm_bias.reshape(1, width)
    gain2, shift2 = trailing_norm_gain.reshape(1, width), trailing_norm_bias.reshape(1, width)

    n_dp = lax.axis_size("dp")
    order = Order()
    halves = order.call(
        pack_kernel,
        "pack",
        (inner_weight, outer_weight),
        (),
        shaped((2, width // 2, hidden), BF),
        [pltpu.SemaphoreType.DMA((2,))],
        hbm=True,
    )
    half_chip = chip_swap(halves)
    inner_core, outer_core = core_swap(inner_weight), core_swap(outer_weight)

    by_seq = (seqs, length, width)
    gates = (seqs, length, LANES)
    states = (pairs, LANES + EXTRA, 2 * feat)
    gate_rows = jnp.transpose(gate_weight)
    sources = (layer_input, qkv_weight, gate_rows, bias, gain1, shift1, random_features)
    normed1, values, c, admit, c_row, a_row, phi_k, away, home = order.call(
        keys_kernel,
        "keys",
        sources,
        (),
        (
            kept(by_seq, BF),
            kept(by_seq, F32),
            kept(gates, F32),
            kept(gates, F32),
            kept((seqs, heads, length), F32),
            kept((seqs, heads, length), F32),
            kept((seqs, heads, length, 2 * feat), BF),
            kept(states, BF),
            kept(states, BF),
        ),
        [pltpu.VMEM(a.shape, a.dtype) for a in sources] + [pltpu.SemaphoreType.DMA((len(sources),))],
        hbm=True,
    )
    partner_home, partner_away = core_swap(away), core_swap(home)
    got = exchange(order, home, partner_home, False, (half_chip,))
    half_twin = lax.ppermute(half_chip, "dp", [(i, i ^ 1) for i in range(n_dp)])

    phi_q, scores, num = order.call(
        scores_kernel,
        "scores",
        (qkv_weight, random_features),
        (normed1, phi_k, values, c, c_row, a_row),
        (
            kept((seqs, heads, length, 2 * feat), BF),
            kept((seqs, heads, length, length), BF),
            kept((seqs, heads, length, LANES), F32),
        ),
    )
    got = after(got, num)
    swapped = core_swap(got)
    half_twin = after(half_twin, num)
    half_both, half_both_twin = core_swap((half_chip, half_twin))
    full, start, mixed_low, resid, normed2 = order.call(
        mix_kernel,
        "mix",
        (layer_input, got, swapped, partner_home, partner_away, out_weight, gain2, shift2),
        (phi_q, c, num),
        (
            kept((seqs, heads, length, LANES), F32),
            kept((seqs, *states), BF),
            kept(by_seq, BF),
            kept(by_seq, F32),
            kept(by_seq, BF),
        ),
    )

    normed1, normed2, mixed_low = (a.reshape(count, width) for a in (normed1, normed2, mixed_low))
    layer_out, dn2, pre_grad, outer_keep, outer_send = order.call(
        feed_kernel,
        "feed",
        (
            output_grad.reshape(count, width), inner_weight, outer_weight, inner_core, outer_core, half_chip, half_twin,
            half_both, half_both_twin,
        ),
        (normed2, resid.reshape(count, width)),
        (
            shaped((count, width), F32),
            kept((count, width), F32),
            kept((4, count, hidden), BF),
            shaped((2, hidden, width), F32),
            shaped((2, hidden, width), BF),
        ),
        [pltpu.VMEM((2, 2, *inner_weight.shape), BF)],
    )
    outer_got = core_swap(outer_send)

    dres, low, sums2, num_grads, r, away_grads, home_grads = order.call(
        turn_kernel,
        "turn",
        (output_grad, gain2, out_weight),
        (dn2.reshape(by_seq), resid, full, phi_q, c),
        (
            kept(by_seq, F32),
            kept((count, width), BF),
            kept((8, width), F32),
            kept((seqs, heads, length, 2 * LANES), BF),
            kept(gates, F32),
            kept(states, BF),
            kept(states, BF),
        ),
    )
    partner_home_grads, partner_away_grads = core_swap(away_grads), core_swap(home_grads)
    got_grads = exchange(order, home_grads, partner_home_grads, True)

    inner_rows = width + width // 4
    inner_keep, inner_send = order.call(
        inner_kernel,
        "inner",
        (),
        (normed2, pre_grad, mixed_low, low),
        (shaped((2, inner_rows, hidden), F32), shaped((2, inner_rows, hidden), BF)),
    )
    stream = Stream(order, outer_keep, outer_got, inner_keep, core_swap(inner_send))
    stream.step()

    q_grad, k_part, v_part, k_col = order.call(
        back_kernel,
        "back",
        (random_features,),
        (phi_q, phi_k, values, num_grads, scores, c, c_row, a_row, start),
        (
            kept((count, width), BF),
            kept(by_seq, F32),
            kept(by_seq, F32),
            kept(gates, F32),
        ),
    )
    keep_q, send_q = order.call(
        queries_kernel,
        "queries",
        (),
        (normed1, q_grad),
        (shaped((width // 2, width), F32), shaped((width // 2, width), BF)),
    )
    got_grads = after(got_grads, k_col)
    swapped_grads = core_swap(got_grads)

    kv_grad, logit_low, bias_sum, keep_kv, send_kv = order.call(
        cross_kernel,
        "cross",
        (got_grads, swapped_grads, partner_home_grads, partner_away_grads, random_features),
        (away, home, start, phi_k, values, c, admit, r, k_col, k_part, v_part, normed1),
        (
            kept((count, 2 * width), BF),
            kept((count, LANES), BF),
            kept((8, LANES), F32),
            shaped((width // 2, 2 * width), F32),
            shaped((width // 2, 2 * width), BF),
        ),
    )
    got_q, got_kv = core_swap(send_q), core_swap(send_kv)
    stream.step()
    dx, small = order.call(
        close_kernel,
        "close",
        (layer_input.reshape(count, width), qkv_weight, gate_rows, gain1),
        (q_grad, kv_grad, logit_low, bias_sum, normed1, dres.reshape(count, width), sums2),
        (shaped((count, width), F32), shaped((width // 2, LANES), BF)),
    )
    ready = order.call(
        ready_kernel,
        "ready",
        (keep_q, got_q, keep_kv, got_kv, small),
        (),
        shaped((width // 2, 3 * width + LANES), BF),
    )
    parts = to_group(ready)
    stream.step()
    total = to_group(totals(order, parts, 3 * width))
    outer_total, inner_total, quarter = stream.finish(
        (shaped((hidden, width), F32), shaped((width, hidden), F32), shaped((width // 4, width), BF))
    )
    quarters = jnp.stack([quarter, chip_swap(quarter)])

    qkv_grad, wo_grad, gate_grad, bias_grad, *norm_grads = order.call(
        assemble_kernel,
        "assemble",
        (total, core_swap(total), quarters, core_swap(quarters)),
        (),
        (
            shaped((width, 3 * width), F32),
            shaped((width, width), F32),
            shaped((heads, width), F32),
            shaped((1, heads), F32),
            *[shaped((1, width), F32)] * 4,
        ),
    )
    return (
        layer_out.reshape(by_seq),
        dx.reshape(by_seq),
        qkv_grad,
        jnp.transpose(gate_grad),
        bias_grad.reshape(heads),
        wo_grad,
        inner_total,
        outer_total,
        *(a.reshape(width) for a in norm_grads),
    )


def solution(mesh):
    in_specs = (
        P("dp", "mp", None),
        P(),
        P(),
        P(),
        P(),
        P(None, "mp"),
        P("mp", None),
        P(),
        P(),
        P(),
        P(),
        P(),
        P("dp", "mp", None),
    )
    out_specs = (
        P("dp", "mp", None),
        P("dp", "mp", None),
        P(),
        P(),
        P(),
        P(),
        P(None, "mp"),
        P("mp", None),
        P(),
        P(),
        P(),
        P(),
    )
    return jax.shard_map(
        per_device, mesh=mesh, in_specs=in_specs, out_specs=out_specs, check_vma=False
    )
```

```python
import functools
import math

import jax
import jax.numpy as jnp
from jax import lax
from jax.experimental import pallas as pl
from jax.experimental.pallas import tpu as pltpu
from jax.sharding import PartitionSpec as P

BF = jnp.bfloat16
F32 = jnp.float32
epsilon = 1e-05
guard = 0.01
LANES = 128
EXTRA = 16
VMEM_BYTES = 16 * 1024 * 1024


def nn(a, b):
    return lax.dot_general(a, b, (((1,), (0,)), ((), ())), preferred_element_type=F32)


def nt(a, b):
    return lax.dot_general(a, b, (((1,), (1,)), ((), ())), preferred_element_type=F32)


def tn(a, b):
    return lax.dot_general(a, b, (((0,), (0,)), ((), ())), preferred_element_type=F32)


def two_terms(v):
    high = v.astype(BF)
    return high, (v - high.astype(F32)).astype(BF)


def iota(shape, dim):
    return lax.broadcasted_iota(jnp.int32, shape, dim)


def triangle(length, upper):
    rows, cols = iota((length, length), 0), iota((length, length), 1)
    return jnp.where((cols >= rows) if upper else (rows >= cols), 1.0, 0.0).astype(BF)


def running_sum(v, upper):
    ones = triangle(v.shape[0], upper)
    high, rest = two_terms(v)
    low = (v - high.astype(F32) - rest.astype(F32)).astype(BF)
    return nn(ones, high) + nn(ones, rest) + nn(ones, low)


def norm_rows(v):
    centred = v - jnp.mean(v, axis=-1, keepdims=True)
    scale = lax.rsqrt(jnp.mean(centred * centred, axis=-1, keepdims=True) + epsilon)
    return centred * scale, scale


def norm_rows_backward(grad, xhat, scale, gain):
    g = grad * gain
    return scale * (
        g
        - jnp.mean(g, axis=-1, keepdims=True)
        - xhat * jnp.mean(g * xhat, axis=-1, keepdims=True)
    )


def pair_frequencies(freq_ref, pair):
    even, odd = freq_ref[2 * pair], freq_ref[2 * pair + 1]
    none = jnp.zeros_like(even)
    return jnp.concatenate(
        [jnp.concatenate([even, none], axis=1), jnp.concatenate([none, odd], axis=1)], axis=0
    )


def scaled_sine_cosine(angles, scale):
    turns = jnp.floor(angles * (1.0 / math.pi) + 0.5)
    r = angles - turns * 3.140625
    r = r - turns * 0.0009675025939941406
    r = r - turns * 1.509958e-07
    odd = turns - 2.0 * jnp.floor(turns * 0.5)
    sign = scale - (2.0 * scale) * odd
    r2 = r * r
    sine = -0.00018362251175623582 * r2 + 0.008306273552368303
    sine = sine * r2 - 0.1666482311215342
    sine = sine * r2 + 0.9999966031254778
    cosine = -0.0012711240835350962 * r2 + 0.041487518673719546
    cosine = cosine * r2 - 0.4999123281046797
    cosine = cosine * r2 + 0.9999933132015835
    return sine * (r * sign), cosine * sign


def pair_features(values, freq, scale):
    high, low = two_terms(values)
    freq_high, freq_low = two_terms(freq)
    both = jnp.concatenate([freq_high, freq_high], axis=0)
    angles = nn(jnp.concatenate([high, low], axis=1), both) + nn(high, freq_low)
    sine, cosine = scaled_sine_cosine(angles, scale)
    sine, cosine = sine.astype(BF), cosine.astype(BF)
    feat = freq.shape[1] // 2
    return [
        jnp.concatenate([sine[:, h * feat : (h + 1) * feat], cosine[:, h * feat : (h + 1) * feat]], axis=1)
        for h in (0, 1)
    ]


def own_lanes(shape, half):
    lane = iota(shape, len(shape) - 1)
    return (lane >= LANES // 2) if half else (lane < LANES // 2)


def one_lane(shape, half):
    return iota(shape, len(shape) - 1) == (0 if half else LANES // 2)


def second_lane(shape, half):
    return iota(shape, len(shape) - 1) == (1 if half else LANES // 2 + 1)


def with_ones(values, half, both=False):
    v = values.astype(F32)
    ones = one_lane(v.shape, half) | (both & second_lane(v.shape, half))
    return jnp.where(own_lanes(v.shape, half), v, jnp.where(ones, 1.0, 0.0))


def pack_states(even, odd, decay_even, decay_odd):
    half = LANES // 2
    row = iota(even.shape, 0)
    states = jnp.where(row < half, even, odd).astype(BF)
    extra = iota((EXTRA, even.shape[1]), 0)
    parts = []
    for value in (even[half : half + 1], odd[0:1], decay_even, decay_odd):
        high = value.astype(BF).astype(F32)
        parts += [high, value - high]
    rows = jnp.zeros((EXTRA, even.shape[1]), F32)
    for at, part in enumerate(parts):
        rows = jnp.where(extra == at, part, rows)
    return states, rows.astype(BF)


def extra_row(packed, at):
    at = LANES + 2 * at
    return packed[at : at + 1] + packed[at + 1 : at + 2]


def decays(packed):
    return extra_row(packed, 2), extra_row(packed, 3)


def unpack_states(packed):
    half = LANES // 2
    states = packed[:LANES]
    row = iota(states.shape, 0)
    even = jnp.where(row < half, states, jnp.where(row == half, extra_row(packed, 0), 0.0))
    odd = jnp.where(row >= half, states, jnp.where(row == 0, extra_row(packed, 1), 0.0))
    return even, odd


def join_states(first, second):
    return [
        a + decay * b
        for a, b, decay in zip(unpack_states(first), unpack_states(second), decays(first))
    ]


def as_operand(state, half):
    at = 0 if half else LANES // 2
    norm = state[at : at + 1]
    rest = norm - norm.astype(BF).astype(F32)
    return jnp.where(iota(state.shape, 0) == at + 1, rest, state).astype(BF)


def decay_weights(c_col, c_row, a_row):
    length = c_col.shape[0]
    gap = jnp.minimum(c_col - c_row, 0.0)
    causal = iota((length, length), 0) >= iota((length, length), 1)
    return jnp.where(causal, jnp.exp(gap) * a_row, 0.0)


def lane_sum(v):
    return jnp.sum(v, axis=1, keepdims=True)


def each(count, step):
    lax.fori_loop(0, count, lambda i, none: (step(i), none)[1], 0)


def wide(v, axis):
    none = list(v.shape)
    none[axis] = LANES - v.shape[axis]
    return jnp.concatenate([v, jnp.zeros(none, v.dtype)], axis=axis)


def aligned(at, size):
    return pl.ds(pl.multiple_of(at * size, size), size)


def my_core():
    return lax.axis_index("mp") % 2


def my_chip():
    return lax.axis_index("mp") // 2


def pack_kernel(inner_ref, outer_ref, out_ref, sems):
    rows = out_ref.shape[1]
    mine = aligned(lax.axis_index("dp") % 2, rows)
    copies = [
        pltpu.make_async_copy(source.at[mine], out_ref.at[i], sems.at[i])
        for i, source in enumerate((inner_ref, outer_ref))
    ]
    for copy in copies:
        copy.start()
    for copy in copies:
        copy.wait()


def by_place(of_sequence):
    even = my_core() == 0
    one, two = of_sequence
    return jnp.where(even, two, one), jnp.where(even, one, two)


def put_states(pair, packed, away_ref, home_ref):
    for rows, parts in ((slice(0, LANES), [p[0] for p in packed]), (slice(LANES, None), [p[1] for p in packed])):
        away_ref[pair, rows], home_ref[pair, rows] = by_place(parts)


def keys_kernel(
    x_hbm, wqkv_hbm, gw_hbm, gb_hbm, gain_hbm, shift_hbm, freq_hbm,
    n1_ref, v_ref, c_ref, a_ref, crow_ref, arow_ref, pk_ref, away_ref, home_ref,
    x_ref, w_ref, gw_ref, gb_ref, gain_ref, shift_ref, freq_ref, sems,
):
    heads, _, feat = freq_ref.shape
    seqs, length, width = x_ref.shape
    sources = (x_hbm, gain_hbm, shift_hbm, gw_hbm, gb_hbm, wqkv_hbm.at[:, pl.ds(width, 2 * width)], freq_hbm)
    buffers = (x_ref, gain_ref, shift_ref, gw_ref, gb_ref, w_ref, freq_ref)
    copies = [
        pltpu.make_async_copy(source, buffer, sems.at[i])
        for i, (source, buffer) in enumerate(zip(sources, buffers))
    ]
    for copy in copies:
        copy.start()
    for copy in copies[:5]:
        copy.wait()
    scale = 1.0 / math.sqrt(feat)
    xhat, _ = norm_rows(x_ref[...].reshape(seqs * length, width))
    n1 = (xhat * gain_ref[...] + shift_ref[...]).astype(BF)
    n1_ref[...] = n1
    z = nt(n1, wide(gw_ref[...], 0)) + wide(gb_ref[...], 1)
    e = jnp.exp(-jnp.abs(z))
    log_keep = jnp.minimum(z, 0.0) - jnp.log1p(e)
    inverse = 1.0 / (1.0 + e)
    admit_all = jnp.where(z > 0.0, e * inverse, inverse)
    tails, decay = [], []
    for s in range(seqs):
        rows = slice(s * length, (s + 1) * length)
        c = running_sum(log_keep[rows], False)
        admit = admit_all[rows]
        c_ref[s] = c
        a_ref[s] = admit
        crow_ref[s] = jnp.transpose(c)[:heads]
        arow_ref[s] = jnp.transpose(admit)[:heads]
        last = c[length - 1 :]
        tails.append(jnp.exp(last - c) * admit)
        decay.append(jnp.exp(last))
    for copy in copies[5:]:
        copy.wait()
    keys = nn(n1, w_ref[:, :width])
    values = nn(n1, w_ref[:, width:])
    v_ref[...] = values.reshape(v_ref.shape)
    for pair in range(heads // 2):
        lanes = slice(pair * LANES, (pair + 1) * LANES)
        phi = pair_features(keys[:, lanes], pair_frequencies(freq_ref, pair), scale)
        packed = []
        for s in range(seqs):
            rows = slice(s * length, (s + 1) * length)
            states = []
            for half in (0, 1):
                h = 2 * pair + half
                phi_k = phi[half][rows]
                pk_ref[s, h] = phi_k
                weighted = with_ones(values[rows, lanes], half) * tails[s][:, h : h + 1]
                both = tn(jnp.concatenate(two_terms(weighted), axis=1), phi_k)
                states.append(both[:LANES] + both[LANES:])
            h = 2 * pair
            packed.append(pack_states(*states, decay[s][:, h : h + 1], decay[s][:, h + 1 : h + 2]))
        put_states(pair, packed, away_ref, home_ref)


def scores_kernel(wqkv_ref, freq_ref, n1_ref, pk_ref, v_ref, c_ref, crow_ref, arow_ref, pq_ref, p_ref, num_ref):
    seqs, heads, length, _ = pk_ref.shape
    scale = 1.0 / math.sqrt(freq_ref.shape[2])
    queries = nn(n1_ref[...], wqkv_ref[:, : n1_ref.shape[1]])
    for pair in range(heads // 2):
        lanes = slice(pair * LANES, (pair + 1) * LANES)
        phi = pair_features(queries[:, lanes], pair_frequencies(freq_ref, pair), scale)
        for s in range(seqs):
            for half in (0, 1):
                h = 2 * pair + half
                phi_q = phi[half][s * length : (s + 1) * length]
                pq_ref[s, h] = phi_q
                v = with_ones(v_ref[s, :, lanes], half)
                weights = decay_weights(
                    c_ref[s, :, h : h + 1], crow_ref[s, h : h + 1], arow_ref[s, h : h + 1]
                )
                p = (nt(phi_q, pk_ref[s, h]) * weights).astype(BF)
                p_ref[s, h] = p
                both = nn(p, jnp.concatenate(two_terms(v), axis=1))
                num_ref[s, h] = both[:, :LANES] + both[:, LANES:]


def mix_kernel(
    x_ref, got_ref, swapped_ref, partner_home_ref, partner_away_ref, wo_ref, gain_ref, shift_ref, pq_ref, c_ref, num_ref,
    full_ref, start_ref, mixed_ref, resid_ref, n2_ref,
):
    seqs, heads = pq_ref.shape[:2]
    core = my_core()

    def one(s):
        growth = jnp.exp(c_ref[s])
        for pair in range(heads // 2):
            before = jnp.where(s == core, got_ref[pair], swapped_ref[pair]).astype(F32)
            partner = jnp.where(s == core, partner_home_ref[pair], partner_away_ref[pair]).astype(F32)
            states = [
                jnp.where(core == 0, a, b)
                for a, b in zip(unpack_states(before), join_states(partner, before))
            ]
            none = jnp.zeros((1, 1), F32)
            main, rest = pack_states(*states, none, none)
            start_ref[s, pair, :LANES] = main
            start_ref[s, pair, LANES:] = rest
            mixed = []
            for half in (0, 1):
                h = 2 * pair + half
                full = num_ref[s, h] + growth[:, h : h + 1] * nt(
                    pq_ref[s, h], as_operand(states[half], half)
                )
                full_ref[s, h] = full
                at = 0 if half else LANES // 2
                sden = full[:, at : at + 1] + full[:, at + 1 : at + 2]
                mixed.append(full * lax.rsqrt(sden * sden + guard))
            pair_mixed = jnp.where(own_lanes(mixed[0].shape, 0), mixed[0], mixed[1])
            mixed_ref[s, :, pair * LANES : (pair + 1) * LANES] = pair_mixed.astype(BF)
        resid = x_ref[s] + nn(mixed_ref[s], wo_ref[...])
        resid_ref[s] = resid
        xhat, _ = norm_rows(resid)
        n2_ref[s] = (xhat * gain_ref[...] + shift_ref[...]).astype(BF)

    for s in range(seqs):
        one(s)


def gelu_and_slope(v):
    root = math.sqrt(2.0 / math.pi)
    v2 = v * v
    t = jnp.tanh(v * (root + (root * 0.044715) * v2))
    half = 0.5 * (1.0 + t)
    slope = half + (0.5 * v) * (1.0 - t * t) * (root + (root * 3.0 * 0.044715) * v2)
    return v * half, slope


def feed_block(n2, out_low, wi_ref, wo_ref):
    active, slope = gelu_and_slope(nn(n2, wi_ref[...]))
    active = active.astype(BF)
    pre_grad = (nt(out_low, wo_ref[...]) * slope).astype(BF)
    return nn(active, wo_ref[...]), nt(pre_grad, wi_ref[...]), tn(n2, pre_grad), tn(active, out_low)


def halves_together(far_ref, one, two):
    twin = lax.axis_index("dp") % 2
    rows = one.shape[1]
    for which in range(2):
        far_ref[which, aligned(twin, rows)] = one[which]
        far_ref[which, aligned(1 - twin, rows)] = two[which]


def feed_near_kernel(og_ref, wi0, wo0, wi2, wo2, n2_ref, resid_ref, out_ref, dn2_ref, low_ref, keep_ref, send_ref):
    low_ref[...] = og_ref[...].astype(BF)
    n2, out_low = n2_ref[...], low_ref[...]
    rows = n2.shape[1]
    out, dn2, inner, outer = feed_block(n2, out_low, wi2, wo2)
    send_ref[:rows] = inner.astype(BF)
    send_ref[rows:] = outer.astype(BF)
    out_own, dn2_own, inner, outer = feed_block(n2, out_low, wi0, wo0)
    keep_ref[:rows] = inner
    keep_ref[rows:] = outer
    out_ref[...] = resid_ref[...] + out + out_own
    dn2_ref[...] = dn2 + dn2_own


def feed_far_kernel(half_ref, twin_ref, n2_ref, low_ref, part_ref, dn2_part_ref, out_ref, dn2_ref, grad_ref, far_ref):
    twin = lax.axis_index("dp") % 2
    rows = half_ref.shape[1]
    for which in range(2):
        far_ref[which, aligned(twin, rows)] = half_ref[which]
        far_ref[which, aligned(1 - twin, rows)] = twin_ref[which]
    n2 = n2_ref[...]
    out, dn2, inner, outer = feed_block(n2, low_ref[...], far_ref.at[0], far_ref.at[1])
    out_ref[...] = part_ref[...] + out
    dn2_ref[...] = dn2_part_ref[...] + dn2
    rows = n2.shape[1]
    grad_ref[:rows] = inner.astype(grad_ref.dtype)
    grad_ref[rows:] = outer.astype(grad_ref.dtype)


def feed_last_kernel(
    half_ref, twin_ref, n2_ref, low_ref, part_ref, dn2_part_ref, out_hbm, dn2_ref, grad_ref, far_ref, out_ref, sem
):
    feed_far_kernel(half_ref, twin_ref, n2_ref, low_ref, part_ref, dn2_part_ref, out_ref, dn2_ref, grad_ref, far_ref)
    copy = pltpu.make_async_copy(out_ref, out_hbm, sem)
    copy.start()
    copy.wait()


def place_bit(bits):
    place = lax.axis_index("dp")
    return jnp.where(my_core() == 0, (place // (1 << bits[0])) % 2, (place // (1 << bits[1])) % 2)


def split_rows(total, bits, mine_ref, send_ref):
    rows = mine_ref.shape[1]
    high = place_bit(bits) == 1
    first, second = total[:, :rows], total[:, rows:]
    mine_ref[...] = jnp.where(high, second, first)
    send_ref[...] = jnp.where(high, first, second).astype(BF)


def halve_kernel(keep_ref, got_ref, mine_ref, send_ref, *, bits):
    split_rows(keep_ref[...] + got_ref[...].astype(F32), bits, mine_ref, send_ref)


def first_kernel(keep0_ref, keep1_ref, got0_ref, got1_ref, mine_ref, send_ref, *, bits):
    for block, (keep_ref, got_ref) in enumerate(((keep0_ref, got0_ref), (keep1_ref, got1_ref))):
        total = (keep_ref[...] + got_ref[...].astype(F32))[None]
        split_rows(total, bits, mine_ref.at[block : block + 1], send_ref.at[block : block + 1])


def third_kernel(keep_ref, got_ref, mine_ref, send_ref, *, bit):
    rows = mine_ref.shape[1]
    total = keep_ref[...] + got_ref[...].astype(F32)
    low, high = total[:, :rows], total[:, rows:]
    by_bit = place_bit((bit, bit)) == 1
    one, two = jnp.where(by_bit, high, low), jnp.where(by_bit, low, high)
    even = my_core() == 0
    for part in range(2):
        of_block = (low, high)[part]
        mine_ref[part] = jnp.where(even, one[part], of_block[0])
        send_ref[part] = jnp.where(even, two[part], of_block[1]).astype(BF)


def fourth_kernel(keep_ref, got_ref, mine_ref, send_ref, *, bit):
    total = keep_ref[...] + got_ref[...].astype(F32)
    second = (my_core() == 1) & (place_bit((bit, bit)) == 1)
    mine_ref[...] = jnp.where(second, total[1], total[0])
    send_ref[...] = jnp.where(second, total[0], total[1]).astype(BF)


def add_kernel(keep_ref, got_ref, out_ref):
    out_ref[...] = (keep_ref[...] + got_ref[...].astype(F32)).astype(out_ref.dtype)


def joined(mine_ref, got_ref, bits):
    high = place_bit(bits) == 1
    mine, got = mine_ref[...].astype(F32), got_ref[...].astype(F32)
    return jnp.concatenate([jnp.where(high, got, mine), jnp.where(high, mine, got)], axis=0)


def join_kernel(mine_ref, got_ref, out_ref, *, bits):
    out_ref[...] = joined(mine_ref, got_ref, bits).astype(BF)


def final_kernel(mine_ref, got_ref, inner_hbm, outer_hbm, mark_ref, whole_ref, sems, *, bits):
    mark_ref[...] = jnp.zeros_like(mark_ref)
    whole_ref[...] = joined(mine_ref, got_ref, bits)
    rows = inner_hbm.shape[0]
    copies = [
        pltpu.make_async_copy(whole_ref.at[pl.ds(at * rows, rows)], out_hbm, sems.at[at])
        for at, out_hbm in enumerate((inner_hbm, outer_hbm))
    ]
    for copy in copies:
        copy.start()
    for copy in copies:
        copy.wait()


def turn_kernel(
    og_ref, gain_ref, wo_ref, dn2_ref, resid_ref, full_ref, pq_ref, c_ref,
    dres_ref, low_ref, sums_ref, ng_ref, r_ref, away_ref, home_ref,
):
    seqs, heads, length, _ = pq_ref.shape
    sums_ref[...] = jnp.zeros_like(sums_ref)
    packed = [[] for _ in range(seqs)]

    def one(s):
        xhat, scale = norm_rows(resid_ref[s])
        dn2 = dn2_ref[s]
        dres = og_ref[s] + norm_rows_backward(dn2, xhat, scale, gain_ref[...])
        dres_ref[s] = dres
        low = dres.astype(BF)
        low_ref[s * length : (s + 1) * length] = low
        sums_ref[2:3] += jnp.sum(dn2 * xhat, axis=0, keepdims=True)
        sums_ref[3:4] += jnp.sum(dn2, axis=0, keepdims=True)
        dmixed = nt(low, wo_ref[...])
        c = c_ref[s]
        growth = jnp.exp(c)
        decay = jnp.exp(c[length - 1 :])
        lane = iota(c.shape, 1)
        r_all = jnp.zeros_like(c)
        for pair in range(heads // 2):
            g = dmixed[:, pair * LANES : (pair + 1) * LANES]
            states = []
            for half in (0, 1):
                h = 2 * pair + half
                full = full_ref[s, h]
                at = 0 if half else LANES // 2
                sden = full[:, at : at + 1] + full[:, at + 1 : at + 2]
                inverse = lax.rsqrt(sden * sden + guard)
                inverse2 = inverse * inverse
                mine = own_lanes(g.shape, half)
                dot = lane_sum(jnp.where(mine, g * full, 0.0)) * inverse
                sden_grad = -dot * sden * inverse2
                r_all = jnp.where(lane == h, dot * inverse2 * guard, r_all)
                grads = jnp.where(
                    mine, g * inverse, jnp.where(one_lane(g.shape, half), sden_grad, 0.0)
                )
                ng_ref[s, h] = jnp.concatenate(two_terms(grads), axis=1)
                lifted = jnp.concatenate(two_terms(grads * growth[:, h : h + 1]), axis=1)
                both = tn(lifted, pq_ref[s, h])
                states.append(both[:LANES] + both[LANES:])
            h = 2 * pair
            packed[s].append(pack_states(*states, decay[:, h : h + 1], decay[:, h + 1 : h + 2]))
        r_ref[s] = r_all

    for s in range(seqs):
        one(s)
    for pair, both in enumerate(zip(*packed)):
        put_states(pair, both, away_ref, home_ref)


def angle_grads(phi, dphi):
    feat = phi.shape[1] // 2
    phi = phi.astype(F32)
    return phi[:, feat:] * dphi[:, :feat] - phi[:, :feat] * dphi[:, feat:]


def weight_grads(left_ref, right_ref, keep_ref, send_refs):
    rows = keep_ref.shape[0]
    core = my_core()
    keep_ref[...] = tn(left_ref[:, aligned(core, rows)], right_ref[...])
    away = tn(left_ref[:, aligned(1 - core, rows)], right_ref[...]).astype(BF)
    rows //= len(send_refs)
    for part, send_ref in enumerate(send_refs):
        send_ref[...] = away[part * rows : (part + 1) * rows]


def back_kernel(
    freq_ref, pq_ref, pk_ref, v_ref, ng_ref, p_ref, c_ref, crow_ref, arow_ref, start_ref,
    qg_ref, kg_ref, vg_ref, kcol_ref,
):
    seqs, heads, length, _ = pq_ref.shape

    def one(s):
        tokens = aligned(s, length)
        c = c_ref[s]
        growth = jnp.exp(c)
        lane = iota(c.shape, 1)
        kcol = jnp.zeros_like(c)
        for pair in range(heads // 2):
            at = pair * LANES
            freq = pair_frequencies(freq_ref, pair).astype(BF)
            states = unpack_states(start_ref[s, pair].astype(F32))
            q_angles, k_angles, v_grads = [], [], []
            for half in (0, 1):
                h = 2 * pair + half
                phi_q, phi_k = pq_ref[s, h], pk_ref[s, h]
                grads = ng_ref[s, h, :, :LANES]
                v = with_ones(v_ref[s, :, at : at + LANES], half)
                weights = decay_weights(c[:, h : h + 1], crow_ref[s, h : h + 1], arow_ref[s, h : h + 1])
                dk = (nt(grads, v.astype(BF)) * weights).astype(BF)
                lifted = (grads.astype(F32) * growth[:, h : h + 1]).astype(BF)
                dphi_q = nn(dk, phi_k) + nn(lifted, states[half].astype(BF))
                q_angles.append(angle_grads(phi_q, dphi_q))
                k_angles.append(angle_grads(phi_k, tn(dk, phi_q)))
                both = tn(p_ref[s, h], ng_ref[s, h])
                dv = both[:, :LANES] + both[:, LANES:]
                v_grads.append(dv)
                kcol = jnp.where(lane == h, lane_sum(v * dv), kcol)
            qg_ref[tokens, at : at + LANES] = nt(
                jnp.concatenate(q_angles, axis=1).astype(BF), freq
            ).astype(BF)
            kg_ref[s, :, at : at + LANES] = nt(jnp.concatenate(k_angles, axis=1).astype(BF), freq)
            vg_ref[s, :, at : at + LANES] = jnp.where(
                own_lanes(v_grads[0].shape, 0), v_grads[0], v_grads[1]
            )
        kcol_ref[s] = kcol

    each(seqs, one)


def products_kernel(x_ref, wqkv_ref, mixed_ref, low_ref, n1_ref, qg_ref, keep_ref, send_ref, part_ref, xhat_ref, scale_ref):
    width = low_ref.shape[1]
    part_ref[...] = nt(qg_ref[...], wqkv_ref[:, :width])
    xhat, scale = norm_rows(x_ref[...])
    xhat_ref[...] = xhat
    scale_ref[...] = jnp.broadcast_to(scale, scale_ref.shape)
    for at, left_ref, right_ref in ((0, mixed_ref, low_ref), (width, n1_ref, qg_ref)):
        lanes = pl.ds(at, width)
        weight_grads(left_ref, right_ref, keep_ref.at[:, lanes], [send_ref.at[:, lanes]])


def cross_kernel(
    got_ref, swapped_ref, partner_home_ref, partner_away_ref, freq_ref, away_ref, home_ref, start_ref, pk_ref, v_ref,
    c_ref, a_ref, r_ref, kcol_ref,
    kg_ref, vg_ref, n1_ref,
    kv_ref, logit_ref, bias_ref, keep_ref, *send_refs,
):
    seqs, heads, length, _ = pk_ref.shape
    core = my_core()
    width = kg_ref.shape[2]
    bias_ref[...] = jnp.zeros_like(bias_ref)

    def one(s):
        tokens = aligned(s, length)
        c, a = c_ref[s], a_ref[s]
        tail = jnp.exp(c[length - 1 :] - c) * a
        lane = iota(c.shape, 1)
        lane_row = iota((1, c.shape[1]), 1)
        kcol = kcol_ref[s]
        ends = jnp.zeros((1, c.shape[1]), F32)
        for pair in range(heads // 2):
            at = pair * LANES
            freq = pair_frequencies(freq_ref, pair).astype(BF)
            after = jnp.where(s == core, got_ref[pair], swapped_ref[pair]).astype(F32)
            partner = jnp.where(s == core, partner_home_ref[pair], partner_away_ref[pair]).astype(F32)
            grads = [
                jnp.where(core == 1, a, b)
                for a, b in zip(unpack_states(after), join_states(partner, after))
            ]
            local = jnp.where(s == core, home_ref[pair], away_ref[pair]).astype(F32)
            reached = join_states(local, start_ref[s, pair].astype(F32))
            k_angles, v_grads = [], []
            for half in (0, 1):
                h = 2 * pair + half
                phi_k = pk_ref[s, h]
                v = with_ones(v_ref[s, :, at : at + LANES], half, True)
                grad_low = as_operand(grads[half], half)
                weight = tail[:, h : h + 1]
                k_angles.append(angle_grads(phi_k, nn(v.astype(BF), grad_low)) * weight)
                dv = nt(phi_k, grad_low) * weight
                v_grads.append(dv)
                kcol = kcol + jnp.where(lane == h, lane_sum(v * dv), 0.0)
                end = jnp.sum(lane_sum(grads[half] * reached[half]), axis=0, keepdims=True)
                ends = jnp.where(lane_row == h, end, ends)
            kg = kg_ref[s, :, at : at + LANES] + nt(
                jnp.concatenate(k_angles, axis=1).astype(BF), freq
            )
            vg = vg_ref[s, :, at : at + LANES] + jnp.where(
                own_lanes(v_grads[0].shape, 0), v_grads[0], v_grads[1]
            )
            kv_ref[tokens, at : at + LANES] = kg.astype(BF)
            kv_ref[tokens, width + at : width + at + LANES] = vg.astype(BF)
        keep_grad = running_sum(r_ref[s] - kcol, True) + ends
        logit_grad = a * keep_grad - (1.0 - a) * kcol
        logit_ref[tokens] = logit_grad.astype(BF)
        bias_ref[0:1] += jnp.sum(logit_grad, axis=0, keepdims=True)

    for i in range(seqs):
        one(i)
    weight_grads(n1_ref, kv_ref, keep_ref, send_refs)


def close_kernel(
    wqkv_ref, gw_ref, gain_ref, part_ref, xhat_ref, scale_ref, kv_ref, logit_ref, bias_ref, n1_ref, dres_ref, sums2_ref,
    dx_ref, small_ref,
):
    width = part_ref.shape[1]
    logit_low = logit_ref[...]
    dn1 = part_ref[...] + nt(kv_ref[...], wqkv_ref[:, width:]) + nn(logit_low, wide(gw_ref[...], 0))
    xhat = xhat_ref[...]
    dx_ref[...] = dres_ref[...] + norm_rows_backward(dn1, xhat, scale_ref[:, :1], gain_ref[...])
    row = iota((8, width), 0)
    sums = jnp.where(row == 0, jnp.sum(dn1 * xhat, axis=0, keepdims=True), sums2_ref[...])
    sums = jnp.where(row == 1, jnp.sum(dn1, axis=0, keepdims=True), sums)
    bias = jnp.concatenate([bias_ref[0:1], jnp.zeros((1, width - LANES), F32)], axis=1)
    sums = jnp.where(row == 4, bias, sums)
    gates = tn(logit_low, n1_ref[...])[:8]
    stacked = jnp.concatenate([sums, gates, jnp.zeros((LANES - 16, width), F32)], axis=0)
    columns = jnp.transpose(stacked)
    rows = small_ref.shape[0]
    small_ref[...] = columns[:rows] + pltpu.roll(columns[rows:], 16, 1)


def chain_kernel(me_ref, partner_ref, out_ref, *, reverse):
    core = my_core()
    lead = (core == 0) if reverse else (core == 1)
    for pair in range(out_ref.shape[0]):
        mine, other = me_ref[pair].astype(F32), partner_ref[pair].astype(F32)
        first = jnp.where(lead, mine, other)
        second = jnp.where(lead, other, mine)
        none = jnp.zeros((1, 1), F32)
        main, rest = pack_states(*join_states(first, second), none, none)
        out_ref[pair, :LANES] = main
        out_ref[pair, LANES:] = rest


def widen(v):
    main, last = v[:, :-LANES].astype(F32), v[:, -LANES:].astype(F32)
    last = jnp.where(iota(last.shape, 1) < LANES // 2, last + pltpu.roll(last, LANES // 2, 1), 0.0)
    return jnp.concatenate([main, last], axis=1)


def narrow(v):
    main, last = v[:, :-LANES].astype(BF), v[:, -LANES:]
    high, low = two_terms(last)
    last = high.astype(F32) + pltpu.roll(low.astype(F32), LANES // 2, 1)
    return jnp.concatenate([main, last.astype(BF)], axis=1)


def link_bit(link):
    return my_chip() if link is None else (lax.axis_index("dp") // (1 << link)) % 2


def piece_number(links):
    number = 0
    for of_zero, of_one in links:
        bit = link_bit(of_zero)
        if of_one != of_zero:
            bit = jnp.where(my_core() == 0, bit, link_bit(of_one))
        number = 2 * number + bit
    return number


def pick(pieces, number):
    taken = pieces[0]
    for at in range(1, len(pieces)):
        taken = jnp.where(number == at, pieces[at], taken)
    return taken


def share_out(total, links, mine_ref, send_refs):
    rows = mine_ref.shape[0]
    pieces = [total[at : at + rows] for at in range(0, total.shape[0], rows)]
    number = piece_number(links)
    mine_ref[...] = pick(pieces, number)
    for k, send_ref in enumerate(send_refs):
        send_ref[...] = narrow(pick(pieces, number ^ (k + 1)))


def gather_kernel(keep1_ref, got1_ref, keep2_ref, *refs, links):
    *got2_refs, small_ref, mine_ref, send_ref = refs
    first = keep1_ref[...] + got1_ref[...].astype(F32)
    second = keep2_ref[...] + jnp.concatenate([ref[...].astype(F32) for ref in got2_refs], axis=0)
    total = jnp.concatenate([first, second, small_ref[...]], axis=1)
    share_out(total, links, mine_ref, [send_ref])


def part_kernel(keep_ref, got_ref, mine_ref, send_ref, *, links):
    share_out(keep_ref[...] + widen(got_ref[...]), links, mine_ref, [send_ref])


def whole_kernel(keep_ref, got_ref, out_ref):
    out_ref[...] = narrow(keep_ref[...] + widen(got_ref[...]))


def sum_kernel(mine_ref, got_ref, out_ref):
    out_ref[...] = narrow(widen(mine_ref[...]) + widen(got_ref[...]))


def group_kernel(*refs, links):
    pieces = [ref[...].astype(F32) for ref in refs[:-1]]
    number = piece_number(links)
    both = [pick(pieces, number ^ at) for at in range(len(pieces))]
    refs[-1][...] = jnp.concatenate(both, axis=0).astype(BF)


def assemble_kernel(mine_ref, other_ref, qkv_ref, wo_ref, gate_ref, bias_ref, *norm_refs):
    rows, width = mine_ref.shape[0], wo_ref.shape[1]
    core = my_core()
    for place, half_ref in ((core, mine_ref), (1 - core, other_ref)):
        wo_ref[aligned(place, rows)] = half_ref[:, :width].astype(F32)
        qkv_ref[aligned(place, rows)] = half_ref[:, width:-LANES].astype(F32)
    columns = mine_ref[:, -LANES:].astype(F32) + other_ref[:, -LANES:].astype(F32)
    columns = columns + pltpu.roll(columns, LANES // 2, 1)
    stacked = jnp.transpose(columns)
    heads = gate_ref.shape[0]
    gate_ref[:, :rows] = stacked[8 : 8 + heads]
    gate_ref[:, rows:] = stacked[24 : 24 + heads]
    bias_ref[...] = stacked[4:5, : bias_ref.shape[1]]
    for row, norm_ref in enumerate(norm_refs):
        norm_ref[:, :rows] = stacked[row : row + 1]
        norm_ref[:, rows:] = stacked[16 + row : 17 + row]


def in_hbm(out):
    return getattr(out, "memory_space", None) == pltpu.HBM


def out_spec(out):
    return pl.BlockSpec(memory_space=pltpu.HBM if in_hbm(out) else pltpu.VMEM)


class Job:
    def __init__(self, kernel, name, operands, outs, use):
        self.kernel, self.name, self.operands, self.outs, self.use = kernel, name, operands, outs, use


class Order:
    def __init__(self):
        self.last = ()

    def call(self, kernel, name, given, kept, outs, scratch=(), wait=(), hbm=False):
        wait = (*self.last, *wait)
        space = pltpu.HBM if hbm else pltpu.VMEM
        given = [pltpu.with_memory_space_constraint(a, space) if hbm else a for a in given]
        kept = [pltpu.with_memory_space_constraint(a, pltpu.VMEM) for a in kept]
        got = pl.pallas_call(
            lambda *refs: kernel(*refs[len(wait) :]),
            out_shape=outs,
            in_specs=[pl.BlockSpec(memory_space=pl.ANY)] * len(wait)
            + [pl.BlockSpec(memory_space=space)] * len(given)
            + [pl.BlockSpec(memory_space=pltpu.VMEM)] * len(kept),
            out_specs=jax.tree.map(out_spec, outs),
            scratch_shapes=scratch,
            compiler_params=pltpu.CompilerParams(vmem_limit_bytes=VMEM_BYTES),
            cost_estimate=pl.CostEstimate(flops=0, bytes_accessed=0, transcendentals=0),
            name=name,
        )(*wait, *given, *kept)
        inside = [a for a, out in zip(jax.tree.leaves(got), jax.tree.leaves(outs)) if not in_hbm(out)]
        if inside:
            self.last = (min(inside, key=lambda a: a.size),)
        return got


    def run(self, *jobs):
        takes = [len(job.operands) for job in jobs]
        gives = [len(job.outs) for job in jobs]

        def kernel(*refs):
            given, made = refs[: sum(takes)], refs[sum(takes) :]
            for job, take, give in zip(jobs, takes, gives):
                job.kernel(*given[:take], *made[:give])
                given, made = given[take:], made[give:]

        operands = [a for job in jobs for a in job.operands]
        outs = tuple(out for job in jobs for out in job.outs)
        got = list(self.call(kernel, "_".join(job.name for job in jobs), operands, (), outs))
        for job, give in zip(jobs, gives):
            job.use(*got[:give])
            got = got[give:]


def kept(shape, dtype):
    return pltpu.VMEM(shape, dtype)


def shaped(shape, dtype):
    return jax.ShapeDtypeStruct(shape, dtype)


def core_swap(v):
    return jax.tree.map(lambda a: lax.ppermute(a, "mp", [(i, i ^ 1) for i in range(4)]), v)


def chip_swap(v):
    return jax.tree.map(lambda a: lax.ppermute(a, "mp", [(i, i ^ 2) for i in range(4)]), v)


def send_along(v, links):
    way = []
    for place in range(lax.axis_size("dp")):
        for spot in range(4):
            to = [place, spot]
            for link in links:
                link = link[spot % 2]
                to = [to[0], to[1] ^ 2] if link is None else [to[0] ^ (1 << link), to[1]]
            way.append((4 * place + spot, 4 * to[0] + to[1]))
    return lax.ppermute(v, ("dp", "mp"), way)


class Gather:
    def __init__(self, *first):
        self.first = first
        bits = list(range(lax.axis_size("dp").bit_length() - 1))
        self.links = [(None, 0), (0, None)] + [(bit, bit) for bit in bits[1:]]
        last = len(self.links) - 1
        self.steps = [functools.partial(self.share, at) for at in range(last)] + [self.swap]
        self.steps += [functools.partial(self.collect, at) for at in range(last, -1, -1)]

    def next(self):
        return self.steps.pop(0)()

    def swap(self):
        def use(keep):
            self.keep, self.got = keep, send_along(keep, [self.links[-1]])

        return Job(whole_kernel, "whole", (self.keep, self.got), (shaped(self.keep.shape, BF),), use)

    def share(self, at):
        links = [self.links[at]]
        if at == 0:
            kernel, name, operands = gather_kernel, "gather", self.first
            rows = self.first[0].shape[0]
            columns = self.first[0].shape[1] + self.first[2].shape[1] + LANES
        else:
            kernel, name, operands = part_kernel, "part", (self.keep, self.got)
            rows, columns = self.keep.shape
        shape = (rows // 2, columns)

        def use(keep, sent):
            self.keep, self.got = keep, send_along(sent, links)

        outs = (shaped(shape, F32), shaped(shape, BF))
        return Job(functools.partial(kernel, links=links), name, operands, outs, use)

    def collect(self, at):
        rows, columns = self.keep.shape
        if at == len(self.links) - 1:
            kernel, name = sum_kernel, "sum"
        else:
            kernel, name, rows = functools.partial(group_kernel, links=[self.links[at]]), "group", 2 * rows

        def use(keep):
            self.keep = keep
            self.got = send_along(keep, [self.links[at - 1]]) if at else core_swap(keep)

        return Job(kernel, name, (self.keep, self.got), (shaped((rows, columns), BF),), use)


class Stream:
    def __init__(self, *first):
        self.first = first
        bits = list(range(lax.axis_size("dp").bit_length() - 1))
        self.bits = [(0, 1), (1, 0)] + [(bit, bit) for bit in bits[2:]]
        self.steps = [self.start]
        self.steps += [functools.partial(self.halve, bits) for bits in self.bits[1:-1]]
        self.steps += [self.third, self.fourth]
        self.steps += [functools.partial(self.double, at) for at in range(len(bits), 0, -1)]

    def next(self):
        return self.steps.pop(0)()

    def split(self, kernel, name, operands, shape, bits):
        def use(keep, sent):
            self.keep, self.got = keep, send_along(sent, [bits])

        return Job(kernel, name, operands, (shaped(shape, F32), shaped(shape, BF)), use)

    def start(self):
        bits = self.bits[0]
        rows, columns = self.first[0].shape
        kernel = functools.partial(first_kernel, bits=bits)
        return self.split(kernel, "first", self.first, (2, rows // 2, columns), bits)

    def halve(self, bits):
        _, rows, columns = self.keep.shape
        kernel = functools.partial(halve_kernel, bits=bits)
        return self.split(kernel, "halve", (self.keep, self.got), (2, rows // 2, columns), bits)

    def third(self):
        _, rows, columns = self.keep.shape
        bit = self.bits[-1][0]
        kernel = functools.partial(third_kernel, bit=bit)
        return self.split(kernel, "third", (self.keep, self.got), (2, rows // 2, columns), (bit, None))

    def fourth(self):
        bit = self.bits[-1][0]
        kernel = functools.partial(fourth_kernel, bit=bit)
        return self.split(kernel, "fourth", (self.keep, self.got), self.keep.shape[1:], (None, bit))

    def double(self, at):
        if at == len(self.bits):
            kernel, name, shape = add_kernel, "add", self.keep.shape
        else:
            kernel, name = functools.partial(join_kernel, bits=self.bits[at]), "join"
            shape = (2 * self.keep.shape[0], self.keep.shape[1])

        def use(keep):
            self.keep, self.got = keep, send_along(keep, [self.bits[at - 1]])

        return Job(kernel, name, (self.keep, self.got), (shaped(shape, BF),), use)

    def finish(self, order, outs):
        kernel = functools.partial(final_kernel, bits=self.bits[0])
        rows, columns = self.keep.shape
        scratch = [pltpu.VMEM((2 * rows, columns), F32), pltpu.SemaphoreType.DMA((2,))]
        outs = (*outs, shaped((8, LANES), F32))
        return order.call(kernel, "final", (self.keep, self.got), (), outs, scratch)[:2]


def after(v, *others):
    return lax.optimization_barrier((v, others))[0]


def exchange(order, home, partner, reverse, wait=()):
    kernel = functools.partial(chain_kernel, reverse=reverse)
    total = order.call(kernel, "chain", (home, partner), (), shaped(home.shape, BF), wait=wait)
    return total, lax.ppermute(total, "mp", [(2, 0), (3, 1)] if reverse else [(0, 2), (1, 3)])


def per_device(
    layer_input,
    qkv_weight,
    gate_weight,
    gate_bias,
    out_weight,
    inner_weight,
    outer_weight,
    leading_norm_gain,
    leading_norm_bias,
    trailing_norm_gain,
    trailing_norm_bias,
    random_features,
    output_grad,
):
    seqs, length, width = layer_input.shape
    heads, head, feat = random_features.shape
    pairs = heads // 2
    count = seqs * length
    hidden = inner_weight.shape[1]
    bias = gate_bias.reshape(1, heads)
    gain1, shift1 = leading_norm_gain.reshape(1, width), leading_norm_bias.reshape(1, width)
    gain2, shift2 = trailing_norm_gain.reshape(1, width), trailing_norm_bias.reshape(1, width)

    n_dp = lax.axis_size("dp")
    order = Order()
    halves = order.call(
        pack_kernel,
        "pack",
        (inner_weight, outer_weight),
        (),
        shaped((2, width // 2, hidden), BF),
        [pltpu.SemaphoreType.DMA((2,))],
        hbm=True,
    )
    half_chip = chip_swap(halves)
    inner_core, outer_core = core_swap(inner_weight), core_swap(outer_weight)

    by_seq = (seqs, length, width)
    gates = (seqs, length, LANES)
    states = (pairs, LANES + EXTRA, 2 * feat)
    gate_rows = jnp.transpose(gate_weight)
    sources = (layer_input, qkv_weight, gate_rows, bias, gain1, shift1, random_features)
    normed1, values, c, admit, c_row, a_row, phi_k, away, home = order.call(
        keys_kernel,
        "keys",
        sources,
        (),
        (
            kept((count, width), BF),
            kept(by_seq, F32),
            kept(gates, F32),
            kept(gates, F32),
            kept((seqs, heads, length), F32),
            kept((seqs, heads, length), F32),
            kept((seqs, heads, length, 2 * feat), BF),
            kept(states, BF),
            kept(states, BF),
        ),
        [pltpu.VMEM((width, 2 * width) if a is qkv_weight else a.shape, a.dtype) for a in sources]
        + [pltpu.SemaphoreType.DMA((len(sources),))],
        hbm=True,
    )
    partner_home, partner_away = core_swap(away), core_swap(home)
    total, got = exchange(order, home, partner_home, False)
    half_chip = after(half_chip, total)
    half_twin = lax.ppermute(half_chip, "dp", [(i, i ^ 1) for i in range(n_dp)])

    phi_q, scores, num = order.call(
        scores_kernel,
        "scores",
        (qkv_weight, random_features),
        (normed1, phi_k, values, c, c_row, a_row),
        (
            kept((seqs, heads, length, 2 * feat), BF),
            kept((seqs, heads, length, length), BF),
            kept((seqs, heads, length, LANES), F32),
        ),
        wait=(half_chip,),
    )
    got = after(got, num)
    swapped = core_swap(got)
    half_both = core_swap(half_chip)
    full, start, mixed_low, resid, normed2 = order.call(
        mix_kernel,
        "mix",
        (layer_input, got, swapped, partner_home, partner_away, out_weight, gain2, shift2),
        (phi_q, c, num),
        (
            kept((seqs, heads, length, LANES), F32),
            kept((seqs, *states), BF),
            kept(by_seq, BF),
            kept(by_seq, F32),
            kept(by_seq, BF),
        ),
    )

    normed2, mixed_low = (a.reshape(count, width) for a in (normed2, mixed_low))
    half_twin = after(half_twin, normed2)
    half_both_twin = core_swap(half_twin)
    shape = (count, width)
    grads = (width + hidden, width)
    out_part, dn2, out_low, keep0, send0 = order.call(
        feed_near_kernel,
        "feed_near",
        (output_grad.reshape(shape), inner_weight, outer_weight, inner_core, outer_core),
        (normed2, resid.reshape(shape)),
        (kept(shape, F32), kept(shape, F32), kept(shape, BF), shaped(grads, F32), shaped(grads, BF)),
    )
    got0 = core_swap(send0)
    far = pltpu.VMEM((2, width, hidden), BF)
    out_part, dn2, send1 = order.call(
        feed_far_kernel,
        "feed_both",
        (half_both, half_both_twin),
        (normed2, out_low, out_part, dn2),
        (kept(shape, F32), kept(shape, F32), shaped(grads, BF)),
        [far],
    )
    got1 = core_swap(send1)
    layer_out, dn2, keep1 = order.call(
        feed_last_kernel,
        "feed_chip",
        (half_chip, half_twin),
        (normed2, out_low, out_part, dn2),
        (pltpu.HBM(shape, F32), kept(shape, F32), shaped(grads, F32)),
        [far, pltpu.VMEM(shape, F32), pltpu.SemaphoreType.DMA],
    )
    stream = Stream(keep0, keep1, got0, got1)
    order.run(stream.next())

    dres, low, sums2, num_grads, r, away_grads, home_grads = order.call(
        turn_kernel,
        "turn",
        (output_grad, gain2, out_weight),
        (dn2.reshape(by_seq), resid, full, phi_q, c),
        (
            kept(by_seq, F32),
            kept((count, width), BF),
            kept((8, width), F32),
            kept((seqs, heads, length, 2 * LANES), BF),
            kept(gates, F32),
            kept(states, BF),
            kept(states, BF),
        ),
    )
    partner_home_grads, partner_away_grads = core_swap(away_grads), core_swap(home_grads)
    _, got_grads = exchange(order, home_grads, partner_home_grads, True)

    q_grad, k_part, v_part, k_col = order.call(
        back_kernel,
        "back",
        (random_features,),
        (phi_q, phi_k, values, num_grads, scores, c, c_row, a_row, start),
        (
            kept((count, width), BF),
            kept(by_seq, F32),
            kept(by_seq, F32),
            kept(gates, F32),
        ),
    )
    order.run(stream.next())
    keep1, send1, dn1_part, xhat1, scale1 = order.call(
        products_kernel,
        "products",
        (layer_input.reshape(shape), qkv_weight),
        (mixed_low, low, normed1, q_grad),
        (
            shaped((width // 2, 2 * width), F32),
            shaped((width // 2, 2 * width), BF),
            kept(shape, F32),
            kept(shape, F32),
            kept((count, LANES), F32),
        ),
    )
    got1 = core_swap(send1)
    got_grads = after(got_grads, keep1)
    swapped_grads = core_swap(got_grads)

    kv_grad, logit_low, bias_sum, keep2, *send2 = order.call(
        cross_kernel,
        "cross",
        (got_grads, swapped_grads, partner_home_grads, partner_away_grads, random_features),
        (away, home, start, phi_k, values, c, admit, r, k_col, k_part, v_part, normed1),
        (
            kept((count, 2 * width), BF),
            kept((count, LANES), BF),
            kept((8, LANES), F32),
            shaped((width // 2, 2 * width), F32),
            *[shaped((width // 8, 2 * width), BF)] * 4,
        ),
    )
    got2 = core_swap(send2)
    order.run(stream.next())
    dx, small = order.call(
        close_kernel,
        "close",
        (qkv_weight, gate_rows, gain1),
        (dn1_part, xhat1, scale1, kv_grad, logit_low, bias_sum, normed1, dres.reshape(shape), sums2),
        (shaped((count, width), F32), shaped((width // 2, LANES), F32)),
    )
    gather = Gather(keep1, got1, keep2, *got2, small)
    order.run(gather.next())
    order.run(stream.next())
    order.run(gather.next(), stream.next())
    order.run(gather.next())
    while stream.steps:
        order.run(gather.next(), stream.next())
    while len(gather.steps) > 2:
        order.run(gather.next())
    inner_total, outer_total = stream.finish(order, (pltpu.HBM((width, hidden), F32), pltpu.HBM((hidden, width), F32)))
    while gather.steps:
        order.run(gather.next())
    qkv_grad, wo_grad, gate_grad, bias_grad, *norm_grads = order.call(
        assemble_kernel,
        "assemble",
        (gather.keep, gather.got),
        (),
        (
            shaped((width, 3 * width), F32),
            shaped((width, width), F32),
            shaped((heads, width), F32),
            shaped((1, heads), F32),
            *[shaped((1, width), F32)] * 4,
        ),
    )
    return (
        layer_out.reshape(by_seq),
        dx.reshape(by_seq),
        qkv_grad,
        jnp.transpose(gate_grad),
        bias_grad.reshape(heads),
        wo_grad,
        inner_total,
        outer_total,
        *(a.reshape(width) for a in norm_grads),
    )


def solution(mesh):
    in_specs = (
        P("dp", "mp", None),
        P(),
        P(),
        P(),
        P(),
        P(None, "mp"),
        P("mp", None),
        P(),
        P(),
        P(),
        P(),
        P(),
        P("dp", "mp", None),
    )
    out_specs = (
        P("dp", "mp", None),
        P("dp", "mp", None),
        P(),
        P(),
        P(),
        P(),
        P(None, "mp"),
        P("mp", None),
        P(),
        P(),
        P(),
        P(),
    )
    return jax.shard_map(
        per_device, mesh=mesh, in_specs=in_specs, out_specs=out_specs, check_vma=False
    )
```

```python
import functools
import math

import jax
import jax.numpy as jnp
from jax import lax
from jax.experimental import pallas as pl
from jax.experimental.pallas import tpu as pltpu
from jax.sharding import PartitionSpec as P

BF = jnp.bfloat16
F32 = jnp.float32
epsilon = 1e-05
guard = 0.01
LANES = 128
EXTRA = 16
VMEM_BYTES = 16 * 1024 * 1024


def nn(a, b):
    return lax.dot_general(a, b, (((1,), (0,)), ((), ())), preferred_element_type=F32)


def nt(a, b):
    return lax.dot_general(a, b, (((1,), (1,)), ((), ())), preferred_element_type=F32)


def tn(a, b):
    return lax.dot_general(a, b, (((0,), (0,)), ((), ())), preferred_element_type=F32)


def two_terms(v):
    high = v.astype(BF)
    return high, (v - high.astype(F32)).astype(BF)


def iota(shape, dim):
    return lax.broadcasted_iota(jnp.int32, shape, dim)


def triangle(length, upper):
    rows, cols = iota((length, length), 0), iota((length, length), 1)
    return jnp.where((cols >= rows) if upper else (rows >= cols), 1.0, 0.0).astype(BF)


def running_sum(v, upper):
    ones = triangle(v.shape[0], upper)
    high, rest = two_terms(v)
    low = (v - high.astype(F32) - rest.astype(F32)).astype(BF)
    return nn(ones, high) + nn(ones, rest) + nn(ones, low)


def norm_rows(v):
    centred = v - jnp.mean(v, axis=-1, keepdims=True)
    scale = lax.rsqrt(jnp.mean(centred * centred, axis=-1, keepdims=True) + epsilon)
    return centred * scale, scale


def norm_rows_backward(grad, xhat, scale, gain):
    g = grad * gain
    return scale * (
        g
        - jnp.mean(g, axis=-1, keepdims=True)
        - xhat * jnp.mean(g * xhat, axis=-1, keepdims=True)
    )


def pair_frequencies(freq_ref, pair):
    even, odd = freq_ref[2 * pair], freq_ref[2 * pair + 1]
    none = jnp.zeros_like(even)
    return jnp.concatenate(
        [jnp.concatenate([even, none], axis=1), jnp.concatenate([none, odd], axis=1)], axis=0
    )


def scaled_sine_cosine(angles, scale):
    turns = jnp.floor(angles * (1.0 / math.pi) + 0.5)
    r = angles - turns * 3.140625
    r = r - turns * 0.0009675025939941406
    r = r - turns * 1.509958e-07
    odd = turns - 2.0 * jnp.floor(turns * 0.5)
    sign = scale - (2.0 * scale) * odd
    r2 = r * r
    sine = -0.00018362251175623582 * r2 + 0.008306273552368303
    sine = sine * r2 - 0.1666482311215342
    sine = sine * r2 + 0.9999966031254778
    cosine = -0.0012711240835350962 * r2 + 0.041487518673719546
    cosine = cosine * r2 - 0.4999123281046797
    cosine = cosine * r2 + 0.9999933132015835
    return sine * (r * sign), cosine * sign


def pair_features(values, freq, scale):
    high, low = two_terms(values)
    freq_high, freq_low = two_terms(freq)
    both = jnp.concatenate([freq_high, freq_high], axis=0)
    angles = nn(jnp.concatenate([high, low], axis=1), both) + nn(high, freq_low)
    sine, cosine = scaled_sine_cosine(angles, scale)
    sine, cosine = sine.astype(BF), cosine.astype(BF)
    feat = freq.shape[1] // 2
    return [
        jnp.concatenate([sine[:, h * feat : (h + 1) * feat], cosine[:, h * feat : (h + 1) * feat]], axis=1)
        for h in (0, 1)
    ]


def own_lanes(shape, half):
    lane = iota(shape, len(shape) - 1)
    return (lane >= LANES // 2) if half else (lane < LANES // 2)


def one_lane(shape, half):
    return iota(shape, len(shape) - 1) == (0 if half else LANES // 2)


def second_lane(shape, half):
    return iota(shape, len(shape) - 1) == (1 if half else LANES // 2 + 1)


def with_ones(values, half, both=False):
    v = values.astype(F32)
    ones = one_lane(v.shape, half) | (both & second_lane(v.shape, half))
    return jnp.where(own_lanes(v.shape, half), v, jnp.where(ones, 1.0, 0.0))


def pack_states(even, odd, decay_even, decay_odd):
    half = LANES // 2
    row = iota(even.shape, 0)
    states = jnp.where(row < half, even, odd).astype(BF)
    extra = iota((EXTRA, even.shape[1]), 0)
    parts = []
    for value in (even[half : half + 1], odd[0:1], decay_even, decay_odd):
        high = value.astype(BF).astype(F32)
        parts += [high, value - high]
    rows = jnp.zeros((EXTRA, even.shape[1]), F32)
    for at, part in enumerate(parts):
        rows = jnp.where(extra == at, part, rows)
    return states, rows.astype(BF)


def extra_row(packed, at):
    at = LANES + 2 * at
    return packed[at : at + 1] + packed[at + 1 : at + 2]


def decays(packed):
    return extra_row(packed, 2), extra_row(packed, 3)


def unpack_states(packed):
    half = LANES // 2
    states = packed[:LANES]
    row = iota(states.shape, 0)
    even = jnp.where(row < half, states, jnp.where(row == half, extra_row(packed, 0), 0.0))
    odd = jnp.where(row >= half, states, jnp.where(row == 0, extra_row(packed, 1), 0.0))
    return even, odd


def join_states(first, second):
    return [
        a + decay * b
        for a, b, decay in zip(unpack_states(first), unpack_states(second), decays(first))
    ]


def as_operand(state, half):
    at = 0 if half else LANES // 2
    norm = state[at : at + 1]
    rest = norm - norm.astype(BF).astype(F32)
    return jnp.where(iota(state.shape, 0) == at + 1, rest, state).astype(BF)


def decay_weights(c_col, c_row, a_row):
    length = c_col.shape[0]
    gap = jnp.minimum(c_col - c_row, 0.0)
    causal = iota((length, length), 0) >= iota((length, length), 1)
    return jnp.where(causal, jnp.exp(gap) * a_row, 0.0)


def lane_sum(v):
    return jnp.sum(v, axis=1, keepdims=True)


def each(count, step):
    lax.fori_loop(0, count, lambda i, none: (step(i), none)[1], 0)


def wide(v, axis):
    none = list(v.shape)
    none[axis] = LANES - v.shape[axis]
    return jnp.concatenate([v, jnp.zeros(none, v.dtype)], axis=axis)


def aligned(at, size):
    return pl.ds(pl.multiple_of(at * size, size), size)


def my_core():
    return lax.axis_index("mp") % 2


def my_chip():
    return lax.axis_index("mp") // 2


def pack_kernel(inner_ref, outer_ref, out_ref, sems):
    rows = out_ref.shape[1]
    mine = aligned(lax.axis_index("dp") % 2, rows)
    copies = [
        pltpu.make_async_copy(source.at[mine], out_ref.at[i], sems.at[i])
        for i, source in enumerate((inner_ref, outer_ref))
    ]
    for copy in copies:
        copy.start()
    for copy in copies:
        copy.wait()


def by_place(of_sequence):
    even = my_core() == 0
    one, two = of_sequence
    return jnp.where(even, two, one), jnp.where(even, one, two)


def put_states(pair, packed, away_ref, home_ref):
    for rows, parts in ((slice(0, LANES), [p[0] for p in packed]), (slice(LANES, None), [p[1] for p in packed])):
        away_ref[pair, rows], home_ref[pair, rows] = by_place(parts)


def keys_kernel(
    x_hbm, wqkv_hbm, gw_hbm, gb_hbm, gain_hbm, shift_hbm, freq_hbm,
    n1_ref, v_ref, c_ref, a_ref, crow_ref, arow_ref, pk_ref, away_ref, home_ref,
    x_ref, w_ref, gw_ref, gb_ref, gain_ref, shift_ref, freq_ref, sems,
):
    heads, _, feat = freq_ref.shape
    seqs, length, width = x_ref.shape
    sources = (x_hbm, gain_hbm, shift_hbm, gw_hbm, gb_hbm, wqkv_hbm.at[:, pl.ds(width, 2 * width)], freq_hbm)
    buffers = (x_ref, gain_ref, shift_ref, gw_ref, gb_ref, w_ref, freq_ref)
    copies = [
        pltpu.make_async_copy(source, buffer, sems.at[i])
        for i, (source, buffer) in enumerate(zip(sources, buffers))
    ]
    for copy in copies:
        copy.start()
    for copy in copies[:5]:
        copy.wait()
    scale = 1.0 / math.sqrt(feat)
    xhat, _ = norm_rows(x_ref[...].reshape(seqs * length, width))
    n1 = (xhat * gain_ref[...] + shift_ref[...]).astype(BF)
    n1_ref[...] = n1
    z = nt(n1, wide(gw_ref[...], 0)) + wide(gb_ref[...], 1)
    e = jnp.exp(-jnp.abs(z))
    log_keep = jnp.minimum(z, 0.0) - jnp.log1p(e)
    inverse = 1.0 / (1.0 + e)
    admit_all = jnp.where(z > 0.0, e * inverse, inverse)
    tails, decay = [], []
    for s in range(seqs):
        rows = slice(s * length, (s + 1) * length)
        c = running_sum(log_keep[rows], False)
        admit = admit_all[rows]
        c_ref[s] = c
        a_ref[s] = admit
        crow_ref[s] = jnp.transpose(c)[:heads]
        arow_ref[s] = jnp.transpose(admit)[:heads]
        last = c[length - 1 :]
        tails.append(jnp.exp(last - c) * admit)
        decay.append(jnp.exp(last))
    for copy in copies[5:]:
        copy.wait()
    keys = nn(n1, w_ref[:, :width])
    values = nn(n1, w_ref[:, width:])
    v_ref[...] = values.reshape(v_ref.shape)
    for pair in range(heads // 2):
        lanes = slice(pair * LANES, (pair + 1) * LANES)
        phi = pair_features(keys[:, lanes], pair_frequencies(freq_ref, pair), scale)
        packed = []
        for s in range(seqs):
            rows = slice(s * length, (s + 1) * length)
            states = []
            for half in (0, 1):
                h = 2 * pair + half
                phi_k = phi[half][rows]
                pk_ref[s, h] = phi_k
                weighted = with_ones(values[rows, lanes], half) * tails[s][:, h : h + 1]
                both = tn(jnp.concatenate(two_terms(weighted), axis=1), phi_k)
                states.append(both[:LANES] + both[LANES:])
            h = 2 * pair
            packed.append(pack_states(*states, decay[s][:, h : h + 1], decay[s][:, h + 1 : h + 2]))
        put_states(pair, packed, away_ref, home_ref)


def scores_kernel(wqkv_ref, freq_ref, n1_ref, pk_ref, v_ref, c_ref, crow_ref, arow_ref, pq_ref, p_ref, num_ref):
    seqs, heads, length, _ = pk_ref.shape
    scale = 1.0 / math.sqrt(freq_ref.shape[2])
    queries = nn(n1_ref[...], wqkv_ref[:, : n1_ref.shape[1]])
    for pair in range(heads // 2):
        lanes = slice(pair * LANES, (pair + 1) * LANES)
        phi = pair_features(queries[:, lanes], pair_frequencies(freq_ref, pair), scale)
        for s in range(seqs):
            for half in (0, 1):
                h = 2 * pair + half
                phi_q = phi[half][s * length : (s + 1) * length]
                pq_ref[s, h] = phi_q
                v = with_ones(v_ref[s, :, lanes], half)
                weights = decay_weights(
                    c_ref[s, :, h : h + 1], crow_ref[s, h : h + 1], arow_ref[s, h : h + 1]
                )
                p = (nt(phi_q, pk_ref[s, h]) * weights).astype(BF)
                p_ref[s, h] = p
                both = nn(p, jnp.concatenate(two_terms(v), axis=1))
                num_ref[s, h] = both[:, :LANES] + both[:, LANES:]


def mix_kernel(
    x_ref, got_ref, swapped_ref, partner_home_ref, partner_away_ref, wo_ref, gain_ref, shift_ref, pq_ref, c_ref, num_ref,
    full_ref, start_ref, mixed_ref, resid_ref, n2_ref,
):
    seqs, heads = pq_ref.shape[:2]
    core = my_core()

    def one(s):
        growth = jnp.exp(c_ref[s])
        for pair in range(heads // 2):
            before = jnp.where(s == core, got_ref[pair], swapped_ref[pair]).astype(F32)
            partner = jnp.where(s == core, partner_home_ref[pair], partner_away_ref[pair]).astype(F32)
            states = [
                jnp.where(core == 0, a, b)
                for a, b in zip(unpack_states(before), join_states(partner, before))
            ]
            none = jnp.zeros((1, 1), F32)
            main, rest = pack_states(*states, none, none)
            start_ref[s, pair, :LANES] = main
            start_ref[s, pair, LANES:] = rest
            mixed = []
            for half in (0, 1):
                h = 2 * pair + half
                full = num_ref[s, h] + growth[:, h : h + 1] * nt(
                    pq_ref[s, h], as_operand(states[half], half)
                )
                full_ref[s, h] = full
                at = 0 if half else LANES // 2
                sden = full[:, at : at + 1] + full[:, at + 1 : at + 2]
                mixed.append(full * lax.rsqrt(sden * sden + guard))
            pair_mixed = jnp.where(own_lanes(mixed[0].shape, 0), mixed[0], mixed[1])
            mixed_ref[s, :, pair * LANES : (pair + 1) * LANES] = pair_mixed.astype(BF)
        resid = x_ref[s] + nn(mixed_ref[s], wo_ref[...])
        resid_ref[s] = resid
        xhat, _ = norm_rows(resid)
        n2_ref[s] = (xhat * gain_ref[...] + shift_ref[...]).astype(BF)

    for s in range(seqs):
        one(s)


def gelu_and_slope(v):
    root = math.sqrt(2.0 / math.pi)
    v2 = v * v
    t = jnp.tanh(v * (root + (root * 0.044715) * v2))
    half = 0.5 * (1.0 + t)
    slope = half + (0.5 * v) * (1.0 - t * t) * (root + (root * 3.0 * 0.044715) * v2)
    return v * half, slope


def feed_block(n2, out_low, wi_ref, wo_ref):
    active, slope = gelu_and_slope(nn(n2, wi_ref[...]))
    active = active.astype(BF)
    pre_grad = (nt(out_low, wo_ref[...]) * slope).astype(BF)
    return nn(active, wo_ref[...]), nt(pre_grad, wi_ref[...]), tn(n2, pre_grad), tn(active, out_low)


def halves_together(far_ref, one, two):
    twin = lax.axis_index("dp") % 2
    rows = one.shape[1]
    for which in range(2):
        far_ref[which, aligned(twin, rows)] = one[which]
        far_ref[which, aligned(1 - twin, rows)] = two[which]


def feed_near_kernel(og_ref, wi0, wo0, wi2, wo2, n2_ref, resid_ref, out_ref, dn2_ref, low_ref, keep_ref, send_ref):
    low_ref[...] = og_ref[...].astype(BF)
    n2, out_low = n2_ref[...], low_ref[...]
    rows = n2.shape[1]
    out, dn2, inner, outer = feed_block(n2, out_low, wi2, wo2)
    send_ref[:rows] = inner.astype(BF)
    send_ref[rows:] = outer.astype(BF)
    out_own, dn2_own, inner, outer = feed_block(n2, out_low, wi0, wo0)
    keep_ref[:rows] = inner
    keep_ref[rows:] = outer
    out_ref[...] = resid_ref[...] + out + out_own
    dn2_ref[...] = dn2 + dn2_own


def feed_far_kernel(half_ref, twin_ref, n2_ref, low_ref, part_ref, dn2_part_ref, out_ref, dn2_ref, grad_ref, far_ref):
    twin = lax.axis_index("dp") % 2
    rows = half_ref.shape[1]
    for which in range(2):
        far_ref[which, aligned(twin, rows)] = half_ref[which]
        far_ref[which, aligned(1 - twin, rows)] = twin_ref[which]
    n2 = n2_ref[...]
    out, dn2, inner, outer = feed_block(n2, low_ref[...], far_ref.at[0], far_ref.at[1])
    out_ref[...] = part_ref[...] + out
    dn2_ref[...] = dn2_part_ref[...] + dn2
    rows = n2.shape[1]
    grad_ref[:rows] = inner.astype(grad_ref.dtype)
    grad_ref[rows:] = outer.astype(grad_ref.dtype)


def feed_last_kernel(
    half_ref, twin_ref, n2_ref, low_ref, part_ref, dn2_part_ref, out_hbm, dn2_ref, grad_ref, far_ref, out_ref, sem
):
    feed_far_kernel(half_ref, twin_ref, n2_ref, low_ref, part_ref, dn2_part_ref, out_ref, dn2_ref, grad_ref, far_ref)
    copy = pltpu.make_async_copy(out_ref, out_hbm, sem)
    copy.start()
    copy.wait()


def place_bit(bits):
    place = lax.axis_index("dp")
    return jnp.where(my_core() == 0, (place // (1 << bits[0])) % 2, (place // (1 << bits[1])) % 2)


def split_rows(total, bits, mine_ref, send_ref):
    rows = mine_ref.shape[1]
    high = place_bit(bits) == 1
    first, second = total[:, :rows], total[:, rows:]
    mine_ref[...] = jnp.where(high, second, first)
    send_ref[...] = jnp.where(high, first, second).astype(BF)


def halve_kernel(keep_ref, got_ref, mine_ref, send_ref, *, bits):
    split_rows(keep_ref[...] + got_ref[...].astype(F32), bits, mine_ref, send_ref)


def first_kernel(keep0_ref, keep1_ref, got0_ref, got1_ref, mine_ref, send_ref, *, bits):
    for block, (keep_ref, got_ref) in enumerate(((keep0_ref, got0_ref), (keep1_ref, got1_ref))):
        total = (keep_ref[...] + got_ref[...].astype(F32))[None]
        split_rows(total, bits, mine_ref.at[block : block + 1], send_ref.at[block : block + 1])


def third_kernel(keep_ref, got_ref, mine_ref, send_ref, *, bit):
    rows = mine_ref.shape[1]
    total = keep_ref[...] + got_ref[...].astype(F32)
    low, high = total[:, :rows], total[:, rows:]
    by_bit = place_bit((bit, bit)) == 1
    one, two = jnp.where(by_bit, high, low), jnp.where(by_bit, low, high)
    even = my_core() == 0
    for part in range(2):
        of_block = (low, high)[part]
        mine_ref[part] = jnp.where(even, one[part], of_block[0])
        send_ref[part] = jnp.where(even, two[part], of_block[1]).astype(BF)


def fourth_kernel(keep_ref, got_ref, mine_ref, send_ref, *, bit):
    total = keep_ref[...] + got_ref[...].astype(F32)
    second = (my_core() == 1) & (place_bit((bit, bit)) == 1)
    mine_ref[...] = jnp.where(second, total[1], total[0])
    send_ref[...] = jnp.where(second, total[0], total[1]).astype(BF)


def add_kernel(keep_ref, got_ref, out_ref):
    out_ref[...] = (keep_ref[...] + got_ref[...].astype(F32)).astype(out_ref.dtype)


def joined(mine_ref, got_ref, bits):
    high = place_bit(bits) == 1
    mine, got = mine_ref[...].astype(F32), got_ref[...].astype(F32)
    return jnp.concatenate([jnp.where(high, got, mine), jnp.where(high, mine, got)], axis=0)


def join_kernel(mine_ref, got_ref, out_ref, *, bits):
    out_ref[...] = joined(mine_ref, got_ref, bits).astype(BF)


def final_kernel(mine_ref, got_ref, inner_hbm, outer_hbm, mark_ref, whole_ref, sems, *, bits):
    mark_ref[...] = jnp.zeros_like(mark_ref)
    both = joined(mine_ref, got_ref, bits)
    quarter = both.shape[0] // 4
    one, two = both[quarter : 2 * quarter], both[2 * quarter : 3 * quarter]
    even = my_core() == 0
    whole_ref[:quarter] = both[:quarter]
    whole_ref[quarter : 2 * quarter] = jnp.where(even, two, one)
    whole_ref[2 * quarter : 3 * quarter] = jnp.where(even, one, two)
    whole_ref[3 * quarter :] = both[3 * quarter :]
    rows = inner_hbm.shape[0]
    copies = [
        pltpu.make_async_copy(whole_ref.at[pl.ds(at * rows, rows)], out_hbm, sems.at[at])
        for at, out_hbm in enumerate((inner_hbm, outer_hbm))
    ]
    for copy in copies:
        copy.start()
    for copy in copies:
        copy.wait()


def turn_kernel(
    og_ref, gain_ref, wo_ref, dn2_ref, resid_ref, full_ref, pq_ref, c_ref,
    dres_ref, low_ref, sums_ref, ng_ref, r_ref, away_ref, home_ref,
):
    seqs, heads, length, _ = pq_ref.shape
    sums_ref[...] = jnp.zeros_like(sums_ref)
    packed = [[] for _ in range(seqs)]

    def one(s):
        xhat, scale = norm_rows(resid_ref[s])
        dn2 = dn2_ref[s]
        dres = og_ref[s] + norm_rows_backward(dn2, xhat, scale, gain_ref[...])
        dres_ref[s] = dres
        low = dres.astype(BF)
        low_ref[s * length : (s + 1) * length] = low
        sums_ref[2:3] += jnp.sum(dn2 * xhat, axis=0, keepdims=True)
        sums_ref[3:4] += jnp.sum(dn2, axis=0, keepdims=True)
        dmixed = nt(low, wo_ref[...])
        c = c_ref[s]
        growth = jnp.exp(c)
        decay = jnp.exp(c[length - 1 :])
        lane = iota(c.shape, 1)
        r_all = jnp.zeros_like(c)
        for pair in range(heads // 2):
            g = dmixed[:, pair * LANES : (pair + 1) * LANES]
            states = []
            for half in (0, 1):
                h = 2 * pair + half
                full = full_ref[s, h]
                at = 0 if half else LANES // 2
                sden = full[:, at : at + 1] + full[:, at + 1 : at + 2]
                inverse = lax.rsqrt(sden * sden + guard)
                inverse2 = inverse * inverse
                mine = own_lanes(g.shape, half)
                dot = lane_sum(jnp.where(mine, g * full, 0.0)) * inverse
                sden_grad = -dot * sden * inverse2
                r_all = jnp.where(lane == h, dot * inverse2 * guard, r_all)
                grads = jnp.where(
                    mine, g * inverse, jnp.where(one_lane(g.shape, half), sden_grad, 0.0)
                )
                ng_ref[s, h] = jnp.concatenate(two_terms(grads), axis=1)
                lifted = jnp.concatenate(two_terms(grads * growth[:, h : h + 1]), axis=1)
                both = tn(lifted, pq_ref[s, h])
                states.append(both[:LANES] + both[LANES:])
            h = 2 * pair
            packed[s].append(pack_states(*states, decay[:, h : h + 1], decay[:, h + 1 : h + 2]))
        r_ref[s] = r_all

    for s in range(seqs):
        one(s)
    for pair, both in enumerate(zip(*packed)):
        put_states(pair, both, away_ref, home_ref)


def angle_grads(phi, dphi):
    feat = phi.shape[1] // 2
    phi = phi.astype(F32)
    return phi[:, feat:] * dphi[:, :feat] - phi[:, :feat] * dphi[:, feat:]


def weight_grads(left_ref, right_ref, keep_ref, send_refs):
    rows = keep_ref.shape[0]
    core = my_core()
    keep_ref[...] = tn(left_ref[:, aligned(core, rows)], right_ref[...])
    away = tn(left_ref[:, aligned(1 - core, rows)], right_ref[...]).astype(BF)
    rows //= len(send_refs)
    for part, send_ref in enumerate(send_refs):
        send_ref[...] = away[part * rows : (part + 1) * rows]


def back_kernel(
    freq_ref, pq_ref, pk_ref, v_ref, ng_ref, p_ref, c_ref, crow_ref, arow_ref, start_ref,
    qg_ref, kg_ref, vg_ref, kcol_ref,
):
    seqs, heads, length, _ = pq_ref.shape

    def one(s):
        tokens = aligned(s, length)
        c = c_ref[s]
        growth = jnp.exp(c)
        lane = iota(c.shape, 1)
        kcol = jnp.zeros_like(c)
        for pair in range(heads // 2):
            at = pair * LANES
            freq = pair_frequencies(freq_ref, pair).astype(BF)
            states = unpack_states(start_ref[s, pair].astype(F32))
            q_angles, k_angles, v_grads = [], [], []
            for half in (0, 1):
                h = 2 * pair + half
                phi_q, phi_k = pq_ref[s, h], pk_ref[s, h]
                grads = ng_ref[s, h, :, :LANES]
                v = with_ones(v_ref[s, :, at : at + LANES], half)
                weights = decay_weights(c[:, h : h + 1], crow_ref[s, h : h + 1], arow_ref[s, h : h + 1])
                dk = (nt(grads, v.astype(BF)) * weights).astype(BF)
                lifted = (grads.astype(F32) * growth[:, h : h + 1]).astype(BF)
                dphi_q = nn(dk, phi_k) + nn(lifted, states[half].astype(BF))
                q_angles.append(angle_grads(phi_q, dphi_q))
                k_angles.append(angle_grads(phi_k, tn(dk, phi_q)))
                both = tn(p_ref[s, h], ng_ref[s, h])
                dv = both[:, :LANES] + both[:, LANES:]
                v_grads.append(dv)
                kcol = jnp.where(lane == h, lane_sum(v * dv), kcol)
            qg_ref[tokens, at : at + LANES] = nt(
                jnp.concatenate(q_angles, axis=1).astype(BF), freq
            ).astype(BF)
            kg_ref[s, :, at : at + LANES] = nt(jnp.concatenate(k_angles, axis=1).astype(BF), freq)
            vg_ref[s, :, at : at + LANES] = jnp.where(
                own_lanes(v_grads[0].shape, 0), v_grads[0], v_grads[1]
            )
        kcol_ref[s] = kcol

    each(seqs, one)


def products_kernel(
    x_ref, wqkv_ref, mixed_ref, low_ref, n1_ref, qg_ref, part_ref, xhat_ref, scale_ref, keep_ref, *send_refs
):
    width = low_ref.shape[1]
    part_ref[...] = nt(qg_ref[...], wqkv_ref[:, :width])
    xhat, scale = norm_rows(x_ref[...])
    xhat_ref[...] = xhat
    scale_ref[...] = jnp.broadcast_to(scale, scale_ref.shape)
    for at, left_ref, right_ref in ((0, mixed_ref, low_ref), (width, n1_ref, qg_ref)):
        lanes = pl.ds(at, width)
        weight_grads(left_ref, right_ref, keep_ref.at[:, lanes], [ref.at[:, lanes] for ref in send_refs])


def cross_kernel(
    got_ref, swapped_ref, partner_home_ref, partner_away_ref, freq_ref, away_ref, home_ref, start_ref, pk_ref, v_ref,
    c_ref, a_ref, r_ref, kcol_ref,
    kg_ref, vg_ref, n1_ref,
    kv_ref, logit_ref, bias_ref, keep_ref, *send_refs,
):
    seqs, heads, length, _ = pk_ref.shape
    core = my_core()
    width = kg_ref.shape[2]
    bias_ref[...] = jnp.zeros_like(bias_ref)

    def one(s):
        tokens = aligned(s, length)
        c, a = c_ref[s], a_ref[s]
        tail = jnp.exp(c[length - 1 :] - c) * a
        lane = iota(c.shape, 1)
        lane_row = iota((1, c.shape[1]), 1)
        kcol = kcol_ref[s]
        ends = jnp.zeros((1, c.shape[1]), F32)
        for pair in range(heads // 2):
            at = pair * LANES
            freq = pair_frequencies(freq_ref, pair).astype(BF)
            after = jnp.where(s == core, got_ref[pair], swapped_ref[pair]).astype(F32)
            partner = jnp.where(s == core, partner_home_ref[pair], partner_away_ref[pair]).astype(F32)
            grads = [
                jnp.where(core == 1, a, b)
                for a, b in zip(unpack_states(after), join_states(partner, after))
            ]
            local = jnp.where(s == core, home_ref[pair], away_ref[pair]).astype(F32)
            reached = join_states(local, start_ref[s, pair].astype(F32))
            k_angles, v_grads = [], []
            for half in (0, 1):
                h = 2 * pair + half
                phi_k = pk_ref[s, h]
                v = with_ones(v_ref[s, :, at : at + LANES], half, True)
                grad_low = as_operand(grads[half], half)
                weight = tail[:, h : h + 1]
                k_angles.append(angle_grads(phi_k, nn(v.astype(BF), grad_low)) * weight)
                dv = nt(phi_k, grad_low) * weight
                v_grads.append(dv)
                kcol = kcol + jnp.where(lane == h, lane_sum(v * dv), 0.0)
                end = jnp.sum(lane_sum(grads[half] * reached[half]), axis=0, keepdims=True)
                ends = jnp.where(lane_row == h, end, ends)
            kg = kg_ref[s, :, at : at + LANES] + nt(
                jnp.concatenate(k_angles, axis=1).astype(BF), freq
            )
            vg = vg_ref[s, :, at : at + LANES] + jnp.where(
                own_lanes(v_grads[0].shape, 0), v_grads[0], v_grads[1]
            )
            kv_ref[tokens, at : at + LANES] = kg.astype(BF)
            kv_ref[tokens, width + at : width + at + LANES] = vg.astype(BF)
        keep_grad = running_sum(r_ref[s] - kcol, True) + ends
        logit_grad = a * keep_grad - (1.0 - a) * kcol
        logit_ref[tokens] = logit_grad.astype(BF)
        bias_ref[0:1] += jnp.sum(logit_grad, axis=0, keepdims=True)

    for i in range(seqs):
        one(i)
    weight_grads(n1_ref, kv_ref, keep_ref, send_refs)


def close_kernel(
    wqkv_ref, gw_ref, part_ref, xhat_ref, kv_ref, logit_ref, bias_ref, n1_ref, sums2_ref, dn1_ref, small_ref
):
    width = part_ref.shape[1]
    logit_low = logit_ref[...]
    dn1 = part_ref[...] + nt(kv_ref[...], wqkv_ref[:, width:]) + nn(logit_low, wide(gw_ref[...], 0))
    xhat = xhat_ref[...]
    dn1_ref[...] = dn1
    row = iota((8, width), 0)
    sums = jnp.where(row == 0, jnp.sum(dn1 * xhat, axis=0, keepdims=True), sums2_ref[...])
    sums = jnp.where(row == 1, jnp.sum(dn1, axis=0, keepdims=True), sums)
    bias = jnp.concatenate([bias_ref[0:1], jnp.zeros((1, width - LANES), F32)], axis=1)
    sums = jnp.where(row == 4, bias, sums)
    gates = tn(logit_low, n1_ref[...])[:8]
    stacked = jnp.concatenate([sums, gates, jnp.zeros((LANES - 16, width), F32)], axis=0)
    columns = jnp.transpose(stacked)
    rows = small_ref.shape[0]
    small_ref[...] = columns[:rows] + pltpu.roll(columns[rows:], 16, 1)


def input_kernel(gain_ref, dn1_ref, xhat_ref, scale_ref, dres_ref, dx_hbm, mark_ref, dx_ref, sem):
    mark_ref[...] = jnp.zeros_like(mark_ref)
    dx_ref[...] = dres_ref[...] + norm_rows_backward(dn1_ref[...], xhat_ref[...], scale_ref[:, :1], gain_ref[...])
    copy = pltpu.make_async_copy(dx_ref, dx_hbm, sem)
    copy.start()
    copy.wait()


def chain_kernel(me_ref, partner_ref, out_ref, *, reverse):
    core = my_core()
    lead = (core == 0) if reverse else (core == 1)
    for pair in range(out_ref.shape[0]):
        mine, other = me_ref[pair].astype(F32), partner_ref[pair].astype(F32)
        first = jnp.where(lead, mine, other)
        second = jnp.where(lead, other, mine)
        none = jnp.zeros((1, 1), F32)
        main, rest = pack_states(*join_states(first, second), none, none)
        out_ref[pair, :LANES] = main
        out_ref[pair, LANES:] = rest


def widen(v):
    main, last = v[:, :-LANES].astype(F32), v[:, -LANES:].astype(F32)
    last = jnp.where(iota(last.shape, 1) < LANES // 2, last + pltpu.roll(last, LANES // 2, 1), 0.0)
    return jnp.concatenate([main, last], axis=1)


def narrow(v):
    main, last = v[:, :-LANES].astype(BF), v[:, -LANES:]
    high, low = two_terms(last)
    last = high.astype(F32) + pltpu.roll(low.astype(F32), LANES // 2, 1)
    return jnp.concatenate([main, last.astype(BF)], axis=1)


def link_bit(link):
    return my_chip() if link is None else (lax.axis_index("dp") // (1 << link)) % 2


def piece_number(links):
    number = 0
    for of_zero, of_one in links:
        bit = link_bit(of_zero)
        if of_one != of_zero:
            bit = jnp.where(my_core() == 0, bit, link_bit(of_one))
        number = 2 * number + bit
    return number


def pick(pieces, number):
    taken = pieces[0]
    for at in range(1, len(pieces)):
        taken = jnp.where(number == at, pieces[at], taken)
    return taken


def share_out(total, links, mine_ref, send_refs):
    rows = mine_ref.shape[0]
    pieces = [total[at : at + rows] for at in range(0, total.shape[0], rows)]
    number = piece_number(links)
    mine_ref[...] = pick(pieces, number)
    for k, send_ref in enumerate(send_refs):
        send_ref[...] = narrow(pick(pieces, number ^ (k + 1)))


def early_kernel(keep_ref, *refs, links):
    *got_refs, mine_ref, send_ref = refs
    rows = mine_ref.shape[0]
    total = keep_ref[...] + jnp.concatenate([ref[...].astype(F32) for ref in got_refs], axis=0)
    number = piece_number(links)
    pieces = [total[:rows], total[rows:]]
    mine_ref[...] = pick(pieces, number)
    send_ref[...] = pick(pieces, number ^ 1).astype(BF)


def late_kernel(early_ref, early_got_ref, keep_ref, *refs, links):
    *got_refs, small_ref, mine_ref, send_ref = refs
    before = early_ref.shape[1]
    mine_ref[:, :before] = early_ref[...] + early_got_ref[...].astype(F32)
    total = keep_ref[...] + jnp.concatenate([ref[...].astype(F32) for ref in got_refs], axis=0)
    total = jnp.concatenate([total, small_ref[...]], axis=1)
    share_out(total, links, mine_ref.at[:, pl.ds(before, total.shape[1])], [send_ref])


def meet_kernel(keep_ref, got_ref, mine_ref, send_ref, *, links):
    before = keep_ref.shape[1] - got_ref.shape[1]
    second = keep_ref[:, before:] + widen(got_ref[...])
    share_out(jnp.concatenate([keep_ref[:, :before], second], axis=1), links, mine_ref, [send_ref])


def part_kernel(keep_ref, got_ref, mine_ref, send_ref, *, links):
    share_out(keep_ref[...] + widen(got_ref[...]), links, mine_ref, [send_ref])


def whole_kernel(keep_ref, got_ref, out_ref):
    out_ref[...] = narrow(keep_ref[...] + widen(got_ref[...]))


def sum_kernel(mine_ref, got_ref, out_ref):
    out_ref[...] = narrow(widen(mine_ref[...]) + widen(got_ref[...]))


def split_group_kernel(mine_ref, got_ref, first_ref, second_ref, *, links):
    mine, got = mine_ref[...], got_ref[...]
    high = piece_number(links) == 1
    first_ref[...] = jnp.where(high, got, mine)
    second_ref[...] = jnp.where(high, mine, got)


def last_group_kernel(mine1_ref, got1_ref, mine2_ref, got2_ref, out_ref, *, links):
    rows = mine1_ref.shape[0]
    high = piece_number(links)
    for at, (mine_ref, got_ref) in enumerate(((mine1_ref, got1_ref), (mine2_ref, got2_ref))):
        out_ref[aligned(2 * high + at, rows)] = mine_ref[...]
        out_ref[aligned(2 * (1 - high) + at, rows)] = got_ref[...]


def group_kernel(*refs, links):
    pieces = [ref[...].astype(F32) for ref in refs[:-1]]
    number = piece_number(links)
    both = [pick(pieces, number ^ at) for at in range(len(pieces))]
    refs[-1][...] = jnp.concatenate(both, axis=0).astype(BF)


def write_half(half_ref, place, qkv_hbm, wo_hbm, qkv_ref, wo_ref, sems):
    parts = sems.shape[0]
    rows, width = half_ref.shape[0] // parts, wo_hbm.shape[1]
    copies = []
    for part in range(parts):
        own, there = slice(part * rows, (part + 1) * rows), aligned(parts * place + part, rows)
        wo_ref[own] = half_ref[own, :width].astype(F32)
        qkv_ref[own] = half_ref[own, width:-LANES].astype(F32)
        for at, (ref, hbm) in enumerate(((wo_ref, wo_hbm), (qkv_ref, qkv_hbm))):
            copies.append(pltpu.make_async_copy(ref.at[pl.ds(part * rows, rows)], hbm.at[there], sems.at[part, at]))
            copies[-1].start()
    return copies


def assemble_mine_kernel(mine_ref, qkv_hbm, wo_hbm, mark_ref, qkv_ref, wo_ref, sems):
    mark_ref[...] = jnp.zeros_like(mark_ref)
    for copy in write_half(mine_ref, my_core(), qkv_hbm, wo_hbm, qkv_ref, wo_ref, sems):
        copy.wait()


def assemble_other_kernel(mine_ref, other_ref, _, __, qkv_hbm, wo_hbm, gate_ref, bias_ref, *refs):
    *norm_refs, qkv_ref, wo_ref, sems = refs
    copies = write_half(other_ref, 1 - my_core(), qkv_hbm, wo_hbm, qkv_ref, wo_ref, sems)
    rows = mine_ref.shape[0]
    columns = mine_ref[:, -LANES:].astype(F32) + other_ref[:, -LANES:].astype(F32)
    columns = columns + pltpu.roll(columns, LANES // 2, 1)
    stacked = jnp.transpose(columns)
    heads = gate_ref.shape[0]
    gate_ref[:, :rows] = stacked[8 : 8 + heads]
    gate_ref[:, rows:] = stacked[24 : 24 + heads]
    bias_ref[...] = stacked[4:5, : bias_ref.shape[1]]
    for row, norm_ref in enumerate(norm_refs):
        norm_ref[:, :rows] = stacked[row : row + 1]
        norm_ref[:, rows:] = stacked[16 + row : 17 + row]
    for copy in copies:
        copy.wait()


def in_hbm(out):
    return getattr(out, "memory_space", None) == pltpu.HBM


def out_spec(out):
    return pl.BlockSpec(memory_space=pltpu.HBM if in_hbm(out) else pltpu.VMEM)


class Job:
    def __init__(self, kernel, name, operands, outs, use):
        self.kernel, self.name, self.operands, self.outs, self.use = kernel, name, operands, outs, use


class Order:
    def __init__(self):
        self.last = ()

    def call(self, kernel, name, given, kept, outs, scratch=(), wait=(), hbm=False, onto=()):
        wait = (*self.last, *wait)
        space = pltpu.HBM if hbm else pltpu.VMEM
        given = [pltpu.with_memory_space_constraint(a, space) if hbm else a for a in given]
        kept = [pltpu.with_memory_space_constraint(a, pltpu.VMEM) for a in kept]
        got = pl.pallas_call(
            lambda *refs: kernel(*refs[len(wait) :]),
            out_shape=outs,
            in_specs=[pl.BlockSpec(memory_space=pl.ANY)] * len(wait)
            + [pl.BlockSpec(memory_space=space)] * len(given)
            + [pl.BlockSpec(memory_space=pltpu.VMEM)] * len(kept)
            + [pl.BlockSpec(memory_space=pltpu.HBM)] * len(onto),
            input_output_aliases={len(wait) + len(given) + len(kept) + at: at for at in range(len(onto))},
            out_specs=jax.tree.map(out_spec, outs),
            scratch_shapes=scratch,
            compiler_params=pltpu.CompilerParams(vmem_limit_bytes=VMEM_BYTES),
            cost_estimate=pl.CostEstimate(flops=0, bytes_accessed=0, transcendentals=0),
            name=name,
        )(*wait, *given, *kept, *onto)
        inside = [a for a, out in zip(jax.tree.leaves(got), jax.tree.leaves(outs)) if not in_hbm(out)]
        if inside:
            self.last = (min(inside, key=lambda a: a.size),)
        return got


    def run(self, *jobs):
        takes = [len(job.operands) for job in jobs]
        gives = [len(job.outs) for job in jobs]

        def kernel(*refs):
            given, made = refs[: sum(takes)], refs[sum(takes) :]
            for job, take, give in zip(jobs, takes, gives):
                job.kernel(*given[:take], *made[:give])
                given, made = given[take:], made[give:]

        operands = [a for job in jobs for a in job.operands]
        outs = tuple(out for job in jobs for out in job.outs)
        got = list(self.call(kernel, "_".join(job.name for job in jobs), operands, (), outs))
        for job, give in zip(jobs, gives):
            job.use(*got[:give])
            got = got[give:]


def kept(shape, dtype):
    return pltpu.VMEM(shape, dtype)


def shaped(shape, dtype):
    return jax.ShapeDtypeStruct(shape, dtype)


def core_swap(v):
    return jax.tree.map(lambda a: lax.ppermute(a, "mp", [(i, i ^ 1) for i in range(4)]), v)


def chip_swap(v):
    return jax.tree.map(lambda a: lax.ppermute(a, "mp", [(i, i ^ 2) for i in range(4)]), v)


def send_along(v, links):
    way = []
    for place in range(lax.axis_size("dp")):
        for spot in range(4):
            to = [place, spot]
            for link in links:
                link = link[spot % 2]
                to = [to[0], to[1] ^ 2] if link is None else [to[0] ^ (1 << link), to[1]]
            way.append((4 * place + spot, 4 * to[0] + to[1]))
    return lax.ppermute(v, ("dp", "mp"), way)


class Gather:
    def __init__(self, keep, got):
        self.first = (keep, *got)
        bits = list(range(lax.axis_size("dp").bit_length() - 1))
        self.links = [(None, 0), (0, None)] + [(bit, bit) for bit in bits[1:]]
        last = len(self.links) - 1
        self.steps = [functools.partial(self.share, at) for at in range(1, last)] + [self.swap]
        self.steps += [functools.partial(self.collect, at) for at in range(last, -1, -1)]

    def next(self):
        return self.steps.pop(0)()

    def early(self):
        return self.halve(early_kernel, "early", self.first, 0)

    def late(self, keep, got, small):
        sent = keep.shape[1] + LANES
        return self.halve(late_kernel, "late", (*self.take(), keep, *got, small), 0, sent)

    def halve(self, kernel, name, operands, at, sent=0):
        rows, columns = operands[0].shape
        shapes = (rows // 2, columns), (rows // 2, columns)
        if sent:
            shapes = (rows, columns + sent), (rows, sent)

        def use(keep, sent):
            self.keep, self.got = [keep], [send_along(sent, [self.links[at]])]

        kernel = functools.partial(kernel, links=[self.links[at]])
        return Job(kernel, name, operands, (shaped(shapes[0], F32), shaped(shapes[1], BF)), use)

    def take(self):
        pairs = [a for pair in zip(self.keep, self.got) for a in pair]
        self.keep, self.got = [], []
        return pairs

    def share(self, at):
        operands = self.take()
        if at > 1:
            return self.halve(part_kernel, "part", operands, at)
        return self.halve(meet_kernel, "meet", operands, at)

    def swap(self):
        operands = self.take()

        def use(keep):
            self.keep, self.got = [keep], [send_along(keep, [self.links[-1]])]

        return Job(whole_kernel, "whole", operands, (shaped(operands[0].shape, BF),), use)

    def collect(self, at):
        operands = self.take()
        rows, columns = operands[0].shape
        if at == 1:
            links = [self.links[at]]

            def use_parts(*parts):
                self.keep, self.got = list(parts), [send_along(part, [self.links[0]]) for part in parts]

            kernel = functools.partial(split_group_kernel, links=links)
            return Job(kernel, "split_group", operands, (shaped((rows, columns), BF),) * 2, use_parts)
        if at == 0:

            def use_all(keep):
                self.keep, self.got = [keep], [core_swap(keep)]

            kernel = functools.partial(last_group_kernel, links=[self.links[0]])
            return Job(kernel, "last_group", operands, (shaped((4 * rows, columns), BF),), use_all)
        if at == len(self.links) - 1:
            kernel, name = sum_kernel, "sum"
        else:
            kernel, name, rows = functools.partial(group_kernel, links=[self.links[at]]), "group", 2 * rows

        def use(keep):
            self.keep, self.got = [keep], [send_along(keep, [self.links[at - 1]])]

        return Job(kernel, name, operands, (shaped((rows, columns), BF),), use)


class Stream:
    def __init__(self, *first):
        self.first = first
        bits = list(range(lax.axis_size("dp").bit_length() - 1))
        self.bits = [(0, 1), (1, 0)] + [(bit, bit) for bit in bits[2:]]
        self.back = [(1, 1), (0, 0)] + self.bits[2:]
        self.steps = [self.start]
        self.steps += [functools.partial(self.halve, bits) for bits in self.bits[1:-1]]
        self.steps += [self.third, self.fourth]
        self.steps += [functools.partial(self.double, at) for at in range(len(bits), 0, -1)]

    def next(self):
        return self.steps.pop(0)()

    def split(self, kernel, name, operands, shape, bits):
        def use(keep, sent):
            self.keep, self.got = keep, send_along(sent, [bits])

        return Job(kernel, name, operands, (shaped(shape, F32), shaped(shape, BF)), use)

    def start(self):
        bits = self.bits[0]
        rows, columns = self.first[0].shape
        kernel = functools.partial(first_kernel, bits=bits)
        return self.split(kernel, "first", self.first, (2, rows // 2, columns), bits)

    def halve(self, bits):
        _, rows, columns = self.keep.shape
        kernel = functools.partial(halve_kernel, bits=bits)
        return self.split(kernel, "halve", (self.keep, self.got), (2, rows // 2, columns), bits)

    def third(self):
        _, rows, columns = self.keep.shape
        bit = self.bits[-1][0]
        kernel = functools.partial(third_kernel, bit=bit)
        return self.split(kernel, "third", (self.keep, self.got), (2, rows // 2, columns), (bit, None))

    def fourth(self):
        bit = self.bits[-1][0]
        kernel = functools.partial(fourth_kernel, bit=bit)
        return self.split(kernel, "fourth", (self.keep, self.got), self.keep.shape[1:], (None, bit))

    def double(self, at):
        if at == len(self.bits):
            kernel, name, shape = add_kernel, "add", self.keep.shape
        else:
            kernel, name = functools.partial(join_kernel, bits=self.back[at]), "join"
            shape = (2 * self.keep.shape[0], self.keep.shape[1])

        def use(keep):
            self.keep, self.got = keep, send_along(keep, [self.back[at - 1]])

        return Job(kernel, name, (self.keep, self.got), (shaped(shape, BF),), use)

    def finish(self, order, outs):
        kernel = functools.partial(final_kernel, bits=self.back[0])
        rows, columns = self.keep.shape
        scratch = [pltpu.VMEM((2 * rows, columns), F32), pltpu.SemaphoreType.DMA((2,))]
        outs = (*outs, shaped((8, LANES), F32))
        return order.call(kernel, "final", (self.keep, self.got), (), outs, scratch)[:2]


def after(v, *others):
    return lax.optimization_barrier((v, others))[0]


def exchange(order, home, partner, reverse, wait=()):
    kernel = functools.partial(chain_kernel, reverse=reverse)
    total = order.call(kernel, "chain", (home, partner), (), shaped(home.shape, BF), wait=wait)
    return total, lax.ppermute(total, "mp", [(2, 0), (3, 1)] if reverse else [(0, 2), (1, 3)])


def per_device(
    layer_input,
    qkv_weight,
    gate_weight,
    gate_bias,
    out_weight,
    inner_weight,
    outer_weight,
    leading_norm_gain,
    leading_norm_bias,
    trailing_norm_gain,
    trailing_norm_bias,
    random_features,
    output_grad,
):
    seqs, length, width = layer_input.shape
    heads, head, feat = random_features.shape
    pairs = heads // 2
    count = seqs * length
    hidden = inner_weight.shape[1]
    bias = gate_bias.reshape(1, heads)
    gain1, shift1 = leading_norm_gain.reshape(1, width), leading_norm_bias.reshape(1, width)
    gain2, shift2 = trailing_norm_gain.reshape(1, width), trailing_norm_bias.reshape(1, width)

    n_dp = lax.axis_size("dp")
    order = Order()
    halves = order.call(
        pack_kernel,
        "pack",
        (inner_weight, outer_weight),
        (),
        shaped((2, width // 2, hidden), BF),
        [pltpu.SemaphoreType.DMA((2,))],
        hbm=True,
    )
    half_chip = chip_swap(halves)
    inner_core, outer_core = core_swap(inner_weight), core_swap(outer_weight)

    by_seq = (seqs, length, width)
    gates = (seqs, length, LANES)
    states = (pairs, LANES + EXTRA, 2 * feat)
    gate_rows = jnp.transpose(gate_weight)
    sources = (layer_input, qkv_weight, gate_rows, bias, gain1, shift1, random_features)
    normed1, values, c, admit, c_row, a_row, phi_k, away, home = order.call(
        keys_kernel,
        "keys",
        sources,
        (),
        (
            kept((count, width), BF),
            kept(by_seq, F32),
            kept(gates, F32),
            kept(gates, F32),
            kept((seqs, heads, length), F32),
            kept((seqs, heads, length), F32),
            kept((seqs, heads, length, 2 * feat), BF),
            kept(states, BF),
            kept(states, BF),
        ),
        [pltpu.VMEM((width, 2 * width) if a is qkv_weight else a.shape, a.dtype) for a in sources]
        + [pltpu.SemaphoreType.DMA((len(sources),))],
        hbm=True,
    )
    partner_home, partner_away = core_swap(away), core_swap(home)
    total, got = exchange(order, home, partner_home, False)
    half_chip = after(half_chip, total)
    half_twin = lax.ppermute(half_chip, "dp", [(i, i ^ 1) for i in range(n_dp)])

    phi_q, scores, num = order.call(
        scores_kernel,
        "scores",
        (qkv_weight, random_features),
        (normed1, phi_k, values, c, c_row, a_row),
        (
            kept((seqs, heads, length, 2 * feat), BF),
            kept((seqs, heads, length, length), BF),
            kept((seqs, heads, length, LANES), F32),
        ),
        wait=(half_chip,),
    )
    got = after(got, num)
    swapped = core_swap(got)
    half_both = core_swap(half_chip)
    full, start, mixed_low, resid, normed2 = order.call(
        mix_kernel,
        "mix",
        (layer_input, got, swapped, partner_home, partner_away, out_weight, gain2, shift2),
        (phi_q, c, num),
        (
            kept((seqs, heads, length, LANES), F32),
            kept((seqs, *states), BF),
            kept(by_seq, BF),
            kept(by_seq, F32),
            kept(by_seq, BF),
        ),
    )

    normed2, mixed_low = (a.reshape(count, width) for a in (normed2, mixed_low))
    half_twin = after(half_twin, normed2)
    half_both_twin = core_swap(half_twin)
    shape = (count, width)
    grads = (width + hidden, width)
    out_part, dn2, out_low, keep0, send0 = order.call(
        feed_near_kernel,
        "feed_near",
        (output_grad.reshape(shape), inner_weight, outer_weight, inner_core, outer_core),
        (normed2, resid.reshape(shape)),
        (kept(shape, F32), kept(shape, F32), kept(shape, BF), shaped(grads, F32), shaped(grads, BF)),
    )
    got0 = core_swap(send0)
    far = pltpu.VMEM((2, width, hidden), BF)
    out_part, dn2, send1 = order.call(
        feed_far_kernel,
        "feed_both",
        (half_both, half_both_twin),
        (normed2, out_low, out_part, dn2),
        (kept(shape, F32), kept(shape, F32), shaped(grads, BF)),
        [far],
    )
    got1 = core_swap(send1)
    layer_out, dn2, keep1 = order.call(
        feed_last_kernel,
        "feed_chip",
        (half_chip, half_twin),
        (normed2, out_low, out_part, dn2),
        (pltpu.HBM(shape, F32), kept(shape, F32), shaped(grads, F32)),
        [far, pltpu.VMEM(shape, F32), pltpu.SemaphoreType.DMA],
    )
    stream = Stream(keep0, keep1, got0, got1)
    order.run(stream.next())

    dres, low, sums2, num_grads, r, away_grads, home_grads = order.call(
        turn_kernel,
        "turn",
        (output_grad, gain2, out_weight),
        (dn2.reshape(by_seq), resid, full, phi_q, c),
        (
            kept(by_seq, F32),
            kept((count, width), BF),
            kept((8, width), F32),
            kept((seqs, heads, length, 2 * LANES), BF),
            kept(gates, F32),
            kept(states, BF),
            kept(states, BF),
        ),
    )
    partner_home_grads, partner_away_grads = core_swap(away_grads), core_swap(home_grads)
    _, got_grads = exchange(order, home_grads, partner_home_grads, True)

    q_grad, k_part, v_part, k_col = order.call(
        back_kernel,
        "back",
        (random_features,),
        (phi_q, phi_k, values, num_grads, scores, c, c_row, a_row, start),
        (
            kept((count, width), BF),
            kept(by_seq, F32),
            kept(by_seq, F32),
            kept(gates, F32),
        ),
    )
    dn1_part, xhat1, scale1, keep1, *send1 = order.call(
        products_kernel,
        "products",
        (layer_input.reshape(shape), qkv_weight),
        (mixed_low, low, normed1, q_grad),
        (
            kept(shape, F32),
            kept(shape, F32),
            kept((count, LANES), F32),
            shaped((width // 2, 2 * width), F32),
            *[shaped((width // 8, 2 * width), BF)] * 4,
        ),
    )
    gather = Gather(keep1, core_swap(send1))
    got_grads = after(got_grads, keep1)
    swapped_grads = core_swap(got_grads)

    order.run(stream.next())
    order.run(gather.early())
    kv_grad, logit_low, bias_sum, keep2, *send2 = order.call(
        cross_kernel,
        "cross",
        (got_grads, swapped_grads, partner_home_grads, partner_away_grads, random_features),
        (away, home, start, phi_k, values, c, admit, r, k_col, k_part, v_part, normed1),
        (
            kept((count, 2 * width), BF),
            kept((count, LANES), BF),
            kept((8, LANES), F32),
            shaped((width // 2, 2 * width), F32),
            *[shaped((width // 8, 2 * width), BF)] * 4,
        ),
    )
    got2 = core_swap(send2)
    while len(stream.steps) > len(stream.bits) + 1:
        order.run(stream.next())
    dn1, small = order.call(
        close_kernel,
        "close",
        (qkv_weight, gate_rows),
        (dn1_part, xhat1, kv_grad, logit_low, bias_sum, normed1, sums2),
        (kept(shape, F32), shaped((width // 2, LANES), F32)),
    )
    order.run(gather.late(keep2, got2, small))
    dx, _ = order.call(
        input_kernel,
        "input",
        (gain1,),
        (dn1, xhat1, scale1, dres.reshape(shape)),
        (pltpu.HBM(shape, F32), shaped((8, LANES), F32)),
        [pltpu.VMEM(shape, F32), pltpu.SemaphoreType.DMA],
    )
    while len(gather.steps) > 6:
        order.run(gather.next())
    while len(stream.steps) > 3:
        order.run(stream.next())
    order.run(gather.next(), stream.next())
    order.run(gather.next(), stream.next())
    order.run(gather.next())
    order.run(gather.next(), stream.next())
    order.run(gather.next())
    inner_total, outer_total = stream.finish(order, (pltpu.HBM((width, hidden), F32), pltpu.HBM((hidden, width), F32)))
    order.run(gather.next())
    scratch = [
        pltpu.VMEM((width // 2, 3 * width), F32), pltpu.VMEM((width // 2, width), F32), pltpu.SemaphoreType.DMA((2, 2)),
    ]
    big = (pltpu.HBM((width, 3 * width), F32), pltpu.HBM((width, width), F32))
    *halves, _ = order.call(
        assemble_mine_kernel, "assemble_mine", tuple(gather.keep), (), (*big, shaped((8, LANES), F32)), scratch
    )
    qkv_grad, wo_grad, gate_grad, bias_grad, *norm_grads = order.call(
        assemble_other_kernel,
        "assemble_other",
        (*gather.keep, *gather.got),
        (),
        (*big, shaped((heads, width), F32), shaped((1, heads), F32), *[shaped((1, width), F32)] * 4),
        scratch,
        onto=halves,
    )
    return (
        layer_out.reshape(by_seq),
        dx.reshape(by_seq),
        qkv_grad,
        jnp.transpose(gate_grad),
        bias_grad.reshape(heads),
        wo_grad,
        inner_total,
        outer_total,
        *(a.reshape(width) for a in norm_grads),
    )


def solution(mesh):
    in_specs = (
        P("dp", "mp", None),
        P(),
        P(),
        P(),
        P(),
        P(None, "mp"),
        P("mp", None),
        P(),
        P(),
        P(),
        P(),
        P(),
        P("dp", "mp", None),
    )
    out_specs = (
        P("dp", "mp", None),
        P("dp", "mp", None),
        P(),
        P(),
        P(),
        P(),
        P(None, "mp"),
        P("mp", None),
        P(),
        P(),
        P(),
        P(),
    )
    return jax.shard_map(
        per_device, mesh=mesh, in_specs=in_specs, out_specs=out_specs, check_vma=False
    )
```

```python
import functools
import math

import jax
import jax.numpy as jnp
from jax import lax
from jax.experimental import pallas as pl
from jax.experimental.pallas import tpu as pltpu
from jax.sharding import PartitionSpec as P

BF = jnp.bfloat16
F32 = jnp.float32
epsilon = 1e-05
guard = 0.01
LANES = 128
EXTRA = 16
VMEM_BYTES = 16 * 1024 * 1024


def nn(a, b):
    return lax.dot_general(a, b, (((1,), (0,)), ((), ())), preferred_element_type=F32)


def nt(a, b):
    return lax.dot_general(a, b, (((1,), (1,)), ((), ())), preferred_element_type=F32)


def tn(a, b):
    return lax.dot_general(a, b, (((0,), (0,)), ((), ())), preferred_element_type=F32)


def two_terms(v):
    high = v.astype(BF)
    return high, (v - high.astype(F32)).astype(BF)


def iota(shape, dim):
    return lax.broadcasted_iota(jnp.int32, shape, dim)


def triangle(length, upper):
    rows, cols = iota((length, length), 0), iota((length, length), 1)
    return jnp.where((cols >= rows) if upper else (rows >= cols), 1.0, 0.0).astype(BF)


def running_sum(v, upper):
    ones = triangle(v.shape[0], upper)
    high, rest = two_terms(v)
    low = (v - high.astype(F32) - rest.astype(F32)).astype(BF)
    return nn(ones, high) + nn(ones, rest) + nn(ones, low)


def norm_rows(v):
    centred = v - jnp.mean(v, axis=-1, keepdims=True)
    scale = lax.rsqrt(jnp.mean(centred * centred, axis=-1, keepdims=True) + epsilon)
    return centred * scale, scale


def norm_rows_backward(grad, xhat, scale, gain):
    g = grad * gain
    return scale * (
        g
        - jnp.mean(g, axis=-1, keepdims=True)
        - xhat * jnp.mean(g * xhat, axis=-1, keepdims=True)
    )


def pair_frequencies(freq_ref, pair):
    even, odd = freq_ref[2 * pair], freq_ref[2 * pair + 1]
    none = jnp.zeros_like(even)
    return jnp.concatenate(
        [jnp.concatenate([even, none], axis=1), jnp.concatenate([none, odd], axis=1)], axis=0
    )


def scaled_sine_cosine(angles, scale):
    turns = jnp.floor(angles * (1.0 / math.pi) + 0.5)
    r = angles - turns * 3.140625
    r = r - turns * 0.0009675025939941406
    r = r - turns * 1.509958e-07
    odd = turns - 2.0 * jnp.floor(turns * 0.5)
    sign = scale - (2.0 * scale) * odd
    r2 = r * r
    sine = -0.00018362251175623582 * r2 + 0.008306273552368303
    sine = sine * r2 - 0.1666482311215342
    sine = sine * r2 + 0.9999966031254778
    cosine = -0.0012711240835350962 * r2 + 0.041487518673719546
    cosine = cosine * r2 - 0.4999123281046797
    cosine = cosine * r2 + 0.9999933132015835
    return sine * (r * sign), cosine * sign


def pair_features(values, freq, scale):
    high, low = two_terms(values)
    freq_high, freq_low = two_terms(freq)
    both = jnp.concatenate([freq_high, freq_high], axis=0)
    angles = nn(jnp.concatenate([high, low], axis=1), both) + nn(high, freq_low)
    sine, cosine = scaled_sine_cosine(angles, scale)
    sine, cosine = sine.astype(BF), cosine.astype(BF)
    feat = freq.shape[1] // 2
    return [
        jnp.concatenate([sine[:, h * feat : (h + 1) * feat], cosine[:, h * feat : (h + 1) * feat]], axis=1)
        for h in (0, 1)
    ]


def own_lanes(shape, half):
    lane = iota(shape, len(shape) - 1)
    return (lane >= LANES // 2) if half else (lane < LANES // 2)


def one_lane(shape, half):
    return iota(shape, len(shape) - 1) == (0 if half else LANES // 2)


def second_lane(shape, half):
    return iota(shape, len(shape) - 1) == (1 if half else LANES // 2 + 1)


def with_ones(values, half, both=False):
    v = values.astype(F32)
    ones = one_lane(v.shape, half) | (both & second_lane(v.shape, half))
    return jnp.where(own_lanes(v.shape, half), v, jnp.where(ones, 1.0, 0.0))


def pack_states(even, odd, decay_even, decay_odd):
    half = LANES // 2
    row = iota(even.shape, 0)
    states = jnp.where(row < half, even, odd).astype(BF)
    extra = iota((EXTRA, even.shape[1]), 0)
    parts = []
    for value in (even[half : half + 1], odd[0:1], decay_even, decay_odd):
        high = value.astype(BF).astype(F32)
        parts += [high, value - high]
    rows = jnp.zeros((EXTRA, even.shape[1]), F32)
    for at, part in enumerate(parts):
        rows = jnp.where(extra == at, part, rows)
    return states, rows.astype(BF)


def extra_row(packed, at):
    at = LANES + 2 * at
    return packed[at : at + 1] + packed[at + 1 : at + 2]


def decays(packed):
    return extra_row(packed, 2), extra_row(packed, 3)


def unpack_states(packed):
    half = LANES // 2
    states = packed[:LANES]
    row = iota(states.shape, 0)
    even = jnp.where(row < half, states, jnp.where(row == half, extra_row(packed, 0), 0.0))
    odd = jnp.where(row >= half, states, jnp.where(row == 0, extra_row(packed, 1), 0.0))
    return even, odd


def join_states(first, second):
    return [
        a + decay * b
        for a, b, decay in zip(unpack_states(first), unpack_states(second), decays(first))
    ]


def as_operand(state, half):
    at = 0 if half else LANES // 2
    norm = state[at : at + 1]
    rest = norm - norm.astype(BF).astype(F32)
    return jnp.where(iota(state.shape, 0) == at + 1, rest, state).astype(BF)


def decay_weights(c_col, c_row, a_row):
    length = c_col.shape[0]
    gap = jnp.minimum(c_col - c_row, 0.0)
    causal = iota((length, length), 0) >= iota((length, length), 1)
    return jnp.where(causal, jnp.exp(gap) * a_row, 0.0)


def lane_sum(v):
    return jnp.sum(v, axis=1, keepdims=True)


def each(count, step):
    lax.fori_loop(0, count, lambda i, none: (step(i), none)[1], 0)


def wide(v, axis):
    none = list(v.shape)
    none[axis] = LANES - v.shape[axis]
    return jnp.concatenate([v, jnp.zeros(none, v.dtype)], axis=axis)


def aligned(at, size):
    return pl.ds(pl.multiple_of(at * size, size), size)


def my_core():
    return lax.axis_index("mp") % 2


def my_chip():
    return lax.axis_index("mp") // 2


def pack_kernel(inner_ref, outer_ref, out_ref, sems):
    rows = out_ref.shape[1]
    mine = aligned(lax.axis_index("dp") % 2, rows)
    copies = [
        pltpu.make_async_copy(source.at[mine], out_ref.at[i], sems.at[i])
        for i, source in enumerate((inner_ref, outer_ref))
    ]
    for copy in copies:
        copy.start()
    for copy in copies:
        copy.wait()


def by_place(of_sequence):
    even = my_core() == 0
    one, two = of_sequence
    return jnp.where(even, two, one), jnp.where(even, one, two)


def put_states(pair, packed, away_ref, home_ref):
    for rows, parts in ((slice(0, LANES), [p[0] for p in packed]), (slice(LANES, None), [p[1] for p in packed])):
        away_ref[pair, rows], home_ref[pair, rows] = by_place(parts)


def keys_kernel(
    x_hbm, wqkv_hbm, gw_hbm, gb_hbm, gain_hbm, shift_hbm, freq_hbm,
    n1_ref, v_ref, c_ref, a_ref, crow_ref, arow_ref, pk_ref, away_ref, home_ref,
    x_ref, w_ref, gw_ref, gb_ref, gain_ref, shift_ref, freq_ref, sems,
):
    heads, _, feat = freq_ref.shape
    seqs, length, width = x_ref.shape
    sources = (x_hbm, gain_hbm, shift_hbm, gw_hbm, gb_hbm, wqkv_hbm.at[:, pl.ds(width, 2 * width)], freq_hbm)
    buffers = (x_ref, gain_ref, shift_ref, gw_ref, gb_ref, w_ref, freq_ref)
    copies = [
        pltpu.make_async_copy(source, buffer, sems.at[i])
        for i, (source, buffer) in enumerate(zip(sources, buffers))
    ]
    for copy in copies:
        copy.start()
    for copy in copies[:5]:
        copy.wait()
    scale = 1.0 / math.sqrt(feat)
    xhat, _ = norm_rows(x_ref[...].reshape(seqs * length, width))
    n1 = (xhat * gain_ref[...] + shift_ref[...]).astype(BF)
    n1_ref[...] = n1
    z = nt(n1, wide(gw_ref[...], 0)) + wide(gb_ref[...], 1)
    e = jnp.exp(-jnp.abs(z))
    log_keep = jnp.minimum(z, 0.0) - jnp.log1p(e)
    inverse = 1.0 / (1.0 + e)
    admit_all = jnp.where(z > 0.0, e * inverse, inverse)
    tails, decay = [], []
    for s in range(seqs):
        rows = slice(s * length, (s + 1) * length)
        c = running_sum(log_keep[rows], False)
        admit = admit_all[rows]
        c_ref[s] = c
        a_ref[s] = admit
        crow_ref[s] = jnp.transpose(c)[:heads]
        arow_ref[s] = jnp.transpose(admit)[:heads]
        last = c[length - 1 :]
        tails.append(jnp.exp(last - c) * admit)
        decay.append(jnp.exp(last))
    for copy in copies[5:]:
        copy.wait()
    keys = nn(n1, w_ref[:, :width])
    values = nn(n1, w_ref[:, width:])
    v_ref[...] = values.reshape(v_ref.shape)
    for pair in range(heads // 2):
        lanes = slice(pair * LANES, (pair + 1) * LANES)
        phi = pair_features(keys[:, lanes], pair_frequencies(freq_ref, pair), scale)
        packed = []
        for s in range(seqs):
            rows = slice(s * length, (s + 1) * length)
            states = []
            for half in (0, 1):
                h = 2 * pair + half
                phi_k = phi[half][rows]
                pk_ref[s, h] = phi_k
                weighted = with_ones(values[rows, lanes], half) * tails[s][:, h : h + 1]
                both = tn(jnp.concatenate(two_terms(weighted), axis=1), phi_k)
                states.append(both[:LANES] + both[LANES:])
            h = 2 * pair
            packed.append(pack_states(*states, decay[s][:, h : h + 1], decay[s][:, h + 1 : h + 2]))
        put_states(pair, packed, away_ref, home_ref)


def scores_kernel(wqkv_ref, freq_ref, n1_ref, pk_ref, v_ref, c_ref, crow_ref, arow_ref, pq_ref, p_ref, num_ref):
    seqs, heads, length, _ = pk_ref.shape
    scale = 1.0 / math.sqrt(freq_ref.shape[2])
    queries = nn(n1_ref[...], wqkv_ref[:, : n1_ref.shape[1]])
    for pair in range(heads // 2):
        lanes = slice(pair * LANES, (pair + 1) * LANES)
        phi = pair_features(queries[:, lanes], pair_frequencies(freq_ref, pair), scale)
        for s in range(seqs):
            for half in (0, 1):
                h = 2 * pair + half
                phi_q = phi[half][s * length : (s + 1) * length]
                pq_ref[s, h] = phi_q
                v = with_ones(v_ref[s, :, lanes], half)
                weights = decay_weights(
                    c_ref[s, :, h : h + 1], crow_ref[s, h : h + 1], arow_ref[s, h : h + 1]
                )
                p = (nt(phi_q, pk_ref[s, h]) * weights).astype(BF)
                p_ref[s, h] = p
                both = nn(p, jnp.concatenate(two_terms(v), axis=1))
                num_ref[s, h] = both[:, :LANES] + both[:, LANES:]


def mix_kernel(
    x_ref, got_ref, swapped_ref, partner_home_ref, partner_away_ref, wo_ref, gain_ref, shift_ref, pq_ref, c_ref, num_ref,
    full_ref, start_ref, mixed_ref, resid_ref, n2_ref,
):
    seqs, heads = pq_ref.shape[:2]
    core = my_core()

    def one(s):
        growth = jnp.exp(c_ref[s])
        for pair in range(heads // 2):
            before = jnp.where(s == core, got_ref[pair], swapped_ref[pair]).astype(F32)
            partner = jnp.where(s == core, partner_home_ref[pair], partner_away_ref[pair]).astype(F32)
            states = [
                jnp.where(core == 0, a, b)
                for a, b in zip(unpack_states(before), join_states(partner, before))
            ]
            none = jnp.zeros((1, 1), F32)
            main, rest = pack_states(*states, none, none)
            start_ref[s, pair, :LANES] = main
            start_ref[s, pair, LANES:] = rest
            mixed = []
            for half in (0, 1):
                h = 2 * pair + half
                full = num_ref[s, h] + growth[:, h : h + 1] * nt(
                    pq_ref[s, h], as_operand(states[half], half)
                )
                full_ref[s, h] = full
                at = 0 if half else LANES // 2
                sden = full[:, at : at + 1] + full[:, at + 1 : at + 2]
                mixed.append(full * lax.rsqrt(sden * sden + guard))
            pair_mixed = jnp.where(own_lanes(mixed[0].shape, 0), mixed[0], mixed[1])
            mixed_ref[s, :, pair * LANES : (pair + 1) * LANES] = pair_mixed.astype(BF)
        resid = x_ref[s] + nn(mixed_ref[s], wo_ref[...])
        resid_ref[s] = resid
        xhat, _ = norm_rows(resid)
        n2_ref[s] = (xhat * gain_ref[...] + shift_ref[...]).astype(BF)

    for s in range(seqs):
        one(s)


def gelu_and_slope(v):
    root = math.sqrt(2.0 / math.pi)
    v2 = v * v
    t = jnp.tanh(v * (root + (root * 0.044715) * v2))
    half = 0.5 * (1.0 + t)
    slope = half + (0.5 * v) * (1.0 - t * t) * (root + (root * 3.0 * 0.044715) * v2)
    return v * half, slope


def feed_block(n2, out_low, wi_ref, wo_ref):
    active, slope = gelu_and_slope(nn(n2, wi_ref[...]))
    active = active.astype(BF)
    pre_grad = (nt(out_low, wo_ref[...]) * slope).astype(BF)
    return nn(active, wo_ref[...]), nt(pre_grad, wi_ref[...]), tn(n2, pre_grad), tn(active, out_low)


def halves_together(far_ref, one, two):
    twin = lax.axis_index("dp") % 2
    rows = one.shape[1]
    for which in range(2):
        far_ref[which, aligned(twin, rows)] = one[which]
        far_ref[which, aligned(1 - twin, rows)] = two[which]


def feed_near_kernel(og_ref, wi0, wo0, wi2, wo2, n2_ref, resid_ref, out_ref, dn2_ref, low_ref, keep_ref, send_ref):
    low_ref[...] = og_ref[...].astype(BF)
    n2, out_low = n2_ref[...], low_ref[...]
    rows = n2.shape[1]
    out, dn2, inner, outer = feed_block(n2, out_low, wi2, wo2)
    send_ref[:rows] = inner.astype(BF)
    send_ref[rows:] = outer.astype(BF)
    out_own, dn2_own, inner, outer = feed_block(n2, out_low, wi0, wo0)
    keep_ref[:rows] = inner
    keep_ref[rows:] = outer
    out_ref[...] = resid_ref[...] + out + out_own
    dn2_ref[...] = dn2 + dn2_own


def feed_far_kernel(half_ref, twin_ref, n2_ref, low_ref, part_ref, dn2_part_ref, out_ref, dn2_ref, grad_ref, far_ref):
    twin = lax.axis_index("dp") % 2
    rows = half_ref.shape[1]
    for which in range(2):
        far_ref[which, aligned(twin, rows)] = half_ref[which]
        far_ref[which, aligned(1 - twin, rows)] = twin_ref[which]
    n2 = n2_ref[...]
    out, dn2, inner, outer = feed_block(n2, low_ref[...], far_ref.at[0], far_ref.at[1])
    out_ref[...] = part_ref[...] + out
    dn2_ref[...] = dn2_part_ref[...] + dn2
    rows = n2.shape[1]
    grad_ref[:rows] = inner.astype(grad_ref.dtype)
    grad_ref[rows:] = outer.astype(grad_ref.dtype)


def feed_last_kernel(
    half_ref, twin_ref, n2_ref, low_ref, part_ref, dn2_part_ref, out_hbm, dn2_ref, grad_ref, far_ref, out_ref, sem
):
    feed_far_kernel(half_ref, twin_ref, n2_ref, low_ref, part_ref, dn2_part_ref, out_ref, dn2_ref, grad_ref, far_ref)
    copy = pltpu.make_async_copy(out_ref, out_hbm, sem)
    copy.start()
    copy.wait()


def place_bit(bits):
    place = lax.axis_index("dp")
    return jnp.where(my_core() == 0, (place // (1 << bits[0])) % 2, (place // (1 << bits[1])) % 2)


def split_rows(total, bits, mine_ref, send_ref):
    rows = mine_ref.shape[1]
    high = place_bit(bits) == 1
    first, second = total[:, :rows], total[:, rows:]
    mine_ref[...] = jnp.where(high, second, first)
    send_ref[...] = jnp.where(high, first, second).astype(BF)


def halve_kernel(keep_ref, got_ref, mine_ref, send_ref, *, bits):
    split_rows(keep_ref[...] + got_ref[...].astype(F32), bits, mine_ref, send_ref)


def first_kernel(keep0_ref, keep1_ref, got0_ref, got1_ref, mine_ref, send_ref, *, bits):
    for block, (keep_ref, got_ref) in enumerate(((keep0_ref, got0_ref), (keep1_ref, got1_ref))):
        total = (keep_ref[...] + got_ref[...].astype(F32))[None]
        split_rows(total, bits, mine_ref.at[block : block + 1], send_ref.at[block : block + 1])


def third_kernel(keep_ref, got_ref, mine_ref, send_ref, *, bit):
    rows = mine_ref.shape[1]
    total = keep_ref[...] + got_ref[...].astype(F32)
    low, high = total[:, :rows], total[:, rows:]
    by_bit = place_bit((bit, bit)) == 1
    one, two = jnp.where(by_bit, high, low), jnp.where(by_bit, low, high)
    even = my_core() == 0
    for part in range(2):
        of_block = (low, high)[part]
        mine_ref[part] = jnp.where(even, one[part], of_block[0])
        send_ref[part] = jnp.where(even, two[part], of_block[1]).astype(BF)


def fourth_kernel(keep_ref, got_ref, mine_ref, send_ref, *, bit):
    total = keep_ref[...] + got_ref[...].astype(F32)
    second = (my_core() == 1) & (place_bit((bit, bit)) == 1)
    mine_ref[...] = jnp.where(second, total[1], total[0])
    send_ref[...] = jnp.where(second, total[0], total[1]).astype(BF)


def add_kernel(keep_ref, got_ref, out_ref):
    out_ref[...] = (keep_ref[...] + got_ref[...].astype(F32)).astype(out_ref.dtype)


def joined(mine_ref, got_ref, bits):
    high = place_bit(bits) == 1
    mine, got = mine_ref[...].astype(F32), got_ref[...].astype(F32)
    return jnp.concatenate([jnp.where(high, got, mine), jnp.where(high, mine, got)], axis=0)


def join_kernel(mine_ref, got_ref, out_ref, *, bits):
    out_ref[...] = joined(mine_ref, got_ref, bits).astype(BF)


def final_kernel(mine_ref, got_ref, inner_hbm, outer_hbm, mark_ref, whole_ref, sems, *, bits):
    mark_ref[...] = jnp.zeros_like(mark_ref)
    both = joined(mine_ref, got_ref, bits)
    quarter = both.shape[0] // 4
    one, two = both[quarter : 2 * quarter], both[2 * quarter : 3 * quarter]
    even = my_core() == 0
    whole_ref[:quarter] = both[:quarter]
    whole_ref[quarter : 2 * quarter] = jnp.where(even, two, one)
    whole_ref[2 * quarter : 3 * quarter] = jnp.where(even, one, two)
    whole_ref[3 * quarter :] = both[3 * quarter :]
    rows = inner_hbm.shape[0]
    copies = [
        pltpu.make_async_copy(whole_ref.at[pl.ds(at * rows, rows)], out_hbm, sems.at[at])
        for at, out_hbm in enumerate((inner_hbm, outer_hbm))
    ]
    for copy in copies:
        copy.start()
    for copy in copies:
        copy.wait()


def turn_kernel(
    og_ref, gain_ref, wo_ref, dn2_ref, resid_ref, full_ref, pq_ref, c_ref,
    dres_ref, low_ref, sums_ref, ng_ref, r_ref, away_ref, home_ref,
):
    seqs, heads, length, _ = pq_ref.shape
    sums_ref[...] = jnp.zeros_like(sums_ref)
    packed = [[] for _ in range(seqs)]

    def one(s):
        xhat, scale = norm_rows(resid_ref[s])
        dn2 = dn2_ref[s]
        dres = og_ref[s] + norm_rows_backward(dn2, xhat, scale, gain_ref[...])
        dres_ref[s] = dres
        low = dres.astype(BF)
        low_ref[s * length : (s + 1) * length] = low
        sums_ref[2:3] += jnp.sum(dn2 * xhat, axis=0, keepdims=True)
        sums_ref[3:4] += jnp.sum(dn2, axis=0, keepdims=True)
        dmixed = nt(low, wo_ref[...])
        c = c_ref[s]
        growth = jnp.exp(c)
        decay = jnp.exp(c[length - 1 :])
        lane = iota(c.shape, 1)
        r_all = jnp.zeros_like(c)
        for pair in range(heads // 2):
            g = dmixed[:, pair * LANES : (pair + 1) * LANES]
            states = []
            for half in (0, 1):
                h = 2 * pair + half
                full = full_ref[s, h]
                at = 0 if half else LANES // 2
                sden = full[:, at : at + 1] + full[:, at + 1 : at + 2]
                inverse = lax.rsqrt(sden * sden + guard)
                inverse2 = inverse * inverse
                mine = own_lanes(g.shape, half)
                dot = lane_sum(jnp.where(mine, g * full, 0.0)) * inverse
                sden_grad = -dot * sden * inverse2
                r_all = jnp.where(lane == h, dot * inverse2 * guard, r_all)
                grads = jnp.where(
                    mine, g * inverse, jnp.where(one_lane(g.shape, half), sden_grad, 0.0)
                )
                ng_ref[s, h] = jnp.concatenate(two_terms(grads), axis=1)
                lifted = jnp.concatenate(two_terms(grads * growth[:, h : h + 1]), axis=1)
                both = tn(lifted, pq_ref[s, h])
                states.append(both[:LANES] + both[LANES:])
            h = 2 * pair
            packed[s].append(pack_states(*states, decay[:, h : h + 1], decay[:, h + 1 : h + 2]))
        r_ref[s] = r_all

    for s in range(seqs):
        one(s)
    for pair, both in enumerate(zip(*packed)):
        put_states(pair, both, away_ref, home_ref)


def angle_grads(phi, dphi):
    feat = phi.shape[1] // 2
    phi = phi.astype(F32)
    return phi[:, feat:] * dphi[:, :feat] - phi[:, :feat] * dphi[:, feat:]


def weight_grads(left_ref, right_ref, keep_ref, send_refs):
    rows = keep_ref.shape[0]
    core = my_core()
    keep_ref[...] = tn(left_ref[:, aligned(core, rows)], right_ref[...])
    away = tn(left_ref[:, aligned(1 - core, rows)], right_ref[...]).astype(BF)
    rows //= len(send_refs)
    for part, send_ref in enumerate(send_refs):
        send_ref[...] = away[part * rows : (part + 1) * rows]


def back_kernel(
    freq_ref, pq_ref, pk_ref, v_ref, ng_ref, p_ref, c_ref, crow_ref, arow_ref, start_ref,
    qg_ref, kg_ref, vg_ref, kcol_ref,
):
    seqs, heads, length, _ = pq_ref.shape

    def one(s):
        tokens = aligned(s, length)
        c = c_ref[s]
        growth = jnp.exp(c)
        lane = iota(c.shape, 1)
        kcol = jnp.zeros_like(c)
        for pair in range(heads // 2):
            at = pair * LANES
            freq = pair_frequencies(freq_ref, pair).astype(BF)
            states = unpack_states(start_ref[s, pair].astype(F32))
            q_angles, k_angles, v_grads = [], [], []
            for half in (0, 1):
                h = 2 * pair + half
                phi_q, phi_k = pq_ref[s, h], pk_ref[s, h]
                grads = ng_ref[s, h, :, :LANES]
                v = with_ones(v_ref[s, :, at : at + LANES], half)
                weights = decay_weights(c[:, h : h + 1], crow_ref[s, h : h + 1], arow_ref[s, h : h + 1])
                dk = (nt(grads, v.astype(BF)) * weights).astype(BF)
                lifted = (grads.astype(F32) * growth[:, h : h + 1]).astype(BF)
                dphi_q = nn(dk, phi_k) + nn(lifted, states[half].astype(BF))
                q_angles.append(angle_grads(phi_q, dphi_q))
                k_angles.append(angle_grads(phi_k, tn(dk, phi_q)))
                both = tn(p_ref[s, h], ng_ref[s, h])
                dv = both[:, :LANES] + both[:, LANES:]
                v_grads.append(dv)
                kcol = jnp.where(lane == h, lane_sum(v * dv), kcol)
            qg_ref[tokens, at : at + LANES] = nt(
                jnp.concatenate(q_angles, axis=1).astype(BF), freq
            ).astype(BF)
            kg_ref[s, :, at : at + LANES] = nt(jnp.concatenate(k_angles, axis=1).astype(BF), freq)
            vg_ref[s, :, at : at + LANES] = jnp.where(
                own_lanes(v_grads[0].shape, 0), v_grads[0], v_grads[1]
            )
        kcol_ref[s] = kcol

    each(seqs, one)


def products_kernel(
    x_ref, wqkv_ref, mixed_ref, low_ref, n1_ref, qg_ref, part_ref, xhat_ref, scale_ref, keep_ref, *send_refs
):
    width = low_ref.shape[1]
    part_ref[...] = nt(qg_ref[...], wqkv_ref[:, :width])
    xhat, scale = norm_rows(x_ref[...])
    xhat_ref[...] = xhat
    scale_ref[...] = jnp.broadcast_to(scale, scale_ref.shape)
    for at, left_ref, right_ref in ((0, mixed_ref, low_ref), (width, n1_ref, qg_ref)):
        lanes = pl.ds(at, width)
        weight_grads(left_ref, right_ref, keep_ref.at[:, lanes], [ref.at[:, lanes] for ref in send_refs])


def cross_kernel(
    got_ref, swapped_ref, partner_home_ref, partner_away_ref, freq_ref, away_ref, home_ref, start_ref, pk_ref, v_ref,
    c_ref, a_ref, r_ref, kcol_ref,
    kg_ref, vg_ref, n1_ref,
    kv_ref, logit_ref, bias_ref, keep_ref, *send_refs,
):
    seqs, heads, length, _ = pk_ref.shape
    core = my_core()
    width = kg_ref.shape[2]
    bias_ref[...] = jnp.zeros_like(bias_ref)

    def one(s):
        tokens = aligned(s, length)
        c, a = c_ref[s], a_ref[s]
        tail = jnp.exp(c[length - 1 :] - c) * a
        lane = iota(c.shape, 1)
        lane_row = iota((1, c.shape[1]), 1)
        kcol = kcol_ref[s]
        ends = jnp.zeros((1, c.shape[1]), F32)
        for pair in range(heads // 2):
            at = pair * LANES
            freq = pair_frequencies(freq_ref, pair).astype(BF)
            after = jnp.where(s == core, got_ref[pair], swapped_ref[pair]).astype(F32)
            partner = jnp.where(s == core, partner_home_ref[pair], partner_away_ref[pair]).astype(F32)
            grads = [
                jnp.where(core == 1, a, b)
                for a, b in zip(unpack_states(after), join_states(partner, after))
            ]
            local = jnp.where(s == core, home_ref[pair], away_ref[pair]).astype(F32)
            reached = join_states(local, start_ref[s, pair].astype(F32))
            k_angles, v_grads = [], []
            for half in (0, 1):
                h = 2 * pair + half
                phi_k = pk_ref[s, h]
                v = with_ones(v_ref[s, :, at : at + LANES], half, True)
                grad_low = as_operand(grads[half], half)
                weight = tail[:, h : h + 1]
                k_angles.append(angle_grads(phi_k, nn(v.astype(BF), grad_low)) * weight)
                dv = nt(phi_k, grad_low) * weight
                v_grads.append(dv)
                kcol = kcol + jnp.where(lane == h, lane_sum(v * dv), 0.0)
                end = jnp.sum(lane_sum(grads[half] * reached[half]), axis=0, keepdims=True)
                ends = jnp.where(lane_row == h, end, ends)
            kg = kg_ref[s, :, at : at + LANES] + nt(
                jnp.concatenate(k_angles, axis=1).astype(BF), freq
            )
            vg = vg_ref[s, :, at : at + LANES] + jnp.where(
                own_lanes(v_grads[0].shape, 0), v_grads[0], v_grads[1]
            )
            kv_ref[tokens, at : at + LANES] = kg.astype(BF)
            kv_ref[tokens, width + at : width + at + LANES] = vg.astype(BF)
        keep_grad = running_sum(r_ref[s] - kcol, True) + ends
        logit_grad = a * keep_grad - (1.0 - a) * kcol
        logit_ref[tokens] = logit_grad.astype(BF)
        bias_ref[0:1] += jnp.sum(logit_grad, axis=0, keepdims=True)

    for i in range(seqs):
        one(i)
    weight_grads(n1_ref, kv_ref, keep_ref, send_refs)


def close_kernel(
    wqkv_ref, gw_ref, part_ref, xhat_ref, kv_ref, logit_ref, bias_ref, n1_ref, sums2_ref, dn1_ref, small_ref
):
    width = part_ref.shape[1]
    logit_low = logit_ref[...]
    dn1 = part_ref[...] + nt(kv_ref[...], wqkv_ref[:, width:]) + nn(logit_low, wide(gw_ref[...], 0))
    xhat = xhat_ref[...]
    dn1_ref[...] = dn1
    row = iota((8, width), 0)
    sums = jnp.where(row == 0, jnp.sum(dn1 * xhat, axis=0, keepdims=True), sums2_ref[...])
    sums = jnp.where(row == 1, jnp.sum(dn1, axis=0, keepdims=True), sums)
    bias = jnp.concatenate([bias_ref[0:1], jnp.zeros((1, width - LANES), F32)], axis=1)
    sums = jnp.where(row == 4, bias, sums)
    gates = tn(logit_low, n1_ref[...])[:8]
    stacked = jnp.concatenate([sums, gates, jnp.zeros((LANES - 16, width), F32)], axis=0)
    columns = jnp.transpose(stacked)
    rows = small_ref.shape[0]
    small_ref[...] = columns[:rows] + pltpu.roll(columns[rows:], 16, 1)


def input_kernel(gain_ref, dn1_ref, xhat_ref, scale_ref, dres_ref, dx_hbm, mark_ref, dx_ref, sem):
    mark_ref[...] = jnp.zeros_like(mark_ref)
    dx_ref[...] = dres_ref[...] + norm_rows_backward(dn1_ref[...], xhat_ref[...], scale_ref[:, :1], gain_ref[...])
    copy = pltpu.make_async_copy(dx_ref, dx_hbm, sem)
    copy.start()
    copy.wait()


def chain_kernel(me_ref, partner_ref, out_ref, *, reverse):
    core = my_core()
    lead = (core == 0) if reverse else (core == 1)
    for pair in range(out_ref.shape[0]):
        mine, other = me_ref[pair].astype(F32), partner_ref[pair].astype(F32)
        first = jnp.where(lead, mine, other)
        second = jnp.where(lead, other, mine)
        none = jnp.zeros((1, 1), F32)
        main, rest = pack_states(*join_states(first, second), none, none)
        out_ref[pair, :LANES] = main
        out_ref[pair, LANES:] = rest


def widen(v):
    main, last = v[:, :-LANES].astype(F32), v[:, -LANES:].astype(F32)
    last = jnp.where(iota(last.shape, 1) < LANES // 2, last + pltpu.roll(last, LANES // 2, 1), 0.0)
    return jnp.concatenate([main, last], axis=1)


def narrow(v):
    main, last = v[:, :-LANES].astype(BF), v[:, -LANES:]
    high, low = two_terms(last)
    last = high.astype(F32) + pltpu.roll(low.astype(F32), LANES // 2, 1)
    return jnp.concatenate([main, last.astype(BF)], axis=1)


def link_bit(link):
    return my_chip() if link is None else (lax.axis_index("dp") // (1 << link)) % 2


def piece_number(links):
    number = 0
    for of_zero, of_one in links:
        bit = link_bit(of_zero)
        if of_one != of_zero:
            bit = jnp.where(my_core() == 0, bit, link_bit(of_one))
        number = 2 * number + bit
    return number


def pick(pieces, number):
    taken = pieces[0]
    for at in range(1, len(pieces)):
        taken = jnp.where(number == at, pieces[at], taken)
    return taken


def share_out(total, links, mine_ref, send_refs):
    rows = mine_ref.shape[0]
    pieces = [total[at : at + rows] for at in range(0, total.shape[0], rows)]
    number = piece_number(links)
    mine_ref[...] = pick(pieces, number)
    for k, send_ref in enumerate(send_refs):
        send_ref[...] = narrow(pick(pieces, number ^ (k + 1)))


def early_kernel(keep_ref, *refs, links):
    *got_refs, mine_ref, send_ref = refs
    rows = mine_ref.shape[0]
    total = keep_ref[...] + jnp.concatenate([ref[...].astype(F32) for ref in got_refs], axis=0)
    number = piece_number(links)
    pieces = [total[:rows], total[rows:]]
    mine_ref[...] = pick(pieces, number)
    send_ref[...] = pick(pieces, number ^ 1).astype(BF)


def late_kernel(early_ref, early_got_ref, keep_ref, *refs, links):
    *got_refs, small_ref, mine_ref, send_ref = refs
    before = early_ref.shape[1]
    mine_ref[:, :before] = early_ref[...] + early_got_ref[...].astype(F32)
    total = keep_ref[...] + jnp.concatenate([ref[...].astype(F32) for ref in got_refs], axis=0)
    total = jnp.concatenate([total, small_ref[...]], axis=1)
    share_out(total, links, mine_ref.at[:, pl.ds(before, total.shape[1])], [send_ref])


def meet_kernel(keep_ref, got_ref, mine_ref, send_ref, *, links):
    before = keep_ref.shape[1] - got_ref.shape[1]
    second = keep_ref[:, before:] + widen(got_ref[...])
    share_out(jnp.concatenate([keep_ref[:, :before], second], axis=1), links, mine_ref, [send_ref])


def part_kernel(keep_ref, got_ref, mine_ref, send_ref, *, links):
    share_out(keep_ref[...] + widen(got_ref[...]), links, mine_ref, [send_ref])


def whole_kernel(keep_ref, got_ref, out_ref):
    out_ref[...] = narrow(keep_ref[...] + widen(got_ref[...]))


def sum_kernel(mine_ref, got_ref, out_ref):
    out_ref[...] = narrow(widen(mine_ref[...]) + widen(got_ref[...]))


def split_group_kernel(mine_ref, got_ref, first_ref, second_ref, *, links):
    mine, got = mine_ref[...], got_ref[...]
    high = piece_number(links) == 1
    first_ref[...] = jnp.where(high, got, mine)
    second_ref[...] = jnp.where(high, mine, got)


def group_kernel(*refs, links):
    pieces = [ref[...].astype(F32) for ref in refs[:-1]]
    number = piece_number(links)
    both = [pick(pieces, number ^ at) for at in range(len(pieces))]
    refs[-1][...] = jnp.concatenate(both, axis=0).astype(BF)


def piece_place(of_partner, far, links):
    core = my_core()
    core = 1 - core if of_partner else core
    high = jnp.where(core == 0, link_bit(links[0]), link_bit(links[1]))
    return 2 * core + (1 - high if far else high)


def write_pieces(pieces, places, qkv_hbm, wo_hbm, qkv_ref, wo_ref, sems):
    rows, width = pieces[0].shape[0], wo_hbm.shape[1]
    copies = []
    for at, (piece_ref, place) in enumerate(zip(pieces, places)):
        own = slice(at * rows, (at + 1) * rows)
        wo_ref[own] = piece_ref[:, :width].astype(F32)
        qkv_ref[own] = piece_ref[:, width:-LANES].astype(F32)
        for which, (ref, hbm) in enumerate(((wo_ref, wo_hbm), (qkv_ref, qkv_hbm))):
            there = hbm.at[aligned(place, rows)]
            copies.append(pltpu.make_async_copy(ref.at[pl.ds(at * rows, rows)], there, sems.at[at, which]))
            copies[-1].start()
    return copies


def write_near_kernel(mine1_ref, mine2_ref, other1_ref, other2_ref, qkv_hbm, wo_hbm, mark_ref, qkv_ref, wo_ref, sems, *, links):
    mark_ref[...] = jnp.zeros_like(mark_ref)
    mine, other = 2 * piece_place(False, False, links), 2 * piece_place(True, False, links)
    pieces, places = (mine1_ref, mine2_ref, other1_ref, other2_ref), (mine, mine + 1, other, other + 1)
    for copy in write_pieces(pieces, places, qkv_hbm, wo_hbm, qkv_ref, wo_ref, sems):
        copy.wait()


def write_far_kernel(*refs, links):
    near, far, outs = refs[:4], refs[4:8], refs[10:]
    qkv_hbm, wo_hbm, gate_hbm, *norm_hbm, bias_hbm, qkv_ref, wo_ref, small_ref, bias_ref, columns_ref, sems, small_sems = outs
    rows = far[0].shape[0]
    for pieces, is_far in ((near, False), (far, True)):
        for at in range(4):
            place = 2 * piece_place(at > 1, is_far, links) + at % 2
            columns_ref[aligned(place, rows)] = pieces[at][:, -LANES:].astype(F32)
    half = columns_ref.shape[0] // 2
    columns = columns_ref[:half] + columns_ref[half:]
    columns = columns + pltpu.roll(columns, LANES // 2, 1)
    stacked = jnp.transpose(columns)
    small_ref[:, :half] = stacked[:16]
    small_ref[:, half:] = stacked[16:32]
    heads = gate_hbm.shape[0]
    bias_ref[...] = stacked[4:5, : bias_ref.shape[1]]
    there = [(8, heads, gate_hbm)] + [(row, 1, hbm) for row, hbm in enumerate(norm_hbm)]
    copies = []
    for at, (row, count, hbm) in enumerate(there):
        copies.append(pltpu.make_async_copy(small_ref.at[pl.ds(row, count)], hbm, small_sems.at[at]))
    copies.append(pltpu.make_async_copy(bias_ref, bias_hbm, small_sems.at[len(there)]))
    for copy in copies:
        copy.start()
    mine, other = 2 * piece_place(False, True, links), 2 * piece_place(True, True, links)
    copies += write_pieces(far, (mine, mine + 1, other, other + 1), qkv_hbm, wo_hbm, qkv_ref, wo_ref, sems)
    for copy in copies:
        copy.wait()


def in_hbm(out):
    return getattr(out, "memory_space", None) == pltpu.HBM


def out_spec(out):
    return pl.BlockSpec(memory_space=pltpu.HBM if in_hbm(out) else pltpu.VMEM)


class Job:
    def __init__(self, kernel, name, operands, outs, use):
        self.kernel, self.name, self.operands, self.outs, self.use = kernel, name, operands, outs, use


class Order:
    def __init__(self):
        self.last = ()

    def call(self, kernel, name, given, kept, outs, scratch=(), wait=(), hbm=False, onto=()):
        wait = (*self.last, *wait)
        space = pltpu.HBM if hbm else pltpu.VMEM
        given = [pltpu.with_memory_space_constraint(a, space) if hbm else a for a in given]
        kept = [pltpu.with_memory_space_constraint(a, pltpu.VMEM) for a in kept]
        got = pl.pallas_call(
            lambda *refs: kernel(*refs[len(wait) :]),
            out_shape=outs,
            in_specs=[pl.BlockSpec(memory_space=pl.ANY)] * len(wait)
            + [pl.BlockSpec(memory_space=space)] * len(given)
            + [pl.BlockSpec(memory_space=pltpu.VMEM)] * len(kept)
            + [pl.BlockSpec(memory_space=pltpu.HBM)] * len(onto),
            input_output_aliases={len(wait) + len(given) + len(kept) + at: at for at in range(len(onto))},
            out_specs=jax.tree.map(out_spec, outs),
            scratch_shapes=scratch,
            compiler_params=pltpu.CompilerParams(vmem_limit_bytes=VMEM_BYTES),
            cost_estimate=pl.CostEstimate(flops=0, bytes_accessed=0, transcendentals=0),
            name=name,
        )(*wait, *given, *kept, *onto)
        inside = [a for a, out in zip(jax.tree.leaves(got), jax.tree.leaves(outs)) if not in_hbm(out)]
        if inside:
            self.last = (min(inside, key=lambda a: a.size),)
        return got


    def run(self, *jobs):
        takes = [len(job.operands) for job in jobs]
        gives = [len(job.outs) for job in jobs]

        def kernel(*refs):
            given, made = refs[: sum(takes)], refs[sum(takes) :]
            for job, take, give in zip(jobs, takes, gives):
                job.kernel(*given[:take], *made[:give])
                given, made = given[take:], made[give:]

        operands = [a for job in jobs for a in job.operands]
        outs = tuple(out for job in jobs for out in job.outs)
        got = list(self.call(kernel, "_".join(job.name for job in jobs), operands, (), outs))
        for job, give in zip(jobs, gives):
            job.use(*got[:give])
            got = got[give:]


def kept(shape, dtype):
    return pltpu.VMEM(shape, dtype)


def shaped(shape, dtype):
    return jax.ShapeDtypeStruct(shape, dtype)


def core_swap(v):
    return jax.tree.map(lambda a: lax.ppermute(a, "mp", [(i, i ^ 1) for i in range(4)]), v)


def chip_swap(v):
    return jax.tree.map(lambda a: lax.ppermute(a, "mp", [(i, i ^ 2) for i in range(4)]), v)


def send_along(v, links):
    way = []
    for place in range(lax.axis_size("dp")):
        for spot in range(4):
            to = [place, spot]
            for link in links:
                link = link[spot % 2]
                to = [to[0], to[1] ^ 2] if link is None else [to[0] ^ (1 << link), to[1]]
            way.append((4 * place + spot, 4 * to[0] + to[1]))
    return lax.ppermute(v, ("dp", "mp"), way)


class Gather:
    def __init__(self, keep, got):
        self.first = (keep, *got)
        bits = list(range(lax.axis_size("dp").bit_length() - 1))
        self.links = [(None, 0), (0, None)] + [(bit, bit) for bit in bits[1:]]
        last = len(self.links) - 1
        self.steps = [functools.partial(self.share, at) for at in range(1, last)] + [self.swap]
        self.steps += [functools.partial(self.collect, at) for at in range(last, 0, -1)]

    def next(self):
        return self.steps.pop(0)()

    def early(self):
        return self.halve(early_kernel, "early", self.first, 0)

    def late(self, keep, got, small):
        sent = keep.shape[1] + LANES
        return self.halve(late_kernel, "late", (*self.take(), keep, *got, small), 0, sent)

    def halve(self, kernel, name, operands, at, sent=0):
        rows, columns = operands[0].shape
        shapes = (rows // 2, columns), (rows // 2, columns)
        if sent:
            shapes = (rows, columns + sent), (rows, sent)

        def use(keep, sent):
            self.keep, self.got = [keep], [send_along(sent, [self.links[at]])]

        kernel = functools.partial(kernel, links=[self.links[at]])
        return Job(kernel, name, operands, (shaped(shapes[0], F32), shaped(shapes[1], BF)), use)

    def take(self):
        pairs = [a for pair in zip(self.keep, self.got) for a in pair]
        self.keep, self.got = [], []
        return pairs

    def share(self, at):
        operands = self.take()
        if at > 1:
            return self.halve(part_kernel, "part", operands, at)
        return self.halve(meet_kernel, "meet", operands, at)

    def swap(self):
        operands = self.take()

        def use(keep):
            self.keep, self.got = [keep], [send_along(keep, [self.links[-1]])]

        return Job(whole_kernel, "whole", operands, (shaped(operands[0].shape, BF),), use)

    def collect(self, at):
        operands = self.take()
        rows, columns = operands[0].shape
        if at == 1:
            links = [self.links[at]]

            def use_parts(*parts):
                self.keep, self.got = list(parts), [send_along(part, [self.links[0]]) for part in parts]

            kernel = functools.partial(split_group_kernel, links=links)
            return Job(kernel, "split_group", operands, (shaped((rows, columns), BF),) * 2, use_parts)
        if at == len(self.links) - 1:
            kernel, name = sum_kernel, "sum"
        else:
            kernel, name, rows = functools.partial(group_kernel, links=[self.links[at]]), "group", 2 * rows

        def use(keep):
            self.keep, self.got = [keep], [send_along(keep, [self.links[at - 1]])]

        return Job(kernel, name, operands, (shaped((rows, columns), BF),), use)


class Stream:
    def __init__(self, *first):
        self.first = first
        bits = list(range(lax.axis_size("dp").bit_length() - 1))
        self.bits = [(0, 1), (1, 0)] + [(bit, bit) for bit in bits[2:]]
        self.back = [(1, 1), (0, 0)] + self.bits[2:]
        self.steps = [self.start]
        self.steps += [functools.partial(self.halve, bits) for bits in self.bits[1:-1]]
        self.steps += [self.third, self.fourth]
        self.steps += [functools.partial(self.double, at) for at in range(len(bits), 0, -1)]

    def next(self):
        return self.steps.pop(0)()

    def split(self, kernel, name, operands, shape, bits):
        def use(keep, sent):
            self.keep, self.got = keep, send_along(sent, [bits])

        return Job(kernel, name, operands, (shaped(shape, F32), shaped(shape, BF)), use)

    def start(self):
        bits = self.bits[0]
        rows, columns = self.first[0].shape
        kernel = functools.partial(first_kernel, bits=bits)
        return self.split(kernel, "first", self.first, (2, rows // 2, columns), bits)

    def halve(self, bits):
        _, rows, columns = self.keep.shape
        kernel = functools.partial(halve_kernel, bits=bits)
        return self.split(kernel, "halve", (self.keep, self.got), (2, rows // 2, columns), bits)

    def third(self):
        _, rows, columns = self.keep.shape
        bit = self.bits[-1][0]
        kernel = functools.partial(third_kernel, bit=bit)
        return self.split(kernel, "third", (self.keep, self.got), (2, rows // 2, columns), (bit, None))

    def fourth(self):
        bit = self.bits[-1][0]
        kernel = functools.partial(fourth_kernel, bit=bit)
        return self.split(kernel, "fourth", (self.keep, self.got), self.keep.shape[1:], (None, bit))

    def double(self, at):
        if at == len(self.bits):
            kernel, name, shape = add_kernel, "add", self.keep.shape
        else:
            kernel, name = functools.partial(join_kernel, bits=self.back[at]), "join"
            shape = (2 * self.keep.shape[0], self.keep.shape[1])

        def use(keep):
            self.keep, self.got = keep, send_along(keep, [self.back[at - 1]])

        return Job(kernel, name, (self.keep, self.got), (shaped(shape, BF),), use)

    def finish(self, order, outs):
        kernel = functools.partial(final_kernel, bits=self.back[0])
        rows, columns = self.keep.shape
        scratch = [pltpu.VMEM((2 * rows, columns), F32), pltpu.SemaphoreType.DMA((2,))]
        outs = (*outs, shaped((8, LANES), F32))
        return order.call(kernel, "final", (self.keep, self.got), (), outs, scratch)[:2]


def after(v, *others):
    return lax.optimization_barrier((v, others))[0]


def exchange(order, home, partner, reverse, wait=()):
    kernel = functools.partial(chain_kernel, reverse=reverse)
    total = order.call(kernel, "chain", (home, partner), (), shaped(home.shape, BF), wait=wait)
    return total, lax.ppermute(total, "mp", [(2, 0), (3, 1)] if reverse else [(0, 2), (1, 3)])


def per_device(
    layer_input,
    qkv_weight,
    gate_weight,
    gate_bias,
    out_weight,
    inner_weight,
    outer_weight,
    leading_norm_gain,
    leading_norm_bias,
    trailing_norm_gain,
    trailing_norm_bias,
    random_features,
    output_grad,
):
    seqs, length, width = layer_input.shape
    heads, head, feat = random_features.shape
    pairs = heads // 2
    count = seqs * length
    hidden = inner_weight.shape[1]
    bias = gate_bias.reshape(1, heads)
    gain1, shift1 = leading_norm_gain.reshape(1, width), leading_norm_bias.reshape(1, width)
    gain2, shift2 = trailing_norm_gain.reshape(1, width), trailing_norm_bias.reshape(1, width)

    n_dp = lax.axis_size("dp")
    order = Order()
    halves = order.call(
        pack_kernel,
        "pack",
        (inner_weight, outer_weight),
        (),
        shaped((2, width // 2, hidden), BF),
        [pltpu.SemaphoreType.DMA((2,))],
        hbm=True,
    )
    half_chip = chip_swap(halves)
    inner_core, outer_core = core_swap(inner_weight), core_swap(outer_weight)

    by_seq = (seqs, length, width)
    gates = (seqs, length, LANES)
    states = (pairs, LANES + EXTRA, 2 * feat)
    gate_rows = jnp.transpose(gate_weight)
    sources = (layer_input, qkv_weight, gate_rows, bias, gain1, shift1, random_features)
    normed1, values, c, admit, c_row, a_row, phi_k, away, home = order.call(
        keys_kernel,
        "keys",
        sources,
        (),
        (
            kept((count, width), BF),
            kept(by_seq, F32),
            kept(gates, F32),
            kept(gates, F32),
            kept((seqs, heads, length), F32),
            kept((seqs, heads, length), F32),
            kept((seqs, heads, length, 2 * feat), BF),
            kept(states, BF),
            kept(states, BF),
        ),
        [pltpu.VMEM((width, 2 * width) if a is qkv_weight else a.shape, a.dtype) for a in sources]
        + [pltpu.SemaphoreType.DMA((len(sources),))],
        hbm=True,
    )
    partner_home, partner_away = core_swap(away), core_swap(home)
    total, got = exchange(order, home, partner_home, False)
    half_chip = after(half_chip, total)
    half_twin = lax.ppermute(half_chip, "dp", [(i, i ^ 1) for i in range(n_dp)])

    phi_q, scores, num = order.call(
        scores_kernel,
        "scores",
        (qkv_weight, random_features),
        (normed1, phi_k, values, c, c_row, a_row),
        (
            kept((seqs, heads, length, 2 * feat), BF),
            kept((seqs, heads, length, length), BF),
            kept((seqs, heads, length, LANES), F32),
        ),
        wait=(half_chip,),
    )
    got = after(got, num)
    swapped = core_swap(got)
    half_both = core_swap(half_chip)
    full, start, mixed_low, resid, normed2 = order.call(
        mix_kernel,
        "mix",
        (layer_input, got, swapped, partner_home, partner_away, out_weight, gain2, shift2),
        (phi_q, c, num),
        (
            kept((seqs, heads, length, LANES), F32),
            kept((seqs, *states), BF),
            kept(by_seq, BF),
            kept(by_seq, F32),
            kept(by_seq, BF),
        ),
    )

    normed2, mixed_low = (a.reshape(count, width) for a in (normed2, mixed_low))
    half_twin = after(half_twin, normed2)
    half_both_twin = core_swap(half_twin)
    shape = (count, width)
    grads = (width + hidden, width)
    out_part, dn2, out_low, keep0, send0 = order.call(
        feed_near_kernel,
        "feed_near",
        (output_grad.reshape(shape), inner_weight, outer_weight, inner_core, outer_core),
        (normed2, resid.reshape(shape)),
        (kept(shape, F32), kept(shape, F32), kept(shape, BF), shaped(grads, F32), shaped(grads, BF)),
    )
    got0 = core_swap(send0)
    far = pltpu.VMEM((2, width, hidden), BF)
    out_part, dn2, send1 = order.call(
        feed_far_kernel,
        "feed_both",
        (half_both, half_both_twin),
        (normed2, out_low, out_part, dn2),
        (kept(shape, F32), kept(shape, F32), shaped(grads, BF)),
        [far],
    )
    got1 = core_swap(send1)
    layer_out, dn2, keep1 = order.call(
        feed_last_kernel,
        "feed_chip",
        (half_chip, half_twin),
        (normed2, out_low, out_part, dn2),
        (pltpu.HBM(shape, F32), kept(shape, F32), shaped(grads, F32)),
        [far, pltpu.VMEM(shape, F32), pltpu.SemaphoreType.DMA],
    )
    stream = Stream(keep0, keep1, got0, got1)
    order.run(stream.next())

    dres, low, sums2, num_grads, r, away_grads, home_grads = order.call(
        turn_kernel,
        "turn",
        (output_grad, gain2, out_weight),
        (dn2.reshape(by_seq), resid, full, phi_q, c),
        (
            kept(by_seq, F32),
            kept((count, width), BF),
            kept((8, width), F32),
            kept((seqs, heads, length, 2 * LANES), BF),
            kept(gates, F32),
            kept(states, BF),
            kept(states, BF),
        ),
    )
    partner_home_grads, partner_away_grads = core_swap(away_grads), core_swap(home_grads)
    _, got_grads = exchange(order, home_grads, partner_home_grads, True)

    q_grad, k_part, v_part, k_col = order.call(
        back_kernel,
        "back",
        (random_features,),
        (phi_q, phi_k, values, num_grads, scores, c, c_row, a_row, start),
        (
            kept((count, width), BF),
            kept(by_seq, F32),
            kept(by_seq, F32),
            kept(gates, F32),
        ),
    )
    dn1_part, xhat1, scale1, keep1, *send1 = order.call(
        products_kernel,
        "products",
        (layer_input.reshape(shape), qkv_weight),
        (mixed_low, low, normed1, q_grad),
        (
            kept(shape, F32),
            kept(shape, F32),
            kept((count, LANES), F32),
            shaped((width // 2, 2 * width), F32),
            *[shaped((width // 8, 2 * width), BF)] * 4,
        ),
    )
    gather = Gather(keep1, core_swap(send1))
    got_grads = after(got_grads, keep1)
    swapped_grads = core_swap(got_grads)

    order.run(stream.next())
    order.run(gather.early())
    kv_grad, logit_low, bias_sum, keep2, *send2 = order.call(
        cross_kernel,
        "cross",
        (got_grads, swapped_grads, partner_home_grads, partner_away_grads, random_features),
        (away, home, start, phi_k, values, c, admit, r, k_col, k_part, v_part, normed1),
        (
            kept((count, 2 * width), BF),
            kept((count, LANES), BF),
            kept((8, LANES), F32),
            shaped((width // 2, 2 * width), F32),
            *[shaped((width // 8, 2 * width), BF)] * 4,
        ),
    )
    got2 = core_swap(send2)
    while len(stream.steps) > len(stream.bits) + 1:
        order.run(stream.next())
    dn1, small = order.call(
        close_kernel,
        "close",
        (qkv_weight, gate_rows),
        (dn1_part, xhat1, kv_grad, logit_low, bias_sum, normed1, sums2),
        (kept(shape, F32), shaped((width // 2, LANES), F32)),
    )
    order.run(gather.late(keep2, got2, small))
    dx, _ = order.call(
        input_kernel,
        "input",
        (gain1,),
        (dn1, xhat1, scale1, dres.reshape(shape)),
        (pltpu.HBM(shape, F32), shaped((8, LANES), F32)),
        [pltpu.VMEM(shape, F32), pltpu.SemaphoreType.DMA],
    )
    while len(gather.steps) > 5:
        order.run(gather.next())
    while len(stream.steps) > 3:
        order.run(stream.next())
    order.run(gather.next(), stream.next())
    order.run(gather.next(), stream.next())
    order.run(gather.next())
    order.run(gather.next(), stream.next())
    order.run(gather.next())
    inner_total, outer_total = stream.finish(order, (pltpu.HBM((width, hidden), F32), pltpu.HBM((hidden, width), F32)))
    links = gather.links[0]
    mine = gather.keep
    near = (*mine, *core_swap(mine))
    scratch = [
        pltpu.VMEM((width // 2, 3 * width), F32), pltpu.VMEM((width // 2, width), F32), pltpu.SemaphoreType.DMA((4, 2)),
    ]
    big = (pltpu.HBM((width, 3 * width), F32), pltpu.HBM((width, width), F32))
    *begun, _ = order.call(
        functools.partial(write_near_kernel, links=links),
        "write_near",
        near,
        (),
        (*big, shaped((8, LANES), F32)),
        scratch,
    )
    got = after(gather.got, order.last)
    far = (*got, *core_swap(got))
    qkv_grad, wo_grad, gate_grad, *norm_grads, bias_grad = order.call(
        functools.partial(write_far_kernel, links=links),
        "write_far",
        (*near, *far),
        (),
        (*big, pltpu.HBM((heads, width), F32), *[pltpu.HBM((1, width), F32)] * 4, pltpu.HBM((1, heads), F32)),
        [
            *scratch[:2], pltpu.VMEM((16, width), F32), pltpu.VMEM((1, heads), F32), pltpu.VMEM((width, LANES), F32),
            scratch[2], pltpu.SemaphoreType.DMA((6,)),
        ],
        onto=begun,
    )
    return (
        layer_out.reshape(by_seq),
        dx.reshape(by_seq),
        qkv_grad,
        jnp.transpose(gate_grad),
        bias_grad.reshape(heads),
        wo_grad,
        inner_total,
        outer_total,
        *(a.reshape(width) for a in norm_grads),
    )


def solution(mesh):
    in_specs = (
        P("dp", "mp", None),
        P(),
        P(),
        P(),
        P(),
        P(None, "mp"),
        P("mp", None),
        P(),
        P(),
        P(),
        P(),
        P(),
        P("dp", "mp", None),
    )
    out_specs = (
        P("dp", "mp", None),
        P("dp", "mp", None),
        P(),
        P(),
        P(),
        P(),
        P(None, "mp"),
        P("mp", None),
        P(),
        P(),
        P(),
        P(),
    )
    return jax.shard_map(
        per_device, mesh=mesh, in_specs=in_specs, out_specs=out_specs, check_vma=False
    )
```

```python
import functools
import math

import jax
import jax.numpy as jnp
from jax import lax
from jax.experimental import pallas as pl
from jax.experimental.pallas import tpu as pltpu
from jax.sharding import PartitionSpec as P

BF = jnp.bfloat16
F32 = jnp.float32
epsilon = 1e-05
guard = 0.01
LANES = 128
EXTRA = 16
VMEM_BYTES = 16 * 1024 * 1024


def nn(a, b):
    return lax.dot_general(a, b, (((1,), (0,)), ((), ())), preferred_element_type=F32)


def nt(a, b):
    return lax.dot_general(a, b, (((1,), (1,)), ((), ())), preferred_element_type=F32)


def tn(a, b):
    return lax.dot_general(a, b, (((0,), (0,)), ((), ())), preferred_element_type=F32)


def two_terms(v):
    high = v.astype(BF)
    return high, (v - high.astype(F32)).astype(BF)


def iota(shape, dim):
    return lax.broadcasted_iota(jnp.int32, shape, dim)


def triangle(length, upper):
    rows, cols = iota((length, length), 0), iota((length, length), 1)
    return jnp.where((cols >= rows) if upper else (rows >= cols), 1.0, 0.0).astype(BF)


def running_sum(v, upper):
    ones = triangle(v.shape[0], upper)
    high, rest = two_terms(v)
    low = (v - high.astype(F32) - rest.astype(F32)).astype(BF)
    return nn(ones, high) + nn(ones, rest) + nn(ones, low)


def norm_rows(v):
    centred = v - jnp.mean(v, axis=-1, keepdims=True)
    scale = lax.rsqrt(jnp.mean(centred * centred, axis=-1, keepdims=True) + epsilon)
    return centred * scale, scale


def norm_rows_backward(grad, xhat, scale, gain):
    g = grad * gain
    return scale * (
        g
        - jnp.mean(g, axis=-1, keepdims=True)
        - xhat * jnp.mean(g * xhat, axis=-1, keepdims=True)
    )


def pair_frequencies(freq_ref, pair):
    even, odd = freq_ref[2 * pair], freq_ref[2 * pair + 1]
    none = jnp.zeros_like(even)
    return jnp.concatenate(
        [jnp.concatenate([even, none], axis=1), jnp.concatenate([none, odd], axis=1)], axis=0
    )


def scaled_sine_cosine(angles, scale):
    turns = jnp.floor(angles * (1.0 / math.pi) + 0.5)
    r = angles - turns * 3.140625
    r = r - turns * 0.0009675025939941406
    r = r - turns * 1.509958e-07
    odd = turns - 2.0 * jnp.floor(turns * 0.5)
    sign = scale - (2.0 * scale) * odd
    r2 = r * r
    sine = -0.00018362251175623582 * r2 + 0.008306273552368303
    sine = sine * r2 - 0.1666482311215342
    sine = sine * r2 + 0.9999966031254778
    cosine = -0.0012711240835350962 * r2 + 0.041487518673719546
    cosine = cosine * r2 - 0.4999123281046797
    cosine = cosine * r2 + 0.9999933132015835
    return sine * (r * sign), cosine * sign


def pair_features(values, freq, scale):
    high, low = two_terms(values)
    freq_high, freq_low = two_terms(freq)
    both = jnp.concatenate([freq_high, freq_high], axis=0)
    angles = nn(jnp.concatenate([high, low], axis=1), both) + nn(high, freq_low)
    sine, cosine = scaled_sine_cosine(angles, scale)
    sine, cosine = sine.astype(BF), cosine.astype(BF)
    feat = freq.shape[1] // 2
    return [
        jnp.concatenate([sine[:, h * feat : (h + 1) * feat], cosine[:, h * feat : (h + 1) * feat]], axis=1)
        for h in (0, 1)
    ]


def own_lanes(shape, half):
    lane = iota(shape, len(shape) - 1)
    return (lane >= LANES // 2) if half else (lane < LANES // 2)


def one_lane(shape, half):
    return iota(shape, len(shape) - 1) == (0 if half else LANES // 2)


def second_lane(shape, half):
    return iota(shape, len(shape) - 1) == (1 if half else LANES // 2 + 1)


def with_ones(values, half, both=False):
    v = values.astype(F32)
    ones = one_lane(v.shape, half) | (both & second_lane(v.shape, half))
    return jnp.where(own_lanes(v.shape, half), v, jnp.where(ones, 1.0, 0.0))


def pack_states(even, odd, decay_even, decay_odd):
    half = LANES // 2
    row = iota(even.shape, 0)
    states = jnp.where(row < half, even, odd).astype(BF)
    extra = iota((EXTRA, even.shape[1]), 0)
    parts = []
    for value in (even[half : half + 1], odd[0:1], decay_even, decay_odd):
        high = value.astype(BF).astype(F32)
        parts += [high, value - high]
    rows = jnp.zeros((EXTRA, even.shape[1]), F32)
    for at, part in enumerate(parts):
        rows = jnp.where(extra == at, part, rows)
    return states, rows.astype(BF)


def extra_row(packed, at):
    at = LANES + 2 * at
    return packed[at : at + 1] + packed[at + 1 : at + 2]


def decays(packed):
    return extra_row(packed, 2), extra_row(packed, 3)


def unpack_states(packed):
    half = LANES // 2
    states = packed[:LANES]
    row = iota(states.shape, 0)
    even = jnp.where(row < half, states, jnp.where(row == half, extra_row(packed, 0), 0.0))
    odd = jnp.where(row >= half, states, jnp.where(row == 0, extra_row(packed, 1), 0.0))
    return even, odd


def join_states(first, second):
    return [
        a + decay * b
        for a, b, decay in zip(unpack_states(first), unpack_states(second), decays(first))
    ]


def as_operand(state, half):
    at = 0 if half else LANES // 2
    norm = state[at : at + 1]
    rest = norm - norm.astype(BF).astype(F32)
    return jnp.where(iota(state.shape, 0) == at + 1, rest, state).astype(BF)


def decay_weights(c_col, c_row, a_row):
    length = c_col.shape[0]
    gap = jnp.minimum(c_col - c_row, 0.0)
    causal = iota((length, length), 0) >= iota((length, length), 1)
    return jnp.where(causal, jnp.exp(gap) * a_row, 0.0)


def head_lanes(pair):
    shape = (2 * LANES, LANES)
    head = 2 * pair + (iota(shape, 0) % LANES) // (LANES // 2)
    return jnp.where(iota(shape, 1) == head, 1.0, 0.0).astype(BF)


def norm_lanes(pair):
    shape = (2 * LANES, LANES)
    row = iota(shape, 0) % LANES
    of_even, of_odd = row // 2 == LANES // 4, row // 2 == 0
    taken = (of_even & (iota(shape, 1) == 2 * pair)) | (of_odd & (iota(shape, 1) == 2 * pair + 1))
    return jnp.where(taken, 1.0, 0.0).astype(BF)


def lane_sum(v):
    return jnp.sum(v, axis=1, keepdims=True)


def each(count, step):
    lax.fori_loop(0, count, lambda i, none: (step(i), none)[1], 0)


def wide(v, axis):
    none = list(v.shape)
    none[axis] = LANES - v.shape[axis]
    return jnp.concatenate([v, jnp.zeros(none, v.dtype)], axis=axis)


def aligned(at, size):
    return pl.ds(pl.multiple_of(at * size, size), size)


def my_core():
    return lax.axis_index("mp") % 2


def my_chip():
    return lax.axis_index("mp") // 2


def pack_kernel(inner_ref, outer_ref, out_ref, sems):
    rows = out_ref.shape[1]
    mine = aligned(lax.axis_index("dp") % 2, rows)
    copies = [
        pltpu.make_async_copy(source.at[mine], out_ref.at[i], sems.at[i])
        for i, source in enumerate((inner_ref, outer_ref))
    ]
    for copy in copies:
        copy.start()
    for copy in copies:
        copy.wait()


def by_place(of_sequence):
    even = my_core() == 0
    one, two = of_sequence
    return jnp.where(even, two, one), jnp.where(even, one, two)


def put_states(pair, packed, away_ref, home_ref):
    for rows, parts in ((slice(0, LANES), [p[0] for p in packed]), (slice(LANES, None), [p[1] for p in packed])):
        away_ref[pair, rows], home_ref[pair, rows] = by_place(parts)


def keys_kernel(
    x_hbm, wqkv_hbm, gw_hbm, gb_hbm, gain_hbm, shift_hbm, freq_hbm,
    n1_ref, v_ref, c_ref, a_ref, crow_ref, arow_ref, pk_ref, away_ref, home_ref,
    x_ref, w_ref, gw_ref, gb_ref, gain_ref, shift_ref, freq_ref, sems,
):
    heads, _, feat = freq_ref.shape
    seqs, length, width = x_ref.shape
    sources = (x_hbm, gain_hbm, shift_hbm, gw_hbm, gb_hbm, wqkv_hbm.at[:, pl.ds(width, 2 * width)], freq_hbm)
    buffers = (x_ref, gain_ref, shift_ref, gw_ref, gb_ref, w_ref, freq_ref)
    copies = [
        pltpu.make_async_copy(source, buffer, sems.at[i])
        for i, (source, buffer) in enumerate(zip(sources, buffers))
    ]
    for copy in copies:
        copy.start()
    for copy in copies[:5]:
        copy.wait()
    scale = 1.0 / math.sqrt(feat)
    xhat, _ = norm_rows(x_ref[...].reshape(seqs * length, width))
    n1 = (xhat * gain_ref[...] + shift_ref[...]).astype(BF)
    n1_ref[...] = n1
    z = nt(n1, wide(gw_ref[...], 0)) + wide(gb_ref[...], 1)
    e = jnp.exp(-jnp.abs(z))
    log_keep = jnp.minimum(z, 0.0) - jnp.log1p(e)
    inverse = 1.0 / (1.0 + e)
    admit_all = jnp.where(z > 0.0, e * inverse, inverse)
    tails, decay = [], []
    for s in range(seqs):
        rows = slice(s * length, (s + 1) * length)
        c = running_sum(log_keep[rows], False)
        admit = admit_all[rows]
        c_ref[s] = c
        a_ref[s] = admit
        crow_ref[s] = jnp.transpose(c)[:heads]
        arow_ref[s] = jnp.transpose(admit)[:heads]
        last = c[length - 1 :]
        tails.append(jnp.exp(last - c) * admit)
        decay.append(jnp.exp(last))
    for copy in copies[5:]:
        copy.wait()
    keys = nn(n1, w_ref[:, :width])
    values = nn(n1, w_ref[:, width:])
    v_ref[...] = values.reshape(v_ref.shape)
    for pair in range(heads // 2):
        lanes = slice(pair * LANES, (pair + 1) * LANES)
        phi = pair_features(keys[:, lanes], pair_frequencies(freq_ref, pair), scale)
        packed = []
        for s in range(seqs):
            rows = slice(s * length, (s + 1) * length)
            states = []
            for half in (0, 1):
                h = 2 * pair + half
                phi_k = phi[half][rows]
                pk_ref[s, h] = phi_k
                weighted = with_ones(values[rows, lanes], half) * tails[s][:, h : h + 1]
                both = tn(jnp.concatenate(two_terms(weighted), axis=1), phi_k)
                states.append(both[:LANES] + both[LANES:])
            h = 2 * pair
            packed.append(pack_states(*states, decay[s][:, h : h + 1], decay[s][:, h + 1 : h + 2]))
        put_states(pair, packed, away_ref, home_ref)


def scores_kernel(wqkv_ref, freq_ref, n1_ref, pk_ref, v_ref, c_ref, crow_ref, arow_ref, pq_ref, p_ref, num_ref):
    seqs, heads, length, _ = pk_ref.shape
    scale = 1.0 / math.sqrt(freq_ref.shape[2])
    queries = nn(n1_ref[...], wqkv_ref[:, : n1_ref.shape[1]])
    for pair in range(heads // 2):
        lanes = slice(pair * LANES, (pair + 1) * LANES)
        phi = pair_features(queries[:, lanes], pair_frequencies(freq_ref, pair), scale)
        for s in range(seqs):
            for half in (0, 1):
                h = 2 * pair + half
                phi_q = phi[half][s * length : (s + 1) * length]
                pq_ref[s, h] = phi_q
                v = with_ones(v_ref[s, :, lanes], half)
                weights = decay_weights(
                    c_ref[s, :, h : h + 1], crow_ref[s, h : h + 1], arow_ref[s, h : h + 1]
                )
                p = (nt(phi_q, pk_ref[s, h]) * weights).astype(BF)
                p_ref[s, h] = p
                both = nn(p, jnp.concatenate(two_terms(v), axis=1))
                num_ref[s, h] = both[:, :LANES] + both[:, LANES:]


def mix_kernel(
    x_ref, got_ref, swapped_ref, partner_home_ref, partner_away_ref, wo_ref, gain_ref, shift_ref, pq_ref, c_ref, num_ref,
    full_ref, start_ref, mixed_ref, resid_ref, n2_ref, sden_ref, inverse_ref, xhat_ref, scale_ref,
):
    seqs, heads = pq_ref.shape[:2]
    core = my_core()

    def one(s):
        growth = jnp.exp(c_ref[s])
        sdens = jnp.zeros_like(growth)
        for pair in range(heads // 2):
            before = jnp.where(s == core, got_ref[pair], swapped_ref[pair]).astype(F32)
            partner = jnp.where(s == core, partner_home_ref[pair], partner_away_ref[pair]).astype(F32)
            states = [
                jnp.where(core == 0, a, b)
                for a, b in zip(unpack_states(before), join_states(partner, before))
            ]
            none = jnp.zeros((1, 1), F32)
            main, rest = pack_states(*states, none, none)
            start_ref[s, pair, :LANES] = main
            start_ref[s, pair, LANES:] = rest
            fulls = []
            for half in (0, 1):
                h = 2 * pair + half
                full = num_ref[s, h] + growth[:, h : h + 1] * nt(
                    pq_ref[s, h], as_operand(states[half], half)
                )
                full_ref[s, h] = full
                fulls.append(full)
            beside = jnp.where(own_lanes(fulls[0].shape, 0), fulls[1], fulls[0])
            sdens = sdens + nn(jnp.concatenate(two_terms(beside), axis=1), norm_lanes(pair))
        inverse = lax.rsqrt(sdens * sdens + guard)
        sden_ref[s] = sdens
        inverse_ref[s] = inverse
        for pair in range(heads // 2):
            mixed = [full_ref[s, h] * inverse[:, h : h + 1] for h in (2 * pair, 2 * pair + 1)]
            pair_mixed = jnp.where(own_lanes(mixed[0].shape, 0), mixed[0], mixed[1])
            mixed_ref[s, :, pair * LANES : (pair + 1) * LANES] = pair_mixed.astype(BF)
        resid = x_ref[s] + nn(mixed_ref[s], wo_ref[...])
        resid_ref[s] = resid
        xhat, scale = norm_rows(resid)
        xhat_ref[s] = xhat
        scale_ref[s] = jnp.broadcast_to(scale, scale_ref.shape[1:])
        n2_ref[s] = (xhat * gain_ref[...] + shift_ref[...]).astype(BF)

    for s in range(seqs):
        one(s)


def gelu_and_slope(v):
    root = math.sqrt(2.0 / math.pi)
    v2 = v * v
    t = jnp.tanh(v * (root + (root * 0.044715) * v2))
    half = 0.5 * (1.0 + t)
    slope = half + (0.5 * v) * (1.0 - t * t) * (root + (root * 3.0 * 0.044715) * v2)
    return v * half, slope


def feed_block(n2, out_low, wi_ref, wo_ref):
    active, slope = gelu_and_slope(nn(n2, wi_ref[...]))
    active = active.astype(BF)
    pre_grad = (nt(out_low, wo_ref[...]) * slope).astype(BF)
    return nn(active, wo_ref[...]), nt(pre_grad, wi_ref[...]), tn(n2, pre_grad), tn(active, out_low)


def halves_together(far_ref, one, two):
    twin = lax.axis_index("dp") % 2
    rows = one.shape[1]
    for which in range(2):
        far_ref[which, aligned(twin, rows)] = one[which]
        far_ref[which, aligned(1 - twin, rows)] = two[which]


def feed_near_kernel(og_ref, wi0, wo0, wi2, wo2, n2_ref, resid_ref, out_ref, dn2_ref, low_ref, keep_ref, send_ref):
    low_ref[...] = og_ref[...].astype(BF)
    n2, out_low = n2_ref[...], low_ref[...]
    rows = n2.shape[1]
    out, dn2, inner, outer = feed_block(n2, out_low, wi2, wo2)
    send_ref[:rows] = inner.astype(BF)
    send_ref[rows:] = outer.astype(BF)
    out_own, dn2_own, inner, outer = feed_block(n2, out_low, wi0, wo0)
    keep_ref[:rows] = inner
    keep_ref[rows:] = outer
    out_ref[...] = resid_ref[...] + out + out_own
    dn2_ref[...] = dn2 + dn2_own


def feed_far_kernel(half_ref, twin_ref, n2_ref, low_ref, part_ref, dn2_part_ref, out_ref, dn2_ref, grad_ref, far_ref):
    twin = lax.axis_index("dp") % 2
    rows = half_ref.shape[1]
    for which in range(2):
        far_ref[which, aligned(twin, rows)] = half_ref[which]
        far_ref[which, aligned(1 - twin, rows)] = twin_ref[which]
    n2 = n2_ref[...]
    out, dn2, inner, outer = feed_block(n2, low_ref[...], far_ref.at[0], far_ref.at[1])
    out_ref[...] = part_ref[...] + out
    dn2_ref[...] = dn2_part_ref[...] + dn2
    rows = n2.shape[1]
    grad_ref[:rows] = inner.astype(grad_ref.dtype)
    grad_ref[rows:] = outer.astype(grad_ref.dtype)


def feed_last_kernel(
    half_ref, twin_ref, n2_ref, low_ref, part_ref, dn2_part_ref, out_hbm, dn2_ref, grad_ref, far_ref, out_ref, sem
):
    feed_far_kernel(half_ref, twin_ref, n2_ref, low_ref, part_ref, dn2_part_ref, out_ref, dn2_ref, grad_ref, far_ref)
    copy = pltpu.make_async_copy(out_ref, out_hbm, sem)
    copy.start()
    copy.wait()


def place_bit(bits):
    place = lax.axis_index("dp")
    return jnp.where(my_core() == 0, (place // (1 << bits[0])) % 2, (place // (1 << bits[1])) % 2)


def split_rows(total, bits, mine_ref, send_ref):
    rows = mine_ref.shape[1]
    high = place_bit(bits) == 1
    first, second = total[:, :rows], total[:, rows:]
    mine_ref[...] = jnp.where(high, second, first)
    send_ref[...] = jnp.where(high, first, second).astype(BF)


def halve_kernel(keep_ref, got_ref, mine_ref, send_ref, *, bits):
    split_rows(keep_ref[...] + got_ref[...].astype(F32), bits, mine_ref, send_ref)


def first_kernel(keep0_ref, keep1_ref, got0_ref, got1_ref, mine_ref, send_ref, *, bits):
    for block, (keep_ref, got_ref) in enumerate(((keep0_ref, got0_ref), (keep1_ref, got1_ref))):
        total = (keep_ref[...] + got_ref[...].astype(F32))[None]
        split_rows(total, bits, mine_ref.at[block : block + 1], send_ref.at[block : block + 1])


def third_kernel(keep_ref, got_ref, mine_ref, send_ref, *, bit):
    rows = mine_ref.shape[1]
    total = keep_ref[...] + got_ref[...].astype(F32)
    low, high = total[:, :rows], total[:, rows:]
    by_bit = place_bit((bit, bit)) == 1
    one, two = jnp.where(by_bit, high, low), jnp.where(by_bit, low, high)
    even = my_core() == 0
    for part in range(2):
        of_block = (low, high)[part]
        mine_ref[part] = jnp.where(even, one[part], of_block[0])
        send_ref[part] = jnp.where(even, two[part], of_block[1]).astype(BF)


def fourth_kernel(keep_ref, got_ref, mine_ref, send_ref, *, bit):
    total = keep_ref[...] + got_ref[...].astype(F32)
    second = (my_core() == 1) & (place_bit((bit, bit)) == 1)
    mine_ref[...] = jnp.where(second, total[1], total[0])
    send_ref[...] = jnp.where(second, total[0], total[1]).astype(BF)


def add_kernel(keep_ref, got_ref, out_ref):
    out_ref[...] = (keep_ref[...] + got_ref[...].astype(F32)).astype(out_ref.dtype)


def joined(mine_ref, got_ref, bits):
    high = place_bit(bits) == 1
    mine, got = mine_ref[...].astype(F32), got_ref[...].astype(F32)
    return jnp.concatenate([jnp.where(high, got, mine), jnp.where(high, mine, got)], axis=0)


def join_kernel(mine_ref, got_ref, out_ref, *, bits):
    out_ref[...] = joined(mine_ref, got_ref, bits).astype(BF)


def final_kernel(mine_ref, got_ref, inner_hbm, outer_hbm, mark_ref, whole_ref, sems, *, bits):
    mark_ref[...] = jnp.zeros_like(mark_ref)
    both = joined(mine_ref, got_ref, bits)
    quarter = both.shape[0] // 4
    one, two = both[quarter : 2 * quarter], both[2 * quarter : 3 * quarter]
    even = my_core() == 0
    whole_ref[:quarter] = both[:quarter]
    whole_ref[quarter : 2 * quarter] = jnp.where(even, two, one)
    whole_ref[2 * quarter : 3 * quarter] = jnp.where(even, one, two)
    whole_ref[3 * quarter :] = both[3 * quarter :]
    rows = inner_hbm.shape[0]
    copies = [
        pltpu.make_async_copy(whole_ref.at[pl.ds(at * rows, rows)], out_hbm, sems.at[at])
        for at, out_hbm in enumerate((inner_hbm, outer_hbm))
    ]
    for copy in copies:
        copy.start()
    for copy in copies:
        copy.wait()


def turn_kernel(
    og_ref, gain_ref, wo_ref, dn2_ref, xhat_ref, scale_ref, full_ref, sden_ref, inverse_ref, pq_ref, c_ref,
    dres_ref, low_ref, sums_ref, ng_ref, r_ref, away_ref, home_ref,
):
    seqs, heads, length, _ = pq_ref.shape
    sums_ref[...] = jnp.zeros_like(sums_ref)
    packed = [[] for _ in range(seqs)]

    def one(s):
        xhat = xhat_ref[s]
        dn2 = dn2_ref[s]
        dres = og_ref[s] + norm_rows_backward(dn2, xhat, scale_ref[s, :, :1], gain_ref[...])
        dres_ref[s] = dres
        low = dres.astype(BF)
        low_ref[s * length : (s + 1) * length] = low
        sums_ref[2:3] += jnp.sum(dn2 * xhat, axis=0, keepdims=True)
        sums_ref[3:4] += jnp.sum(dn2, axis=0, keepdims=True)
        dmixed = nt(low, wo_ref[...])
        c = c_ref[s]
        growth = jnp.exp(c)
        decay = jnp.exp(c[length - 1 :])
        lane = iota(c.shape, 1)
        sden, inverse = sden_ref[s], inverse_ref[s]
        dots = jnp.zeros_like(c)
        for pair in range(heads // 2):
            g = dmixed[:, pair * LANES : (pair + 1) * LANES]
            h = 2 * pair
            values = jnp.where(own_lanes(g.shape, 0), full_ref[s, h], full_ref[s, h + 1])
            dots = dots + nn(jnp.concatenate(two_terms(g * values), axis=1), head_lanes(pair))
        dots = dots * inverse
        inverse2 = inverse * inverse
        r_ref[s] = dots * inverse2 * guard
        sden_grads = -dots * sden * inverse2
        growing = sden_grads * growth
        lifting = inverse * growth
        for pair in range(heads // 2):
            g = dmixed[:, pair * LANES : (pair + 1) * LANES]
            states = []
            for half in (0, 1):
                h = 2 * pair + half
                mine, one_at = own_lanes(g.shape, half), one_lane(g.shape, half)
                column = slice(h, h + 1)
                grads = jnp.where(mine, g * inverse[:, column], jnp.where(one_at, sden_grads[:, column], 0.0))
                ng_ref[s, h] = jnp.concatenate(two_terms(grads), axis=1)
                lifted = jnp.where(mine, g * lifting[:, column], jnp.where(one_at, growing[:, column], 0.0))
                both = tn(jnp.concatenate(two_terms(lifted), axis=1), pq_ref[s, h])
                states.append(both[:LANES] + both[LANES:])
            h = 2 * pair
            packed[s].append(pack_states(*states, decay[:, h : h + 1], decay[:, h + 1 : h + 2]))

    for s in range(seqs):
        one(s)
    for pair, both in enumerate(zip(*packed)):
        put_states(pair, both, away_ref, home_ref)


def angle_grads(phi, dphi):
    feat = phi.shape[1] // 2
    phi = phi.astype(F32)
    return phi[:, feat:] * dphi[:, :feat] - phi[:, :feat] * dphi[:, feat:]


def weight_grads(left_ref, right_ref, keep_ref, send_refs):
    rows = keep_ref.shape[0]
    core = my_core()
    keep_ref[...] = tn(left_ref[:, aligned(core, rows)], right_ref[...])
    away = tn(left_ref[:, aligned(1 - core, rows)], right_ref[...]).astype(BF)
    rows //= len(send_refs)
    for part, send_ref in enumerate(send_refs):
        send_ref[...] = away[part * rows : (part + 1) * rows]


def back_kernel(
    freq_ref, pq_ref, pk_ref, v_ref, ng_ref, p_ref, c_ref, crow_ref, arow_ref, start_ref,
    qg_ref, kg_ref, vg_ref, kcol_ref,
):
    seqs, heads, length, _ = pq_ref.shape

    def one(s):
        tokens = aligned(s, length)
        c = c_ref[s]
        growth = jnp.exp(c)
        lane = iota(c.shape, 1)
        kcol = jnp.zeros_like(c)
        for pair in range(heads // 2):
            at = pair * LANES
            freq = pair_frequencies(freq_ref, pair).astype(BF)
            states = unpack_states(start_ref[s, pair].astype(F32))
            q_angles, k_angles, v_grads = [], [], []
            for half in (0, 1):
                h = 2 * pair + half
                phi_q, phi_k = pq_ref[s, h], pk_ref[s, h]
                grads = ng_ref[s, h, :, :LANES]
                v = with_ones(v_ref[s, :, at : at + LANES], half)
                weights = decay_weights(c[:, h : h + 1], crow_ref[s, h : h + 1], arow_ref[s, h : h + 1])
                dk = (nt(grads, v.astype(BF)) * weights).astype(BF)
                lifted = (grads.astype(F32) * growth[:, h : h + 1]).astype(BF)
                dphi_q = nn(dk, phi_k) + nn(lifted, states[half].astype(BF))
                q_angles.append(angle_grads(phi_q, dphi_q))
                k_angles.append(angle_grads(phi_k, tn(dk, phi_q)))
                both = tn(p_ref[s, h], ng_ref[s, h])
                dv = both[:, :LANES] + both[:, LANES:]
                v_grads.append(dv)
                kcol = jnp.where(lane == h, lane_sum(v * dv), kcol)
            qg_ref[tokens, at : at + LANES] = nt(
                jnp.concatenate(q_angles, axis=1).astype(BF), freq
            ).astype(BF)
            kg_ref[s, :, at : at + LANES] = nt(jnp.concatenate(k_angles, axis=1).astype(BF), freq)
            vg_ref[s, :, at : at + LANES] = jnp.where(
                own_lanes(v_grads[0].shape, 0), v_grads[0], v_grads[1]
            )
        kcol_ref[s] = kcol

    each(seqs, one)


def products_kernel(
    x_ref, wqkv_ref, mixed_ref, low_ref, n1_ref, qg_ref, part_ref, xhat_ref, scale_ref, keep_ref, *send_refs
):
    width = low_ref.shape[1]
    part_ref[...] = nt(qg_ref[...], wqkv_ref[:, :width])
    xhat, scale = norm_rows(x_ref[...])
    xhat_ref[...] = xhat
    scale_ref[...] = jnp.broadcast_to(scale, scale_ref.shape)
    for at, left_ref, right_ref in ((0, mixed_ref, low_ref), (width, n1_ref, qg_ref)):
        lanes = pl.ds(at, width)
        weight_grads(left_ref, right_ref, keep_ref.at[:, lanes], [ref.at[:, lanes] for ref in send_refs])


def cross_kernel(
    got_ref, swapped_ref, partner_home_ref, partner_away_ref, freq_ref, away_ref, home_ref, start_ref, pk_ref, v_ref,
    c_ref, a_ref, r_ref, kcol_ref,
    kg_ref, vg_ref, n1_ref,
    kv_ref, logit_ref, bias_ref, keep_ref, *send_refs,
):
    seqs, heads, length, _ = pk_ref.shape
    core = my_core()
    width = kg_ref.shape[2]
    bias_ref[...] = jnp.zeros_like(bias_ref)

    def one(s):
        tokens = aligned(s, length)
        c, a = c_ref[s], a_ref[s]
        tail = jnp.exp(c[length - 1 :] - c) * a
        lane = iota(c.shape, 1)
        lane_row = iota((1, c.shape[1]), 1)
        kcol = kcol_ref[s]
        ends = jnp.zeros((1, c.shape[1]), F32)
        for pair in range(heads // 2):
            at = pair * LANES
            freq = pair_frequencies(freq_ref, pair).astype(BF)
            after = jnp.where(s == core, got_ref[pair], swapped_ref[pair]).astype(F32)
            partner = jnp.where(s == core, partner_home_ref[pair], partner_away_ref[pair]).astype(F32)
            grads = [
                jnp.where(core == 1, a, b)
                for a, b in zip(unpack_states(after), join_states(partner, after))
            ]
            local = jnp.where(s == core, home_ref[pair], away_ref[pair]).astype(F32)
            reached = join_states(local, start_ref[s, pair].astype(F32))
            k_angles, v_grads = [], []
            for half in (0, 1):
                h = 2 * pair + half
                phi_k = pk_ref[s, h]
                v = with_ones(v_ref[s, :, at : at + LANES], half, True)
                grad_low = as_operand(grads[half], half)
                weight = tail[:, h : h + 1]
                k_angles.append(angle_grads(phi_k, nn(v.astype(BF), grad_low)) * weight)
                dv = nt(phi_k, grad_low) * weight
                v_grads.append(dv)
                kcol = kcol + jnp.where(lane == h, lane_sum(v * dv), 0.0)
                end = jnp.sum(lane_sum(grads[half] * reached[half]), axis=0, keepdims=True)
                ends = jnp.where(lane_row == h, end, ends)
            kg = kg_ref[s, :, at : at + LANES] + nt(
                jnp.concatenate(k_angles, axis=1).astype(BF), freq
            )
            vg = vg_ref[s, :, at : at + LANES] + jnp.where(
                own_lanes(v_grads[0].shape, 0), v_grads[0], v_grads[1]
            )
            kv_ref[tokens, at : at + LANES] = kg.astype(BF)
            kv_ref[tokens, width + at : width + at + LANES] = vg.astype(BF)
        keep_grad = running_sum(r_ref[s] - kcol, True) + ends
        logit_grad = a * keep_grad - (1.0 - a) * kcol
        logit_ref[tokens] = logit_grad.astype(BF)
        bias_ref[0:1] += jnp.sum(logit_grad, axis=0, keepdims=True)

    for i in range(seqs):
        one(i)
    weight_grads(n1_ref, kv_ref, keep_ref, send_refs)


def close_kernel(
    wqkv_ref, gw_ref, part_ref, xhat_ref, kv_ref, logit_ref, bias_ref, n1_ref, sums2_ref, dn1_ref, small_ref
):
    width = part_ref.shape[1]
    logit_low = logit_ref[...]
    dn1 = part_ref[...] + nt(kv_ref[...], wqkv_ref[:, width:]) + nn(logit_low, wide(gw_ref[...], 0))
    xhat = xhat_ref[...]
    dn1_ref[...] = dn1
    row = iota((8, width), 0)
    sums = jnp.where(row == 0, jnp.sum(dn1 * xhat, axis=0, keepdims=True), sums2_ref[...])
    sums = jnp.where(row == 1, jnp.sum(dn1, axis=0, keepdims=True), sums)
    bias = jnp.concatenate([bias_ref[0:1], jnp.zeros((1, width - LANES), F32)], axis=1)
    sums = jnp.where(row == 4, bias, sums)
    gates = tn(logit_low, n1_ref[...])[:8]
    stacked = jnp.concatenate([sums, gates, jnp.zeros((LANES - 16, width), F32)], axis=0)
    columns = jnp.transpose(stacked)
    rows = small_ref.shape[0]
    small_ref[...] = columns[:rows] + pltpu.roll(columns[rows:], 16, 1)


def input_kernel(gain_ref, dn1_ref, xhat_ref, scale_ref, dres_ref, dx_hbm, mark_ref, dx_ref, sem):
    mark_ref[...] = jnp.zeros_like(mark_ref)
    dx_ref[...] = dres_ref[...] + norm_rows_backward(dn1_ref[...], xhat_ref[...], scale_ref[:, :1], gain_ref[...])
    copy = pltpu.make_async_copy(dx_ref, dx_hbm, sem)
    copy.start()
    copy.wait()


def chain_kernel(me_ref, partner_ref, out_ref, *, reverse):
    core = my_core()
    lead = (core == 0) if reverse else (core == 1)
    for pair in range(out_ref.shape[0]):
        mine, other = me_ref[pair].astype(F32), partner_ref[pair].astype(F32)
        first = jnp.where(lead, mine, other)
        second = jnp.where(lead, other, mine)
        none = jnp.zeros((1, 1), F32)
        main, rest = pack_states(*join_states(first, second), none, none)
        out_ref[pair, :LANES] = main
        out_ref[pair, LANES:] = rest


def widen(v):
    main, last = v[:, :-LANES].astype(F32), v[:, -LANES:].astype(F32)
    last = jnp.where(iota(last.shape, 1) < LANES // 2, last + pltpu.roll(last, LANES // 2, 1), 0.0)
    return jnp.concatenate([main, last], axis=1)


def narrow(v):
    main, last = v[:, :-LANES].astype(BF), v[:, -LANES:]
    high, low = two_terms(last)
    last = high.astype(F32) + pltpu.roll(low.astype(F32), LANES // 2, 1)
    return jnp.concatenate([main, last.astype(BF)], axis=1)


def link_bit(link):
    return my_chip() if link is None else (lax.axis_index("dp") // (1 << link)) % 2


def piece_number(links):
    number = 0
    for of_zero, of_one in links:
        bit = link_bit(of_zero)
        if of_one != of_zero:
            bit = jnp.where(my_core() == 0, bit, link_bit(of_one))
        number = 2 * number + bit
    return number


def pick(pieces, number):
    taken = pieces[0]
    for at in range(1, len(pieces)):
        taken = jnp.where(number == at, pieces[at], taken)
    return taken


def share_out(total, links, mine_ref, send_refs):
    rows = mine_ref.shape[0]
    pieces = [total[at : at + rows] for at in range(0, total.shape[0], rows)]
    number = piece_number(links)
    mine_ref[...] = pick(pieces, number)
    for k, send_ref in enumerate(send_refs):
        send_ref[...] = narrow(pick(pieces, number ^ (k + 1)))


def early_kernel(keep_ref, *refs, links):
    *got_refs, mine_ref, send_ref = refs
    rows = mine_ref.shape[0]
    total = keep_ref[...] + jnp.concatenate([ref[...].astype(F32) for ref in got_refs], axis=0)
    number = piece_number(links)
    pieces = [total[:rows], total[rows:]]
    mine_ref[...] = pick(pieces, number)
    send_ref[...] = pick(pieces, number ^ 1).astype(BF)


def late_kernel(early_ref, early_got_ref, keep_ref, *refs, links):
    *got_refs, small_ref, mine_ref, send_ref = refs
    before = early_ref.shape[1]
    mine_ref[:, :before] = early_ref[...] + early_got_ref[...].astype(F32)
    total = keep_ref[...] + jnp.concatenate([ref[...].astype(F32) for ref in got_refs], axis=0)
    total = jnp.concatenate([total, small_ref[...]], axis=1)
    share_out(total, links, mine_ref.at[:, pl.ds(before, total.shape[1])], [send_ref])


def meet_kernel(keep_ref, got_ref, mine_ref, send_ref, *, links):
    before = keep_ref.shape[1] - got_ref.shape[1]
    second = keep_ref[:, before:] + widen(got_ref[...])
    share_out(jnp.concatenate([keep_ref[:, :before], second], axis=1), links, mine_ref, [send_ref])


def part_kernel(keep_ref, got_ref, mine_ref, send_ref, *, links):
    share_out(keep_ref[...] + widen(got_ref[...]), links, mine_ref, [send_ref])


def whole_kernel(keep_ref, got_ref, out_ref):
    out_ref[...] = narrow(keep_ref[...] + widen(got_ref[...]))


def sum_kernel(mine_ref, got_ref, out_ref):
    out_ref[...] = narrow(widen(mine_ref[...]) + widen(got_ref[...]))


def split_group_kernel(mine_ref, got_ref, first_ref, second_ref, *, links):
    mine, got = mine_ref[...], got_ref[...]
    high = piece_number(links) == 1
    first_ref[...] = jnp.where(high, got, mine)
    second_ref[...] = jnp.where(high, mine, got)


def group_kernel(*refs, links):
    pieces = [ref[...].astype(F32) for ref in refs[:-1]]
    number = piece_number(links)
    both = [pick(pieces, number ^ at) for at in range(len(pieces))]
    refs[-1][...] = jnp.concatenate(both, axis=0).astype(BF)


def piece_place(of_partner, far, links):
    core = my_core()
    core = 1 - core if of_partner else core
    high = jnp.where(core == 0, link_bit(links[0]), link_bit(links[1]))
    return 2 * core + (1 - high if far else high)


def write_pieces(pieces, places, qkv_hbm, wo_hbm, qkv_ref, wo_ref, sems):
    rows, width = pieces[0].shape[0], wo_hbm.shape[1]
    copies = []
    for at, (piece_ref, place) in enumerate(zip(pieces, places)):
        own = slice(at * rows, (at + 1) * rows)
        wo_ref[own] = piece_ref[:, :width].astype(F32)
        qkv_ref[own] = piece_ref[:, width:-LANES].astype(F32)
        for which, (ref, hbm) in enumerate(((wo_ref, wo_hbm), (qkv_ref, qkv_hbm))):
            there = hbm.at[aligned(place, rows)]
            copies.append(pltpu.make_async_copy(ref.at[pl.ds(at * rows, rows)], there, sems.at[at, which]))
            copies[-1].start()
    return copies


def write_near_kernel(mine1_ref, mine2_ref, other1_ref, other2_ref, qkv_hbm, wo_hbm, mark_ref, qkv_ref, wo_ref, sems, *, links):
    mark_ref[...] = jnp.zeros_like(mark_ref)
    mine, other = 2 * piece_place(False, False, links), 2 * piece_place(True, False, links)
    pieces, places = (mine1_ref, mine2_ref, other1_ref, other2_ref), (mine, mine + 1, other, other + 1)
    for copy in write_pieces(pieces, places, qkv_hbm, wo_hbm, qkv_ref, wo_ref, sems):
        copy.wait()


def write_far_kernel(*refs, links):
    near, far, outs = refs[:4], refs[4:8], refs[10:]
    qkv_hbm, wo_hbm, gate_hbm, *norm_hbm, bias_hbm, qkv_ref, wo_ref, small_ref, bias_ref, columns_ref, sems, small_sems = outs
    rows = far[0].shape[0]
    for pieces, is_far in ((near, False), (far, True)):
        for at in range(4):
            place = 2 * piece_place(at > 1, is_far, links) + at % 2
            columns_ref[aligned(place, rows)] = pieces[at][:, -LANES:].astype(F32)
    half = columns_ref.shape[0] // 2
    columns = columns_ref[:half] + columns_ref[half:]
    columns = columns + pltpu.roll(columns, LANES // 2, 1)
    stacked = jnp.transpose(columns)
    small_ref[:, :half] = stacked[:16]
    small_ref[:, half:] = stacked[16:32]
    heads = gate_hbm.shape[0]
    bias_ref[...] = stacked[4:5, : bias_ref.shape[1]]
    there = [(8, heads, gate_hbm)] + [(row, 1, hbm) for row, hbm in enumerate(norm_hbm)]
    copies = []
    for at, (row, count, hbm) in enumerate(there):
        copies.append(pltpu.make_async_copy(small_ref.at[pl.ds(row, count)], hbm, small_sems.at[at]))
    copies.append(pltpu.make_async_copy(bias_ref, bias_hbm, small_sems.at[len(there)]))
    for copy in copies:
        copy.start()
    mine, other = 2 * piece_place(False, True, links), 2 * piece_place(True, True, links)
    copies += write_pieces(far, (mine, mine + 1, other, other + 1), qkv_hbm, wo_hbm, qkv_ref, wo_ref, sems)
    for copy in copies:
        copy.wait()


def in_hbm(out):
    return getattr(out, "memory_space", None) == pltpu.HBM


def out_spec(out):
    return pl.BlockSpec(memory_space=pltpu.HBM if in_hbm(out) else pltpu.VMEM)


class Job:
    def __init__(self, kernel, name, operands, outs, use):
        self.kernel, self.name, self.operands, self.outs, self.use = kernel, name, operands, outs, use


class Order:
    def __init__(self):
        self.last = ()

    def call(self, kernel, name, given, kept, outs, scratch=(), wait=(), hbm=False, onto=()):
        wait = (*self.last, *wait)
        space = pltpu.HBM if hbm else pltpu.VMEM
        given = [pltpu.with_memory_space_constraint(a, space) if hbm else a for a in given]
        kept = [pltpu.with_memory_space_constraint(a, pltpu.VMEM) for a in kept]
        got = pl.pallas_call(
            lambda *refs: kernel(*refs[len(wait) :]),
            out_shape=outs,
            in_specs=[pl.BlockSpec(memory_space=pl.ANY)] * len(wait)
            + [pl.BlockSpec(memory_space=space)] * len(given)
            + [pl.BlockSpec(memory_space=pltpu.VMEM)] * len(kept)
            + [pl.BlockSpec(memory_space=pltpu.HBM)] * len(onto),
            input_output_aliases={len(wait) + len(given) + len(kept) + at: at for at in range(len(onto))},
            out_specs=jax.tree.map(out_spec, outs),
            scratch_shapes=scratch,
            compiler_params=pltpu.CompilerParams(vmem_limit_bytes=VMEM_BYTES),
            cost_estimate=pl.CostEstimate(flops=0, bytes_accessed=0, transcendentals=0),
            name=name,
        )(*wait, *given, *kept, *onto)
        inside = [a for a, out in zip(jax.tree.leaves(got), jax.tree.leaves(outs)) if not in_hbm(out)]
        if inside:
            self.last = (min(inside, key=lambda a: a.size),)
        return got


    def run(self, *jobs):
        takes = [len(job.operands) for job in jobs]
        gives = [len(job.outs) for job in jobs]

        def kernel(*refs):
            given, made = refs[: sum(takes)], refs[sum(takes) :]
            for job, take, give in zip(jobs, takes, gives):
                job.kernel(*given[:take], *made[:give])
                given, made = given[take:], made[give:]

        operands = [a for job in jobs for a in job.operands]
        outs = tuple(out for job in jobs for out in job.outs)
        got = list(self.call(kernel, "_".join(job.name for job in jobs), operands, (), outs))
        for job, give in zip(jobs, gives):
            job.use(*got[:give])
            got = got[give:]


def kept(shape, dtype):
    return pltpu.VMEM(shape, dtype)


def shaped(shape, dtype):
    return jax.ShapeDtypeStruct(shape, dtype)


def core_swap(v):
    return jax.tree.map(lambda a: lax.ppermute(a, "mp", [(i, i ^ 1) for i in range(4)]), v)


def chip_swap(v):
    return jax.tree.map(lambda a: lax.ppermute(a, "mp", [(i, i ^ 2) for i in range(4)]), v)


def send_along(v, links):
    way = []
    for place in range(lax.axis_size("dp")):
        for spot in range(4):
            to = [place, spot]
            for link in links:
                link = link[spot % 2]
                to = [to[0], to[1] ^ 2] if link is None else [to[0] ^ (1 << link), to[1]]
            way.append((4 * place + spot, 4 * to[0] + to[1]))
    return lax.ppermute(v, ("dp", "mp"), way)


class Gather:
    def __init__(self, keep, got):
        self.first = (keep, *got)
        bits = list(range(lax.axis_size("dp").bit_length() - 1))
        self.links = [(None, 0), (0, None)] + [(bit, bit) for bit in bits[1:]]
        last = len(self.links) - 1
        self.steps = [functools.partial(self.share, at) for at in range(1, last)] + [self.swap]
        self.steps += [functools.partial(self.collect, at) for at in range(last, 0, -1)]

    def next(self):
        return self.steps.pop(0)()

    def early(self):
        return self.halve(early_kernel, "early", self.first, 0)

    def late(self, keep, got, small):
        sent = keep.shape[1] + LANES
        return self.halve(late_kernel, "late", (*self.take(), keep, *got, small), 0, sent)

    def halve(self, kernel, name, operands, at, sent=0):
        rows, columns = operands[0].shape
        shapes = (rows // 2, columns), (rows // 2, columns)
        if sent:
            shapes = (rows, columns + sent), (rows, sent)

        def use(keep, sent):
            self.keep, self.got = [keep], [send_along(sent, [self.links[at]])]

        kernel = functools.partial(kernel, links=[self.links[at]])
        return Job(kernel, name, operands, (shaped(shapes[0], F32), shaped(shapes[1], BF)), use)

    def take(self):
        pairs = [a for pair in zip(self.keep, self.got) for a in pair]
        self.keep, self.got = [], []
        return pairs

    def share(self, at):
        operands = self.take()
        if at > 1:
            return self.halve(part_kernel, "part", operands, at)
        return self.halve(meet_kernel, "meet", operands, at)

    def swap(self):
        operands = self.take()

        def use(keep):
            self.keep, self.got = [keep], [send_along(keep, [self.links[-1]])]

        return Job(whole_kernel, "whole", operands, (shaped(operands[0].shape, BF),), use)

    def collect(self, at):
        operands = self.take()
        rows, columns = operands[0].shape
        if at == 1:
            links = [self.links[at]]

            def use_parts(*parts):
                self.keep, self.got = list(parts), [send_along(part, [self.links[0]]) for part in parts]

            kernel = functools.partial(split_group_kernel, links=links)
            return Job(kernel, "split_group", operands, (shaped((rows, columns), BF),) * 2, use_parts)
        if at == len(self.links) - 1:
            kernel, name = sum_kernel, "sum"
        else:
            kernel, name, rows = functools.partial(group_kernel, links=[self.links[at]]), "group", 2 * rows

        def use(keep):
            self.keep, self.got = [keep], [send_along(keep, [self.links[at - 1]])]

        return Job(kernel, name, operands, (shaped((rows, columns), BF),), use)


class Stream:
    def __init__(self, *first):
        self.first = first
        bits = list(range(lax.axis_size("dp").bit_length() - 1))
        self.bits = [(0, 1), (1, 0)] + [(bit, bit) for bit in bits[2:]]
        self.back = [(1, 1), (0, 0)] + self.bits[2:]
        self.steps = [self.start]
        self.steps += [functools.partial(self.halve, bits) for bits in self.bits[1:-1]]
        self.steps += [self.third, self.fourth]
        self.steps += [functools.partial(self.double, at) for at in range(len(bits), 0, -1)]

    def next(self):
        return self.steps.pop(0)()

    def split(self, kernel, name, operands, shape, bits):
        def use(keep, sent):
            self.keep, self.got = keep, send_along(sent, [bits])

        return Job(kernel, name, operands, (shaped(shape, F32), shaped(shape, BF)), use)

    def start(self):
        bits = self.bits[0]
        rows, columns = self.first[0].shape
        kernel = functools.partial(first_kernel, bits=bits)
        return self.split(kernel, "first", self.first, (2, rows // 2, columns), bits)

    def halve(self, bits):
        _, rows, columns = self.keep.shape
        kernel = functools.partial(halve_kernel, bits=bits)
        return self.split(kernel, "halve", (self.keep, self.got), (2, rows // 2, columns), bits)

    def third(self):
        _, rows, columns = self.keep.shape
        bit = self.bits[-1][0]
        kernel = functools.partial(third_kernel, bit=bit)
        return self.split(kernel, "third", (self.keep, self.got), (2, rows // 2, columns), (bit, None))

    def fourth(self):
        bit = self.bits[-1][0]
        kernel = functools.partial(fourth_kernel, bit=bit)
        return self.split(kernel, "fourth", (self.keep, self.got), self.keep.shape[1:], (None, bit))

    def double(self, at):
        if at == len(self.bits):
            kernel, name, shape = add_kernel, "add", self.keep.shape
        else:
            kernel, name = functools.partial(join_kernel, bits=self.back[at]), "join"
            shape = (2 * self.keep.shape[0], self.keep.shape[1])

        def use(keep):
            self.keep, self.got = keep, send_along(keep, [self.back[at - 1]])

        return Job(kernel, name, (self.keep, self.got), (shaped(shape, BF),), use)

    def finish(self, order, outs):
        kernel = functools.partial(final_kernel, bits=self.back[0])
        rows, columns = self.keep.shape
        scratch = [pltpu.VMEM((2 * rows, columns), F32), pltpu.SemaphoreType.DMA((2,))]
        outs = (*outs, shaped((8, LANES), F32))
        return order.call(kernel, "final", (self.keep, self.got), (), outs, scratch)[:2]


def after(v, *others):
    return lax.optimization_barrier((v, others))[0]


def exchange(order, home, partner, reverse, wait=()):
    kernel = functools.partial(chain_kernel, reverse=reverse)
    total = order.call(kernel, "chain", (home, partner), (), shaped(home.shape, BF), wait=wait)
    return total, lax.ppermute(total, "mp", [(2, 0), (3, 1)] if reverse else [(0, 2), (1, 3)])


def per_device(
    layer_input,
    qkv_weight,
    gate_weight,
    gate_bias,
    out_weight,
    inner_weight,
    outer_weight,
    leading_norm_gain,
    leading_norm_bias,
    trailing_norm_gain,
    trailing_norm_bias,
    random_features,
    output_grad,
):
    seqs, length, width = layer_input.shape
    heads, head, feat = random_features.shape
    pairs = heads // 2
    count = seqs * length
    hidden = inner_weight.shape[1]
    bias = gate_bias.reshape(1, heads)
    gain1, shift1 = leading_norm_gain.reshape(1, width), leading_norm_bias.reshape(1, width)
    gain2, shift2 = trailing_norm_gain.reshape(1, width), trailing_norm_bias.reshape(1, width)

    n_dp = lax.axis_size("dp")
    order = Order()
    halves = order.call(
        pack_kernel,
        "pack",
        (inner_weight, outer_weight),
        (),
        shaped((2, width // 2, hidden), BF),
        [pltpu.SemaphoreType.DMA((2,))],
        hbm=True,
    )
    half_chip = chip_swap(halves)
    inner_core, outer_core = core_swap(inner_weight), core_swap(outer_weight)

    by_seq = (seqs, length, width)
    gates = (seqs, length, LANES)
    states = (pairs, LANES + EXTRA, 2 * feat)
    gate_rows = jnp.transpose(gate_weight)
    sources = (layer_input, qkv_weight, gate_rows, bias, gain1, shift1, random_features)
    normed1, values, c, admit, c_row, a_row, phi_k, away, home = order.call(
        keys_kernel,
        "keys",
        sources,
        (),
        (
            kept((count, width), BF),
            kept(by_seq, F32),
            kept(gates, F32),
            kept(gates, F32),
            kept((seqs, heads, length), F32),
            kept((seqs, heads, length), F32),
            kept((seqs, heads, length, 2 * feat), BF),
            kept(states, BF),
            kept(states, BF),
        ),
        [pltpu.VMEM((width, 2 * width) if a is qkv_weight else a.shape, a.dtype) for a in sources]
        + [pltpu.SemaphoreType.DMA((len(sources),))],
        hbm=True,
    )
    partner_home, partner_away = core_swap(away), core_swap(home)
    total, got = exchange(order, home, partner_home, False)
    half_chip = after(half_chip, total)
    half_twin = lax.ppermute(half_chip, "dp", [(i, i ^ 1) for i in range(n_dp)])

    phi_q, scores, num = order.call(
        scores_kernel,
        "scores",
        (qkv_weight, random_features),
        (normed1, phi_k, values, c, c_row, a_row),
        (
            kept((seqs, heads, length, 2 * feat), BF),
            kept((seqs, heads, length, length), BF),
            kept((seqs, heads, length, LANES), F32),
        ),
        wait=(half_chip,),
    )
    got = after(got, num)
    swapped = core_swap(got)
    half_both = core_swap(half_chip)
    full, start, mixed_low, resid, normed2, sden, inverse, xhat2, scale2 = order.call(
        mix_kernel,
        "mix",
        (layer_input, got, swapped, partner_home, partner_away, out_weight, gain2, shift2),
        (phi_q, c, num),
        (
            kept((seqs, heads, length, LANES), F32),
            kept((seqs, *states), BF),
            kept(by_seq, BF),
            kept(by_seq, F32),
            kept(by_seq, BF),
            kept(gates, F32),
            kept(gates, F32),
            kept(by_seq, F32),
            kept(gates, F32),
        ),
    )

    normed2, mixed_low = (a.reshape(count, width) for a in (normed2, mixed_low))
    half_twin = after(half_twin, normed2)
    half_both_twin = core_swap(half_twin)
    shape = (count, width)
    grads = (width + hidden, width)
    out_part, dn2, out_low, keep0, send0 = order.call(
        feed_near_kernel,
        "feed_near",
        (output_grad.reshape(shape), inner_weight, outer_weight, inner_core, outer_core),
        (normed2, resid.reshape(shape)),
        (kept(shape, F32), kept(shape, F32), kept(shape, BF), shaped(grads, F32), shaped(grads, BF)),
    )
    got0 = core_swap(send0)
    far = pltpu.VMEM((2, width, hidden), BF)
    out_part, dn2, send1 = order.call(
        feed_far_kernel,
        "feed_both",
        (half_both, half_both_twin),
        (normed2, out_low, out_part, dn2),
        (kept(shape, F32), kept(shape, F32), shaped(grads, BF)),
        [far],
    )
    got1 = core_swap(send1)
    layer_out, dn2, keep1 = order.call(
        feed_last_kernel,
        "feed_chip",
        (half_chip, half_twin),
        (normed2, out_low, out_part, dn2),
        (pltpu.HBM(shape, F32), kept(shape, F32), shaped(grads, F32)),
        [far, pltpu.VMEM(shape, F32), pltpu.SemaphoreType.DMA],
    )
    stream = Stream(keep0, keep1, got0, got1)
    order.run(stream.next())

    dres, low, sums2, num_grads, r, away_grads, home_grads = order.call(
        turn_kernel,
        "turn",
        (output_grad, gain2, out_weight),
        (dn2.reshape(by_seq), xhat2, scale2, full, sden, inverse, phi_q, c),
        (
            kept(by_seq, F32),
            kept((count, width), BF),
            kept((8, width), F32),
            kept((seqs, heads, length, 2 * LANES), BF),
            kept(gates, F32),
            kept(states, BF),
            kept(states, BF),
        ),
    )
    partner_home_grads, partner_away_grads = core_swap(away_grads), core_swap(home_grads)
    _, got_grads = exchange(order, home_grads, partner_home_grads, True)

    q_grad, k_part, v_part, k_col = order.call(
        back_kernel,
        "back",
        (random_features,),
        (phi_q, phi_k, values, num_grads, scores, c, c_row, a_row, start),
        (
            kept((count, width), BF),
            kept(by_seq, F32),
            kept(by_seq, F32),
            kept(gates, F32),
        ),
    )
    dn1_part, xhat1, scale1, keep1, *send1 = order.call(
        products_kernel,
        "products",
        (layer_input.reshape(shape), qkv_weight),
        (mixed_low, low, normed1, q_grad),
        (
            kept(shape, F32),
            kept(shape, F32),
            kept((count, LANES), F32),
            shaped((width // 2, 2 * width), F32),
            *[shaped((width // 8, 2 * width), BF)] * 4,
        ),
    )
    gather = Gather(keep1, core_swap(send1))
    got_grads = after(got_grads, keep1)
    swapped_grads = core_swap(got_grads)

    order.run(stream.next())
    order.run(gather.early())
    kv_grad, logit_low, bias_sum, keep2, *send2 = order.call(
        cross_kernel,
        "cross",
        (got_grads, swapped_grads, partner_home_grads, partner_away_grads, random_features),
        (away, home, start, phi_k, values, c, admit, r, k_col, k_part, v_part, normed1),
        (
            kept((count, 2 * width), BF),
            kept((count, LANES), BF),
            kept((8, LANES), F32),
            shaped((width // 2, 2 * width), F32),
            *[shaped((width // 8, 2 * width), BF)] * 4,
        ),
    )
    got2 = core_swap(send2)
    while len(stream.steps) > len(stream.bits) + 1:
        order.run(stream.next())
    dn1, small = order.call(
        close_kernel,
        "close",
        (qkv_weight, gate_rows),
        (dn1_part, xhat1, kv_grad, logit_low, bias_sum, normed1, sums2),
        (kept(shape, F32), shaped((width // 2, LANES), F32)),
    )
    order.run(gather.late(keep2, got2, small))
    dx, _ = order.call(
        input_kernel,
        "input",
        (gain1,),
        (dn1, xhat1, scale1, dres.reshape(shape)),
        (pltpu.HBM(shape, F32), shaped((8, LANES), F32)),
        [pltpu.VMEM(shape, F32), pltpu.SemaphoreType.DMA],
    )
    while len(gather.steps) > 5:
        order.run(gather.next())
    while len(stream.steps) > 3:
        order.run(stream.next())
    order.run(gather.next(), stream.next())
    order.run(gather.next(), stream.next())
    order.run(gather.next())
    order.run(gather.next(), stream.next())
    order.run(gather.next())
    inner_total, outer_total = stream.finish(order, (pltpu.HBM((width, hidden), F32), pltpu.HBM((hidden, width), F32)))
    links = gather.links[0]
    mine = gather.keep
    near = (*mine, *core_swap(mine))
    scratch = [
        pltpu.VMEM((width // 2, 3 * width), F32), pltpu.VMEM((width // 2, width), F32), pltpu.SemaphoreType.DMA((4, 2)),
    ]
    big = (pltpu.HBM((width, 3 * width), F32), pltpu.HBM((width, width), F32))
    *begun, _ = order.call(
        functools.partial(write_near_kernel, links=links),
        "write_near",
        near,
        (),
        (*big, shaped((8, LANES), F32)),
        scratch,
    )
    got = after(gather.got, order.last)
    far = (*got, *core_swap(got))
    qkv_grad, wo_grad, gate_grad, *norm_grads, bias_grad = order.call(
        functools.partial(write_far_kernel, links=links),
        "write_far",
        (*near, *far),
        (),
        (*big, pltpu.HBM((heads, width), F32), *[pltpu.HBM((1, width), F32)] * 4, pltpu.HBM((1, heads), F32)),
        [
            *scratch[:2], pltpu.VMEM((16, width), F32), pltpu.VMEM((1, heads), F32), pltpu.VMEM((width, LANES), F32),
            scratch[2], pltpu.SemaphoreType.DMA((6,)),
        ],
        onto=begun,
    )
    return (
        layer_out.reshape(by_seq),
        dx.reshape(by_seq),
        qkv_grad,
        jnp.transpose(gate_grad),
        bias_grad.reshape(heads),
        wo_grad,
        inner_total,
        outer_total,
        *(a.reshape(width) for a in norm_grads),
    )


def solution(mesh):
    in_specs = (
        P("dp", "mp", None),
        P(),
        P(),
        P(),
        P(),
        P(None, "mp"),
        P("mp", None),
        P(),
        P(),
        P(),
        P(),
        P(),
        P("dp", "mp", None),
    )
    out_specs = (
        P("dp", "mp", None),
        P("dp", "mp", None),
        P(),
        P(),
        P(),
        P(),
        P(None, "mp"),
        P("mp", None),
        P(),
        P(),
        P(),
        P(),
    )
    return jax.shard_map(
        per_device, mesh=mesh, in_specs=in_specs, out_specs=out_specs, check_vma=False
    )
```

```python
import functools
import math

import jax
import jax.numpy as jnp
from jax import lax
from jax.experimental import pallas as pl
from jax.experimental.pallas import tpu as pltpu
from jax.sharding import PartitionSpec as P

BF = jnp.bfloat16
F32 = jnp.float32
epsilon = 1e-05
guard = 0.01
LANES = 128
EXTRA = 16
VMEM_BYTES = 16 * 1024 * 1024


def nn(a, b):
    return lax.dot_general(a, b, (((1,), (0,)), ((), ())), preferred_element_type=F32)


def nt(a, b):
    return lax.dot_general(a, b, (((1,), (1,)), ((), ())), preferred_element_type=F32)


def tn(a, b):
    return lax.dot_general(a, b, (((0,), (0,)), ((), ())), preferred_element_type=F32)


def two_terms(v):
    high = v.astype(BF)
    return high, (v - high.astype(F32)).astype(BF)


def iota(shape, dim):
    return lax.broadcasted_iota(jnp.int32, shape, dim)


def triangle(length, upper):
    rows, cols = iota((length, length), 0), iota((length, length), 1)
    return jnp.where((cols >= rows) if upper else (rows >= cols), 1.0, 0.0).astype(BF)


def running_sum(v, upper):
    ones = triangle(v.shape[0], upper)
    high, rest = two_terms(v)
    low = (v - high.astype(F32) - rest.astype(F32)).astype(BF)
    return nn(ones, high) + nn(ones, rest) + nn(ones, low)


def norm_rows(v):
    centred = v - jnp.mean(v, axis=-1, keepdims=True)
    scale = lax.rsqrt(jnp.mean(centred * centred, axis=-1, keepdims=True) + epsilon)
    return centred * scale, scale


def norm_rows_backward(grad, xhat, scale, gain):
    g = grad * gain
    return scale * (
        g
        - jnp.mean(g, axis=-1, keepdims=True)
        - xhat * jnp.mean(g * xhat, axis=-1, keepdims=True)
    )


def pair_frequencies(freq_ref, pair):
    even, odd = freq_ref[2 * pair], freq_ref[2 * pair + 1]
    none = jnp.zeros_like(even)
    return jnp.concatenate(
        [jnp.concatenate([even, none], axis=1), jnp.concatenate([none, odd], axis=1)], axis=0
    )


def scaled_sine_cosine(angles, scale):
    turns = jnp.floor(angles * (1.0 / math.pi) + 0.5)
    r = angles - turns * 3.140625
    r = r - turns * 0.0009675025939941406
    r = r - turns * 1.509958e-07
    odd = turns - 2.0 * jnp.floor(turns * 0.5)
    sign = scale - (2.0 * scale) * odd
    r2 = r * r
    sine = -0.00018362251175623582 * r2 + 0.008306273552368303
    sine = sine * r2 - 0.1666482311215342
    sine = sine * r2 + 0.9999966031254778
    cosine = -0.0012711240835350962 * r2 + 0.041487518673719546
    cosine = cosine * r2 - 0.4999123281046797
    cosine = cosine * r2 + 0.9999933132015835
    return sine * (r * sign), cosine * sign


def pair_features(values, freq, scale):
    high, low = two_terms(values)
    freq_high, freq_low = two_terms(freq)
    both = jnp.concatenate([freq_high, freq_high], axis=0)
    angles = nn(jnp.concatenate([high, low], axis=1), both) + nn(high, freq_low)
    sine, cosine = scaled_sine_cosine(angles, scale)
    sine, cosine = sine.astype(BF), cosine.astype(BF)
    feat = freq.shape[1] // 2
    return [
        jnp.concatenate([sine[:, h * feat : (h + 1) * feat], cosine[:, h * feat : (h + 1) * feat]], axis=1)
        for h in (0, 1)
    ]


def own_lanes(shape, half):
    lane = iota(shape, len(shape) - 1)
    return (lane >= LANES // 2) if half else (lane < LANES // 2)


def one_lane(shape, half):
    return iota(shape, len(shape) - 1) == (0 if half else LANES // 2)


def second_lane(shape, half):
    return iota(shape, len(shape) - 1) == (1 if half else LANES // 2 + 1)


def with_ones(values, half, both=False):
    v = values.astype(F32)
    ones = one_lane(v.shape, half) | (both & second_lane(v.shape, half))
    return jnp.where(own_lanes(v.shape, half), v, jnp.where(ones, 1.0, 0.0))


def pack_states(even, odd, decay_even, decay_odd):
    half = LANES // 2
    row = iota(even.shape, 0)
    states = jnp.where(row < half, even, odd).astype(BF)
    extra = iota((EXTRA, even.shape[1]), 0)
    parts = []
    for value in (even[half : half + 1], odd[0:1], decay_even, decay_odd):
        high = value.astype(BF).astype(F32)
        parts += [high, value - high]
    rows = jnp.zeros((EXTRA, even.shape[1]), F32)
    for at, part in enumerate(parts):
        rows = jnp.where(extra == at, part, rows)
    return states, rows.astype(BF)


def extra_row(packed, at):
    at = LANES + 2 * at
    return packed[at : at + 1] + packed[at + 1 : at + 2]


def decays(packed):
    return extra_row(packed, 2), extra_row(packed, 3)


def unpack_states(packed):
    half = LANES // 2
    states = packed[:LANES]
    row = iota(states.shape, 0)
    even = jnp.where(row < half, states, jnp.where(row == half, extra_row(packed, 0), 0.0))
    odd = jnp.where(row >= half, states, jnp.where(row == 0, extra_row(packed, 1), 0.0))
    return even, odd


def join_states(first, second):
    return [
        a + decay * b
        for a, b, decay in zip(unpack_states(first), unpack_states(second), decays(first))
    ]


def as_operand(state, half):
    at = 0 if half else LANES // 2
    norm = state[at : at + 1]
    rest = norm - norm.astype(BF).astype(F32)
    return jnp.where(iota(state.shape, 0) == at + 1, rest, state).astype(BF)


def decay_weights(c_col, c_row, a_row):
    length = c_col.shape[0]
    gap = jnp.minimum(c_col - c_row, 0.0)
    causal = iota((length, length), 0) >= iota((length, length), 1)
    return jnp.where(causal, jnp.exp(gap) * a_row, 0.0)


def head_lanes(pair):
    shape = (2 * LANES, LANES)
    head = 2 * pair + (iota(shape, 0) % LANES) // (LANES // 2)
    return jnp.where(iota(shape, 1) == head, 1.0, 0.0).astype(BF)


def norm_lanes(pair):
    shape = (2 * LANES, LANES)
    row = iota(shape, 0) % LANES
    of_even, of_odd = row // 2 == LANES // 4, row // 2 == 0
    taken = (of_even & (iota(shape, 1) == 2 * pair)) | (of_odd & (iota(shape, 1) == 2 * pair + 1))
    return jnp.where(taken, 1.0, 0.0).astype(BF)


def lane_sum(v):
    return jnp.sum(v, axis=1, keepdims=True)


def each(count, step):
    lax.fori_loop(0, count, lambda i, none: (step(i), none)[1], 0)


def wide(v, axis):
    none = list(v.shape)
    none[axis] = LANES - v.shape[axis]
    return jnp.concatenate([v, jnp.zeros(none, v.dtype)], axis=axis)


def aligned(at, size):
    return pl.ds(pl.multiple_of(at * size, size), size)


def my_core():
    return lax.axis_index("mp") % 2


def my_chip():
    return lax.axis_index("mp") // 2


def pack_kernel(inner_ref, outer_ref, out_ref, sems):
    rows = out_ref.shape[1]
    mine = aligned(lax.axis_index("dp") % 2, rows)
    copies = [
        pltpu.make_async_copy(source.at[mine], out_ref.at[i], sems.at[i])
        for i, source in enumerate((inner_ref, outer_ref))
    ]
    for copy in copies:
        copy.start()
    for copy in copies:
        copy.wait()


def by_place(of_sequence):
    even = my_core() == 0
    one, two = of_sequence
    return jnp.where(even, two, one), jnp.where(even, one, two)


def put_states(pair, packed, away_ref, home_ref):
    for rows, parts in ((slice(0, LANES), [p[0] for p in packed]), (slice(LANES, None), [p[1] for p in packed])):
        away_ref[pair, rows], home_ref[pair, rows] = by_place(parts)


def keys_kernel(
    x_hbm, wqkv_hbm, gw_hbm, gb_hbm, gain_hbm, shift_hbm, freq_hbm,
    n1_ref, v_ref, c_ref, a_ref, crow_ref, arow_ref, pk_ref, away_ref, home_ref,
    x_ref, w_ref, gw_ref, gb_ref, gain_ref, shift_ref, freq_ref, sems,
):
    heads, _, feat = freq_ref.shape
    seqs, length, width = x_ref.shape
    sources = (x_hbm, gain_hbm, shift_hbm, gw_hbm, gb_hbm, wqkv_hbm.at[:, pl.ds(width, 2 * width)], freq_hbm)
    buffers = (x_ref, gain_ref, shift_ref, gw_ref, gb_ref, w_ref, freq_ref)
    copies = [
        pltpu.make_async_copy(source, buffer, sems.at[i])
        for i, (source, buffer) in enumerate(zip(sources, buffers))
    ]
    for copy in copies:
        copy.start()
    for copy in copies[:5]:
        copy.wait()
    scale = 1.0 / math.sqrt(feat)
    xhat, _ = norm_rows(x_ref[...].reshape(seqs * length, width))
    n1 = (xhat * gain_ref[...] + shift_ref[...]).astype(BF)
    n1_ref[...] = n1
    z = nt(n1, wide(gw_ref[...], 0)) + wide(gb_ref[...], 1)
    e = jnp.exp(-jnp.abs(z))
    log_keep = jnp.minimum(z, 0.0) - jnp.log1p(e)
    inverse = 1.0 / (1.0 + e)
    admit_all = jnp.where(z > 0.0, e * inverse, inverse)
    tails, decay = [], []
    for s in range(seqs):
        rows = slice(s * length, (s + 1) * length)
        c = running_sum(log_keep[rows], False)
        admit = admit_all[rows]
        c_ref[s] = c
        a_ref[s] = admit
        crow_ref[s] = jnp.transpose(c)[:heads]
        arow_ref[s] = jnp.transpose(admit)[:heads]
        last = c[length - 1 :]
        tails.append(jnp.exp(last - c) * admit)
        decay.append(jnp.exp(last))
    for copy in copies[5:]:
        copy.wait()
    keys = nn(n1, w_ref[:, :width])
    values = nn(n1, w_ref[:, width:])
    v_ref[...] = values.reshape(v_ref.shape)
    for pair in range(heads // 2):
        lanes = slice(pair * LANES, (pair + 1) * LANES)
        phi = pair_features(keys[:, lanes], pair_frequencies(freq_ref, pair), scale)
        packed = []
        for s in range(seqs):
            rows = slice(s * length, (s + 1) * length)
            states = []
            for half in (0, 1):
                h = 2 * pair + half
                phi_k = phi[half][rows]
                pk_ref[s, h] = phi_k
                weighted = with_ones(values[rows, lanes], half) * tails[s][:, h : h + 1]
                both = tn(jnp.concatenate(two_terms(weighted), axis=1), phi_k)
                states.append(both[:LANES] + both[LANES:])
            h = 2 * pair
            packed.append(pack_states(*states, decay[s][:, h : h + 1], decay[s][:, h + 1 : h + 2]))
        put_states(pair, packed, away_ref, home_ref)


def scores_kernel(wqkv_ref, freq_ref, n1_ref, pk_ref, v_ref, c_ref, crow_ref, arow_ref, pq_ref, p_ref, num_ref):
    seqs, heads, length, _ = pk_ref.shape
    scale = 1.0 / math.sqrt(freq_ref.shape[2])
    queries = nn(n1_ref[...], wqkv_ref[:, : n1_ref.shape[1]])
    for pair in range(heads // 2):
        lanes = slice(pair * LANES, (pair + 1) * LANES)
        phi = pair_features(queries[:, lanes], pair_frequencies(freq_ref, pair), scale)
        for s in range(seqs):
            for half in (0, 1):
                h = 2 * pair + half
                phi_q = phi[half][s * length : (s + 1) * length]
                pq_ref[s, h] = phi_q
                v = with_ones(v_ref[s, :, lanes], half)
                weights = decay_weights(
                    c_ref[s, :, h : h + 1], crow_ref[s, h : h + 1], arow_ref[s, h : h + 1]
                )
                p = jnp.concatenate(two_terms(nt(phi_q, pk_ref[s, h]) * weights), axis=1)
                p_ref[s, h] = p
                v = jnp.concatenate(two_terms(v), axis=1)
                both = nn(p, jnp.concatenate([v, v], axis=0))
                num_ref[s, h] = both[:, :LANES] + both[:, LANES:]


def mix_kernel(
    x_ref, got_ref, swapped_ref, partner_home_ref, partner_away_ref, wo_ref, gain_ref, shift_ref, pq_ref, c_ref, num_ref,
    full_ref, start_ref, mixed_ref, resid_ref, n2_ref, sden_ref, inverse_ref, xhat_ref, scale_ref,
):
    seqs, heads = pq_ref.shape[:2]
    core = my_core()

    def one(s):
        growth = jnp.exp(c_ref[s])
        sdens = jnp.zeros_like(growth)
        for pair in range(heads // 2):
            before = jnp.where(s == core, got_ref[pair], swapped_ref[pair]).astype(F32)
            partner = jnp.where(s == core, partner_home_ref[pair], partner_away_ref[pair]).astype(F32)
            states = [
                jnp.where(core == 0, a, b)
                for a, b in zip(unpack_states(before), join_states(partner, before))
            ]
            none = jnp.zeros((1, 1), F32)
            main, rest = pack_states(*states, none, none)
            start_ref[s, pair, :LANES] = main
            start_ref[s, pair, LANES:] = rest
            fulls = []
            for half in (0, 1):
                h = 2 * pair + half
                full = num_ref[s, h] + growth[:, h : h + 1] * nt(
                    pq_ref[s, h], as_operand(states[half], half)
                )
                full_ref[s, h] = full
                fulls.append(full)
            beside = jnp.where(own_lanes(fulls[0].shape, 0), fulls[1], fulls[0])
            sdens = sdens + nn(jnp.concatenate(two_terms(beside), axis=1), norm_lanes(pair))
        inverse = lax.rsqrt(sdens * sdens + guard)
        sden_ref[s] = sdens
        inverse_ref[s] = inverse
        for pair in range(heads // 2):
            mixed = [full_ref[s, h] * inverse[:, h : h + 1] for h in (2 * pair, 2 * pair + 1)]
            pair_mixed = jnp.where(own_lanes(mixed[0].shape, 0), mixed[0], mixed[1])
            mixed_ref[s, :, pair * LANES : (pair + 1) * LANES] = pair_mixed.astype(BF)
        resid = x_ref[s] + nn(mixed_ref[s], wo_ref[...])
        resid_ref[s] = resid
        xhat, scale = norm_rows(resid)
        xhat_ref[s] = xhat
        scale_ref[s] = jnp.broadcast_to(scale, scale_ref.shape[1:])
        n2_ref[s] = (xhat * gain_ref[...] + shift_ref[...]).astype(BF)

    for s in range(seqs):
        one(s)


def gelu_and_slope(v):
    root = math.sqrt(2.0 / math.pi)
    v2 = v * v
    t = jnp.tanh(v * (root + (root * 0.044715) * v2))
    half = 0.5 * (1.0 + t)
    slope = half + (0.5 * v) * (1.0 - t * t) * (root + (root * 3.0 * 0.044715) * v2)
    return v * half, slope


def feed_block(n2, out_low, wi_ref, wo_ref):
    active, slope = gelu_and_slope(nn(n2, wi_ref[...]))
    active = active.astype(BF)
    pre_grad = (nt(out_low, wo_ref[...]) * slope).astype(BF)
    return nn(active, wo_ref[...]), nt(pre_grad, wi_ref[...]), tn(n2, pre_grad), tn(active, out_low)


def halves_together(far_ref, one, two):
    twin = lax.axis_index("dp") % 2
    rows = one.shape[1]
    for which in range(2):
        far_ref[which, aligned(twin, rows)] = one[which]
        far_ref[which, aligned(1 - twin, rows)] = two[which]


def feed_near_kernel(og_ref, wi0, wo0, wi2, wo2, n2_ref, resid_ref, out_ref, dn2_ref, low_ref, keep_ref, send_ref):
    low_ref[...] = og_ref[...].astype(BF)
    n2, out_low = n2_ref[...], low_ref[...]
    rows = n2.shape[1]
    out, dn2, inner, outer = feed_block(n2, out_low, wi2, wo2)
    send_ref[:rows] = inner.astype(BF)
    send_ref[rows:] = outer.astype(BF)
    out_own, dn2_own, inner, outer = feed_block(n2, out_low, wi0, wo0)
    keep_ref[:rows] = inner
    keep_ref[rows:] = outer
    out_ref[...] = resid_ref[...] + out + out_own
    dn2_ref[...] = dn2 + dn2_own


def feed_far_kernel(half_ref, twin_ref, n2_ref, low_ref, part_ref, dn2_part_ref, out_ref, dn2_ref, grad_ref, far_ref):
    twin = lax.axis_index("dp") % 2
    rows = half_ref.shape[1]
    for which in range(2):
        far_ref[which, aligned(twin, rows)] = half_ref[which]
        far_ref[which, aligned(1 - twin, rows)] = twin_ref[which]
    n2 = n2_ref[...]
    out, dn2, inner, outer = feed_block(n2, low_ref[...], far_ref.at[0], far_ref.at[1])
    out_ref[...] = part_ref[...] + out
    dn2_ref[...] = dn2_part_ref[...] + dn2
    rows = n2.shape[1]
    grad_ref[:rows] = inner.astype(grad_ref.dtype)
    grad_ref[rows:] = outer.astype(grad_ref.dtype)


def feed_last_kernel(
    half_ref, twin_ref, n2_ref, low_ref, part_ref, dn2_part_ref, out_hbm, dn2_ref, grad_ref, far_ref, out_ref, sem
):
    feed_far_kernel(half_ref, twin_ref, n2_ref, low_ref, part_ref, dn2_part_ref, out_ref, dn2_ref, grad_ref, far_ref)
    copy = pltpu.make_async_copy(out_ref, out_hbm, sem)
    copy.start()
    copy.wait()


def place_bit(bits):
    place = lax.axis_index("dp")
    return jnp.where(my_core() == 0, (place // (1 << bits[0])) % 2, (place // (1 << bits[1])) % 2)


def split_rows(total, bits, mine_ref, send_ref):
    rows = mine_ref.shape[1]
    high = place_bit(bits) == 1
    first, second = total[:, :rows], total[:, rows:]
    mine_ref[...] = jnp.where(high, second, first)
    send_ref[...] = jnp.where(high, first, second).astype(BF)


def halve_kernel(keep_ref, got_ref, mine_ref, send_ref, *, bits):
    split_rows(keep_ref[...] + got_ref[...].astype(F32), bits, mine_ref, send_ref)


def first_kernel(keep0_ref, keep1_ref, got0_ref, got1_ref, mine_ref, send_ref, *, bits):
    for block, (keep_ref, got_ref) in enumerate(((keep0_ref, got0_ref), (keep1_ref, got1_ref))):
        total = (keep_ref[...] + got_ref[...].astype(F32))[None]
        split_rows(total, bits, mine_ref.at[block : block + 1], send_ref.at[block : block + 1])


def third_kernel(keep_ref, got_ref, mine_ref, send_ref, *, bit):
    rows = mine_ref.shape[1]
    total = keep_ref[...] + got_ref[...].astype(F32)
    low, high = total[:, :rows], total[:, rows:]
    by_bit = place_bit((bit, bit)) == 1
    one, two = jnp.where(by_bit, high, low), jnp.where(by_bit, low, high)
    even = my_core() == 0
    for part in range(2):
        of_block = (low, high)[part]
        mine_ref[part] = jnp.where(even, one[part], of_block[0])
        send_ref[part] = jnp.where(even, two[part], of_block[1]).astype(BF)


def fourth_kernel(keep_ref, got_ref, mine_ref, send_ref, *, bit):
    total = keep_ref[...] + got_ref[...].astype(F32)
    second = (my_core() == 1) & (place_bit((bit, bit)) == 1)
    mine_ref[...] = jnp.where(second, total[1], total[0])
    send_ref[...] = jnp.where(second, total[0], total[1]).astype(BF)


def add_kernel(keep_ref, got_ref, out_ref):
    out_ref[...] = (keep_ref[...] + got_ref[...].astype(F32)).astype(out_ref.dtype)


def joined(mine_ref, got_ref, bits):
    high = place_bit(bits) == 1
    mine, got = mine_ref[...].astype(F32), got_ref[...].astype(F32)
    return jnp.concatenate([jnp.where(high, got, mine), jnp.where(high, mine, got)], axis=0)


def join_kernel(mine_ref, got_ref, out_ref, *, bits):
    out_ref[...] = joined(mine_ref, got_ref, bits).astype(BF)


def final_kernel(mine_ref, got_ref, inner_hbm, outer_hbm, mark_ref, whole_ref, sems, *, bits):
    mark_ref[...] = jnp.zeros_like(mark_ref)
    both = joined(mine_ref, got_ref, bits)
    quarter = both.shape[0] // 4
    one, two = both[quarter : 2 * quarter], both[2 * quarter : 3 * quarter]
    even = my_core() == 0
    whole_ref[:quarter] = both[:quarter]
    whole_ref[quarter : 2 * quarter] = jnp.where(even, two, one)
    whole_ref[2 * quarter : 3 * quarter] = jnp.where(even, one, two)
    whole_ref[3 * quarter :] = both[3 * quarter :]
    rows = inner_hbm.shape[0]
    copies = [
        pltpu.make_async_copy(whole_ref.at[pl.ds(at * rows, rows)], out_hbm, sems.at[at])
        for at, out_hbm in enumerate((inner_hbm, outer_hbm))
    ]
    for copy in copies:
        copy.start()
    for copy in copies:
        copy.wait()


def turn_kernel(
    og_ref, gain_ref, wo_ref, dn2_ref, xhat_ref, scale_ref, full_ref, sden_ref, inverse_ref, pq_ref, c_ref,
    dres_ref, low_ref, sums_ref, ng_ref, r_ref, away_ref, home_ref,
):
    seqs, heads, length, _ = pq_ref.shape
    sums_ref[...] = jnp.zeros_like(sums_ref)
    packed = [[] for _ in range(seqs)]

    def one(s):
        xhat = xhat_ref[s]
        dn2 = dn2_ref[s]
        dres = og_ref[s] + norm_rows_backward(dn2, xhat, scale_ref[s, :, :1], gain_ref[...])
        dres_ref[s] = dres
        low = dres.astype(BF)
        low_ref[s * length : (s + 1) * length] = low
        sums_ref[2:3] += jnp.sum(dn2 * xhat, axis=0, keepdims=True)
        sums_ref[3:4] += jnp.sum(dn2, axis=0, keepdims=True)
        dmixed = nt(low, wo_ref[...])
        c = c_ref[s]
        growth = jnp.exp(c)
        decay = jnp.exp(c[length - 1 :])
        lane = iota(c.shape, 1)
        sden, inverse = sden_ref[s], inverse_ref[s]
        dots = jnp.zeros_like(c)
        for pair in range(heads // 2):
            g = dmixed[:, pair * LANES : (pair + 1) * LANES]
            h = 2 * pair
            values = jnp.where(own_lanes(g.shape, 0), full_ref[s, h], full_ref[s, h + 1])
            dots = dots + nn(jnp.concatenate(two_terms(g * values), axis=1), head_lanes(pair))
        dots = dots * inverse
        inverse2 = inverse * inverse
        r_ref[s] = dots * inverse2 * guard
        sden_grads = -dots * sden * inverse2
        growing = sden_grads * growth
        lifting = inverse * growth
        for pair in range(heads // 2):
            g = dmixed[:, pair * LANES : (pair + 1) * LANES]
            states = []
            for half in (0, 1):
                h = 2 * pair + half
                mine, one_at = own_lanes(g.shape, half), one_lane(g.shape, half)
                column = slice(h, h + 1)
                grads = jnp.where(mine, g * inverse[:, column], jnp.where(one_at, sden_grads[:, column], 0.0))
                ng_ref[s, h] = jnp.concatenate(two_terms(grads), axis=1)
                lifted = jnp.where(mine, g * lifting[:, column], jnp.where(one_at, growing[:, column], 0.0))
                both = tn(jnp.concatenate(two_terms(lifted), axis=1), pq_ref[s, h])
                states.append(both[:LANES] + both[LANES:])
            h = 2 * pair
            packed[s].append(pack_states(*states, decay[:, h : h + 1], decay[:, h + 1 : h + 2]))

    for s in range(seqs):
        one(s)
    for pair, both in enumerate(zip(*packed)):
        put_states(pair, both, away_ref, home_ref)


def angle_grads(phi, dphi):
    feat = phi.shape[1] // 2
    phi = phi.astype(F32)
    return phi[:, feat:] * dphi[:, :feat] - phi[:, :feat] * dphi[:, feat:]


def weight_grads(left_ref, right_ref, keep_ref, send_refs):
    rows = keep_ref.shape[0]
    core = my_core()
    keep_ref[...] = tn(left_ref[:, aligned(core, rows)], right_ref[...])
    away = tn(left_ref[:, aligned(1 - core, rows)], right_ref[...]).astype(BF)
    rows //= len(send_refs)
    for part, send_ref in enumerate(send_refs):
        send_ref[...] = away[part * rows : (part + 1) * rows]


def back_kernel(
    freq_ref, pq_ref, pk_ref, v_ref, ng_ref, p_ref, c_ref, crow_ref, arow_ref, start_ref,
    qg_ref, kg_ref, vg_ref, kcol_ref,
):
    seqs, heads, length, _ = pq_ref.shape

    def one(s):
        tokens = aligned(s, length)
        c = c_ref[s]
        growth = jnp.exp(c)
        lane = iota(c.shape, 1)
        kcol = jnp.zeros_like(c)
        for pair in range(heads // 2):
            at = pair * LANES
            freq = pair_frequencies(freq_ref, pair).astype(BF)
            states = unpack_states(start_ref[s, pair].astype(F32))
            q_angles, k_angles, v_grads = [], [], []
            for half in (0, 1):
                h = 2 * pair + half
                phi_q, phi_k = pq_ref[s, h], pk_ref[s, h]
                grads = ng_ref[s, h, :, :LANES]
                v = with_ones(v_ref[s, :, at : at + LANES], half)
                weights = decay_weights(c[:, h : h + 1], crow_ref[s, h : h + 1], arow_ref[s, h : h + 1])
                dk = (nt(grads, v.astype(BF)) * weights).astype(BF)
                lifted = (grads.astype(F32) * growth[:, h : h + 1]).astype(BF)
                dphi_q = nn(dk, phi_k) + nn(lifted, states[half].astype(BF))
                q_angles.append(angle_grads(phi_q, dphi_q))
                k_angles.append(angle_grads(phi_k, tn(dk, phi_q)))
                both = tn(p_ref[s, h], ng_ref[s, h])
                both = both[:length] + both[length:]
                dv = both[:, :LANES] + both[:, LANES:]
                v_grads.append(dv)
                kcol = jnp.where(lane == h, lane_sum(v * dv), kcol)
            qg_ref[tokens, at : at + LANES] = nt(
                jnp.concatenate(q_angles, axis=1).astype(BF), freq
            ).astype(BF)
            kg_ref[s, :, at : at + LANES] = nt(jnp.concatenate(k_angles, axis=1).astype(BF), freq)
            vg_ref[s, :, at : at + LANES] = jnp.where(
                own_lanes(v_grads[0].shape, 0), v_grads[0], v_grads[1]
            )
        kcol_ref[s] = kcol

    each(seqs, one)


def products_kernel(
    x_ref, wqkv_ref, mixed_ref, low_ref, n1_ref, qg_ref, part_ref, xhat_ref, scale_ref, keep_ref, *send_refs
):
    width = low_ref.shape[1]
    part_ref[...] = nt(qg_ref[...], wqkv_ref[:, :width])
    xhat, scale = norm_rows(x_ref[...])
    xhat_ref[...] = xhat
    scale_ref[...] = jnp.broadcast_to(scale, scale_ref.shape)
    for at, left_ref, right_ref in ((0, mixed_ref, low_ref), (width, n1_ref, qg_ref)):
        lanes = pl.ds(at, width)
        weight_grads(left_ref, right_ref, keep_ref.at[:, lanes], [ref.at[:, lanes] for ref in send_refs])


def cross_kernel(
    got_ref, swapped_ref, partner_home_ref, partner_away_ref, freq_ref, away_ref, home_ref, start_ref, pk_ref, v_ref,
    c_ref, a_ref, r_ref, kcol_ref,
    kg_ref, vg_ref, n1_ref,
    kv_ref, logit_ref, bias_ref, keep_ref, *send_refs,
):
    seqs, heads, length, _ = pk_ref.shape
    core = my_core()
    width = kg_ref.shape[2]
    bias_ref[...] = jnp.zeros_like(bias_ref)

    def one(s):
        tokens = aligned(s, length)
        c, a = c_ref[s], a_ref[s]
        tail = jnp.exp(c[length - 1 :] - c) * a
        lane = iota(c.shape, 1)
        lane_row = iota((1, c.shape[1]), 1)
        kcol = kcol_ref[s]
        ends = jnp.zeros((1, c.shape[1]), F32)
        for pair in range(heads // 2):
            at = pair * LANES
            freq = pair_frequencies(freq_ref, pair).astype(BF)
            after = jnp.where(s == core, got_ref[pair], swapped_ref[pair]).astype(F32)
            partner = jnp.where(s == core, partner_home_ref[pair], partner_away_ref[pair]).astype(F32)
            grads = [
                jnp.where(core == 1, a, b)
                for a, b in zip(unpack_states(after), join_states(partner, after))
            ]
            local = jnp.where(s == core, home_ref[pair], away_ref[pair]).astype(F32)
            reached = join_states(local, start_ref[s, pair].astype(F32))
            k_angles, v_grads = [], []
            for half in (0, 1):
                h = 2 * pair + half
                phi_k = pk_ref[s, h]
                v = with_ones(v_ref[s, :, at : at + LANES], half, True)
                grad_low = as_operand(grads[half], half)
                weight = tail[:, h : h + 1]
                k_angles.append(angle_grads(phi_k, nn(v.astype(BF), grad_low)) * weight)
                dv = nt(phi_k, grad_low) * weight
                v_grads.append(dv)
                kcol = kcol + jnp.where(lane == h, lane_sum(v * dv), 0.0)
                end = jnp.sum(lane_sum(grads[half] * reached[half]), axis=0, keepdims=True)
                ends = jnp.where(lane_row == h, end, ends)
            kg = kg_ref[s, :, at : at + LANES] + nt(
                jnp.concatenate(k_angles, axis=1).astype(BF), freq
            )
            vg = vg_ref[s, :, at : at + LANES] + jnp.where(
                own_lanes(v_grads[0].shape, 0), v_grads[0], v_grads[1]
            )
            kv_ref[tokens, at : at + LANES] = kg.astype(BF)
            kv_ref[tokens, width + at : width + at + LANES] = vg.astype(BF)
        keep_grad = running_sum(r_ref[s] - kcol, True) + ends
        logit_grad = a * keep_grad - (1.0 - a) * kcol
        logit_ref[tokens] = logit_grad.astype(BF)
        bias_ref[0:1] += jnp.sum(logit_grad, axis=0, keepdims=True)

    for i in range(seqs):
        one(i)
    weight_grads(n1_ref, kv_ref, keep_ref, send_refs)


def close_kernel(
    wqkv_ref, gw_ref, part_ref, xhat_ref, kv_ref, logit_ref, bias_ref, n1_ref, sums2_ref, dn1_ref, small_ref
):
    width = part_ref.shape[1]
    logit_low = logit_ref[...]
    dn1 = part_ref[...] + nt(kv_ref[...], wqkv_ref[:, width:]) + nn(logit_low, wide(gw_ref[...], 0))
    xhat = xhat_ref[...]
    dn1_ref[...] = dn1
    row = iota((8, width), 0)
    sums = jnp.where(row == 0, jnp.sum(dn1 * xhat, axis=0, keepdims=True), sums2_ref[...])
    sums = jnp.where(row == 1, jnp.sum(dn1, axis=0, keepdims=True), sums)
    bias = jnp.concatenate([bias_ref[0:1], jnp.zeros((1, width - LANES), F32)], axis=1)
    sums = jnp.where(row == 4, bias, sums)
    gates = tn(logit_low, n1_ref[...])[:8]
    stacked = jnp.concatenate([sums, gates, jnp.zeros((LANES - 16, width), F32)], axis=0)
    columns = jnp.transpose(stacked)
    rows = small_ref.shape[0]
    small_ref[...] = columns[:rows] + pltpu.roll(columns[rows:], 16, 1)


def input_kernel(gain_ref, dn1_ref, xhat_ref, scale_ref, dres_ref, dx_hbm, mark_ref, dx_ref, sem):
    mark_ref[...] = jnp.zeros_like(mark_ref)
    dx_ref[...] = dres_ref[...] + norm_rows_backward(dn1_ref[...], xhat_ref[...], scale_ref[:, :1], gain_ref[...])
    copy = pltpu.make_async_copy(dx_ref, dx_hbm, sem)
    copy.start()
    copy.wait()


def chain_kernel(me_ref, partner_ref, out_ref, *, reverse):
    core = my_core()
    lead = (core == 0) if reverse else (core == 1)
    for pair in range(out_ref.shape[0]):
        mine, other = me_ref[pair].astype(F32), partner_ref[pair].astype(F32)
        first = jnp.where(lead, mine, other)
        second = jnp.where(lead, other, mine)
        none = jnp.zeros((1, 1), F32)
        main, rest = pack_states(*join_states(first, second), none, none)
        out_ref[pair, :LANES] = main
        out_ref[pair, LANES:] = rest


def widen(v):
    main, last = v[:, :-LANES].astype(F32), v[:, -LANES:].astype(F32)
    last = jnp.where(iota(last.shape, 1) < LANES // 2, last + pltpu.roll(last, LANES // 2, 1), 0.0)
    return jnp.concatenate([main, last], axis=1)


def narrow(v):
    main, last = v[:, :-LANES].astype(BF), v[:, -LANES:]
    high, low = two_terms(last)
    last = high.astype(F32) + pltpu.roll(low.astype(F32), LANES // 2, 1)
    return jnp.concatenate([main, last.astype(BF)], axis=1)


def link_bit(link):
    return my_chip() if link is None else (lax.axis_index("dp") // (1 << link)) % 2


def piece_number(links):
    number = 0
    for of_zero, of_one in links:
        bit = link_bit(of_zero)
        if of_one != of_zero:
            bit = jnp.where(my_core() == 0, bit, link_bit(of_one))
        number = 2 * number + bit
    return number


def pick(pieces, number):
    taken = pieces[0]
    for at in range(1, len(pieces)):
        taken = jnp.where(number == at, pieces[at], taken)
    return taken


def share_out(total, links, mine_ref, send_refs):
    rows = mine_ref.shape[0]
    pieces = [total[at : at + rows] for at in range(0, total.shape[0], rows)]
    number = piece_number(links)
    mine_ref[...] = pick(pieces, number)
    for k, send_ref in enumerate(send_refs):
        send_ref[...] = narrow(pick(pieces, number ^ (k + 1)))


def early_kernel(keep_ref, *refs, links):
    *got_refs, mine_ref, send_ref = refs
    rows = mine_ref.shape[0]
    total = keep_ref[...] + jnp.concatenate([ref[...].astype(F32) for ref in got_refs], axis=0)
    number = piece_number(links)
    pieces = [total[:rows], total[rows:]]
    mine_ref[...] = pick(pieces, number)
    send_ref[...] = pick(pieces, number ^ 1).astype(BF)


def late_kernel(early_ref, early_got_ref, keep_ref, *refs, links):
    *got_refs, small_ref, mine_ref, send_ref = refs
    before = early_ref.shape[1]
    mine_ref[:, :before] = early_ref[...] + early_got_ref[...].astype(F32)
    total = keep_ref[...] + jnp.concatenate([ref[...].astype(F32) for ref in got_refs], axis=0)
    total = jnp.concatenate([total, small_ref[...]], axis=1)
    share_out(total, links, mine_ref.at[:, pl.ds(before, total.shape[1])], [send_ref])


def meet_kernel(keep_ref, got_ref, mine_ref, send_ref, *, links):
    before = keep_ref.shape[1] - got_ref.shape[1]
    second = keep_ref[:, before:] + widen(got_ref[...])
    share_out(jnp.concatenate([keep_ref[:, :before], second], axis=1), links, mine_ref, [send_ref])


def part_kernel(keep_ref, got_ref, mine_ref, send_ref, *, links):
    share_out(keep_ref[...] + widen(got_ref[...]), links, mine_ref, [send_ref])


def whole_kernel(keep_ref, got_ref, out_ref):
    out_ref[...] = narrow(keep_ref[...] + widen(got_ref[...]))


def sum_kernel(mine_ref, got_ref, out_ref):
    out_ref[...] = narrow(widen(mine_ref[...]) + widen(got_ref[...]))


def split_group_kernel(mine_ref, got_ref, first_ref, second_ref, *, links):
    mine, got = mine_ref[...], got_ref[...]
    high = piece_number(links) == 1
    first_ref[...] = jnp.where(high, got, mine)
    second_ref[...] = jnp.where(high, mine, got)


def group_kernel(*refs, links):
    pieces = [ref[...].astype(F32) for ref in refs[:-1]]
    number = piece_number(links)
    both = [pick(pieces, number ^ at) for at in range(len(pieces))]
    refs[-1][...] = jnp.concatenate(both, axis=0).astype(BF)


def piece_place(of_partner, far, links):
    core = my_core()
    core = 1 - core if of_partner else core
    high = jnp.where(core == 0, link_bit(links[0]), link_bit(links[1]))
    return 2 * core + (1 - high if far else high)


def write_pieces(pieces, places, qkv_hbm, wo_hbm, qkv_ref, wo_ref, sems):
    rows, width = pieces[0].shape[0], wo_hbm.shape[1]
    copies = []
    for at, (piece_ref, place) in enumerate(zip(pieces, places)):
        own = slice(at * rows, (at + 1) * rows)
        wo_ref[own] = piece_ref[:, :width].astype(F32)
        qkv_ref[own] = piece_ref[:, width:-LANES].astype(F32)
        for which, (ref, hbm) in enumerate(((wo_ref, wo_hbm), (qkv_ref, qkv_hbm))):
            there = hbm.at[aligned(place, rows)]
            copies.append(pltpu.make_async_copy(ref.at[pl.ds(at * rows, rows)], there, sems.at[at, which]))
            copies[-1].start()
    return copies


def write_near_kernel(mine1_ref, mine2_ref, other1_ref, other2_ref, qkv_hbm, wo_hbm, mark_ref, qkv_ref, wo_ref, sems, *, links):
    mark_ref[...] = jnp.zeros_like(mark_ref)
    mine, other = 2 * piece_place(False, False, links), 2 * piece_place(True, False, links)
    pieces, places = (mine1_ref, mine2_ref, other1_ref, other2_ref), (mine, mine + 1, other, other + 1)
    for copy in write_pieces(pieces, places, qkv_hbm, wo_hbm, qkv_ref, wo_ref, sems):
        copy.wait()


def write_far_kernel(*refs, links):
    near, far, outs = refs[:4], refs[4:8], refs[10:]
    qkv_hbm, wo_hbm, gate_hbm, *norm_hbm, bias_hbm, qkv_ref, wo_ref, small_ref, bias_ref, columns_ref, sems, small_sems = outs
    rows = far[0].shape[0]
    for pieces, is_far in ((near, False), (far, True)):
        for at in range(4):
            place = 2 * piece_place(at > 1, is_far, links) + at % 2
            columns_ref[aligned(place, rows)] = pieces[at][:, -LANES:].astype(F32)
    half = columns_ref.shape[0] // 2
    columns = columns_ref[:half] + columns_ref[half:]
    columns = columns + pltpu.roll(columns, LANES // 2, 1)
    stacked = jnp.transpose(columns)
    small_ref[:, :half] = stacked[:16]
    small_ref[:, half:] = stacked[16:32]
    heads = gate_hbm.shape[0]
    bias_ref[...] = stacked[4:5, : bias_ref.shape[1]]
    there = [(8, heads, gate_hbm)] + [(row, 1, hbm) for row, hbm in enumerate(norm_hbm)]
    copies = []
    for at, (row, count, hbm) in enumerate(there):
        copies.append(pltpu.make_async_copy(small_ref.at[pl.ds(row, count)], hbm, small_sems.at[at]))
    copies.append(pltpu.make_async_copy(bias_ref, bias_hbm, small_sems.at[len(there)]))
    for copy in copies:
        copy.start()
    mine, other = 2 * piece_place(False, True, links), 2 * piece_place(True, True, links)
    copies += write_pieces(far, (mine, mine + 1, other, other + 1), qkv_hbm, wo_hbm, qkv_ref, wo_ref, sems)
    for copy in copies:
        copy.wait()


def in_hbm(out):
    return getattr(out, "memory_space", None) == pltpu.HBM


def out_spec(out):
    return pl.BlockSpec(memory_space=pltpu.HBM if in_hbm(out) else pltpu.VMEM)


class Job:
    def __init__(self, kernel, name, operands, outs, use):
        self.kernel, self.name, self.operands, self.outs, self.use = kernel, name, operands, outs, use


class Order:
    def __init__(self):
        self.last = ()

    def call(self, kernel, name, given, kept, outs, scratch=(), wait=(), hbm=False, onto=()):
        wait = (*self.last, *wait)
        space = pltpu.HBM if hbm else pltpu.VMEM
        given = [pltpu.with_memory_space_constraint(a, space) if hbm else a for a in given]
        kept = [pltpu.with_memory_space_constraint(a, pltpu.VMEM) for a in kept]
        got = pl.pallas_call(
            lambda *refs: kernel(*refs[len(wait) :]),
            out_shape=outs,
            in_specs=[pl.BlockSpec(memory_space=pl.ANY)] * len(wait)
            + [pl.BlockSpec(memory_space=space)] * len(given)
            + [pl.BlockSpec(memory_space=pltpu.VMEM)] * len(kept)
            + [pl.BlockSpec(memory_space=pltpu.HBM)] * len(onto),
            input_output_aliases={len(wait) + len(given) + len(kept) + at: at for at in range(len(onto))},
            out_specs=jax.tree.map(out_spec, outs),
            scratch_shapes=scratch,
            compiler_params=pltpu.CompilerParams(vmem_limit_bytes=VMEM_BYTES),
            cost_estimate=pl.CostEstimate(flops=0, bytes_accessed=0, transcendentals=0),
            name=name,
        )(*wait, *given, *kept, *onto)
        inside = [a for a, out in zip(jax.tree.leaves(got), jax.tree.leaves(outs)) if not in_hbm(out)]
        if inside:
            self.last = (min(inside, key=lambda a: a.size),)
        return got


    def run(self, *jobs):
        takes = [len(job.operands) for job in jobs]
        gives = [len(job.outs) for job in jobs]

        def kernel(*refs):
            given, made = refs[: sum(takes)], refs[sum(takes) :]
            for job, take, give in zip(jobs, takes, gives):
                job.kernel(*given[:take], *made[:give])
                given, made = given[take:], made[give:]

        operands = [a for job in jobs for a in job.operands]
        outs = tuple(out for job in jobs for out in job.outs)
        got = list(self.call(kernel, "_".join(job.name for job in jobs), operands, (), outs))
        for job, give in zip(jobs, gives):
            job.use(*got[:give])
            got = got[give:]


def kept(shape, dtype):
    return pltpu.VMEM(shape, dtype)


def shaped(shape, dtype):
    return jax.ShapeDtypeStruct(shape, dtype)


def core_swap(v):
    return jax.tree.map(lambda a: lax.ppermute(a, "mp", [(i, i ^ 1) for i in range(4)]), v)


def chip_swap(v):
    return jax.tree.map(lambda a: lax.ppermute(a, "mp", [(i, i ^ 2) for i in range(4)]), v)


def send_along(v, links):
    way = []
    for place in range(lax.axis_size("dp")):
        for spot in range(4):
            to = [place, spot]
            for link in links:
                link = link[spot % 2]
                to = [to[0], to[1] ^ 2] if link is None else [to[0] ^ (1 << link), to[1]]
            way.append((4 * place + spot, 4 * to[0] + to[1]))
    return lax.ppermute(v, ("dp", "mp"), way)


class Gather:
    def __init__(self, keep, got):
        self.first = (keep, *got)
        bits = list(range(lax.axis_size("dp").bit_length() - 1))
        self.links = [(None, 0), (0, None)] + [(bit, bit) for bit in bits[1:]]
        last = len(self.links) - 1
        self.steps = [functools.partial(self.share, at) for at in range(1, last)] + [self.swap]
        self.steps += [functools.partial(self.collect, at) for at in range(last, 0, -1)]

    def next(self):
        return self.steps.pop(0)()

    def early(self):
        return self.halve(early_kernel, "early", self.first, 0)

    def late(self, keep, got, small):
        sent = keep.shape[1] + LANES
        return self.halve(late_kernel, "late", (*self.take(), keep, *got, small), 0, sent)

    def halve(self, kernel, name, operands, at, sent=0):
        rows, columns = operands[0].shape
        shapes = (rows // 2, columns), (rows // 2, columns)
        if sent:
            shapes = (rows, columns + sent), (rows, sent)

        def use(keep, sent):
            self.keep, self.got = [keep], [send_along(sent, [self.links[at]])]

        kernel = functools.partial(kernel, links=[self.links[at]])
        return Job(kernel, name, operands, (shaped(shapes[0], F32), shaped(shapes[1], BF)), use)

    def take(self):
        pairs = [a for pair in zip(self.keep, self.got) for a in pair]
        self.keep, self.got = [], []
        return pairs

    def share(self, at):
        operands = self.take()
        if at > 1:
            return self.halve(part_kernel, "part", operands, at)
        return self.halve(meet_kernel, "meet", operands, at)

    def swap(self):
        operands = self.take()

        def use(keep):
            self.keep, self.got = [keep], [send_along(keep, [self.links[-1]])]

        return Job(whole_kernel, "whole", operands, (shaped(operands[0].shape, BF),), use)

    def collect(self, at):
        operands = self.take()
        rows, columns = operands[0].shape
        if at == 1:
            links = [self.links[at]]

            def use_parts(*parts):
                self.keep, self.got = list(parts), [send_along(part, [self.links[0]]) for part in parts]

            kernel = functools.partial(split_group_kernel, links=links)
            return Job(kernel, "split_group", operands, (shaped((rows, columns), BF),) * 2, use_parts)
        if at == len(self.links) - 1:
            kernel, name = sum_kernel, "sum"
        else:
            kernel, name, rows = functools.partial(group_kernel, links=[self.links[at]]), "group", 2 * rows

        def use(keep):
            self.keep, self.got = [keep], [send_along(keep, [self.links[at - 1]])]

        return Job(kernel, name, operands, (shaped((rows, columns), BF),), use)


class Stream:
    def __init__(self, *first):
        self.first = first
        bits = list(range(lax.axis_size("dp").bit_length() - 1))
        self.bits = [(0, 1), (1, 0)] + [(bit, bit) for bit in bits[2:]]
        self.back = [(1, 1), (0, 0)] + self.bits[2:]
        self.steps = [self.start]
        self.steps += [functools.partial(self.halve, bits) for bits in self.bits[1:-1]]
        self.steps += [self.third, self.fourth]
        self.steps += [functools.partial(self.double, at) for at in range(len(bits), 0, -1)]

    def next(self):
        return self.steps.pop(0)()

    def split(self, kernel, name, operands, shape, bits):
        def use(keep, sent):
            self.keep, self.got = keep, send_along(sent, [bits])

        return Job(kernel, name, operands, (shaped(shape, F32), shaped(shape, BF)), use)

    def start(self):
        bits = self.bits[0]
        rows, columns = self.first[0].shape
        kernel = functools.partial(first_kernel, bits=bits)
        return self.split(kernel, "first", self.first, (2, rows // 2, columns), bits)

    def halve(self, bits):
        _, rows, columns = self.keep.shape
        kernel = functools.partial(halve_kernel, bits=bits)
        return self.split(kernel, "halve", (self.keep, self.got), (2, rows // 2, columns), bits)

    def third(self):
        _, rows, columns = self.keep.shape
        bit = self.bits[-1][0]
        kernel = functools.partial(third_kernel, bit=bit)
        return self.split(kernel, "third", (self.keep, self.got), (2, rows // 2, columns), (bit, None))

    def fourth(self):
        bit = self.bits[-1][0]
        kernel = functools.partial(fourth_kernel, bit=bit)
        return self.split(kernel, "fourth", (self.keep, self.got), self.keep.shape[1:], (None, bit))

    def double(self, at):
        if at == len(self.bits):
            kernel, name, shape = add_kernel, "add", self.keep.shape
        else:
            kernel, name = functools.partial(join_kernel, bits=self.back[at]), "join"
            shape = (2 * self.keep.shape[0], self.keep.shape[1])

        def use(keep):
            self.keep, self.got = keep, send_along(keep, [self.back[at - 1]])

        return Job(kernel, name, (self.keep, self.got), (shaped(shape, BF),), use)

    def finish(self, order, outs):
        kernel = functools.partial(final_kernel, bits=self.back[0])
        rows, columns = self.keep.shape
        scratch = [pltpu.VMEM((2 * rows, columns), F32), pltpu.SemaphoreType.DMA((2,))]
        outs = (*outs, shaped((8, LANES), F32))
        return order.call(kernel, "final", (self.keep, self.got), (), outs, scratch)[:2]


def after(v, *others):
    return lax.optimization_barrier((v, others))[0]


def exchange(order, home, partner, reverse, wait=()):
    kernel = functools.partial(chain_kernel, reverse=reverse)
    total = order.call(kernel, "chain", (home, partner), (), shaped(home.shape, BF), wait=wait)
    return total, lax.ppermute(total, "mp", [(2, 0), (3, 1)] if reverse else [(0, 2), (1, 3)])


def per_device(
    layer_input,
    qkv_weight,
    gate_weight,
    gate_bias,
    out_weight,
    inner_weight,
    outer_weight,
    leading_norm_gain,
    leading_norm_bias,
    trailing_norm_gain,
    trailing_norm_bias,
    random_features,
    output_grad,
):
    seqs, length, width = layer_input.shape
    heads, head, feat = random_features.shape
    pairs = heads // 2
    count = seqs * length
    hidden = inner_weight.shape[1]
    bias = gate_bias.reshape(1, heads)
    gain1, shift1 = leading_norm_gain.reshape(1, width), leading_norm_bias.reshape(1, width)
    gain2, shift2 = trailing_norm_gain.reshape(1, width), trailing_norm_bias.reshape(1, width)

    n_dp = lax.axis_size("dp")
    order = Order()
    halves = order.call(
        pack_kernel,
        "pack",
        (inner_weight, outer_weight),
        (),
        shaped((2, width // 2, hidden), BF),
        [pltpu.SemaphoreType.DMA((2,))],
        hbm=True,
    )
    half_chip = chip_swap(halves)
    inner_core, outer_core = core_swap(inner_weight), core_swap(outer_weight)

    by_seq = (seqs, length, width)
    gates = (seqs, length, LANES)
    states = (pairs, LANES + EXTRA, 2 * feat)
    gate_rows = jnp.transpose(gate_weight)
    sources = (layer_input, qkv_weight, gate_rows, bias, gain1, shift1, random_features)
    normed1, values, c, admit, c_row, a_row, phi_k, away, home = order.call(
        keys_kernel,
        "keys",
        sources,
        (),
        (
            kept((count, width), BF),
            kept(by_seq, F32),
            kept(gates, F32),
            kept(gates, F32),
            kept((seqs, heads, length), F32),
            kept((seqs, heads, length), F32),
            kept((seqs, heads, length, 2 * feat), BF),
            kept(states, BF),
            kept(states, BF),
        ),
        [pltpu.VMEM((width, 2 * width) if a is qkv_weight else a.shape, a.dtype) for a in sources]
        + [pltpu.SemaphoreType.DMA((len(sources),))],
        hbm=True,
    )
    partner_home, partner_away = core_swap(away), core_swap(home)
    total, got = exchange(order, home, partner_home, False)
    half_chip = after(half_chip, total)
    half_twin = lax.ppermute(half_chip, "dp", [(i, i ^ 1) for i in range(n_dp)])

    phi_q, scores, num = order.call(
        scores_kernel,
        "scores",
        (qkv_weight, random_features),
        (normed1, phi_k, values, c, c_row, a_row),
        (
            kept((seqs, heads, length, 2 * feat), BF),
            kept((seqs, heads, length, 2 * length), BF),
            kept((seqs, heads, length, LANES), F32),
        ),
        wait=(half_chip,),
    )
    got = after(got, num)
    swapped = core_swap(got)
    half_both = core_swap(half_chip)
    full, start, mixed_low, resid, normed2, sden, inverse, xhat2, scale2 = order.call(
        mix_kernel,
        "mix",
        (layer_input, got, swapped, partner_home, partner_away, out_weight, gain2, shift2),
        (phi_q, c, num),
        (
            kept((seqs, heads, length, LANES), F32),
            kept((seqs, *states), BF),
            kept(by_seq, BF),
            kept(by_seq, F32),
            kept(by_seq, BF),
            kept(gates, F32),
            kept(gates, F32),
            kept(by_seq, F32),
            kept(gates, F32),
        ),
    )

    normed2, mixed_low = (a.reshape(count, width) for a in (normed2, mixed_low))
    half_twin = after(half_twin, normed2)
    half_both_twin = core_swap(half_twin)
    shape = (count, width)
    grads = (width + hidden, width)
    out_part, dn2, out_low, keep0, send0 = order.call(
        feed_near_kernel,
        "feed_near",
        (output_grad.reshape(shape), inner_weight, outer_weight, inner_core, outer_core),
        (normed2, resid.reshape(shape)),
        (kept(shape, F32), kept(shape, F32), kept(shape, BF), shaped(grads, F32), shaped(grads, BF)),
    )
    got0 = core_swap(send0)
    far = pltpu.VMEM((2, width, hidden), BF)
    out_part, dn2, send1 = order.call(
        feed_far_kernel,
        "feed_both",
        (half_both, half_both_twin),
        (normed2, out_low, out_part, dn2),
        (kept(shape, F32), kept(shape, F32), shaped(grads, BF)),
        [far],
    )
    got1 = core_swap(send1)
    layer_out, dn2, keep1 = order.call(
        feed_last_kernel,
        "feed_chip",
        (half_chip, half_twin),
        (normed2, out_low, out_part, dn2),
        (pltpu.HBM(shape, F32), kept(shape, F32), shaped(grads, F32)),
        [far, pltpu.VMEM(shape, F32), pltpu.SemaphoreType.DMA],
    )
    stream = Stream(keep0, keep1, got0, got1)
    order.run(stream.next())

    dres, low, sums2, num_grads, r, away_grads, home_grads = order.call(
        turn_kernel,
        "turn",
        (output_grad, gain2, out_weight),
        (dn2.reshape(by_seq), xhat2, scale2, full, sden, inverse, phi_q, c),
        (
            kept(by_seq, F32),
            kept((count, width), BF),
            kept((8, width), F32),
            kept((seqs, heads, length, 2 * LANES), BF),
            kept(gates, F32),
            kept(states, BF),
            kept(states, BF),
        ),
    )
    partner_home_grads, partner_away_grads = core_swap(away_grads), core_swap(home_grads)
    _, got_grads = exchange(order, home_grads, partner_home_grads, True)

    q_grad, k_part, v_part, k_col = order.call(
        back_kernel,
        "back",
        (random_features,),
        (phi_q, phi_k, values, num_grads, scores, c, c_row, a_row, start),
        (
            kept((count, width), BF),
            kept(by_seq, F32),
            kept(by_seq, F32),
            kept(gates, F32),
        ),
    )
    dn1_part, xhat1, scale1, keep1, *send1 = order.call(
        products_kernel,
        "products",
        (layer_input.reshape(shape), qkv_weight),
        (mixed_low, low, normed1, q_grad),
        (
            kept(shape, F32),
            kept(shape, F32),
            kept((count, LANES), F32),
            shaped((width // 2, 2 * width), F32),
            *[shaped((width // 4, 2 * width), BF)] * 2,
        ),
    )
    gather = Gather(keep1, core_swap(send1))
    got_grads = after(got_grads, keep1)
    swapped_grads = core_swap(got_grads)

    order.run(stream.next())
    order.run(gather.early())
    kv_grad, logit_low, bias_sum, keep2, *send2 = order.call(
        cross_kernel,
        "cross",
        (got_grads, swapped_grads, partner_home_grads, partner_away_grads, random_features),
        (away, home, start, phi_k, values, c, admit, r, k_col, k_part, v_part, normed1),
        (
            kept((count, 2 * width), BF),
            kept((count, LANES), BF),
            kept((8, LANES), F32),
            shaped((width // 2, 2 * width), F32),
            *[shaped((width // 8, 2 * width), BF)] * 4,
        ),
    )
    got2 = core_swap(send2)
    while len(stream.steps) > len(stream.bits) + 1:
        order.run(stream.next())
    dn1, small = order.call(
        close_kernel,
        "close",
        (qkv_weight, gate_rows),
        (dn1_part, xhat1, kv_grad, logit_low, bias_sum, normed1, sums2),
        (kept(shape, F32), shaped((width // 2, LANES), F32)),
    )
    order.run(gather.late(keep2, got2, small))
    dx, _ = order.call(
        input_kernel,
        "input",
        (gain1,),
        (dn1, xhat1, scale1, dres.reshape(shape)),
        (pltpu.HBM(shape, F32), shaped((8, LANES), F32)),
        [pltpu.VMEM(shape, F32), pltpu.SemaphoreType.DMA],
    )
    while len(gather.steps) > 5:
        order.run(gather.next())
    while len(stream.steps) > 3:
        order.run(stream.next())
    order.run(gather.next(), stream.next())
    order.run(gather.next(), stream.next())
    order.run(gather.next())
    order.run(gather.next(), stream.next())
    order.run(gather.next())
    inner_total, outer_total = stream.finish(order, (pltpu.HBM((width, hidden), F32), pltpu.HBM((hidden, width), F32)))
    links = gather.links[0]
    mine = gather.keep
    near = (*mine, *core_swap(mine))
    scratch = [
        pltpu.VMEM((width // 2, 3 * width), F32), pltpu.VMEM((width // 2, width), F32), pltpu.SemaphoreType.DMA((4, 2)),
    ]
    big = (pltpu.HBM((width, 3 * width), F32), pltpu.HBM((width, width), F32))
    *begun, _ = order.call(
        functools.partial(write_near_kernel, links=links),
        "write_near",
        near,
        (),
        (*big, shaped((8, LANES), F32)),
        scratch,
    )
    got = after(gather.got, order.last)
    far = (*got, *core_swap(got))
    qkv_grad, wo_grad, gate_grad, *norm_grads, bias_grad = order.call(
        functools.partial(write_far_kernel, links=links),
        "write_far",
        (*near, *far),
        (),
        (*big, pltpu.HBM((heads, width), F32), *[pltpu.HBM((1, width), F32)] * 4, pltpu.HBM((1, heads), F32)),
        [
            *scratch[:2], pltpu.VMEM((16, width), F32), pltpu.VMEM((1, heads), F32), pltpu.VMEM((width, LANES), F32),
            scratch[2], pltpu.SemaphoreType.DMA((6,)),
        ],
        onto=begun,
    )
    return (
        layer_out.reshape(by_seq),
        dx.reshape(by_seq),
        qkv_grad,
        jnp.transpose(gate_grad),
        bias_grad.reshape(heads),
        wo_grad,
        inner_total,
        outer_total,
        *(a.reshape(width) for a in norm_grads),
    )


def solution(mesh):
    in_specs = (
        P("dp", "mp", None),
        P(),
        P(),
        P(),
        P(),
        P(None, "mp"),
        P("mp", None),
        P(),
        P(),
        P(),
        P(),
        P(),
        P("dp", "mp", None),
    )
    out_specs = (
        P("dp", "mp", None),
        P("dp", "mp", None),
        P(),
        P(),
        P(),
        P(),
        P(None, "mp"),
        P("mp", None),
        P(),
        P(),
        P(),
        P(),
    )
    return jax.shard_map(
        per_device, mesh=mesh, in_specs=in_specs, out_specs=out_specs, check_vma=False
    )
```

```python
import functools
import math

import jax
import jax.numpy as jnp
from jax import lax
from jax.experimental import pallas as pl
from jax.experimental.pallas import tpu as pltpu
from jax.sharding import PartitionSpec as P

BF = jnp.bfloat16
F32 = jnp.float32
epsilon = 1e-05
guard = 0.01
LANES = 128
EXTRA = 16
VMEM_BYTES = 16 * 1024 * 1024


def nn(a, b):
    return lax.dot_general(a, b, (((1,), (0,)), ((), ())), preferred_element_type=F32)


def nt(a, b):
    return lax.dot_general(a, b, (((1,), (1,)), ((), ())), preferred_element_type=F32)


def tn(a, b):
    return lax.dot_general(a, b, (((0,), (0,)), ((), ())), preferred_element_type=F32)


def two_terms(v):
    high = v.astype(BF)
    return high, (v - high.astype(F32)).astype(BF)


def iota(shape, dim):
    return lax.broadcasted_iota(jnp.int32, shape, dim)


def triangle(length, upper):
    rows, cols = iota((length, length), 0), iota((length, length), 1)
    return jnp.where((cols >= rows) if upper else (rows >= cols), 1.0, 0.0).astype(BF)


def running_sum(v, upper):
    ones = triangle(v.shape[0], upper)
    high, rest = two_terms(v)
    low = (v - high.astype(F32) - rest.astype(F32)).astype(BF)
    return nn(ones, high) + nn(ones, rest) + nn(ones, low)


def norm_rows(v):
    centred = v - jnp.mean(v, axis=-1, keepdims=True)
    scale = lax.rsqrt(jnp.mean(centred * centred, axis=-1, keepdims=True) + epsilon)
    return centred * scale, scale


def norm_rows_backward(grad, xhat, scale, gain):
    g = grad * gain
    return scale * (
        g
        - jnp.mean(g, axis=-1, keepdims=True)
        - xhat * jnp.mean(g * xhat, axis=-1, keepdims=True)
    )


def pair_frequencies(freq_ref, pair):
    even, odd = freq_ref[2 * pair], freq_ref[2 * pair + 1]
    none = jnp.zeros_like(even)
    return jnp.concatenate(
        [jnp.concatenate([even, none], axis=1), jnp.concatenate([none, odd], axis=1)], axis=0
    )


def scaled_sine_cosine(angles, scale):
    turns = jnp.floor(angles * (1.0 / math.pi) + 0.5)
    r = angles - turns * 3.140625
    r = r - turns * 0.0009675025939941406
    r = r - turns * 1.509958e-07
    odd = turns - 2.0 * jnp.floor(turns * 0.5)
    sign = scale - (2.0 * scale) * odd
    r2 = r * r
    sine = -0.00018362251175623582 * r2 + 0.008306273552368303
    sine = sine * r2 - 0.1666482311215342
    sine = sine * r2 + 0.9999966031254778
    cosine = -0.0012711240835350962 * r2 + 0.041487518673719546
    cosine = cosine * r2 - 0.4999123281046797
    cosine = cosine * r2 + 0.9999933132015835
    return sine * (r * sign), cosine * sign


def pair_features(values, freq, scale):
    high, low = two_terms(values)
    freq_high, freq_low = two_terms(freq)
    both = jnp.concatenate([freq_high, freq_high], axis=0)
    angles = nn(jnp.concatenate([high, low], axis=1), both) + nn(high, freq_low)
    sine, cosine = scaled_sine_cosine(angles, scale)
    sine, cosine = sine.astype(BF), cosine.astype(BF)
    feat = freq.shape[1] // 2
    return [
        jnp.concatenate([sine[:, h * feat : (h + 1) * feat], cosine[:, h * feat : (h + 1) * feat]], axis=1)
        for h in (0, 1)
    ]


def own_lanes(shape, half):
    lane = iota(shape, len(shape) - 1)
    return (lane >= LANES // 2) if half else (lane < LANES // 2)


def one_lane(shape, half):
    return iota(shape, len(shape) - 1) == (0 if half else LANES // 2)


def second_lane(shape, half):
    return iota(shape, len(shape) - 1) == (1 if half else LANES // 2 + 1)


def with_ones(values, half, both=False):
    v = values.astype(F32)
    ones = one_lane(v.shape, half) | (both & second_lane(v.shape, half))
    return jnp.where(own_lanes(v.shape, half), v, jnp.where(ones, 1.0, 0.0))


def pack_states(even, odd, decay_even, decay_odd):
    half = LANES // 2
    row = iota(even.shape, 0)
    states = jnp.where(row < half, even, odd).astype(BF)
    extra = iota((EXTRA, even.shape[1]), 0)
    parts = []
    for value in (even[half : half + 1], odd[0:1], decay_even, decay_odd):
        high = value.astype(BF).astype(F32)
        parts += [high, value - high]
    rows = jnp.zeros((EXTRA, even.shape[1]), F32)
    for at, part in enumerate(parts):
        rows = jnp.where(extra == at, part, rows)
    return states, rows.astype(BF)


def extra_row(packed, at):
    at = LANES + 2 * at
    return packed[at : at + 1] + packed[at + 1 : at + 2]


def decays(packed):
    return extra_row(packed, 2), extra_row(packed, 3)


def unpack_states(packed):
    half = LANES // 2
    states = packed[:LANES]
    row = iota(states.shape, 0)
    even = jnp.where(row < half, states, jnp.where(row == half, extra_row(packed, 0), 0.0))
    odd = jnp.where(row >= half, states, jnp.where(row == 0, extra_row(packed, 1), 0.0))
    return even, odd


def join_states(first, second):
    return [
        a + decay * b
        for a, b, decay in zip(unpack_states(first), unpack_states(second), decays(first))
    ]


def as_operand(state, half):
    at = 0 if half else LANES // 2
    norm = state[at : at + 1]
    rest = norm - norm.astype(BF).astype(F32)
    return jnp.where(iota(state.shape, 0) == at + 1, rest, state).astype(BF)


def decay_weights(c_col, c_row, a_row):
    length = c_col.shape[0]
    gap = jnp.minimum(c_col - c_row, 0.0)
    causal = iota((length, length), 0) >= iota((length, length), 1)
    return jnp.where(causal, jnp.exp(gap) * a_row, 0.0)


def head_lanes(pair):
    shape = (2 * LANES, LANES)
    head = 2 * pair + (iota(shape, 0) % LANES) // (LANES // 2)
    return jnp.where(iota(shape, 1) == head, 1.0, 0.0).astype(BF)


def norm_lanes(pair):
    shape = (2 * LANES, LANES)
    row = iota(shape, 0) % LANES
    of_even, of_odd = row // 2 == LANES // 4, row // 2 == 0
    taken = (of_even & (iota(shape, 1) == 2 * pair)) | (of_odd & (iota(shape, 1) == 2 * pair + 1))
    return jnp.where(taken, 1.0, 0.0).astype(BF)


def lane_sum(v):
    return jnp.sum(v, axis=1, keepdims=True)


def each(count, step):
    lax.fori_loop(0, count, lambda i, none: (step(i), none)[1], 0)


def wide(v, axis):
    none = list(v.shape)
    none[axis] = LANES - v.shape[axis]
    return jnp.concatenate([v, jnp.zeros(none, v.dtype)], axis=axis)


def aligned(at, size):
    return pl.ds(pl.multiple_of(at * size, size), size)


def my_core():
    return lax.axis_index("mp") % 2


def my_chip():
    return lax.axis_index("mp") // 2


def pack_kernel(inner_ref, outer_ref, out_ref, sems):
    rows = out_ref.shape[1]
    mine = aligned(lax.axis_index("dp") % 2, rows)
    copies = [
        pltpu.make_async_copy(source.at[mine], out_ref.at[i], sems.at[i])
        for i, source in enumerate((inner_ref, outer_ref))
    ]
    for copy in copies:
        copy.start()
    for copy in copies:
        copy.wait()


def by_place(of_sequence):
    even = my_core() == 0
    one, two = of_sequence
    return jnp.where(even, two, one), jnp.where(even, one, two)


def put_states(pair, packed, away_ref, home_ref):
    for rows, parts in ((slice(0, LANES), [p[0] for p in packed]), (slice(LANES, None), [p[1] for p in packed])):
        away_ref[pair, rows], home_ref[pair, rows] = by_place(parts)


def keys_kernel(
    x_hbm, wqkv_hbm, gw_hbm, gb_hbm, gain_hbm, shift_hbm, freq_hbm,
    n1_ref, v_ref, c_ref, a_ref, crow_ref, arow_ref, pk_ref, away_ref, home_ref,
    x_ref, w_ref, gw_ref, gb_ref, gain_ref, shift_ref, freq_ref, sems,
):
    heads, _, feat = freq_ref.shape
    seqs, length, width = x_ref.shape
    sources = (x_hbm, gain_hbm, shift_hbm, gw_hbm, gb_hbm, wqkv_hbm.at[:, pl.ds(width, 2 * width)], freq_hbm)
    buffers = (x_ref, gain_ref, shift_ref, gw_ref, gb_ref, w_ref, freq_ref)
    copies = [
        pltpu.make_async_copy(source, buffer, sems.at[i])
        for i, (source, buffer) in enumerate(zip(sources, buffers))
    ]
    for copy in copies:
        copy.start()
    for copy in copies[:5]:
        copy.wait()
    scale = 1.0 / math.sqrt(feat)
    xhat, _ = norm_rows(x_ref[...].reshape(seqs * length, width))
    n1 = (xhat * gain_ref[...] + shift_ref[...]).astype(BF)
    n1_ref[...] = n1
    z = nt(n1, wide(gw_ref[...], 0)) + wide(gb_ref[...], 1)
    e = jnp.exp(-jnp.abs(z))
    log_keep = jnp.minimum(z, 0.0) - jnp.log1p(e)
    inverse = 1.0 / (1.0 + e)
    admit_all = jnp.where(z > 0.0, e * inverse, inverse)
    tails, decay = [], []
    for s in range(seqs):
        rows = slice(s * length, (s + 1) * length)
        c = running_sum(log_keep[rows], False)
        admit = admit_all[rows]
        c_ref[s] = c
        a_ref[s] = admit
        crow_ref[s] = jnp.transpose(c)[:heads]
        arow_ref[s] = jnp.transpose(admit)[:heads]
        last = c[length - 1 :]
        tails.append(jnp.exp(last - c) * admit)
        decay.append(jnp.exp(last))
    for copy in copies[5:]:
        copy.wait()
    keys = nn(n1, w_ref[:, :width])
    values = nn(n1, w_ref[:, width:])
    v_ref[...] = values.reshape(v_ref.shape)
    for pair in range(heads // 2):
        lanes = slice(pair * LANES, (pair + 1) * LANES)
        phi = pair_features(keys[:, lanes], pair_frequencies(freq_ref, pair), scale)
        packed = []
        for s in range(seqs):
            rows = slice(s * length, (s + 1) * length)
            states = []
            for half in (0, 1):
                h = 2 * pair + half
                phi_k = phi[half][rows]
                pk_ref[s, h] = phi_k
                weighted = with_ones(values[rows, lanes], half) * tails[s][:, h : h + 1]
                both = tn(jnp.concatenate(two_terms(weighted), axis=1), phi_k)
                states.append(both[:LANES] + both[LANES:])
            h = 2 * pair
            packed.append(pack_states(*states, decay[s][:, h : h + 1], decay[s][:, h + 1 : h + 2]))
        put_states(pair, packed, away_ref, home_ref)


def scores_kernel(wqkv_ref, freq_ref, n1_ref, pk_ref, v_ref, c_ref, crow_ref, arow_ref, pq_ref, p_ref, num_ref):
    seqs, heads, length, _ = pk_ref.shape
    scale = 1.0 / math.sqrt(freq_ref.shape[2])
    queries = nn(n1_ref[...], wqkv_ref[:, : n1_ref.shape[1]])
    for pair in range(heads // 2):
        lanes = slice(pair * LANES, (pair + 1) * LANES)
        phi = pair_features(queries[:, lanes], pair_frequencies(freq_ref, pair), scale)
        for s in range(seqs):
            for half in (0, 1):
                h = 2 * pair + half
                phi_q = phi[half][s * length : (s + 1) * length]
                pq_ref[s, h] = phi_q
                v = with_ones(v_ref[s, :, lanes], half)
                weights = decay_weights(
                    c_ref[s, :, h : h + 1], crow_ref[s, h : h + 1], arow_ref[s, h : h + 1]
                )
                p = jnp.concatenate(two_terms(nt(phi_q, pk_ref[s, h]) * weights), axis=1)
                p_ref[s, h] = p
                v = jnp.concatenate(two_terms(v), axis=1)
                both = nn(p, jnp.concatenate([v, v], axis=0))
                num_ref[s, h] = both[:, :LANES] + both[:, LANES:]


def mix_kernel(
    x_ref, got_ref, swapped_ref, partner_home_ref, partner_away_ref, wo_ref, gain_ref, shift_ref, pq_ref, c_ref, num_ref,
    full_ref, start_ref, mixed_ref, resid_ref, n2_ref, sden_ref, inverse_ref, xhat_ref, scale_ref,
):
    seqs, heads = pq_ref.shape[:2]
    core = my_core()

    def one(s):
        growth = jnp.exp(c_ref[s])
        sdens = jnp.zeros_like(growth)
        for pair in range(heads // 2):
            before = jnp.where(s == core, got_ref[pair], swapped_ref[pair]).astype(F32)
            partner = jnp.where(s == core, partner_home_ref[pair], partner_away_ref[pair]).astype(F32)
            states = [
                jnp.where(core == 0, a, b)
                for a, b in zip(unpack_states(before), join_states(partner, before))
            ]
            none = jnp.zeros((1, 1), F32)
            main, rest = pack_states(*states, none, none)
            start_ref[s, pair, :LANES] = main
            start_ref[s, pair, LANES:] = rest
            fulls = []
            for half in (0, 1):
                h = 2 * pair + half
                full = num_ref[s, h] + growth[:, h : h + 1] * nt(
                    pq_ref[s, h], as_operand(states[half], half)
                )
                full_ref[s, h] = full
                fulls.append(full)
            beside = jnp.where(own_lanes(fulls[0].shape, 0), fulls[1], fulls[0])
            sdens = sdens + nn(jnp.concatenate(two_terms(beside), axis=1), norm_lanes(pair))
        inverse = lax.rsqrt(sdens * sdens + guard)
        sden_ref[s] = sdens
        inverse_ref[s] = inverse
        for pair in range(heads // 2):
            mixed = [full_ref[s, h] * inverse[:, h : h + 1] for h in (2 * pair, 2 * pair + 1)]
            pair_mixed = jnp.where(own_lanes(mixed[0].shape, 0), mixed[0], mixed[1])
            mixed_ref[s, :, pair * LANES : (pair + 1) * LANES] = pair_mixed.astype(BF)
        resid = x_ref[s] + nn(mixed_ref[s], wo_ref[...])
        resid_ref[s] = resid
        xhat, scale = norm_rows(resid)
        xhat_ref[s] = xhat
        scale_ref[s] = jnp.broadcast_to(scale, scale_ref.shape[1:])
        n2_ref[s] = (xhat * gain_ref[...] + shift_ref[...]).astype(BF)

    for s in range(seqs):
        one(s)


def gelu_and_slope(v):
    root = math.sqrt(2.0 / math.pi)
    v2 = v * v
    t = jnp.tanh(v * (root + (root * 0.044715) * v2))
    half = 0.5 * (1.0 + t)
    slope = half + (0.5 * v) * (1.0 - t * t) * (root + (root * 3.0 * 0.044715) * v2)
    return v * half, slope


def feed_block(n2, out_low, wi_ref, wo_ref):
    active, slope = gelu_and_slope(nn(n2, wi_ref[...]))
    active = active.astype(BF)
    pre_grad = (nt(out_low, wo_ref[...]) * slope).astype(BF)
    return nn(active, wo_ref[...]), nt(pre_grad, wi_ref[...]), tn(n2, pre_grad), tn(active, out_low)


def halves_together(far_ref, one, two):
    twin = lax.axis_index("dp") % 2
    rows = one.shape[1]
    for which in range(2):
        far_ref[which, aligned(twin, rows)] = one[which]
        far_ref[which, aligned(1 - twin, rows)] = two[which]


def feed_near_kernel(og_ref, wi0, wo0, wi2, wo2, n2_ref, resid_ref, out_ref, dn2_ref, low_ref, keep_ref, send_ref):
    low_ref[...] = og_ref[...].astype(BF)
    n2, out_low = n2_ref[...], low_ref[...]
    rows = n2.shape[1]
    out, dn2, inner, outer = feed_block(n2, out_low, wi2, wo2)
    send_ref[:rows] = inner.astype(BF)
    send_ref[rows:] = outer.astype(BF)
    out_own, dn2_own, inner, outer = feed_block(n2, out_low, wi0, wo0)
    keep_ref[:rows] = inner
    keep_ref[rows:] = outer
    out_ref[...] = resid_ref[...] + out + out_own
    dn2_ref[...] = dn2 + dn2_own


def feed_far_kernel(half_ref, twin_ref, n2_ref, low_ref, part_ref, dn2_part_ref, out_ref, dn2_ref, grad_ref, far_ref):
    twin = lax.axis_index("dp") % 2
    rows = half_ref.shape[1]
    for which in range(2):
        far_ref[which, aligned(twin, rows)] = half_ref[which]
        far_ref[which, aligned(1 - twin, rows)] = twin_ref[which]
    n2 = n2_ref[...]
    out, dn2, inner, outer = feed_block(n2, low_ref[...], far_ref.at[0], far_ref.at[1])
    out_ref[...] = part_ref[...] + out
    dn2_ref[...] = dn2_part_ref[...] + dn2
    rows = n2.shape[1]
    grad_ref[:rows] = inner.astype(grad_ref.dtype)
    grad_ref[rows:] = outer.astype(grad_ref.dtype)


def feed_last_kernel(
    half_ref, twin_ref, n2_ref, low_ref, part_ref, dn2_part_ref, out_hbm, dn2_ref, grad_ref, far_ref, out_ref, sem
):
    feed_far_kernel(half_ref, twin_ref, n2_ref, low_ref, part_ref, dn2_part_ref, out_ref, dn2_ref, grad_ref, far_ref)
    copy = pltpu.make_async_copy(out_ref, out_hbm, sem)
    copy.start()
    copy.wait()


def place_bit(bits):
    place = lax.axis_index("dp")
    return jnp.where(my_core() == 0, (place // (1 << bits[0])) % 2, (place // (1 << bits[1])) % 2)


def split_rows(total, bits, mine_ref, send_ref):
    rows = mine_ref.shape[1]
    high = place_bit(bits) == 1
    first, second = total[:, :rows], total[:, rows:]
    mine_ref[...] = jnp.where(high, second, first)
    send_ref[...] = jnp.where(high, first, second).astype(BF)


def halve_kernel(keep_ref, got_ref, mine_ref, send_ref, *, bits):
    split_rows(keep_ref[...] + got_ref[...].astype(F32), bits, mine_ref, send_ref)


def first_kernel(keep0_ref, keep1_ref, got0_ref, got1_ref, mine_ref, send_ref, *, bits):
    for block, (keep_ref, got_ref) in enumerate(((keep0_ref, got0_ref), (keep1_ref, got1_ref))):
        total = (keep_ref[...] + got_ref[...].astype(F32))[None]
        split_rows(total, bits, mine_ref.at[block : block + 1], send_ref.at[block : block + 1])


def third_kernel(keep_ref, got_ref, mine_ref, send_ref, *, bit):
    rows = mine_ref.shape[1]
    total = keep_ref[...] + got_ref[...].astype(F32)
    low, high = total[:, :rows], total[:, rows:]
    by_bit = place_bit((bit, bit)) == 1
    one, two = jnp.where(by_bit, high, low), jnp.where(by_bit, low, high)
    even = my_core() == 0
    for part in range(2):
        of_block = (low, high)[part]
        mine_ref[part] = jnp.where(even, one[part], of_block[0])
        send_ref[part] = jnp.where(even, two[part], of_block[1]).astype(BF)


def fourth_kernel(keep_ref, got_ref, mine_ref, send_ref, *, bit):
    total = keep_ref[...] + got_ref[...].astype(F32)
    second = (my_core() == 1) & (place_bit((bit, bit)) == 1)
    mine_ref[...] = jnp.where(second, total[1], total[0])
    send_ref[...] = jnp.where(second, total[0], total[1]).astype(BF)


def add_kernel(keep_ref, got_ref, out_ref):
    out_ref[...] = (keep_ref[...] + got_ref[...].astype(F32)).astype(out_ref.dtype)


def joined(mine_ref, got_ref, bits):
    high = place_bit(bits) == 1
    mine, got = mine_ref[...].astype(F32), got_ref[...].astype(F32)
    return jnp.concatenate([jnp.where(high, got, mine), jnp.where(high, mine, got)], axis=0)


def join_kernel(mine_ref, got_ref, out_ref, *, bits):
    out_ref[...] = joined(mine_ref, got_ref, bits).astype(BF)


def final_kernel(mine_ref, got_ref, inner_hbm, outer_hbm, mark_ref, whole_ref, sems, *, bits):
    mark_ref[...] = jnp.zeros_like(mark_ref)
    both = joined(mine_ref, got_ref, bits)
    quarter = both.shape[0] // 4
    one, two = both[quarter : 2 * quarter], both[2 * quarter : 3 * quarter]
    even = my_core() == 0
    whole_ref[:quarter] = both[:quarter]
    whole_ref[quarter : 2 * quarter] = jnp.where(even, two, one)
    whole_ref[2 * quarter : 3 * quarter] = jnp.where(even, one, two)
    whole_ref[3 * quarter :] = both[3 * quarter :]
    rows = inner_hbm.shape[0]
    copies = [
        pltpu.make_async_copy(whole_ref.at[pl.ds(at * rows, rows)], out_hbm, sems.at[at])
        for at, out_hbm in enumerate((inner_hbm, outer_hbm))
    ]
    for copy in copies:
        copy.start()
    for copy in copies:
        copy.wait()


def turn_one(
    which, og_ref, gain_ref, wo_ref, dn2_ref, xhat_ref, scale_ref, full_ref, sden_ref, inverse_ref, pq_ref, c_ref,
    dres_ref, low_ref, sums_ref, ng_ref, r_ref,
):
    seqs, heads, length, _ = pq_ref.shape
    packed = [[] for _ in range(seqs)]

    def one(s):
        xhat = xhat_ref[s]
        dn2 = dn2_ref[s]
        dres = og_ref[s] + norm_rows_backward(dn2, xhat, scale_ref[s, :, :1], gain_ref[...])
        dres_ref[s] = dres
        low = dres.astype(BF)
        low_ref[s * length : (s + 1) * length] = low
        sums_ref[2:3] += jnp.sum(dn2 * xhat, axis=0, keepdims=True)
        sums_ref[3:4] += jnp.sum(dn2, axis=0, keepdims=True)
        dmixed = nt(low, wo_ref[...])
        c = c_ref[s]
        growth = jnp.exp(c)
        decay = jnp.exp(c[length - 1 :])
        lane = iota(c.shape, 1)
        sden, inverse = sden_ref[s], inverse_ref[s]
        dots = jnp.zeros_like(c)
        for pair in range(heads // 2):
            g = dmixed[:, pair * LANES : (pair + 1) * LANES]
            h = 2 * pair
            values = jnp.where(own_lanes(g.shape, 0), full_ref[s, h], full_ref[s, h + 1])
            dots = dots + nn(jnp.concatenate(two_terms(g * values), axis=1), head_lanes(pair))
        dots = dots * inverse
        inverse2 = inverse * inverse
        r_ref[s] = dots * inverse2 * guard
        sden_grads = -dots * sden * inverse2
        growing = sden_grads * growth
        lifting = inverse * growth
        for pair in range(heads // 2):
            g = dmixed[:, pair * LANES : (pair + 1) * LANES]
            states = []
            for half in (0, 1):
                h = 2 * pair + half
                mine, one_at = own_lanes(g.shape, half), one_lane(g.shape, half)
                column = slice(h, h + 1)
                grads = jnp.where(mine, g * inverse[:, column], jnp.where(one_at, sden_grads[:, column], 0.0))
                ng_ref[s, h] = jnp.concatenate(two_terms(grads), axis=1)
                lifted = jnp.where(mine, g * lifting[:, column], jnp.where(one_at, growing[:, column], 0.0))
                both = tn(jnp.concatenate(two_terms(lifted), axis=1), pq_ref[s, h])
                states.append(both[:LANES] + both[LANES:])
            h = 2 * pair
            packed[s].append(pack_states(*states, decay[:, h : h + 1], decay[:, h + 1 : h + 2]))

    one(which)
    return packed[which]


def turn_first_kernel(*refs):
    *refs, packed_ref = refs
    refs[13][...] = jnp.zeros_like(refs[13])
    for pair, (main, rest) in enumerate(turn_one(0, *refs)):
        packed_ref[pair, :LANES] = main
        packed_ref[pair, LANES:] = rest


def turn_second_kernel(*refs):
    given, packed_ref, refs = refs[:11], refs[11], refs[17:]
    *made, away_ref, home_ref = refs
    for pair, mine in enumerate(turn_one(1, *given, *made)):
        before = packed_ref[pair, :LANES], packed_ref[pair, LANES:]
        put_states(pair, (before, mine), away_ref, home_ref)


def angle_grads(phi, dphi):
    feat = phi.shape[1] // 2
    phi = phi.astype(F32)
    return phi[:, feat:] * dphi[:, :feat] - phi[:, :feat] * dphi[:, feat:]


def weight_grads(left_ref, right_ref, keep_ref, send_refs):
    rows = keep_ref.shape[0]
    core = my_core()
    keep_ref[...] = tn(left_ref[:, aligned(core, rows)], right_ref[...])
    away = tn(left_ref[:, aligned(1 - core, rows)], right_ref[...]).astype(BF)
    rows //= len(send_refs)
    for part, send_ref in enumerate(send_refs):
        send_ref[...] = away[part * rows : (part + 1) * rows]


def back_kernel(
    freq_ref, pq_ref, pk_ref, v_ref, ng_ref, p_ref, c_ref, crow_ref, arow_ref, start_ref,
    qg_ref, kg_ref, vg_ref, kcol_ref,
):
    seqs, heads, length, _ = pq_ref.shape

    def one(s):
        tokens = aligned(s, length)
        c = c_ref[s]
        growth = jnp.exp(c)
        lane = iota(c.shape, 1)
        kcol = jnp.zeros_like(c)
        for pair in range(heads // 2):
            at = pair * LANES
            freq = pair_frequencies(freq_ref, pair).astype(BF)
            states = unpack_states(start_ref[s, pair].astype(F32))
            q_angles, k_angles, v_grads = [], [], []
            for half in (0, 1):
                h = 2 * pair + half
                phi_q, phi_k = pq_ref[s, h], pk_ref[s, h]
                grads = ng_ref[s, h, :, :LANES]
                v = with_ones(v_ref[s, :, at : at + LANES], half)
                weights = decay_weights(c[:, h : h + 1], crow_ref[s, h : h + 1], arow_ref[s, h : h + 1])
                dk = (nt(grads, v.astype(BF)) * weights).astype(BF)
                lifted = (grads.astype(F32) * growth[:, h : h + 1]).astype(BF)
                dphi_q = nn(dk, phi_k) + nn(lifted, states[half].astype(BF))
                q_angles.append(angle_grads(phi_q, dphi_q))
                k_angles.append(angle_grads(phi_k, tn(dk, phi_q)))
                both = tn(p_ref[s, h], ng_ref[s, h])
                both = both[:length] + both[length:]
                dv = both[:, :LANES] + both[:, LANES:]
                v_grads.append(dv)
                kcol = jnp.where(lane == h, lane_sum(v * dv), kcol)
            qg_ref[tokens, at : at + LANES] = nt(
                jnp.concatenate(q_angles, axis=1).astype(BF), freq
            ).astype(BF)
            kg_ref[s, :, at : at + LANES] = nt(jnp.concatenate(k_angles, axis=1).astype(BF), freq)
            vg_ref[s, :, at : at + LANES] = jnp.where(
                own_lanes(v_grads[0].shape, 0), v_grads[0], v_grads[1]
            )
        kcol_ref[s] = kcol

    each(seqs, one)


def products_kernel(
    x_ref, wqkv_ref, mixed_ref, low_ref, n1_ref, qg_ref, part_ref, xhat_ref, scale_ref, keep_ref, *send_refs
):
    width = low_ref.shape[1]
    part_ref[...] = nt(qg_ref[...], wqkv_ref[:, :width])
    xhat, scale = norm_rows(x_ref[...])
    xhat_ref[...] = xhat
    scale_ref[...] = jnp.broadcast_to(scale, scale_ref.shape)
    for at, left_ref, right_ref in ((0, mixed_ref, low_ref), (width, n1_ref, qg_ref)):
        lanes = pl.ds(at, width)
        weight_grads(left_ref, right_ref, keep_ref.at[:, lanes], [ref.at[:, lanes] for ref in send_refs])


def cross_kernel(
    got_ref, swapped_ref, partner_home_ref, partner_away_ref, freq_ref, away_ref, home_ref, start_ref, pk_ref, v_ref,
    c_ref, a_ref, r_ref, kcol_ref,
    kg_ref, vg_ref, n1_ref,
    kv_ref, logit_ref, bias_ref, keep_ref, *send_refs,
):
    seqs, heads, length, _ = pk_ref.shape
    core = my_core()
    width = kg_ref.shape[2]
    bias_ref[...] = jnp.zeros_like(bias_ref)

    def one(s):
        tokens = aligned(s, length)
        c, a = c_ref[s], a_ref[s]
        tail = jnp.exp(c[length - 1 :] - c) * a
        lane = iota(c.shape, 1)
        lane_row = iota((1, c.shape[1]), 1)
        kcol = kcol_ref[s]
        ends = jnp.zeros((1, c.shape[1]), F32)
        for pair in range(heads // 2):
            at = pair * LANES
            freq = pair_frequencies(freq_ref, pair).astype(BF)
            after = jnp.where(s == core, got_ref[pair], swapped_ref[pair]).astype(F32)
            partner = jnp.where(s == core, partner_home_ref[pair], partner_away_ref[pair]).astype(F32)
            grads = [
                jnp.where(core == 1, a, b)
                for a, b in zip(unpack_states(after), join_states(partner, after))
            ]
            local = jnp.where(s == core, home_ref[pair], away_ref[pair]).astype(F32)
            reached = join_states(local, start_ref[s, pair].astype(F32))
            k_angles, v_grads = [], []
            for half in (0, 1):
                h = 2 * pair + half
                phi_k = pk_ref[s, h]
                v = with_ones(v_ref[s, :, at : at + LANES], half, True)
                grad_low = as_operand(grads[half], half)
                weight = tail[:, h : h + 1]
                k_angles.append(angle_grads(phi_k, nn(v.astype(BF), grad_low)) * weight)
                dv = nt(phi_k, grad_low) * weight
                v_grads.append(dv)
                kcol = kcol + jnp.where(lane == h, lane_sum(v * dv), 0.0)
                end = jnp.sum(lane_sum(grads[half] * reached[half]), axis=0, keepdims=True)
                ends = jnp.where(lane_row == h, end, ends)
            kg = kg_ref[s, :, at : at + LANES] + nt(
                jnp.concatenate(k_angles, axis=1).astype(BF), freq
            )
            vg = vg_ref[s, :, at : at + LANES] + jnp.where(
                own_lanes(v_grads[0].shape, 0), v_grads[0], v_grads[1]
            )
            kv_ref[tokens, at : at + LANES] = kg.astype(BF)
            kv_ref[tokens, width + at : width + at + LANES] = vg.astype(BF)
        keep_grad = running_sum(r_ref[s] - kcol, True) + ends
        logit_grad = a * keep_grad - (1.0 - a) * kcol
        logit_ref[tokens] = logit_grad.astype(BF)
        bias_ref[0:1] += jnp.sum(logit_grad, axis=0, keepdims=True)

    for i in range(seqs):
        one(i)
    weight_grads(n1_ref, kv_ref, keep_ref, send_refs)


def close_kernel(
    wqkv_ref, gw_ref, part_ref, xhat_ref, kv_ref, logit_ref, bias_ref, n1_ref, sums2_ref, dn1_ref, small_ref
):
    width = part_ref.shape[1]
    logit_low = logit_ref[...]
    dn1 = part_ref[...] + nt(kv_ref[...], wqkv_ref[:, width:]) + nn(logit_low, wide(gw_ref[...], 0))
    xhat = xhat_ref[...]
    dn1_ref[...] = dn1
    row = iota((8, width), 0)
    sums = jnp.where(row == 0, jnp.sum(dn1 * xhat, axis=0, keepdims=True), sums2_ref[...])
    sums = jnp.where(row == 1, jnp.sum(dn1, axis=0, keepdims=True), sums)
    bias = jnp.concatenate([bias_ref[0:1], jnp.zeros((1, width - LANES), F32)], axis=1)
    sums = jnp.where(row == 4, bias, sums)
    gates = tn(logit_low, n1_ref[...])[:8]
    stacked = jnp.concatenate([sums, gates, jnp.zeros((LANES - 16, width), F32)], axis=0)
    columns = jnp.transpose(stacked)
    rows = small_ref.shape[0]
    small_ref[...] = columns[:rows] + pltpu.roll(columns[rows:], 16, 1)


def input_kernel(gain_ref, dn1_ref, xhat_ref, scale_ref, dres_ref, dx_hbm, mark_ref, dx_ref, sem):
    mark_ref[...] = jnp.zeros_like(mark_ref)
    dx_ref[...] = dres_ref[...] + norm_rows_backward(dn1_ref[...], xhat_ref[...], scale_ref[:, :1], gain_ref[...])
    copy = pltpu.make_async_copy(dx_ref, dx_hbm, sem)
    copy.start()
    copy.wait()


def chain_kernel(me_ref, partner_ref, out_ref, *, reverse):
    core = my_core()
    lead = (core == 0) if reverse else (core == 1)
    for pair in range(out_ref.shape[0]):
        mine, other = me_ref[pair].astype(F32), partner_ref[pair].astype(F32)
        first = jnp.where(lead, mine, other)
        second = jnp.where(lead, other, mine)
        none = jnp.zeros((1, 1), F32)
        main, rest = pack_states(*join_states(first, second), none, none)
        out_ref[pair, :LANES] = main
        out_ref[pair, LANES:] = rest


def widen(v):
    main, last = v[:, :-LANES].astype(F32), v[:, -LANES:].astype(F32)
    last = jnp.where(iota(last.shape, 1) < LANES // 2, last + pltpu.roll(last, LANES // 2, 1), 0.0)
    return jnp.concatenate([main, last], axis=1)


def narrow(v):
    main, last = v[:, :-LANES].astype(BF), v[:, -LANES:]
    high, low = two_terms(last)
    last = high.astype(F32) + pltpu.roll(low.astype(F32), LANES // 2, 1)
    return jnp.concatenate([main, last.astype(BF)], axis=1)


def link_bit(link):
    return my_chip() if link is None else (lax.axis_index("dp") // (1 << link)) % 2


def piece_number(links):
    number = 0
    for of_zero, of_one in links:
        bit = link_bit(of_zero)
        if of_one != of_zero:
            bit = jnp.where(my_core() == 0, bit, link_bit(of_one))
        number = 2 * number + bit
    return number


def pick(pieces, number):
    taken = pieces[0]
    for at in range(1, len(pieces)):
        taken = jnp.where(number == at, pieces[at], taken)
    return taken


def share_out(total, links, mine_ref, send_refs):
    rows = mine_ref.shape[0]
    pieces = [total[at : at + rows] for at in range(0, total.shape[0], rows)]
    number = piece_number(links)
    mine_ref[...] = pick(pieces, number)
    for k, send_ref in enumerate(send_refs):
        send_ref[...] = narrow(pick(pieces, number ^ (k + 1)))


def early_kernel(keep_ref, *refs, links):
    *got_refs, mine_ref, send_ref = refs
    rows = mine_ref.shape[0]
    total = keep_ref[...] + jnp.concatenate([ref[...].astype(F32) for ref in got_refs], axis=0)
    number = piece_number(links)
    pieces = [total[:rows], total[rows:]]
    mine_ref[...] = pick(pieces, number)
    send_ref[...] = pick(pieces, number ^ 1).astype(BF)


def late_kernel(early_ref, early_got_ref, keep_ref, *refs, links):
    *got_refs, small_ref, mine_ref, send_ref = refs
    before = early_ref.shape[1]
    mine_ref[:, :before] = early_ref[...] + early_got_ref[...].astype(F32)
    total = keep_ref[...] + jnp.concatenate([ref[...].astype(F32) for ref in got_refs], axis=0)
    total = jnp.concatenate([total, small_ref[...]], axis=1)
    share_out(total, links, mine_ref.at[:, pl.ds(before, total.shape[1])], [send_ref])


def meet_kernel(keep_ref, got_ref, mine_ref, send_ref, *, links):
    before = keep_ref.shape[1] - got_ref.shape[1]
    second = keep_ref[:, before:] + widen(got_ref[...])
    share_out(jnp.concatenate([keep_ref[:, :before], second], axis=1), links, mine_ref, [send_ref])


def part_kernel(keep_ref, got_ref, mine_ref, send_ref, *, links):
    share_out(keep_ref[...] + widen(got_ref[...]), links, mine_ref, [send_ref])


def whole_kernel(keep_ref, got_ref, out_ref):
    out_ref[...] = narrow(keep_ref[...] + widen(got_ref[...]))


def sum_kernel(mine_ref, got_ref, out_ref):
    out_ref[...] = narrow(widen(mine_ref[...]) + widen(got_ref[...]))


def split_group_kernel(mine_ref, got_ref, first_ref, second_ref, *, links):
    mine, got = mine_ref[...], got_ref[...]
    high = piece_number(links) == 1
    first_ref[...] = jnp.where(high, got, mine)
    second_ref[...] = jnp.where(high, mine, got)


def group_kernel(*refs, links):
    pieces = [ref[...].astype(F32) for ref in refs[:-1]]
    number = piece_number(links)
    both = [pick(pieces, number ^ at) for at in range(len(pieces))]
    refs[-1][...] = jnp.concatenate(both, axis=0).astype(BF)


def piece_place(of_partner, far, links):
    core = my_core()
    core = 1 - core if of_partner else core
    high = jnp.where(core == 0, link_bit(links[0]), link_bit(links[1]))
    return 2 * core + (1 - high if far else high)


def write_pieces(pieces, places, qkv_hbm, wo_hbm, qkv_ref, wo_ref, sems):
    rows, width = pieces[0].shape[0], wo_hbm.shape[1]
    copies = []
    for at, (piece_ref, place) in enumerate(zip(pieces, places)):
        own = slice(at * rows, (at + 1) * rows)
        wo_ref[own] = piece_ref[:, :width].astype(F32)
        qkv_ref[own] = piece_ref[:, width:-LANES].astype(F32)
        for which, (ref, hbm) in enumerate(((wo_ref, wo_hbm), (qkv_ref, qkv_hbm))):
            there = hbm.at[aligned(place, rows)]
            copies.append(pltpu.make_async_copy(ref.at[pl.ds(at * rows, rows)], there, sems.at[at, which]))
            copies[-1].start()
    return copies


def write_near_kernel(mine1_ref, mine2_ref, other1_ref, other2_ref, qkv_hbm, wo_hbm, mark_ref, qkv_ref, wo_ref, sems, *, links):
    mark_ref[...] = jnp.zeros_like(mark_ref)
    mine, other = 2 * piece_place(False, False, links), 2 * piece_place(True, False, links)
    pieces, places = (mine1_ref, mine2_ref, other1_ref, other2_ref), (mine, mine + 1, other, other + 1)
    for copy in write_pieces(pieces, places, qkv_hbm, wo_hbm, qkv_ref, wo_ref, sems):
        copy.wait()


def write_far_kernel(*refs, links):
    near, far, outs = refs[:4], refs[4:8], refs[10:]
    qkv_hbm, wo_hbm, gate_hbm, *norm_hbm, bias_hbm, qkv_ref, wo_ref, small_ref, bias_ref, columns_ref, sems, small_sems = outs
    rows = far[0].shape[0]
    for pieces, is_far in ((near, False), (far, True)):
        for at in range(4):
            place = 2 * piece_place(at > 1, is_far, links) + at % 2
            columns_ref[aligned(place, rows)] = pieces[at][:, -LANES:].astype(F32)
    half = columns_ref.shape[0] // 2
    columns = columns_ref[:half] + columns_ref[half:]
    columns = columns + pltpu.roll(columns, LANES // 2, 1)
    stacked = jnp.transpose(columns)
    small_ref[:, :half] = stacked[:16]
    small_ref[:, half:] = stacked[16:32]
    heads = gate_hbm.shape[0]
    bias_ref[...] = stacked[4:5, : bias_ref.shape[1]]
    there = [(8, heads, gate_hbm)] + [(row, 1, hbm) for row, hbm in enumerate(norm_hbm)]
    copies = []
    for at, (row, count, hbm) in enumerate(there):
        copies.append(pltpu.make_async_copy(small_ref.at[pl.ds(row, count)], hbm, small_sems.at[at]))
    copies.append(pltpu.make_async_copy(bias_ref, bias_hbm, small_sems.at[len(there)]))
    for copy in copies:
        copy.start()
    mine, other = 2 * piece_place(False, True, links), 2 * piece_place(True, True, links)
    copies += write_pieces(far, (mine, mine + 1, other, other + 1), qkv_hbm, wo_hbm, qkv_ref, wo_ref, sems)
    for copy in copies:
        copy.wait()


def in_hbm(out):
    return getattr(out, "memory_space", None) == pltpu.HBM


def out_spec(out):
    return pl.BlockSpec(memory_space=pltpu.HBM if in_hbm(out) else pltpu.VMEM)


class Job:
    def __init__(self, kernel, name, operands, outs, use):
        self.kernel, self.name, self.operands, self.outs, self.use = kernel, name, operands, outs, use


class Order:
    def __init__(self):
        self.last = ()

    def call(self, kernel, name, given, kept, outs, scratch=(), wait=(), hbm=False, onto=(), onto_vmem=False):
        wait = (*self.last, *wait)
        space = pltpu.HBM if hbm else pltpu.VMEM
        given = [pltpu.with_memory_space_constraint(a, space) if hbm else a for a in given]
        kept = [pltpu.with_memory_space_constraint(a, pltpu.VMEM) for a in kept]
        if onto_vmem:
            onto = [pltpu.with_memory_space_constraint(a, pltpu.VMEM) for a in onto]
        got = pl.pallas_call(
            lambda *refs: kernel(*refs[len(wait) :]),
            out_shape=outs,
            in_specs=[pl.BlockSpec(memory_space=pl.ANY)] * len(wait)
            + [pl.BlockSpec(memory_space=space)] * len(given)
            + [pl.BlockSpec(memory_space=pltpu.VMEM)] * len(kept)
            + [pl.BlockSpec(memory_space=pltpu.VMEM if onto_vmem else pltpu.HBM)] * len(onto),
            input_output_aliases={len(wait) + len(given) + len(kept) + at: at for at in range(len(onto))},
            out_specs=jax.tree.map(out_spec, outs),
            scratch_shapes=scratch,
            compiler_params=pltpu.CompilerParams(vmem_limit_bytes=VMEM_BYTES),
            cost_estimate=pl.CostEstimate(flops=0, bytes_accessed=0, transcendentals=0),
            name=name,
        )(*wait, *given, *kept, *onto)
        inside = [a for a, out in zip(jax.tree.leaves(got), jax.tree.leaves(outs)) if not in_hbm(out)]
        if inside:
            self.last = (min(inside, key=lambda a: a.size),)
        return got


    def run(self, *jobs):
        takes = [len(job.operands) for job in jobs]
        gives = [len(job.outs) for job in jobs]

        def kernel(*refs):
            given, made = refs[: sum(takes)], refs[sum(takes) :]
            for job, take, give in zip(jobs, takes, gives):
                job.kernel(*given[:take], *made[:give])
                given, made = given[take:], made[give:]

        operands = [a for job in jobs for a in job.operands]
        outs = tuple(out for job in jobs for out in job.outs)
        got = list(self.call(kernel, "_".join(job.name for job in jobs), operands, (), outs))
        for job, give in zip(jobs, gives):
            job.use(*got[:give])
            got = got[give:]


def kept(shape, dtype):
    return pltpu.VMEM(shape, dtype)


def shaped(shape, dtype):
    return jax.ShapeDtypeStruct(shape, dtype)


def core_swap(v):
    return jax.tree.map(lambda a: lax.ppermute(a, "mp", [(i, i ^ 1) for i in range(4)]), v)


def chip_swap(v):
    return jax.tree.map(lambda a: lax.ppermute(a, "mp", [(i, i ^ 2) for i in range(4)]), v)


def send_along(v, links):
    way = []
    for place in range(lax.axis_size("dp")):
        for spot in range(4):
            to = [place, spot]
            for link in links:
                link = link[spot % 2]
                to = [to[0], to[1] ^ 2] if link is None else [to[0] ^ (1 << link), to[1]]
            way.append((4 * place + spot, 4 * to[0] + to[1]))
    return lax.ppermute(v, ("dp", "mp"), way)


class Gather:
    def __init__(self, keep, got):
        self.first = (keep, *got)
        bits = list(range(lax.axis_size("dp").bit_length() - 1))
        self.links = [(None, 0), (0, None)] + [(bit, bit) for bit in bits[1:]]
        last = len(self.links) - 1
        self.steps = [functools.partial(self.share, at) for at in range(1, last)] + [self.swap]
        self.steps += [functools.partial(self.collect, at) for at in range(last, 0, -1)]

    def next(self):
        return self.steps.pop(0)()

    def early(self):
        return self.halve(early_kernel, "early", self.first, 0)

    def late(self, keep, got, small):
        sent = keep.shape[1] + LANES
        return self.halve(late_kernel, "late", (*self.take(), keep, *got, small), 0, sent)

    def halve(self, kernel, name, operands, at, sent=0):
        rows, columns = operands[0].shape
        shapes = (rows // 2, columns), (rows // 2, columns)
        if sent:
            shapes = (rows, columns + sent), (rows, sent)

        def use(keep, sent):
            self.keep, self.got = [keep], [send_along(sent, [self.links[at]])]

        kernel = functools.partial(kernel, links=[self.links[at]])
        return Job(kernel, name, operands, (shaped(shapes[0], F32), shaped(shapes[1], BF)), use)

    def take(self):
        pairs = [a for pair in zip(self.keep, self.got) for a in pair]
        self.keep, self.got = [], []
        return pairs

    def share(self, at):
        operands = self.take()
        if at > 1:
            return self.halve(part_kernel, "part", operands, at)
        return self.halve(meet_kernel, "meet", operands, at)

    def swap(self):
        operands = self.take()

        def use(keep):
            self.keep, self.got = [keep], [send_along(keep, [self.links[-1]])]

        return Job(whole_kernel, "whole", operands, (shaped(operands[0].shape, BF),), use)

    def collect(self, at):
        operands = self.take()
        rows, columns = operands[0].shape
        if at == 1:
            links = [self.links[at]]

            def use_parts(*parts):
                self.keep, self.got = list(parts), [send_along(part, [self.links[0]]) for part in parts]

            kernel = functools.partial(split_group_kernel, links=links)
            return Job(kernel, "split_group", operands, (shaped((rows, columns), BF),) * 2, use_parts)
        if at == len(self.links) - 1:
            kernel, name = sum_kernel, "sum"
        else:
            kernel, name, rows = functools.partial(group_kernel, links=[self.links[at]]), "group", 2 * rows

        def use(keep):
            self.keep, self.got = [keep], [send_along(keep, [self.links[at - 1]])]

        return Job(kernel, name, operands, (shaped((rows, columns), BF),), use)


class Stream:
    def __init__(self, *first):
        self.first = first
        bits = list(range(lax.axis_size("dp").bit_length() - 1))
        self.bits = [(0, 1), (1, 0)] + [(bit, bit) for bit in bits[2:]]
        self.back = [(1, 1), (0, 0)] + self.bits[2:]
        self.steps = [self.start]
        self.steps += [functools.partial(self.halve, bits) for bits in self.bits[1:-1]]
        self.steps += [self.third, self.fourth]
        self.steps += [functools.partial(self.double, at) for at in range(len(bits), 0, -1)]

    def next(self):
        return self.steps.pop(0)()

    def split(self, kernel, name, operands, shape, bits):
        def use(keep, sent):
            self.keep, self.got = keep, send_along(sent, [bits])

        return Job(kernel, name, operands, (shaped(shape, F32), shaped(shape, BF)), use)

    def start(self):
        bits = self.bits[0]
        rows, columns = self.first[0].shape
        kernel = functools.partial(first_kernel, bits=bits)
        return self.split(kernel, "first", self.first, (2, rows // 2, columns), bits)

    def halve(self, bits):
        _, rows, columns = self.keep.shape
        kernel = functools.partial(halve_kernel, bits=bits)
        return self.split(kernel, "halve", (self.keep, self.got), (2, rows // 2, columns), bits)

    def third(self):
        _, rows, columns = self.keep.shape
        bit = self.bits[-1][0]
        kernel = functools.partial(third_kernel, bit=bit)
        return self.split(kernel, "third", (self.keep, self.got), (2, rows // 2, columns), (bit, None))

    def fourth(self):
        bit = self.bits[-1][0]
        kernel = functools.partial(fourth_kernel, bit=bit)
        return self.split(kernel, "fourth", (self.keep, self.got), self.keep.shape[1:], (None, bit))

    def double(self, at):
        if at == len(self.bits):
            kernel, name, shape = add_kernel, "add", self.keep.shape
        else:
            kernel, name = functools.partial(join_kernel, bits=self.back[at]), "join"
            shape = (2 * self.keep.shape[0], self.keep.shape[1])

        def use(keep):
            self.keep, self.got = keep, send_along(keep, [self.back[at - 1]])

        return Job(kernel, name, (self.keep, self.got), (shaped(shape, BF),), use)

    def finish(self, order, outs):
        kernel = functools.partial(final_kernel, bits=self.back[0])
        rows, columns = self.keep.shape
        scratch = [pltpu.VMEM((2 * rows, columns), F32), pltpu.SemaphoreType.DMA((2,))]
        outs = (*outs, shaped((8, LANES), F32))
        return order.call(kernel, "final", (self.keep, self.got), (), outs, scratch)[:2]


def after(v, *others):
    return lax.optimization_barrier((v, others))[0]


def exchange(order, home, partner, reverse, wait=()):
    kernel = functools.partial(chain_kernel, reverse=reverse)
    total = order.call(kernel, "chain", (home, partner), (), shaped(home.shape, BF), wait=wait)
    return total, lax.ppermute(total, "mp", [(2, 0), (3, 1)] if reverse else [(0, 2), (1, 3)])


def per_device(
    layer_input,
    qkv_weight,
    gate_weight,
    gate_bias,
    out_weight,
    inner_weight,
    outer_weight,
    leading_norm_gain,
    leading_norm_bias,
    trailing_norm_gain,
    trailing_norm_bias,
    random_features,
    output_grad,
):
    seqs, length, width = layer_input.shape
    heads, head, feat = random_features.shape
    pairs = heads // 2
    count = seqs * length
    hidden = inner_weight.shape[1]
    bias = gate_bias.reshape(1, heads)
    gain1, shift1 = leading_norm_gain.reshape(1, width), leading_norm_bias.reshape(1, width)
    gain2, shift2 = trailing_norm_gain.reshape(1, width), trailing_norm_bias.reshape(1, width)

    n_dp = lax.axis_size("dp")
    order = Order()
    halves = order.call(
        pack_kernel,
        "pack",
        (inner_weight, outer_weight),
        (),
        shaped((2, width // 2, hidden), BF),
        [pltpu.SemaphoreType.DMA((2,))],
        hbm=True,
    )
    half_chip = chip_swap(halves)
    inner_core, outer_core = core_swap(inner_weight), core_swap(outer_weight)

    by_seq = (seqs, length, width)
    gates = (seqs, length, LANES)
    states = (pairs, LANES + EXTRA, 2 * feat)
    gate_rows = jnp.transpose(gate_weight)
    sources = (layer_input, qkv_weight, gate_rows, bias, gain1, shift1, random_features)
    normed1, values, c, admit, c_row, a_row, phi_k, away, home = order.call(
        keys_kernel,
        "keys",
        sources,
        (),
        (
            kept((count, width), BF),
            kept(by_seq, F32),
            kept(gates, F32),
            kept(gates, F32),
            kept((seqs, heads, length), F32),
            kept((seqs, heads, length), F32),
            kept((seqs, heads, length, 2 * feat), BF),
            kept(states, BF),
            kept(states, BF),
        ),
        [pltpu.VMEM((width, 2 * width) if a is qkv_weight else a.shape, a.dtype) for a in sources]
        + [pltpu.SemaphoreType.DMA((len(sources),))],
        hbm=True,
    )
    partner_home, partner_away = core_swap(away), core_swap(home)
    total, got = exchange(order, home, partner_home, False)
    half_chip = after(half_chip, total)
    half_twin = lax.ppermute(half_chip, "dp", [(i, i ^ 1) for i in range(n_dp)])

    phi_q, scores, num = order.call(
        scores_kernel,
        "scores",
        (qkv_weight, random_features),
        (normed1, phi_k, values, c, c_row, a_row),
        (
            kept((seqs, heads, length, 2 * feat), BF),
            kept((seqs, heads, length, 2 * length), BF),
            kept((seqs, heads, length, LANES), F32),
        ),
        wait=(half_chip,),
    )
    got = after(got, num)
    swapped = core_swap(got)
    half_both = core_swap(half_chip)
    full, start, mixed_low, resid, normed2, sden, inverse, xhat2, scale2 = order.call(
        mix_kernel,
        "mix",
        (layer_input, got, swapped, partner_home, partner_away, out_weight, gain2, shift2),
        (phi_q, c, num),
        (
            kept((seqs, heads, length, LANES), F32),
            kept((seqs, *states), BF),
            kept(by_seq, BF),
            kept(by_seq, F32),
            kept(by_seq, BF),
            kept(gates, F32),
            kept(gates, F32),
            kept(by_seq, F32),
            kept(gates, F32),
        ),
    )

    normed2, mixed_low = (a.reshape(count, width) for a in (normed2, mixed_low))
    shape = (count, width)
    grads = (width + hidden, width)
    out_part, dn2, out_low, keep0, send0 = order.call(
        feed_near_kernel,
        "feed_near",
        (output_grad.reshape(shape), inner_weight, outer_weight, inner_core, outer_core),
        (normed2, resid.reshape(shape)),
        (kept(shape, F32), kept(shape, F32), kept(shape, BF), shaped(grads, F32), shaped(grads, BF)),
    )
    got0 = core_swap(send0)
    half_twin = after(half_twin, out_low)
    half_both_twin = core_swap(half_twin)
    far = pltpu.VMEM((2, width, hidden), BF)
    out_part, dn2, keep1 = order.call(
        feed_far_kernel,
        "feed_chip",
        (half_chip, half_twin),
        (normed2, out_low, out_part, dn2),
        (kept(shape, F32), kept(shape, F32), shaped(grads, F32)),
        [far],
    )
    layer_out, dn2, send1 = order.call(
        feed_last_kernel,
        "feed_both",
        (half_both, half_both_twin),
        (normed2, out_low, out_part, dn2),
        (pltpu.HBM(shape, F32), kept(shape, F32), shaped(grads, BF)),
        [far, pltpu.VMEM(shape, F32), pltpu.SemaphoreType.DMA],
    )
    got1 = core_swap(send1)
    stream = Stream(keep0, keep1, got0, got1)

    given = (output_grad, gain2, out_weight)
    inside = (dn2.reshape(by_seq), xhat2, scale2, full, sden, inverse, phi_q, c)
    made = (
        kept(by_seq, F32),
        kept((count, width), BF),
        kept((8, width), F32),
        kept((seqs, heads, length, 2 * LANES), BF),
        kept(gates, F32),
    )
    *begun, packed_grads = order.call(turn_first_kernel, "turn_first", given, inside, (*made, kept(states, BF)))
    order.run(stream.next())
    dres, low, sums2, num_grads, r, away_grads, home_grads = order.call(
        turn_second_kernel,
        "turn_second",
        given,
        (*inside, packed_grads),
        (*made, kept(states, BF), kept(states, BF)),
        onto=begun,
        onto_vmem=True,
    )
    partner_home_grads, partner_away_grads = core_swap(away_grads), core_swap(home_grads)
    _, got_grads = exchange(order, home_grads, partner_home_grads, True)

    q_grad, k_part, v_part, k_col = order.call(
        back_kernel,
        "back",
        (random_features,),
        (phi_q, phi_k, values, num_grads, scores, c, c_row, a_row, start),
        (
            kept((count, width), BF),
            kept(by_seq, F32),
            kept(by_seq, F32),
            kept(gates, F32),
        ),
    )
    dn1_part, xhat1, scale1, keep1, *send1 = order.call(
        products_kernel,
        "products",
        (layer_input.reshape(shape), qkv_weight),
        (mixed_low, low, normed1, q_grad),
        (
            kept(shape, F32),
            kept(shape, F32),
            kept((count, LANES), F32),
            shaped((width // 2, 2 * width), F32),
            *[shaped((width // 4, 2 * width), BF)] * 2,
        ),
    )
    gather = Gather(keep1, core_swap(send1))
    got_grads = after(got_grads, keep1)
    swapped_grads = core_swap(got_grads)

    order.run(stream.next())
    order.run(gather.early())
    kv_grad, logit_low, bias_sum, keep2, *send2 = order.call(
        cross_kernel,
        "cross",
        (got_grads, swapped_grads, partner_home_grads, partner_away_grads, random_features),
        (away, home, start, phi_k, values, c, admit, r, k_col, k_part, v_part, normed1),
        (
            kept((count, 2 * width), BF),
            kept((count, LANES), BF),
            kept((8, LANES), F32),
            shaped((width // 2, 2 * width), F32),
            *[shaped((width // 8, 2 * width), BF)] * 4,
        ),
    )
    got2 = core_swap(send2)
    while len(stream.steps) > len(stream.bits) + 1:
        order.run(stream.next())
    dn1, small = order.call(
        close_kernel,
        "close",
        (qkv_weight, gate_rows),
        (dn1_part, xhat1, kv_grad, logit_low, bias_sum, normed1, sums2),
        (kept(shape, F32), shaped((width // 2, LANES), F32)),
    )
    order.run(gather.late(keep2, got2, small))
    dx, _ = order.call(
        input_kernel,
        "input",
        (gain1,),
        (dn1, xhat1, scale1, dres.reshape(shape)),
        (pltpu.HBM(shape, F32), shaped((8, LANES), F32)),
        [pltpu.VMEM(shape, F32), pltpu.SemaphoreType.DMA],
    )
    while len(gather.steps) > 5:
        order.run(gather.next())
    while len(stream.steps) > 3:
        order.run(stream.next())
    order.run(gather.next(), stream.next())
    order.run(gather.next(), stream.next())
    order.run(gather.next())
    order.run(gather.next(), stream.next())
    order.run(gather.next())
    inner_total, outer_total = stream.finish(order, (pltpu.HBM((width, hidden), F32), pltpu.HBM((hidden, width), F32)))
    links = gather.links[0]
    mine = gather.keep
    near = (*mine, *core_swap(mine))
    scratch = [
        pltpu.VMEM((width // 2, 3 * width), F32), pltpu.VMEM((width // 2, width), F32), pltpu.SemaphoreType.DMA((4, 2)),
    ]
    big = (pltpu.HBM((width, 3 * width), F32), pltpu.HBM((width, width), F32))
    *begun, _ = order.call(
        functools.partial(write_near_kernel, links=links),
        "write_near",
        near,
        (),
        (*big, shaped((8, LANES), F32)),
        scratch,
    )
    got = after(gather.got, order.last)
    far = (*got, *core_swap(got))
    qkv_grad, wo_grad, gate_grad, *norm_grads, bias_grad = order.call(
        functools.partial(write_far_kernel, links=links),
        "write_far",
        (*near, *far),
        (),
        (*big, pltpu.HBM((heads, width), F32), *[pltpu.HBM((1, width), F32)] * 4, pltpu.HBM((1, heads), F32)),
        [
            *scratch[:2], pltpu.VMEM((16, width), F32), pltpu.VMEM((1, heads), F32), pltpu.VMEM((width, LANES), F32),
            scratch[2], pltpu.SemaphoreType.DMA((6,)),
        ],
        onto=begun,
    )
    return (
        layer_out.reshape(by_seq),
        dx.reshape(by_seq),
        qkv_grad,
        jnp.transpose(gate_grad),
        bias_grad.reshape(heads),
        wo_grad,
        inner_total,
        outer_total,
        *(a.reshape(width) for a in norm_grads),
    )


def solution(mesh):
    in_specs = (
        P("dp", "mp", None),
        P(),
        P(),
        P(),
        P(),
        P(None, "mp"),
        P("mp", None),
        P(),
        P(),
        P(),
        P(),
        P(),
        P("dp", "mp", None),
    )
    out_specs = (
        P("dp", "mp", None),
        P("dp", "mp", None),
        P(),
        P(),
        P(),
        P(),
        P(None, "mp"),
        P("mp", None),
        P(),
        P(),
        P(),
        P(),
    )
    return jax.shard_map(
        per_device, mesh=mesh, in_specs=in_specs, out_specs=out_specs, check_vma=False
    )
```
